32 devices in a mesh: sp: 16 (over z, y, core), tp: 2 (over x).
Axes of the slice: x: 2, y: 2, z: 4, core: 2. Of those that a mesh axis runs over, the one named last changes fastest.
Arguments:
- patches: bfloat16 [2048, 1536], P('sp'), may hold values from -6 to 6
- caption: bfloat16 [256, 4096], replicated, may hold values from -6 to 6
- band_table: float32 [16, 1024], P(None, 'sp'), may hold values from -6 to 6
- block_item: int32 [64], replicated, may hold values from 0 to 1, as said below
- item_band: int32 [2], replicated, may hold values from 0 to 15
- positions: int32 [2, 2048], P(None, 'sp'), may hold values from 0 to 63
- out_grad: bfloat16 [2048, 1536], P('sp'), may hold values from -6 to 6
- w_query: bfloat16 [1536, 1536], P('sp', 'tp'), may hold values from -0.15625 to 0.15625
- w_key: bfloat16 [1536, 1536], P('sp', 'tp'), may hold values from -0.15625 to 0.15625
- w_value: bfloat16 [1536, 1536], P('sp', 'tp'), may hold values from -0.15625 to 0.15625
- w_out: bfloat16 [1536, 1536], P('tp', 'sp'), may hold values from -0.15625 to 0.15625
- w_gate: bfloat16 [1536, 4096], P('sp', 'tp'), may hold values from -0.15625 to 0.15625
- w_up: bfloat16 [1536, 4096], P('sp', 'tp'), may hold values from -0.15625 to 0.15625
- w_down: bfloat16 [4096, 1536], P('tp', 'sp'), may hold values from -0.09375 to 0.09375
- w_ckey: bfloat16 [4096, 1536], P('sp', 'tp'), may hold values from -0.09375 to 0.09375
- w_cvalue: bfloat16 [4096, 1536], P('sp', 'tp'), may hold values from -0.09375 to 0.09375
- w_ada: bfloat16 [1024, 6144], P('sp'), may hold values from -0.1875 to 0.1875
- b_ada: float32 [6144], replicated, may hold values from -3 to 3
- g_attn_in: float32 [1536], replicated, may hold values from 0.5 to 1.5
- g_attn_out: float32 [1536], replicated, may hold values from 0.5 to 1.5
- g_ffn_in: float32 [1536], replicated, may hold values from 0.5 to 1.5
- g_ffn_out: float32 [1536], replicated, may hold values from 0.5 to 1.5
- g_query: float32 [1536], P('tp'), may hold values from 0.5 to 1.5
- g_key: float32 [1536], P('tp'), may hold values from 0.5 to 1.5
- g_ckey: float32 [1536], P('tp'), may hold values from 0.5 to 1.5
- cross_gate: float32 [24], P('tp'), may hold values from -1.5 to 1.5
Outputs:
- output: float32 [2048, 1536], P('sp')
- d_patches: float32 [2048, 1536], P('sp')
- d_w_query: float32 [1536, 1536], P('sp', 'tp')
- d_w_key: float32 [1536, 1536], P('sp', 'tp')
- d_w_value: float32 [1536, 1536], P('sp', 'tp')
- d_w_out: float32 [1536, 1536], P('tp', 'sp')
- d_w_gate: float32 [1536, 4096], P('sp', 'tp')
- d_w_up: float32 [1536, 4096], P('sp', 'tp')
- d_w_down: float32 [4096, 1536], P('tp', 'sp')
- d_w_ckey: float32 [4096, 1536], P('sp', 'tp')
- d_w_cvalue: float32 [4096, 1536], P('sp', 'tp')
- d_w_ada: float32 [1024, 6144], P('sp')
- d_b_ada: float32 [6144], replicated
- d_g_attn_in: float32 [1536], replicated
- d_g_attn_out: float32 [1536], replicated
- d_g_ffn_in: float32 [1536], replicated
- d_g_ffn_out: float32 [1536], replicated
- d_g_query: float32 [1536], P('tp')
- d_g_key: float32 [1536], P('tp')
- d_g_ckey: float32 [1536], P('tp')
- d_cross_gate: float32 [24], P('tp')
- d_band_table: float32 [16, 1024], P(None, 'sp')
The draws below stay inside these ranges and needn't reach their ends.
Inputs may be any that keep to these rules, and one draw needn't show every extreme that they name: `block_item`: every item has at least one block. Items occupy consecutive places in the order that lists each device's first block of 32 tokens along sp, then each device's second block, and so on; one item holds a block on every device of sp, which one varies from draw to draw.
All inputs are finite; a program needn't handle non-finite values.
Results may differ from the reference program's by a relative error of at most 0.025.
Values may be sent and summed in bfloat16 or wider, within the bound.
A program may use at most 384 MiB of HBM per device.

```python
import math
import jax
import jax.numpy as jnp
from jax import lax

D = 1536
H = 24
FF = 4096
TD = 4096
CDIM = 1024
TXT = 256
BANDS = 16
ITEMS = 2
BLK = 32
TOK_DEV = 128
TOKENS = 2048


def draw_block_item(key, part):
    key = jax.random.fold_in(key, 7)
    key_long, key_cuts, key_place = jax.random.split(key, 3)
    total_blocks = TOKENS // BLK
    cycle_size = TOKENS // TOK_DEV
    per_dev = TOK_DEV // BLK
    least_long = max(cycle_size, total_blocks // ITEMS)
    longest = least_long + jax.random.randint(key_long, (), 0, total_blocks - least_long - ITEMS + 2, dtype=jnp.int32)
    remain = total_blocks - longest
    places = jnp.arange(total_blocks, dtype=jnp.int32)
    scores = jax.random.randint(key_cuts, (total_blocks,), 0, 1 << 16, dtype=jnp.int32) * total_blocks + places
    usable = (places >= 1) & (places < remain)
    scores = jnp.where(usable, scores, jnp.int32(1 << 30))
    cut_points = jnp.sort(jnp.sort(scores)[:ITEMS - 2] % total_blocks)
    boundary = jnp.concatenate([jnp.zeros((1,), jnp.int32), cut_points.astype(jnp.int32), jnp.reshape(remain, (1,)).astype(jnp.int32)])
    short_lens = boundary[1:] - boundary[:-1]
    where_long = jax.random.randint(key_place, (), 0, ITEMS, dtype=jnp.int32)
    item_order = jnp.arange(ITEMS, dtype=jnp.int32)
    short_pick = jnp.clip(item_order - (item_order > where_long).astype(jnp.int32), 0, ITEMS - 2)
    lengths = jnp.where(item_order == where_long, longest, short_lens[short_pick])
    item_ends = jnp.cumsum(lengths)
    logical = jnp.sum((places[:, None] >= item_ends[None, :]).astype(jnp.int32), axis=1).astype(jnp.int32)
    device = places // per_dev
    slot_idx = places % per_dev
    return logical[slot_idx * cycle_size + device]


def with_ends(values, own_key, smallest, largest):
    index_at = [jax.random.randint(jax.random.fold_in(own_key, axis), (), 0, length) for axis, length in enumerate(values.shape)]
    widest = values.shape.index(max(values.shape))
    next_to = index_at[:widest] + [(index_at[widest] + 1) % values.shape[widest]] + index_at[widest + 1:]
    return values.at[tuple(index_at)].set(smallest).at[tuple(next_to)].set(largest)


def with_spikes(entries, rng, source, target, parts, factor):
    def block_of(dim):
        return (jnp.arange(entries.shape[dim]) // (entries.shape[dim] // parts)).reshape((-1,) + (1,) * (entries.ndim - 1 - dim))

    near = jax.random.permutation(rng, parts)[block_of(target)]
    second = (block_of(target) + parts // 2) % parts
    return jnp.where((block_of(source) == near) | (block_of(source) == second), factor * entries, entries)


def block_levels(stream_key, extent, pieces, least, high):
    loudness, own = 1.0, jax.random.fold_in(stream_key, 6)
    for position, parts in pieces:
        heights = jnp.exp(jax.random.uniform(jax.random.fold_in(own, position), (parts,), jnp.float32, least / len(pieces), high / len(pieces)))
        loudness = loudness * jnp.repeat(heights, extent[position] // parts).reshape([-1 if axis == position else 1 for axis in range(len(extent))])
    return loudness


def gaussian(stream_key, extent, width, most, shards=(), held_as=jnp.bfloat16):
    entries = width * jax.random.normal(stream_key, extent, jnp.float32)
    if shards:
        entries = entries * block_levels(stream_key, extent, shards, -0.22, 0.18)
    return jnp.clip(entries, -most, most).astype(held_as)


def heavy_noise(stream_key, dims, spread, bound, cuts, heavy, held_as=jnp.bfloat16):
    entries = spread * jax.random.normal(stream_key, dims, jnp.float32)
    if cuts:
        entries = entries * block_levels(stream_key, dims, cuts, -0.22, 0.18)
    return jnp.clip(with_spikes(entries, jax.random.fold_in(stream_key, 3), *heavy), -bound, bound).astype(held_as)


def setup_inputs(seed: int = 0) -> dict:
    splits = jax.random.split(jax.random.key(seed), 27)
    patches = heavy_noise(splits[0], (TOKENS, D), 1.0, 6.0, ((0, 16),), (0, 1, 16, 2.0))
    caption = gaussian(splits[1], (TXT, TD), 1.0, 6.0)
    band_table = gaussian(splits[2], (BANDS, CDIM), 1.0, 6.0, ((1, 16),), jnp.float32)
    block_item = draw_block_item(jax.random.fold_in(splits[26], 71), 0)
    item_band = jax.random.randint(splits[4], (ITEMS,), 0, BANDS).astype(jnp.int32)
    positions = with_ends(jax.random.randint(splits[5], (2, TOKENS), 0, 64), jax.random.fold_in(splits[5], 1), 0, 63).astype(jnp.int32)
    out_grad = heavy_noise(splits[6], (TOKENS, D), 1.0, 6.0, ((0, 16),), (0, 1, 16, 2.0))
    w_query = gaussian(splits[7], (D, D), D ** -0.5, 0.15625, ((0, 16), (1, 2)))
    w_key = gaussian(splits[8], (D, D), D ** -0.5, 0.15625, ((0, 16), (1, 2)))
    w_value = gaussian(splits[9], (D, D), D ** -0.5, 0.15625, ((0, 16), (1, 2)))
    w_out = gaussian(splits[10], (D, D), D ** -0.5, 0.15625, ((0, 2), (1, 16)))
    w_gate = gaussian(splits[11], (D, FF), D ** -0.5, 0.15625, ((0, 16), (1, 2)))
    w_up = gaussian(splits[12], (D, FF), D ** -0.5, 0.15625, ((0, 16), (1, 2)))
    w_down = gaussian(splits[13], (FF, D), FF ** -0.5, 0.09375, ((0, 2), (1, 16)))
    w_ckey = gaussian(splits[14], (TD, D), TD ** -0.5, 0.09375, ((0, 16), (1, 2)))
    w_cvalue = gaussian(splits[15], (TD, D), TD ** -0.5, 0.09375, ((0, 16), (1, 2)))
    w_ada = gaussian(splits[16], (CDIM, 4 * D), CDIM ** -0.5, 0.1875, ((0, 16),))
    b_ada = gaussian(splits[17], (4 * D,), 0.5, 3.0, (), jnp.float32)
    g_attn_in = jnp.clip(1.0 + 0.1 * jax.random.normal(splits[18], (D,), jnp.float32), 0.5, 1.5)
    g_attn_out = jnp.clip(1.0 + 0.1 * jax.random.normal(splits[19], (D,), jnp.float32), 0.5, 1.5)
    g_ffn_in = jnp.clip(1.0 + 0.1 * jax.random.normal(splits[20], (D,), jnp.float32), 0.5, 1.5)
    g_ffn_out = jnp.clip(1.0 + 0.1 * jax.random.normal(splits[21], (D,), jnp.float32), 0.5, 1.5)
    g_query = jnp.clip(1.0 + 0.1 * jax.random.normal(splits[22], (D,), jnp.float32), 0.5, 1.5)
    g_key = jnp.clip(1.0 + 0.1 * jax.random.normal(splits[23], (D,), jnp.float32), 0.5, 1.5)
    g_ckey = jnp.clip(1.0 + 0.1 * jax.random.normal(splits[24], (D,), jnp.float32), 0.5, 1.5)
    cross_gate = jnp.clip(jax.random.uniform(splits[25], (H,), jnp.float32, -1.5, 1.5) * block_levels(splits[25], (H,), ((0, 2),), -0.4, 0.0), -1.5, 1.5)
    return {"patches": patches, "caption": caption, "band_table": band_table, "block_item": block_item, "item_band": item_band, "positions": positions, "out_grad": out_grad, "w_query": w_query, "w_key": w_key, "w_value": w_value, "w_out": w_out, "w_gate": w_gate, "w_up": w_up, "w_down": w_down, "w_ckey": w_ckey, "w_cvalue": w_cvalue, "w_ada": w_ada, "b_ada": b_ada, "g_attn_in": g_attn_in, "g_attn_out": g_attn_out, "g_ffn_in": g_ffn_in, "g_ffn_out": g_ffn_out, "g_query": g_query, "g_key": g_key, "g_ckey": g_ckey, "cross_gate": cross_gate}


EPS = 1e-06
NEG = -1e+30
FREQ_BASE = 10000.0
HIGH = lax.Precision.HIGHEST

@jax.custom_vjp
def low(v):
    return lax.optimization_barrier(v.astype(jnp.bfloat16)).astype(jnp.float32)

@jax.custom_vjp
def low_back(v):
    return v

def low_keep(v):
    return (low(v), None)

def low_pass(kept, grad):
    return (grad,)

def back_keep(v):
    return (v, None)

def back_low(kept, grad):
    return (low(grad),)
low.defvjp(low_keep, low_pass)
low_back.defvjp(back_keep, back_low)

def matmul(left, right):
    return jnp.dot(left, right, precision=HIGH)

def normed(value):
    return value * lax.rsqrt(lax.optimization_barrier(jnp.mean(value * value, axis=-1, keepdims=True)) + EPS)

def rotate(value, cos_row, sin_row, cos_col, sin_col):
    quarter = value.shape[-1] // 4
    part_a = value[..., :quarter]
    part_b = value[..., quarter:2 * quarter]
    part_c = value[..., 2 * quarter:3 * quarter]
    part_e = value[..., 3 * quarter:]
    return jnp.concatenate([part_a * cos_row - part_b * sin_row, part_a * sin_row + part_b * cos_row, part_c * cos_col - part_e * sin_col, part_c * sin_col + part_e * cos_col], axis=-1)

def angles(positions):
    quarter = D // H // 4
    freqs = FREQ_BASE ** (-jnp.arange(quarter, dtype=jnp.float32) / quarter)
    row_angle = positions[0].astype(jnp.float32)[:, None] * freqs[None, :]
    col_angle = positions[1].astype(jnp.float32)[:, None] * freqs[None, :]
    return (jnp.cos(row_angle)[:, None, :], jnp.sin(row_angle)[:, None, :], jnp.cos(col_angle)[:, None, :], jnp.sin(col_angle)[:, None, :])

def reference(patches, caption, band_table, block_item, item_band, positions, out_grad, w_query, w_key, w_value, w_out, w_gate, w_up, w_down, w_ckey, w_cvalue, w_ada, b_ada, g_attn_in, g_attn_out, g_ffn_in, g_ffn_out, g_query, g_key, g_ckey, cross_gate):
    head_dim = D // H
    scale = 1.0 / math.sqrt(head_dim)
    token_item = jnp.repeat(block_item, BLK)
    cos_row, sin_row, cos_col, sin_col = angles(positions)
    text_f = caption.astype(jnp.float32)
    q_block = math.gcd(TOKENS, 512)

    def block_forward(patches, band_table, w_query, w_key, w_value, w_out, w_gate, w_up, w_down, w_ckey, w_cvalue, w_ada, b_ada, g_attn_in, g_attn_out, g_ffn_in, g_ffn_out, g_query, g_key, g_ckey, cross_gate):
        cond_act = jax.nn.silu(band_table[item_band])
        modulation = matmul(low(cond_act), w_ada) + b_ada
        mod_tok = modulation[token_item]
        scale_attn = mod_tok[:, :D]
        gate_attn = mod_tok[:, D:2 * D]
        scale_ffn = mod_tok[:, 2 * D:3 * D]
        gate_ffn = mod_tok[:, 3 * D:]
        norm_in = low(normed(patches) * g_attn_in * (1.0 + scale_attn))
        query_raw = low_back(matmul(norm_in, w_query)).reshape(TOKENS, H, head_dim)
        key_raw = low_back(matmul(norm_in, w_key)).reshape(TOKENS, H, head_dim)
        values = low_back(low(matmul(norm_in, w_value))).reshape(TOKENS, H, head_dim)
        queries = low_back(low(rotate(normed(query_raw) * g_query.reshape(H, head_dim), cos_row, sin_row, cos_col, sin_col)))
        keys = low_back(low(rotate(normed(key_raw) * g_key.reshape(H, head_dim), cos_row, sin_row, cos_col, sin_col)))
        ckey_raw = low_back(matmul(text_f, w_ckey)).reshape(TXT, H, head_dim)
        cap_keys = low_back(low(normed(ckey_raw) * g_ckey.reshape(H, head_dim)))
        cap_values = low_back(low(matmul(text_f, w_cvalue))).reshape(TXT, H, head_dim)

        def attend_block(inputs):
            query_blk, item_blk = inputs
            scores = low_back(jnp.einsum('qhd,khd->hqk', query_blk, keys, precision=HIGH) * scale)
            same = (item_blk[:, None] == token_item[None, :])[None]
            scores = jnp.where(same, scores, NEG)
            probs = jax.nn.softmax(scores, axis=-1)
            self_part = jnp.einsum('hqk,khd->qhd', low(probs), values, precision=HIGH)
            cross_scores = low_back(jnp.einsum('qhd,khd->hqk', query_blk, cap_keys, precision=HIGH) * scale)
            cross_probs = jax.nn.softmax(cross_scores, axis=-1)
            cross_part = jnp.einsum('hqk,khd->qhd', low(cross_probs), cap_values, precision=HIGH)
            return (self_part, cross_part)
        q_blocks = queries.reshape(TOKENS // q_block, q_block, H, head_dim)
        item_blocks = token_item.reshape(TOKENS // q_block, q_block)
        self_all, cross_all = lax.map(jax.checkpoint(attend_block), (q_blocks, item_blocks))
        attn_self = self_all.reshape(TOKENS, H, head_dim)
        attn_cross = low_back(cross_all.reshape(TOKENS, H, head_dim))
        mixed = low_back(low(attn_self + jnp.tanh(cross_gate)[None, :, None] * attn_cross)).reshape(TOKENS, D)
        attn_branch = low_back(matmul(mixed, w_out))
        resid = patches + jnp.tanh(gate_attn) * normed(attn_branch) * g_attn_out
        norm_ffn = low(normed(resid) * g_ffn_in * (1.0 + scale_ffn))
        gate_val = low_back(matmul(norm_ffn, w_gate))
        up_val = low_back(matmul(norm_ffn, w_up))
        hidden = low(jax.nn.silu(gate_val) * up_val)
        ffn_branch = low_back(matmul(hidden, w_down))
        return resid + jnp.tanh(gate_ffn) * normed(ffn_branch) * g_ffn_out
    params = (patches.astype(jnp.float32), band_table.astype(jnp.float32), w_query.astype(jnp.float32), w_key.astype(jnp.float32), w_value.astype(jnp.float32), w_out.astype(jnp.float32), w_gate.astype(jnp.float32), w_up.astype(jnp.float32), w_down.astype(jnp.float32), w_ckey.astype(jnp.float32), w_cvalue.astype(jnp.float32), w_ada.astype(jnp.float32), b_ada.astype(jnp.float32), g_attn_in.astype(jnp.float32), g_attn_out.astype(jnp.float32), g_ffn_in.astype(jnp.float32), g_ffn_out.astype(jnp.float32), g_query.astype(jnp.float32), g_key.astype(jnp.float32), g_ckey.astype(jnp.float32), cross_gate.astype(jnp.float32))
    result, pullback = jax.vjp(block_forward, *params)
    grads = pullback(out_grad.astype(jnp.float32))
    return (result, grads[0], grads[2], grads[3], grads[4], grads[5], grads[6], grads[7], grads[8], grads[9], grads[10], grads[11], grads[12], grads[13], grads[14], grads[15], grads[16], grads[17], grads[18], grads[19], grads[20], grads[1])
```

```python
import math

import jax
import jax.numpy as jnp
from jax import lax
from jax.sharding import PartitionSpec as P

BANDS = 16
ITEMS = 2
BLK = 32
HEAD = 64
EPS = 1e-06
NEG = -1e30
FREQ_BASE = 10000.0
HIGH = lax.Precision.HIGHEST
BF = jnp.bfloat16
F32 = jnp.float32
SPLIT = 4


def groups_of(cycle_size):
    lanes = cycle_size // SPLIT
    along_z = [[z * lanes + g for z in range(SPLIT)] for g in range(lanes)]
    along_g = [[z * lanes + g for g in range(lanes)] for z in range(SPLIT)]
    return along_z, along_g


def normed_pair(value):
    recip = lax.rsqrt(jnp.mean(value * value, axis=-1, keepdims=True) + EPS)
    return value * recip, recip


def normed_back(grad_hat, normal, recip):
    return recip * (grad_hat - normal * jnp.mean(grad_hat * normal, axis=-1, keepdims=True))


def rotate(value, cos_row, sin_row, cos_col, sin_col):
    quarter = value.shape[-1] // 4
    part_a = value[..., :quarter]
    part_b = value[..., quarter : 2 * quarter]
    part_c = value[..., 2 * quarter : 3 * quarter]
    part_e = value[..., 3 * quarter :]
    return jnp.concatenate(
        [
            part_a * cos_row - part_b * sin_row,
            part_a * sin_row + part_b * cos_row,
            part_c * cos_col - part_e * sin_col,
            part_c * sin_col + part_e * cos_col,
        ],
        axis=-1,
    )


def angles(positions):
    quarter = HEAD // 4
    freqs = FREQ_BASE ** (-jnp.arange(quarter, dtype=F32) / quarter)
    row_angle = positions[0].astype(F32)[:, None] * freqs[None, :]
    col_angle = positions[1].astype(F32)[:, None] * freqs[None, :]
    return (
        jnp.cos(row_angle)[:, None, :],
        jnp.sin(row_angle)[:, None, :],
        jnp.cos(col_angle)[:, None, :],
        jnp.sin(col_angle)[:, None, :],
    )


def bdot(left, right):
    return jnp.dot(left, right, preferred_element_type=F32)


def dot_t(left, right):
    return lax.dot_general(left, right, (((1,), (1,)), ((), ())), preferred_element_type=F32)


def t_dot(left, right):
    return lax.dot_general(left, right, (((0,), (0,)), ((), ())), preferred_element_type=F32)


def local(
    patches,
    caption,
    band_table,
    block_item,
    item_band,
    positions,
    out_grad,
    w_query,
    w_key,
    w_value,
    w_out,
    w_gate,
    w_up,
    w_down,
    w_ckey,
    w_cvalue,
    w_ada,
    b_ada,
    g_attn_in,
    g_attn_out,
    g_ffn_in,
    g_ffn_out,
    g_query,
    g_key,
    g_ckey,
    cross_gate,
):
    scale = 1.0 / math.sqrt(HEAD)
    rank = lax.axis_index("sp")
    half = lax.axis_index("tp")
    cycle = lax.axis_size("sp")
    halves = lax.axis_size("tp")
    lanes = cycle // SPLIT
    along_z, along_g = groups_of(cycle)
    my_z, my_g = rank // lanes, rank % lanes
    tok_rows, width = patches.shape
    own_rows = tok_rows // halves
    text_count = caption.shape[0]
    blocks_dev = tok_rows // BLK
    wq, wf = w_query.shape[1] // SPLIT, w_gate.shape[1] // SPLIT
    heads = wq // HEAD
    sizes = (wq, wq, wq, wq, wf, wf, wf)
    starts = [sum(sizes[:i]) for i in range(8)]

    def gather_z(block):
        return lax.all_gather(block, "sp", axis_index_groups=along_z, axis=0, tiled=False)

    def gather_g(block):
        return lax.all_gather(block, "sp", axis_index_groups=along_g, axis=0, tiled=False)

    def scatter_z(block):
        return lax.psum_scatter(
            block, "sp", axis_index_groups=along_z, scatter_dimension=0, tiled=False
        )

    def scatter_g(block):
        return lax.psum_scatter(
            block, "sp", axis_index_groups=along_g, scatter_dimension=0, tiled=False
        )

    def turn_z(block):
        return lax.all_to_all(
            block, "sp", 0, 0, axis_index_groups=along_z, tiled=True
        )

    def sum_g(block):
        return lax.psum(block, "sp", axis_index_groups=along_g)

    def gather_tokens(own):
        both = lax.all_gather(own, "tp", axis=0, tiled=True)
        return gather_z(both).reshape(SPLIT * tok_rows, -1)

    def scatter_tokens(part):
        part = part.astype(BF).reshape(SPLIT, halves, own_rows, width)
        mine = lax.psum_scatter(part, "tp", scatter_dimension=1, tiled=False)
        return scatter_z(mine.astype(BF)).astype(F32)

    def by_z(block):
        rows, cols = block.shape
        return block.reshape(rows, SPLIT, cols // SPLIT).transpose(1, 0, 2)

    shards = jnp.concatenate(
        [by_z(m) for m in (w_query, w_key, w_value, w_out.T, w_gate, w_up, w_down.T)], axis=2
    )
    rows_dev = shards.shape[1]
    merged = gather_g(turn_z(shards)).transpose(1, 0, 2, 3).reshape(cycle * rows_dev, -1)
    f_query, f_key, f_value, f_out, f_gate, f_up, f_down = (
        merged[:, starts[i] : starts[i + 1]] for i in range(7)
    )

    items_all = block_item.reshape(SPLIT, lanes, blocks_dev)
    grp_items = jnp.repeat(
        lax.dynamic_index_in_dim(items_all, my_g, 1, keepdims=False).reshape(-1), BLK
    )
    key_items = jnp.repeat(items_all.transpose(1, 0, 2).reshape(-1), BLK)
    row0 = half * own_rows

    def own_part(block):
        return lax.dynamic_slice_in_dim(block, row0, own_rows, 0)

    own_items = own_part(
        jnp.repeat(lax.dynamic_slice_in_dim(block_item, rank * blocks_dev, blocks_dev), BLK)
    )

    band_hot = (item_band[:, None] == jnp.arange(BANDS, dtype=jnp.int32)[None, :]).astype(F32)
    cond_pre = jnp.dot(band_hot, band_table, precision=HIGH)
    cond_sig = jax.nn.sigmoid(cond_pre)
    cond_low = (cond_pre * cond_sig).astype(BF)
    text_rows = w_ckey.shape[0]
    text_local = lax.dynamic_slice_in_dim(caption, rank * text_rows, text_rows, 1)
    modulation = lax.psum(bdot(cond_low, w_ada), "sp") + b_ada
    cap_part = jnp.stack([by_z(bdot(text_local, w_ckey)), by_z(bdot(text_local, w_cvalue))], 1)
    cap_raw = sum_g(scatter_z(cap_part))
    ckey_hat, ckey_recip = normed_pair(cap_raw[0].reshape(text_count, heads, HEAD))

    def per_head(vector):
        return lax.dynamic_slice_in_dim(vector, my_z * wq, wq, 0).reshape(heads, HEAD)

    gain_query, gain_key, gain_ckey = per_head(g_query), per_head(g_key), per_head(g_ckey)
    gate_tanh = jnp.tanh(lax.dynamic_slice_in_dim(cross_gate, my_z * heads, heads, 0))
    cap_keys = (ckey_hat * gain_ckey).astype(BF)
    cap_values = cap_raw[1].astype(BF).reshape(text_count, heads, HEAD)

    def of_items(rows, items):
        return jnp.where(items[:, None] == 0, rows[0], rows[1])

    mod_own = of_items(modulation, own_items)
    scale_attn, gate_attn, scale_ffn, gate_ffn = (
        mod_own[:, i * width : (i + 1) * width] for i in range(4)
    )
    group_rows = SPLIT * tok_rows

    patch_f = own_part(patches).astype(F32)
    grad_out = own_part(out_grad).astype(F32)
    hat_one, recip_one = normed_pair(patch_f)
    factor_one = g_attn_in * (1.0 + scale_attn)
    norm_in = gather_tokens((hat_one * factor_one).astype(BF))
    pos_all = gather_z(positions).transpose(1, 0, 2).reshape(2, group_rows)
    cos_row, sin_row, cos_col, sin_col = angles(pos_all)
    split_heads = (group_rows, heads, HEAD)
    query_raw = bdot(norm_in, f_query).reshape(split_heads)
    key_raw = bdot(norm_in, f_key).reshape(split_heads)
    values_low = bdot(norm_in, f_value).astype(BF)
    query_hat, query_recip = normed_pair(query_raw)
    queries = rotate(query_hat * gain_query, cos_row, sin_row, cos_col, sin_col).astype(BF)
    key_hat, key_recip = normed_pair(key_raw)
    keys_low = rotate(key_hat * gain_key, cos_row, sin_row, cos_col, sin_col).astype(BF)
    all_keys, all_values = (
        gather_g(block).reshape(lanes * group_rows, heads, HEAD)
        for block in (keys_low.reshape(group_rows, wq), values_low)
    )
    same = (grp_items[:, None] == key_items[None, :])[None]
    scores = jnp.einsum("qhd,khd->hqk", queries, all_keys, preferred_element_type=F32) * scale
    scores = jnp.where(same, scores, NEG)
    exps = jnp.exp(scores - jnp.max(scores, axis=-1, keepdims=True))
    probs = exps / jnp.sum(exps, axis=-1, keepdims=True)
    probs_low = probs.astype(BF)
    attn_self = jnp.einsum("hqk,khd->qhd", probs_low, all_values, preferred_element_type=F32)
    cross_scores = (
        jnp.einsum("qhd,khd->hqk", queries, cap_keys, preferred_element_type=F32) * scale
    )
    cross_exp = jnp.exp(cross_scores - jnp.max(cross_scores, axis=-1, keepdims=True))
    cross_probs = cross_exp / jnp.sum(cross_exp, axis=-1, keepdims=True)
    cross_low = cross_probs.astype(BF)
    attn_cross = jnp.einsum("hqk,khd->qhd", cross_low, cap_values, preferred_element_type=F32)
    mixed = (attn_self + gate_tanh[None, :, None] * attn_cross).astype(BF).reshape(group_rows, wq)
    attn_branch = scatter_tokens(dot_t(mixed, f_out))

    hat_two, recip_two = normed_pair(attn_branch)
    tanh_one = jnp.tanh(gate_attn)
    resid = patch_f + tanh_one * hat_two * g_attn_out
    hat_three, recip_three = normed_pair(resid)
    factor_three = g_ffn_in * (1.0 + scale_ffn)
    norm_ffn = gather_tokens((hat_three * factor_three).astype(BF))
    gate_val = bdot(norm_ffn, f_gate)
    up_val = bdot(norm_ffn, f_up)
    gate_sig = jax.nn.sigmoid(gate_val)
    hidden = (gate_val * gate_sig * up_val).astype(BF)
    ffn_branch = scatter_tokens(dot_t(hidden, f_down))
    hat_four, recip_four = normed_pair(ffn_branch)
    tanh_two = jnp.tanh(gate_ffn)
    output = resid + tanh_two * hat_four * g_ffn_out

    grad_gate_ffn = grad_out * hat_four * g_ffn_out * (1.0 - tanh_two * tanh_two)
    grad_four = grad_out * tanh_two
    grad_g_ffn_out = jnp.sum(grad_four * hat_four, axis=0)
    grad_ffn = gather_tokens(
        normed_back(grad_four * g_ffn_out, hat_four, recip_four).astype(BF)
    )
    grad_hidden = bdot(grad_ffn, f_down)
    grad_gate = (grad_hidden * up_val * gate_sig * (1.0 + gate_val * (1.0 - gate_sig))).astype(BF)
    grad_up = (grad_hidden * gate_val * gate_sig).astype(BF)
    grad_norm_ffn = scatter_tokens(dot_t(grad_gate, f_gate) + dot_t(grad_up, f_up))
    grad_scale_ffn = grad_norm_ffn * hat_three * g_ffn_in
    grad_g_ffn_in = jnp.sum(grad_norm_ffn * hat_three * (1.0 + scale_ffn), axis=0)
    grad_resid = grad_out + normed_back(grad_norm_ffn * factor_three, hat_three, recip_three)

    grad_gate_attn = grad_resid * hat_two * g_attn_out * (1.0 - tanh_one * tanh_one)
    grad_two = grad_resid * tanh_one
    grad_g_attn_out = jnp.sum(grad_two * hat_two, axis=0)
    grad_attn = gather_tokens(normed_back(grad_two * g_attn_out, hat_two, recip_two).astype(BF))
    grad_mixed = bdot(grad_attn, f_out).astype(BF).reshape(split_heads)
    grad_mixed_f = grad_mixed.astype(F32)
    grad_cross_gate = jnp.sum(grad_mixed_f * attn_cross, axis=(0, 2)) * (
        1.0 - gate_tanh * gate_tanh
    )
    grad_cross = (gate_tanh[None, :, None] * grad_mixed_f).astype(BF)
    grad_cprobs = jnp.einsum("qhd,khd->hqk", grad_cross, cap_values, preferred_element_type=F32)
    grad_cscores = (
        cross_probs * (grad_cprobs - jnp.sum(cross_probs * grad_cprobs, axis=-1, keepdims=True))
    ).astype(BF)
    query_grad = jnp.einsum("hqk,khd->qhd", grad_cscores, cap_keys, preferred_element_type=F32)
    grad_ckeys_part = (
        jnp.einsum("hqk,qhd->khd", grad_cscores, queries, preferred_element_type=F32) * scale
    )
    grad_cvals_part = jnp.einsum(
        "hqk,qhd->khd", cross_low, grad_cross, preferred_element_type=F32
    )
    row_delta = jnp.sum(grad_mixed_f * attn_self, axis=-1).T
    grad_probs = jnp.einsum("qhd,khd->hqk", grad_mixed, all_values, preferred_element_type=F32)
    grad_scores = (probs * (grad_probs - row_delta[..., None])).astype(BF)
    query_grad = query_grad + jnp.einsum(
        "hqk,khd->qhd", grad_scores, all_keys, preferred_element_type=F32
    )
    key_part = (
        jnp.einsum("hqk,qhd->khd", grad_scores, queries, preferred_element_type=F32) * scale
    )
    value_part = jnp.einsum("hqk,qhd->khd", probs_low, grad_mixed, preferred_element_type=F32)
    key_grad, value_grad = (
        scatter_g(block.astype(BF).reshape(lanes, group_rows, wq)) for block in (key_part, value_part)
    )
    grad_queries = (query_grad * scale).astype(BF).astype(F32)
    grad_qnorm = rotate(grad_queries, cos_row, -sin_row, cos_col, -sin_col)
    grad_g_query = jnp.sum(grad_qnorm * query_hat, axis=0).reshape(-1)
    grad_query_raw = (
        normed_back(grad_qnorm * gain_query, query_hat, query_recip).astype(BF).reshape(-1, wq)
    )
    grad_keys = key_grad.astype(F32).reshape(split_heads)
    grad_knorm = rotate(grad_keys, cos_row, -sin_row, cos_col, -sin_col)
    grad_g_key = jnp.sum(grad_knorm * key_hat, axis=0).reshape(-1)
    grad_key_raw = (
        normed_back(grad_knorm * gain_key, key_hat, key_recip).astype(BF).reshape(-1, wq)
    )
    grad_values = value_grad.astype(BF)
    grad_norm_in = scatter_tokens(
        dot_t(grad_query_raw, f_query) + dot_t(grad_key_raw, f_key) + dot_t(grad_values, f_value)
    )
    grad_scale_attn = grad_norm_in * hat_one * g_attn_in
    grad_g_attn_in = jnp.sum(grad_norm_in * hat_one * (1.0 + scale_attn), axis=0)
    grad_patches = grad_resid + normed_back(grad_norm_in * factor_one, hat_one, recip_one)

    grad_merged = jnp.concatenate(
        [
            t_dot(norm_in, grad_query_raw),
            t_dot(norm_in, grad_key_raw),
            t_dot(norm_in, grad_values),
            t_dot(grad_attn, mixed),
            t_dot(norm_ffn, grad_gate),
            t_dot(norm_ffn, grad_up),
            t_dot(grad_ffn, hidden),
        ],
        axis=1,
    ).astype(BF)
    grad_merged = grad_merged.reshape(SPLIT, lanes, rows_dev, -1).transpose(1, 0, 2, 3)
    shard_grads = turn_z(scatter_g(grad_merged)).astype(F32)
    (shard_query, shard_key, shard_value, shard_out, shard_gate, shard_up, shard_down) = (
        shard_grads[:, :, starts[i] : starts[i + 1]].transpose(1, 0, 2).reshape(rows_dev, -1)
        for i in range(7)
    )

    token_sums = lax.psum(
        (
            jnp.stack(
                [
                    jnp.concatenate(
                        [
                            jnp.sum(
                                jnp.where((own_items == item)[:, None], block, 0.0), axis=0
                            )
                            for block in (
                                grad_scale_attn,
                                grad_gate_attn,
                                grad_scale_ffn,
                                grad_gate_ffn,
                            )
                        ]
                    )
                    for item in range(ITEMS)
                ]
            ),
            grad_g_attn_in,
            grad_g_attn_out,
            grad_g_ffn_in,
            grad_g_ffn_out,
        ),
        ("sp", "tp"),
    )
    head_sums = jnp.concatenate([grad_g_query, grad_g_key, grad_cross_gate])
    head_sums = gather_z(sum_g(head_sums))
    grad_ckeys = sum_g(grad_ckeys_part).astype(BF).astype(F32)
    grad_cvals = sum_g(grad_cvals_part).astype(BF).reshape(text_count, wq)
    grad_g_ckey = gather_z(jnp.sum(grad_ckeys * ckey_hat, axis=0).reshape(-1)).reshape(-1)
    grad_ckey_raw = (
        normed_back(grad_ckeys * gain_ckey, ckey_hat, ckey_recip).astype(BF).reshape(text_count, wq)
    )
    cap_grads = gather_z(jnp.stack([grad_ckey_raw, grad_cvals])).transpose(1, 2, 0, 3)
    cap_grads = cap_grads.reshape(2, text_count, SPLIT * wq)
    grad_mod = token_sums[0]
    grad_b_ada = jnp.sum(grad_mod, axis=0)
    grad_w_ada = jnp.dot(cond_low.astype(F32).T, grad_mod, precision=HIGH)
    grad_cond_act = jnp.dot(grad_mod, w_ada.astype(F32).T, precision=HIGH)
    grad_cond_pre = grad_cond_act * cond_sig * (1.0 + cond_pre * (1.0 - cond_sig))
    grad_band_table = jnp.dot(band_hot.T, grad_cond_pre, precision=HIGH)
    return (
        lax.all_gather(output, "tp", axis=0, tiled=True),
        lax.all_gather(grad_patches, "tp", axis=0, tiled=True),
        shard_query,
        shard_key,
        shard_value,
        shard_out.T,
        shard_gate,
        shard_up,
        shard_down.T,
        t_dot(text_local, cap_grads[0]),
        t_dot(text_local, cap_grads[1]),
        grad_w_ada,
        grad_b_ada,
        token_sums[1],
        token_sums[2],
        token_sums[3],
        token_sums[4],
        head_sums[:, :wq].reshape(-1),
        head_sums[:, wq : 2 * wq].reshape(-1),
        grad_g_ckey,
        head_sums[:, 2 * wq :].reshape(-1),
        grad_band_table,
    )


def solution(mesh):
    in_specs = (
        P("sp", None),
        P(),
        P(None, "sp"),
        P(),
        P(),
        P(None, "sp"),
        P("sp", None),
        P("sp", "tp"),
        P("sp", "tp"),
        P("sp", "tp"),
        P("tp", "sp"),
        P("sp", "tp"),
        P("sp", "tp"),
        P("tp", "sp"),
        P("sp", "tp"),
        P("sp", "tp"),
        P("sp", None),
        P(),
        P(),
        P(),
        P(),
        P(),
        P("tp"),
        P("tp"),
        P("tp"),
        P("tp"),
    )
    out_specs = (
        P("sp", None),
        P("sp", None),
        P("sp", "tp"),
        P("sp", "tp"),
        P("sp", "tp"),
        P("tp", "sp"),
        P("sp", "tp"),
        P("sp", "tp"),
        P("tp", "sp"),
        P("sp", "tp"),
        P("sp", "tp"),
        P("sp", None),
        P(),
        P(),
        P(),
        P(),
        P(),
        P("tp"),
        P("tp"),
        P("tp"),
        P("tp"),
        P(None, "sp"),
    )
    return jax.shard_map(local, mesh=mesh, in_specs=in_specs, out_specs=out_specs, check_vma=False)
```

```python
import math

import jax
import jax.numpy as jnp
from jax import lax
from jax.experimental import pallas as pl
from jax.experimental.pallas import tpu as pltpu
from jax.sharding import PartitionSpec as P

BANDS = 16
ITEMS = 2
BLK = 32
HEAD = 64
EPS = 1e-06
NEG = -1e30
FREQ_BASE = 10000.0
HIGH = lax.Precision.HIGHEST
BF = jnp.bfloat16
F32 = jnp.float32
SPLIT = 4


def groups_of(cycle_size):
    lanes = cycle_size // SPLIT
    along_z = [[z * lanes + g for z in range(SPLIT)] for g in range(lanes)]
    along_g = [[z * lanes + g for g in range(lanes)] for z in range(SPLIT)]
    return along_z, along_g


def normed_pair(value):
    recip = lax.rsqrt(jnp.mean(value * value, axis=-1, keepdims=True) + EPS)
    return value * recip, recip


def normed_back(grad_hat, normal, recip):
    return recip * (grad_hat - normal * jnp.mean(grad_hat * normal, axis=-1, keepdims=True))


def rotate(value, cos_row, sin_row, cos_col, sin_col):
    quarter = value.shape[-1] // 4
    part_a = value[..., :quarter]
    part_b = value[..., quarter : 2 * quarter]
    part_c = value[..., 2 * quarter : 3 * quarter]
    part_e = value[..., 3 * quarter :]
    return jnp.concatenate(
        [
            part_a * cos_row - part_b * sin_row,
            part_a * sin_row + part_b * cos_row,
            part_c * cos_col - part_e * sin_col,
            part_c * sin_col + part_e * cos_col,
        ],
        axis=-1,
    )


def angles(positions):
    quarter = HEAD // 4
    freqs = FREQ_BASE ** (-jnp.arange(quarter, dtype=F32) / quarter)
    row_angle = positions[0].astype(F32)[:, None] * freqs[None, :]
    col_angle = positions[1].astype(F32)[:, None] * freqs[None, :]
    return (
        jnp.cos(row_angle)[:, None, :],
        jnp.sin(row_angle)[:, None, :],
        jnp.cos(col_angle)[:, None, :],
        jnp.sin(col_angle)[:, None, :],
    )


def bdot(left, right):
    return jnp.dot(left, right, preferred_element_type=F32)


def dot_t(left, right):
    return lax.dot_general(left, right, (((1,), (1,)), ((), ())), preferred_element_type=F32)


def t_dot(left, right):
    return lax.dot_general(left, right, (((0,), (0,)), ((), ())), preferred_element_type=F32)


MESH = pl.DeviceIdType.MESH
VMEM_LIMIT = 60 * 2**20


class Place:
    def __init__(self):
        rank = lax.axis_index("sp")
        self.lanes = lax.axis_size("sp") // SPLIT
        self.x = lax.axis_index("tp")
        self.z = rank // self.lanes
        self.g = rank % self.lanes
        self.x_peer = (rank, 1 - self.x)
        self.z_peer = {
            d: (lax.rem(self.z + d, SPLIT) * self.lanes + self.g, self.x) for d in (1, 2, 3)
        }
        self.y, self.c = self.g // 2, self.g % 2
        self.g_y = (1 - self.y) * 2 + self.c
        self.g_c = self.y * 2 + 1 - self.c
        self.g_yc = (1 - self.y) * 2 + 1 - self.c
        self.y_peer = (self.z * self.lanes + self.g_y, self.x)
        self.c_peer = (self.z * self.lanes + self.g_c, self.x)

    def z_from(self, d):
        return lax.rem(self.z + SPLIT - d, SPLIT)

    def z_to(self, d):
        return lax.rem(self.z + d, SPLIT)


def enter(peers):
    barrier = pltpu.get_barrier_semaphore()
    for peer in peers:
        pl.semaphore_signal(barrier, inc=1, device_id=peer, device_id_type=MESH)
    pl.semaphore_wait(barrier, len(peers))


def remote(src, dst, send, recv, peer):
    return pltpu.make_async_remote_copy(
        src_ref=src, dst_ref=dst, send_sem=send, recv_sem=recv, device_id=peer, device_id_type=MESH
    )


NEAR = (1, 3, 2)


class Gather:
    def __init__(self, place, buf, send, recv):
        self.place, self.buf = place, buf
        own = buf.at[place.z * 2 + place.x]
        self.own = own
        self.along_z = [
            remote(own, own, send.at[i], recv.at[i], place.z_peer[d]) for i, d in enumerate(NEAR)
        ]
        self.to_x = remote(own, own, send.at[3], recv.at[3], place.x_peer)
        self.landed = []
        self.forward = []
        for i, d in enumerate(NEAR):
            block = buf.at[place.z_from(d) * 2 + place.x]
            self.landed.append(remote(block, block, send.at[i], recv.at[i], place.z_peer[d]))
            self.forward.append(remote(block, block, send.at[4 + i], recv.at[4 + i], place.x_peer))
        self.other = [buf.at[place.z * 2 + 1 - place.x]] + [
            buf.at[place.z_from(d) * 2 + 1 - place.x] for d in NEAR
        ]
        self.arrive_x = [
            remote(block, block, send.at[3 + i], recv.at[3 + i], place.x_peer)
            for i, block in enumerate(self.other)
        ]

    def start(self):
        for copy in self.along_z:
            copy.start()
        self.to_x.start()

    def pass_on(self):
        for landed, forward in zip(self.landed, self.forward):
            landed.wait_recv()
            forward.start()

    def finish(self):
        for copy in self.arrive_x:
            copy.wait_recv()
        for copy in self.along_z + [self.to_x] + self.forward:
            copy.wait_send()


class Scatter:
    def __init__(self, place, part, from_x, to_z, from_z, send, recv):
        self.place, self.part, self.from_x = place, part, from_x
        self.to_z, self.from_z = to_z, from_z
        self.order = [place.z_to(d) for d in NEAR] + [place.z]
        self.across = [
            remote(
                part.at[target, 1 - place.x], from_x.at[i], send.at[i], recv.at[i], place.x_peer
            )
            for i, target in enumerate(self.order)
        ]
        self.along = [
            remote(to_z.at[i], from_z.at[i], send.at[4 + i], recv.at[4 + i], place.z_peer[d])
            for i, d in enumerate(NEAR)
        ]

    def send_x(self, i):
        self.across[i].start()

    def pass_on(self):
        for i in range(3):
            self.across[i].wait_recv()
            self.to_z[i] = (
                self.part[self.order[i], self.place.x].astype(F32) + self.from_x[i].astype(F32)
            ).astype(BF)
            self.along[i].start()

    def finish(self):
        self.across[3].wait_recv()
        total = self.part[self.place.z, self.place.x].astype(F32) + self.from_x[3].astype(F32)
        for i in range(3):
            self.along[i].wait_recv()
            total = total + self.from_z[i].astype(F32)
        for copy in self.across + self.along:
            copy.wait_send()
        return total


def gather_scratch(rows, width):
    return [
        pltpu.VMEM((2 * SPLIT, rows, width), BF),
        pltpu.SemaphoreType.DMA((7,)),
        pltpu.SemaphoreType.DMA((7,)),
    ]


def scatter_scratch(rows, width):
    return [
        pltpu.VMEM((SPLIT, 2, rows, width), BF),
        pltpu.VMEM((SPLIT, rows, width), BF),
        pltpu.VMEM((3, rows, width), BF),
        pltpu.VMEM((3, rows, width), BF),
        pltpu.SemaphoreType.DMA((7,)),
        pltpu.SemaphoreType.DMA((7,)),
    ]


def item_rows(mod, items, index, width):
    first = mod[0:1, index * width : (index + 1) * width]
    second = mod[1:2, index * width : (index + 1) * width]
    return jnp.where(items == 0, first, second)


def item_sums(value, items):
    return [
        jnp.sum(jnp.where(items == item, value, 0.0), axis=0, keepdims=True)
        for item in range(ITEMS)
    ]


def ffn_kernel(
    branch, patches, out_grad, mod, items, gain_out, gain_in, gain_ffn, w_gate, w_up, w_down,
    output, grad_resid, grad_attn, sums, grad_w,
    n_buf, n_send, n_recv, g_buf, g_send, g_recv,
    p1, fx1, tz1, fz1, s1, r1, p2, fx2, tz2, fz2, s2, r2,
    gate_s, up_s, hid_s, gg_s, gu_s, out_send, out_recv,
):
    place = Place()
    rows, width = branch.shape
    item = items[...]
    enter([place.x_peer] + [place.z_peer[d] for d in (1, 2, 3)])
    norms = Gather(place, n_buf, n_send, n_recv)
    grads = Gather(place, g_buf, g_send, g_recv)
    down = Scatter(place, p1, fx1, tz1, fz1, s1, r1)
    back = Scatter(place, p2, fx2, tz2, fz2, s2, r2)

    hat_two, recip_two = normed_pair(branch[...])
    tanh_one = jnp.tanh(item_rows(mod, item, 1, width))
    resid = patches[...].astype(F32) + tanh_one * hat_two * gain_out[...]
    hat_three, recip_three = normed_pair(resid)
    factor_three = gain_in[...] * (1.0 + item_rows(mod, item, 2, width))
    norms.own[...] = (hat_three * factor_three).astype(BF)
    norms.start()
    norms.pass_on()
    norms.finish()

    def forward(i, carry):
        target = lax.rem(place.z + 1 + i, SPLIT)
        block = n_buf[pl.ds(target * 2, 2)].reshape(2 * rows, width)
        gate_val = bdot(block, w_gate[...])
        up_val = bdot(block, w_up[...])
        gate_s[target] = gate_val
        up_s[target] = up_val
        hidden = (gate_val * jax.nn.sigmoid(gate_val) * up_val).astype(BF)
        hid_s[target] = hidden
        p1[target] = dot_t(hidden, w_down[...]).astype(BF).reshape(2, rows, width)
        return carry

    lax.fori_loop(0, SPLIT, forward, 0)
    for i in range(4):
        down.send_x(i)
    down.pass_on()
    ffn = down.finish()

    hat_four, recip_four = normed_pair(ffn)
    tanh_two = jnp.tanh(item_rows(mod, item, 3, width))
    output[place.x] = resid + tanh_two * hat_four * gain_ffn[...]
    out_copy = remote(output.at[place.x], output.at[place.x], out_send, out_recv, place.x_peer)
    grad_out = out_grad[...].astype(F32)
    grad_four = grad_out * tanh_two
    grads.own[...] = normed_back(grad_four * gain_ffn[...], hat_four, recip_four).astype(BF)
    grads.start()
    out_copy.start()
    gate_sums = item_sums(
        grad_out * hat_four * gain_ffn[...] * (1.0 - tanh_two * tanh_two), item
    )
    sum_ffn_out = jnp.sum(grad_four * hat_four, axis=0, keepdims=True)
    sums[...] = jnp.zeros_like(sums)
    sums[2:3] = sum_ffn_out
    sums[8:9] = gate_sums[0]
    sums[9:10] = gate_sums[1]
    grads.pass_on()
    grads.finish()

    def backward(i, carry):
        target = lax.rem(place.z + 1 + i, SPLIT)
        block = g_buf[pl.ds(target * 2, 2)].reshape(2 * rows, width)
        grad_hidden = bdot(block, w_down[...])
        gate_val = gate_s[target]
        gate_sig = jax.nn.sigmoid(gate_val)
        grad_gate = (
            grad_hidden * up_s[target] * gate_sig * (1.0 + gate_val * (1.0 - gate_sig))
        ).astype(BF)
        grad_up = (grad_hidden * gate_val * gate_sig).astype(BF)
        gg_s[target] = grad_gate
        gu_s[target] = grad_up
        p2[target] = (
            (dot_t(grad_gate, w_gate[...]) + dot_t(grad_up, w_up[...]))
            .astype(BF)
            .reshape(2, rows, width)
        )
        return carry

    lax.fori_loop(0, SPLIT, backward, 0)
    for i in range(4):
        back.send_x(i)
    back.pass_on()

    hid = w_gate.shape[1]
    step = 256

    def weights(i, carry):
        cols = pl.ds(pl.multiple_of(i * step, step), step)
        left = n_buf[:, :, cols].reshape(SPLIT * 2 * rows, step)
        grad_w[cols, 0:hid] = t_dot(left, gg_s[...].reshape(-1, hid)).astype(BF)
        grad_w[cols, hid : 2 * hid] = t_dot(left, gu_s[...].reshape(-1, hid)).astype(BF)
        left = g_buf[:, :, cols].reshape(SPLIT * 2 * rows, step)
        grad_w[cols, 2 * hid : 3 * hid] = t_dot(left, hid_s[...].reshape(-1, hid)).astype(BF)
        return carry

    lax.fori_loop(0, width // step, weights, 0)

    grad_norm = back.finish()
    scale_sums = item_sums(grad_norm * hat_three * gain_in[...], item)
    sums[1:2] = jnp.sum(
        grad_norm * hat_three * (1.0 + item_rows(mod, item, 2, width)), axis=0, keepdims=True
    )
    sums[6:7] = scale_sums[0]
    sums[7:8] = scale_sums[1]
    grad_res = grad_out + normed_back(grad_norm * factor_three, hat_three, recip_three)
    grad_resid[...] = grad_res
    gate_sums = item_sums(
        grad_res * hat_two * gain_out[...] * (1.0 - tanh_one * tanh_one), item
    )
    grad_two = grad_res * tanh_one
    sums[0:1] = jnp.sum(grad_two * hat_two, axis=0, keepdims=True)
    sums[4:5] = gate_sums[0]
    sums[5:6] = gate_sums[1]
    grad_attn[...] = normed_back(grad_two * gain_out[...], hat_two, recip_two).astype(BF)
    out_copy.wait_send()
    remote(
        output.at[1 - place.x], output.at[1 - place.x], out_send, out_recv, place.x_peer
    ).wait_recv()


def ffn_call(branch, patches, out_grad, mod, items, gain_out, gain_in, gain_ffn, wg, wu, wd):
    rows, width = branch.shape
    hid = wg.shape[1]
    vmem = pl.BlockSpec(memory_space=pltpu.VMEM)
    shape = jax.ShapeDtypeStruct
    return pl.pallas_call(
        ffn_kernel,
        out_shape=(
            shape((2, rows, width), F32),
            shape((rows, width), F32),
            shape((rows, width), BF),
            shape((16, width), F32),
            shape((width, 3 * hid), BF),
        ),
        in_specs=[vmem] * 11,
        out_specs=[vmem] * 5,
        scratch_shapes=gather_scratch(rows, width)
        + gather_scratch(rows, width)
        + scatter_scratch(rows, width)
        + scatter_scratch(rows, width)
        + [
            pltpu.VMEM((SPLIT, 2 * rows, hid), F32),
            pltpu.VMEM((SPLIT, 2 * rows, hid), F32),
            pltpu.VMEM((SPLIT, 2 * rows, hid), BF),
            pltpu.VMEM((SPLIT, 2 * rows, hid), BF),
            pltpu.VMEM((SPLIT, 2 * rows, hid), BF),
            pltpu.SemaphoreType.DMA,
            pltpu.SemaphoreType.DMA,
        ],
        compiler_params=pltpu.CompilerParams(
            collective_id=2, has_side_effects=True, vmem_limit_bytes=VMEM_LIMIT
        ),
        name="feed_forward",
    )(branch, patches, out_grad, mod, items, gain_out, gain_in, gain_ffn, wg, wu, wd)


class LaneGather:
    def __init__(self, place, buf, send, recv):
        own = buf.at[place.g]
        self.own = own
        self.to_y = remote(own, own, send.at[0], recv.at[0], place.y_peer)
        self.to_c = remote(own, own, send.at[1], recv.at[1], place.c_peer)
        across = buf.at[place.g_y]
        self.from_y = remote(across, across, send.at[2], recv.at[0], place.c_peer)
        self.on = remote(across, across, send.at[2], recv.at[2], place.c_peer)
        pair = buf.at[place.g_c]
        self.from_c = remote(pair, pair, send.at[1], recv.at[1], place.c_peer)
        diagonal = buf.at[place.g_yc]
        self.from_diagonal = remote(diagonal, diagonal, send.at[2], recv.at[2], place.c_peer)

    def start(self):
        self.to_y.start()
        self.to_c.start()

    def pass_on(self):
        self.from_y.wait_recv()
        self.on.start()

    def finish(self):
        self.from_c.wait_recv()
        self.from_diagonal.wait_recv()
        self.to_y.wait_send()
        self.to_c.wait_send()
        self.on.wait_send()


class WeightGather:
    def __init__(self, place, shards, buf, send, recv):
        self.place = place
        lanes = place.lanes
        order = [place.z] + [place.z_from(d) for d in NEAR]
        own = buf.at[place.z * lanes + place.g]
        self.keep = pltpu.make_async_copy(shards.at[place.z], own, recv.at[3])
        self.along_z = [
            remote(shards.at[place.z_to(d)], own, send.at[i], recv.at[i], place.z_peer[d])
            for i, d in enumerate(NEAR)
        ]
        self.blocks, self.to_y, self.to_c, self.from_y, self.on = [], [], [], [], []
        self.from_c, self.from_diagonal = [], []
        for i, z in enumerate(order):
            block = buf.at[z * lanes + place.g]
            self.blocks.append(block)
            self.to_y.append(remote(block, block, send.at[4 + i], recv.at[4 + i], place.y_peer))
            self.to_c.append(remote(block, block, send.at[8 + i], recv.at[8 + i], place.c_peer))
            across = buf.at[z * lanes + place.g_y]
            self.from_y.append(
                remote(across, across, send.at[12 + i], recv.at[4 + i], place.c_peer)
            )
            self.on.append(
                remote(across, across, send.at[12 + i], recv.at[12 + i], place.c_peer)
            )
            pair = buf.at[z * lanes + place.g_c]
            self.from_c.append(remote(pair, pair, send.at[8 + i], recv.at[8 + i], place.c_peer))
            diagonal = buf.at[z * lanes + place.g_yc]
            self.from_diagonal.append(
                remote(diagonal, diagonal, send.at[12 + i], recv.at[12 + i], place.c_peer)
            )
        self.landed = [
            remote(self.blocks[1 + i], self.blocks[1 + i], send.at[i], recv.at[i], place.z_peer[d])
            for i, d in enumerate(NEAR)
        ]

    def start(self):
        for copy in self.along_z:
            copy.start()
        self.keep.start()

    def pass_own(self):
        self.keep.wait()
        self.to_y[0].start()
        self.to_c[0].start()

    def pass_z(self, i):
        self.landed[i].wait_recv()
        self.to_y[1 + i].start()
        self.to_c[1 + i].start()

    def pass_y(self, i):
        self.from_y[i].wait_recv()
        self.on[i].start()

    def finish(self):
        for copy in self.from_c + self.from_diagonal:
            copy.wait_recv()
        for copy in self.along_z + self.to_y + self.to_c + self.on:
            copy.wait_send()


class AllSum:
    def __init__(self, place, acc, land, slots, send, recv, over_x):
        self.place, self.acc, self.land, self.slots = place, acc, land, slots
        peers = [place.c_peer, place.y_peer] + ([place.x_peer] if over_x else [])
        self.steps = len(peers)
        self.pairs = [
            remote(acc.at[i], land.at[i], send.at[i], recv.at[i], peer)
            for i, peer in enumerate(peers)
        ]
        own = slots.at[place.z]
        self.own = own
        self.along_z = [
            remote(own, own, send.at[3 + i], recv.at[3 + i], place.z_peer[d])
            for i, d in enumerate(NEAR)
        ]
        self.landed = []
        for i, d in enumerate(NEAR):
            slot = slots.at[place.z_from(d)]
            self.landed.append(remote(slot, slot, send.at[3 + i], recv.at[3 + i], place.z_peer[d]))

    def start(self):
        self.pairs[0].start()

    def step(self, i):
        self.pairs[i].wait_recv()
        total = self.acc[i] + self.land[i]
        if i + 1 < self.steps:
            self.acc[i + 1] = total
            self.pairs[i + 1].start()
        else:
            self.own[...] = total
            for copy in self.along_z:
                copy.start()

    def finish(self):
        for copy in self.landed:
            copy.wait_recv()
        for copy in self.pairs + self.along_z:
            copy.wait_send()
        return (self.slots[0] + self.slots[1]) + (self.slots[2] + self.slots[3])


class LaneScatter:
    def __init__(self, place, part, from_c, acc, from_y, send, recv):
        self.place, self.part, self.from_c = place, part, from_c
        self.acc, self.from_y = acc, from_y
        self.to_c = remote(part.at[1 - place.c], from_c, send.at[0], recv.at[0], place.c_peer)
        self.to_y = remote(acc.at[1 - place.y], from_y, send.at[1], recv.at[1], place.y_peer)

    def start(self):
        self.to_c.start()

    def step(self):
        self.to_c.wait_recv()
        c, y = self.place.c, self.place.y
        self.acc[1 - y] = (
            self.part[c, 1 - y].astype(F32) + self.from_c[1 - y].astype(F32)
        ).astype(BF)
        self.to_y.start()

    def finish(self):
        c, y = self.place.c, self.place.y
        near = self.part[c, y].astype(F32) + self.from_c[y].astype(F32)
        self.to_y.wait_recv()
        self.to_c.wait_send()
        self.to_y.wait_send()
        return near + self.from_y[...].astype(F32)


def segments(lanes):
    row = lax.broadcasted_iota(jnp.int32, (lanes, lanes), 0) // HEAD
    col = lax.broadcasted_iota(jnp.int32, (lanes, lanes), 1) // HEAD
    return jnp.where(row == col, 1.0 / HEAD, 0.0).astype(F32)


def head_mean(value, mean):
    return jnp.dot(value, mean, precision=HIGH, preferred_element_type=F32)


def swap_quarters(value):
    lanes = value.shape[1]
    lane = lax.broadcasted_iota(jnp.int32, value.shape, 1)
    even = (lane // (HEAD // 4)) % 2 == 0
    return jnp.where(
        even, pltpu.roll(value, lanes - HEAD // 4, 1), pltpu.roll(value, HEAD // 4, 1)
    )


def head_lanes(shape, head):
    lane = lax.broadcasted_iota(jnp.int32, shape, 1)
    return (lane >= head * HEAD) & (lane < (head + 1) * HEAD)


def of_head(value, head):
    return jnp.where(head_lanes(value.shape, head), value, jnp.zeros_like(value))


def attention_kernel(
    patches, mod_in, b_ada, pos_in, freqs, cap_in, qkvo_in, ffn_in, grp_items, key_items,
    gain_in, gain_kq, gain_ckey, gate_row,
    branch, norm_in, qkvo, ffn, mod, queries, kv, k_all, v_all, kq_hat, kq_recip,
    cos_t, sin_t, totals, attn_self, attn_cross, mixed, cap_k, cap_v, cap_hat, cap_recip,
    x_buf, x_send, x_recv, w_send, w_recv, f_send, f_recv,
    m_acc, m_land, m_slots, m_send, m_recv,
    pos_buf, pos_send, pos_recv,
    cap_fc, cap_acc, cap_fy, cap_s, cap_r, cap_out, cap_z, cz_send, cz_recv,
    cap_kv, ckv_send, ckv_recv, kv_send, kv_recv, p1, fx1, tz1, fz1, s1, r1,
):
    place = Place()
    rows, width = patches.shape
    wq = queries.shape[1]
    heads = wq // HEAD
    both = 2 * rows
    enter([place.x_peer, place.c_peer, place.y_peer] + [place.z_peer[d] for d in (1, 2, 3)])

    weights = WeightGather(place, qkvo_in, qkvo, w_send, w_recv)
    weights.start()
    tokens = Gather(place, x_buf, x_send, x_recv)
    tokens.own[...] = patches[...]
    tokens.start()
    sums = AllSum(place, m_acc, m_land, m_slots, m_send, m_recv, False)
    m_acc[0] = mod_in[...]
    sums.start()
    caption = LaneScatter(place, cap_in, cap_fc, cap_acc, cap_fy, cap_s, cap_r)
    caption.start()
    pos_buf[place.z] = pos_in[...]
    own_pos = pos_buf.at[place.z]
    pos_out = [
        remote(own_pos, own_pos, pos_send.at[i], pos_recv.at[i], place.z_peer[d])
        for i, d in enumerate(NEAR)
    ]
    for copy in pos_out:
        copy.start()
    weights.pass_own()
    sums.step(0)
    sums.step(1)
    caption.step()
    mean = segments(2 * wq)
    lane = lax.broadcasted_iota(jnp.int32, (1, 2 * wq), 1)

    for i, d in enumerate(NEAR):
        slot = pos_buf.at[place.z_from(d)]
        remote(slot, slot, pos_send.at[i], pos_recv.at[i], place.z_peer[d]).wait_recv()
    lane_row = lax.broadcasted_iota(jnp.int32, (1, 2 * HEAD), 1)
    by_row = (lane_row // (HEAD // 2)) % 2 == 0
    sign = jnp.where((lane_row // (HEAD // 4)) % 2 == 0, -1.0, 1.0)
    for i in range(SPLIT):
        cols = pos_buf[i].T
        angle = jnp.where(by_row, cols[:, 0:1], cols[:, 1:2]) * freqs[...]
        cos_t[i] = jnp.cos(angle)
        sin_t[i] = jnp.sin(angle) * sign

    cap_out[...] = caption.finish().astype(BF)
    cap_sends = [
        remote(
            cap_out.at[place.z_to(d)], cap_z.at[place.z], cz_send.at[i], cz_recv.at[i],
            place.z_peer[d],
        )
        for i, d in enumerate(NEAR)
    ]
    for copy in cap_sends:
        copy.start()
    cap_z[place.z] = cap_out[place.z]
    tokens.pass_on()
    for i in range(3):
        weights.pass_z(i)
    for i in range(4):
        weights.pass_y(i)
    feed = WeightGather(place, ffn_in, ffn, f_send, f_recv)
    feed.start()
    feed.pass_own()
    mod[...] = sums.finish() + b_ada[...]
    for i, d in enumerate(NEAR):
        slot = cap_z.at[place.z_from(d)]
        remote(slot, slot, cz_send.at[i], cz_recv.at[i], place.z_peer[d]).wait_recv()
    cap_raw = (cap_z[0].astype(F32) + cap_z[1].astype(F32)) + (
        cap_z[2].astype(F32) + cap_z[3].astype(F32)
    )
    recip = lax.rsqrt(head_mean(cap_raw * cap_raw, mean) + EPS)
    hat = cap_raw * recip
    cap_hat[...] = hat
    cap_recip[...] = recip
    cap_gather = LaneGather(place, cap_kv, ckv_send, ckv_recv)
    cap_gather.own[...] = jnp.where(lane < wq, hat * gain_ckey[...], cap_raw).astype(BF)
    cap_gather.start()
    tokens.finish()
    cap_gather.pass_on()
    weights.finish()

    keep = LaneGather(place, kv, kv_send, kv_recv)

    def project(i, carry):
        at = pl.ds(pl.multiple_of(i * both, both), both)
        block = x_buf[pl.ds(i * 2, 2)].reshape(both, width).astype(F32)
        unit, _ = normed_pair(block)
        factor = gain_in[...] * (1.0 + item_rows(mod, grp_items[at], 0, width))
        norm = (unit * factor).astype(BF)
        norm_in[i] = norm
        raw = bdot(norm, qkvo[:, :, 0 : 2 * wq].reshape(width, 2 * wq))
        own_v = bdot(norm, qkvo[:, :, 2 * wq : 4 * wq].reshape(width, 2 * wq))
        recip = lax.rsqrt(head_mean(raw * raw, mean) + EPS)
        hat = raw * recip
        kq_hat[i] = hat
        kq_recip[i] = recip
        cos = jnp.concatenate([cos_t[i]] * heads, axis=1)
        sin = jnp.concatenate([sin_t[i]] * heads, axis=1)
        gained = hat * gain_kq[...]
        turned = gained * cos + swap_quarters(gained) * sin
        kv[place.g, at] = jnp.where(lane < wq, turned, own_v).astype(BF)
        queries[at] = turned[:, wq:].astype(BF)
        return carry

    lax.fori_loop(0, SPLIT, project, 0)
    keep.start()
    for i in range(3):
        feed.pass_z(i)
    cap_gather.finish()
    kv_text = cap_kv[...].reshape(SPLIT * cap_kv.shape[1], 2 * wq)
    cap_k[...] = kv_text[:, :wq]
    cap_v[...] = kv_text[:, wq:]
    scale = 1.0 / math.sqrt(HEAD)
    gates = gate_row[...]

    def one_head(block, keys, vals, head, same):
        scores = dot_t(of_head(block, head), keys)
        if same is not None:
            scores = jnp.where(same, scores, NEG)
        most = jnp.max(scores, axis=1, keepdims=True)
        weight = jnp.exp(scores - most)
        total = jnp.sum(weight, axis=1, keepdims=True)
        out = bdot((weight * (1.0 / total)).astype(BF), vals)
        return of_head(out, head), most + jnp.log(total)

    slot_lane = lax.broadcasted_iota(jnp.int32, (1, totals.shape[1]), 1)

    def cross(i, carry):
        at = pl.ds(pl.multiple_of(i * both, both), both)
        block = (queries[at].astype(F32) * scale).astype(BF)
        out = jnp.zeros((both, wq), F32)
        logs = jnp.zeros((both, totals.shape[1]), F32)
        for head in range(heads):
            part, log = one_head(block, cap_k[...], cap_v[...], head, None)
            out = out + part
            logs = logs + jnp.where(slot_lane == heads + head, log, 0.0)
        attn_cross[at] = out
        totals[at] = logs
        return carry

    lax.fori_loop(0, SPLIT, cross, 0)
    keep.pass_on()
    keep.finish()
    for i in range(SPLIT):
        lump = kv[i]
        at = pl.ds(i * lump.shape[0], lump.shape[0])
        k_all[at] = lump[:, :wq]
        v_all[at] = lump[:, wq:]
    for i in range(4):
        feed.pass_y(i)

    def attend(i, carry):
        at = pl.ds(pl.multiple_of(i * both, both), both)
        block = (queries[at].astype(F32) * scale).astype(BF)
        same = grp_items[at] == key_items[...]
        out = jnp.zeros((both, wq), F32)
        logs = totals[at]
        for head in range(heads):
            part, log = one_head(block, k_all[...], v_all[...], head, same)
            out = out + part
            logs = logs + jnp.where(slot_lane == head, log, 0.0)
        attn_self[at] = out
        totals[at] = logs
        blend = (out + gates * attn_cross[at]).astype(BF)
        mixed[at] = blend
        wide = jnp.concatenate([blend, jnp.zeros_like(blend)], axis=1)
        p1[i] = (
            dot_t(wide, qkvo[:, :, 2 * wq : 4 * wq].reshape(width, 2 * wq))
            .astype(BF)
            .reshape(2, rows, width)
        )
        return carry

    lax.fori_loop(0, SPLIT, attend, 0)
    out = Scatter(place, p1, fx1, tz1, fz1, s1, r1)
    for i in range(4):
        out.send_x(i)
    out.pass_on()
    feed.finish()
    branch[...] = out.finish()
    for copy in pos_out + cap_sends:
        copy.wait_send()


def attention_call(
    patches, mod_in, b_ada, pos_in, freqs, cap_in, qkvo_in, ffn_in, grp_items, key_items,
    gain_in, gain_kq, gain_ckey, gate_row,
):
    rows, width = patches.shape
    wq = qkvo_in.shape[2] // 4
    lanes = cap_in.shape[0] * cap_in.shape[1]
    text = cap_in.shape[3]
    both = 2 * rows
    group = SPLIT * both
    vmem = pl.BlockSpec(memory_space=pltpu.VMEM)
    hbm = pl.BlockSpec(memory_space=pl.ANY)
    shape = jax.ShapeDtypeStruct
    dma = pltpu.SemaphoreType.DMA
    outs = {
        "branch": shape((rows, width), F32),
        "norm_in": shape((SPLIT, both, width), BF),
        "qkvo": shape((SPLIT * lanes,) + qkvo_in.shape[1:], BF),
        "ffn": shape((SPLIT * lanes,) + ffn_in.shape[1:], BF),
        "mod": shape(mod_in.shape, F32),
        "queries": shape((group, wq), BF),
        "kv": shape((lanes, group, 2 * wq), BF),
        "k_all": shape((lanes * group, wq), BF),
        "v_all": shape((lanes * group, wq), BF),
        "kq_hat": shape((SPLIT, both, 2 * wq), F32),
        "kq_recip": shape((SPLIT, both, 2 * wq), F32),
        "cos": shape((SPLIT, both, 2 * HEAD), F32),
        "sin": shape((SPLIT, both, 2 * HEAD), F32),
        "totals": shape((group, 128), F32),
        "attn_self": shape((group, wq), F32),
        "attn_cross": shape((group, wq), F32),
        "mixed": shape((group, wq), BF),
        "cap_k": shape((lanes * text, wq), BF),
        "cap_v": shape((lanes * text, wq), BF),
        "cap_hat": shape((text, 2 * wq), F32),
        "cap_recip": shape((text, 2 * wq), F32),
    }
    results = pl.pallas_call(
        attention_kernel,
        out_shape=tuple(outs.values()),
        in_specs=[vmem] * 7 + [hbm] + [vmem] * 6,
        out_specs=[hbm if name == "ffn" else vmem for name in outs],
        scratch_shapes=gather_scratch(rows, width)
        + [dma((16,)), dma((16,)), dma((16,)), dma((16,))]
        + [
            pltpu.VMEM((2,) + mod_in.shape, F32),
            pltpu.VMEM((2,) + mod_in.shape, F32),
            pltpu.VMEM((SPLIT,) + mod_in.shape, F32),
            dma((6,)),
            dma((6,)),
        ]
        + [pltpu.VMEM((SPLIT,) + pos_in.shape, F32), dma((3,)), dma((3,))]
        + [
            pltpu.VMEM(cap_in.shape[1:], BF),
            pltpu.VMEM(cap_in.shape[1:], BF),
            pltpu.VMEM(cap_in.shape[2:], BF),
            dma((2,)),
            dma((2,)),
            pltpu.VMEM(cap_in.shape[2:], BF),
            pltpu.VMEM(cap_in.shape[2:], BF),
            dma((3,)),
            dma((3,)),
            pltpu.VMEM((lanes, text, 2 * wq), BF),
            dma((3,)),
            dma((3,)),
        ]
        + [dma((3,)), dma((3,))]
        + scatter_scratch(rows, width),
        compiler_params=pltpu.CompilerParams(
            collective_id=1, has_side_effects=True, vmem_limit_bytes=VMEM_LIMIT
        ),
        name="attention",
    )(
        patches, mod_in, b_ada, pos_in, freqs, cap_in, qkvo_in, ffn_in, grp_items, key_items,
        gain_in, gain_kq, gain_ckey, gate_row,
    )
    return dict(zip(outs, results))


def local_any(
    patches,
    caption,
    band_table,
    block_item,
    item_band,
    positions,
    out_grad,
    w_query,
    w_key,
    w_value,
    w_out,
    w_gate,
    w_up,
    w_down,
    w_ckey,
    w_cvalue,
    w_ada,
    b_ada,
    g_attn_in,
    g_attn_out,
    g_ffn_in,
    g_ffn_out,
    g_query,
    g_key,
    g_ckey,
    cross_gate,
):
    scale = 1.0 / math.sqrt(HEAD)
    rank = lax.axis_index("sp")
    half = lax.axis_index("tp")
    cycle = lax.axis_size("sp")
    halves = lax.axis_size("tp")
    lanes = cycle // SPLIT
    along_z, along_g = groups_of(cycle)
    my_z, my_g = rank // lanes, rank % lanes
    tok_rows, width = patches.shape
    own_rows = tok_rows // halves
    text_count = caption.shape[0]
    blocks_dev = tok_rows // BLK
    wq, wf = w_query.shape[1] // SPLIT, w_gate.shape[1] // SPLIT
    heads = wq // HEAD
    sizes = (wq, wq, wq, wq, wf, wf, wf)
    starts = [sum(sizes[:i]) for i in range(8)]

    def gather_z(block):
        return lax.all_gather(block, "sp", axis_index_groups=along_z, axis=0, tiled=False)

    def gather_g(block):
        return lax.all_gather(block, "sp", axis_index_groups=along_g, axis=0, tiled=False)

    def scatter_z(block):
        return lax.psum_scatter(
            block, "sp", axis_index_groups=along_z, scatter_dimension=0, tiled=False
        )

    def scatter_g(block):
        return lax.psum_scatter(
            block, "sp", axis_index_groups=along_g, scatter_dimension=0, tiled=False
        )

    def turn_z(block):
        return lax.all_to_all(
            block, "sp", 0, 0, axis_index_groups=along_z, tiled=True
        )

    def sum_g(block):
        return lax.psum(block, "sp", axis_index_groups=along_g)

    def gather_tokens(own):
        both = lax.all_gather(own, "tp", axis=0, tiled=True)
        return gather_z(both).reshape(SPLIT * tok_rows, -1)

    def scatter_tokens(part):
        part = part.astype(BF).reshape(SPLIT, halves, own_rows, width)
        mine = lax.psum_scatter(part, "tp", scatter_dimension=1, tiled=False)
        return scatter_z(mine.astype(BF)).astype(F32)

    def by_z(block):
        rows, cols = block.shape
        return block.reshape(rows, SPLIT, cols // SPLIT).transpose(1, 0, 2)

    shards = jnp.concatenate(
        [by_z(m) for m in (w_query, w_key, w_value, w_out.T, w_gate, w_up, w_down.T)], axis=2
    )
    rows_dev = shards.shape[1]
    merged = gather_g(turn_z(shards)).transpose(1, 0, 2, 3).reshape(cycle * rows_dev, -1)
    f_query, f_key, f_value, f_out, f_gate, f_up, f_down = (
        merged[:, starts[i] : starts[i + 1]] for i in range(7)
    )

    items_all = block_item.reshape(SPLIT, lanes, blocks_dev)
    grp_items = jnp.repeat(
        lax.dynamic_index_in_dim(items_all, my_g, 1, keepdims=False).reshape(-1), BLK
    )
    key_items = jnp.repeat(items_all.transpose(1, 0, 2).reshape(-1), BLK)
    row0 = half * own_rows

    def own_part(block):
        return lax.dynamic_slice_in_dim(block, row0, own_rows, 0)

    own_items = own_part(
        jnp.repeat(lax.dynamic_slice_in_dim(block_item, rank * blocks_dev, blocks_dev), BLK)
    )

    band_hot = (item_band[:, None] == jnp.arange(BANDS, dtype=jnp.int32)[None, :]).astype(F32)
    cond_pre = jnp.dot(band_hot, band_table, precision=HIGH)
    cond_sig = jax.nn.sigmoid(cond_pre)
    cond_low = (cond_pre * cond_sig).astype(BF)
    text_rows = w_ckey.shape[0]
    text_local = lax.dynamic_slice_in_dim(caption, rank * text_rows, text_rows, 1)
    modulation = lax.psum(bdot(cond_low, w_ada), "sp") + b_ada
    cap_part = jnp.stack([by_z(bdot(text_local, w_ckey)), by_z(bdot(text_local, w_cvalue))], 1)
    cap_raw = sum_g(scatter_z(cap_part))
    ckey_hat, ckey_recip = normed_pair(cap_raw[0].reshape(text_count, heads, HEAD))

    def per_head(vector):
        return lax.dynamic_slice_in_dim(vector, my_z * wq, wq, 0).reshape(heads, HEAD)

    gain_query, gain_key, gain_ckey = per_head(g_query), per_head(g_key), per_head(g_ckey)
    gate_tanh = jnp.tanh(lax.dynamic_slice_in_dim(cross_gate, my_z * heads, heads, 0))
    cap_keys = (ckey_hat * gain_ckey).astype(BF)
    cap_values = cap_raw[1].astype(BF).reshape(text_count, heads, HEAD)

    def of_items(rows, items):
        return jnp.where(items[:, None] == 0, rows[0], rows[1])

    mod_own = of_items(modulation, own_items)
    scale_attn, gate_attn, scale_ffn, gate_ffn = (
        mod_own[:, i * width : (i + 1) * width] for i in range(4)
    )
    group_rows = SPLIT * tok_rows

    patch_f = own_part(patches).astype(F32)
    grad_out = own_part(out_grad).astype(F32)
    hat_one, recip_one = normed_pair(patch_f)
    factor_one = g_attn_in * (1.0 + scale_attn)
    norm_in = gather_tokens((hat_one * factor_one).astype(BF))
    pos_all = gather_z(positions).transpose(1, 0, 2).reshape(2, group_rows)
    cos_row, sin_row, cos_col, sin_col = angles(pos_all)
    split_heads = (group_rows, heads, HEAD)
    query_raw = bdot(norm_in, f_query).reshape(split_heads)
    key_raw = bdot(norm_in, f_key).reshape(split_heads)
    values_low = bdot(norm_in, f_value).astype(BF)
    query_hat, query_recip = normed_pair(query_raw)
    queries = rotate(query_hat * gain_query, cos_row, sin_row, cos_col, sin_col).astype(BF)
    key_hat, key_recip = normed_pair(key_raw)
    keys_low = rotate(key_hat * gain_key, cos_row, sin_row, cos_col, sin_col).astype(BF)
    all_keys, all_values = (
        gather_g(block).reshape(lanes * group_rows, heads, HEAD)
        for block in (keys_low.reshape(group_rows, wq), values_low)
    )
    same = (grp_items[:, None] == key_items[None, :])[None]
    scores = jnp.einsum("qhd,khd->hqk", queries, all_keys, preferred_element_type=F32) * scale
    scores = jnp.where(same, scores, NEG)
    exps = jnp.exp(scores - jnp.max(scores, axis=-1, keepdims=True))
    probs = exps / jnp.sum(exps, axis=-1, keepdims=True)
    probs_low = probs.astype(BF)
    attn_self = jnp.einsum("hqk,khd->qhd", probs_low, all_values, preferred_element_type=F32)
    cross_scores = (
        jnp.einsum("qhd,khd->hqk", queries, cap_keys, preferred_element_type=F32) * scale
    )
    cross_exp = jnp.exp(cross_scores - jnp.max(cross_scores, axis=-1, keepdims=True))
    cross_probs = cross_exp / jnp.sum(cross_exp, axis=-1, keepdims=True)
    cross_low = cross_probs.astype(BF)
    attn_cross = jnp.einsum("hqk,khd->qhd", cross_low, cap_values, preferred_element_type=F32)
    mixed = (attn_self + gate_tanh[None, :, None] * attn_cross).astype(BF).reshape(group_rows, wq)
    attn_branch = scatter_tokens(dot_t(mixed, f_out))

    hat_two, recip_two = normed_pair(attn_branch)
    tanh_one = jnp.tanh(gate_attn)
    resid = patch_f + tanh_one * hat_two * g_attn_out
    hat_three, recip_three = normed_pair(resid)
    factor_three = g_ffn_in * (1.0 + scale_ffn)
    norm_ffn = gather_tokens((hat_three * factor_three).astype(BF))
    gate_val = bdot(norm_ffn, f_gate)
    up_val = bdot(norm_ffn, f_up)
    gate_sig = jax.nn.sigmoid(gate_val)
    hidden = (gate_val * gate_sig * up_val).astype(BF)
    ffn_branch = scatter_tokens(dot_t(hidden, f_down))
    hat_four, recip_four = normed_pair(ffn_branch)
    tanh_two = jnp.tanh(gate_ffn)
    output = resid + tanh_two * hat_four * g_ffn_out

    grad_gate_ffn = grad_out * hat_four * g_ffn_out * (1.0 - tanh_two * tanh_two)
    grad_four = grad_out * tanh_two
    grad_g_ffn_out = jnp.sum(grad_four * hat_four, axis=0)
    grad_ffn = gather_tokens(
        normed_back(grad_four * g_ffn_out, hat_four, recip_four).astype(BF)
    )
    grad_hidden = bdot(grad_ffn, f_down)
    grad_gate = (grad_hidden * up_val * gate_sig * (1.0 + gate_val * (1.0 - gate_sig))).astype(BF)
    grad_up = (grad_hidden * gate_val * gate_sig).astype(BF)
    grad_norm_ffn = scatter_tokens(dot_t(grad_gate, f_gate) + dot_t(grad_up, f_up))
    grad_scale_ffn = grad_norm_ffn * hat_three * g_ffn_in
    grad_g_ffn_in = jnp.sum(grad_norm_ffn * hat_three * (1.0 + scale_ffn), axis=0)
    grad_resid = grad_out + normed_back(grad_norm_ffn * factor_three, hat_three, recip_three)

    grad_gate_attn = grad_resid * hat_two * g_attn_out * (1.0 - tanh_one * tanh_one)
    grad_two = grad_resid * tanh_one
    grad_g_attn_out = jnp.sum(grad_two * hat_two, axis=0)
    grad_attn = gather_tokens(normed_back(grad_two * g_attn_out, hat_two, recip_two).astype(BF))
    grad_mixed = bdot(grad_attn, f_out).astype(BF).reshape(split_heads)
    grad_mixed_f = grad_mixed.astype(F32)
    grad_cross_gate = jnp.sum(grad_mixed_f * attn_cross, axis=(0, 2)) * (
        1.0 - gate_tanh * gate_tanh
    )
    grad_cross = (gate_tanh[None, :, None] * grad_mixed_f).astype(BF)
    grad_cprobs = jnp.einsum("qhd,khd->hqk", grad_cross, cap_values, preferred_element_type=F32)
    grad_cscores = (
        cross_probs * (grad_cprobs - jnp.sum(cross_probs * grad_cprobs, axis=-1, keepdims=True))
    ).astype(BF)
    query_grad = jnp.einsum("hqk,khd->qhd", grad_cscores, cap_keys, preferred_element_type=F32)
    grad_ckeys_part = (
        jnp.einsum("hqk,qhd->khd", grad_cscores, queries, preferred_element_type=F32) * scale
    )
    grad_cvals_part = jnp.einsum(
        "hqk,qhd->khd", cross_low, grad_cross, preferred_element_type=F32
    )
    row_delta = jnp.sum(grad_mixed_f * attn_self, axis=-1).T
    grad_probs = jnp.einsum("qhd,khd->hqk", grad_mixed, all_values, preferred_element_type=F32)
    grad_scores = (probs * (grad_probs - row_delta[..., None])).astype(BF)
    query_grad = query_grad + jnp.einsum(
        "hqk,khd->qhd", grad_scores, all_keys, preferred_element_type=F32
    )
    key_part = (
        jnp.einsum("hqk,qhd->khd", grad_scores, queries, preferred_element_type=F32) * scale
    )
    value_part = jnp.einsum("hqk,qhd->khd", probs_low, grad_mixed, preferred_element_type=F32)
    key_grad, value_grad = (
        scatter_g(block.astype(BF).reshape(lanes, group_rows, wq)) for block in (key_part, value_part)
    )
    grad_queries = (query_grad * scale).astype(BF).astype(F32)
    grad_qnorm = rotate(grad_queries, cos_row, -sin_row, cos_col, -sin_col)
    grad_g_query = jnp.sum(grad_qnorm * query_hat, axis=0).reshape(-1)
    grad_query_raw = (
        normed_back(grad_qnorm * gain_query, query_hat, query_recip).astype(BF).reshape(-1, wq)
    )
    grad_keys = key_grad.astype(F32).reshape(split_heads)
    grad_knorm = rotate(grad_keys, cos_row, -sin_row, cos_col, -sin_col)
    grad_g_key = jnp.sum(grad_knorm * key_hat, axis=0).reshape(-1)
    grad_key_raw = (
        normed_back(grad_knorm * gain_key, key_hat, key_recip).astype(BF).reshape(-1, wq)
    )
    grad_values = value_grad.astype(BF)
    grad_norm_in = scatter_tokens(
        dot_t(grad_query_raw, f_query) + dot_t(grad_key_raw, f_key) + dot_t(grad_values, f_value)
    )
    grad_scale_attn = grad_norm_in * hat_one * g_attn_in
    grad_g_attn_in = jnp.sum(grad_norm_in * hat_one * (1.0 + scale_attn), axis=0)
    grad_patches = grad_resid + normed_back(grad_norm_in * factor_one, hat_one, recip_one)

    grad_merged = jnp.concatenate(
        [
            t_dot(norm_in, grad_query_raw),
            t_dot(norm_in, grad_key_raw),
            t_dot(norm_in, grad_values),
            t_dot(grad_attn, mixed),
            t_dot(norm_ffn, grad_gate),
            t_dot(norm_ffn, grad_up),
            t_dot(grad_ffn, hidden),
        ],
        axis=1,
    ).astype(BF)
    grad_merged = grad_merged.reshape(SPLIT, lanes, rows_dev, -1).transpose(1, 0, 2, 3)
    shard_grads = turn_z(scatter_g(grad_merged)).astype(F32)
    (shard_query, shard_key, shard_value, shard_out, shard_gate, shard_up, shard_down) = (
        shard_grads[:, :, starts[i] : starts[i + 1]].transpose(1, 0, 2).reshape(rows_dev, -1)
        for i in range(7)
    )

    token_sums = lax.psum(
        (
            jnp.stack(
                [
                    jnp.concatenate(
                        [
                            jnp.sum(
                                jnp.where((own_items == item)[:, None], block, 0.0), axis=0
                            )
                            for block in (
                                grad_scale_attn,
                                grad_gate_attn,
                                grad_scale_ffn,
                                grad_gate_ffn,
                            )
                        ]
                    )
                    for item in range(ITEMS)
                ]
            ),
            grad_g_attn_in,
            grad_g_attn_out,
            grad_g_ffn_in,
            grad_g_ffn_out,
        ),
        ("sp", "tp"),
    )
    head_sums = jnp.concatenate([grad_g_query, grad_g_key, grad_cross_gate])
    head_sums = gather_z(sum_g(head_sums))
    grad_ckeys = sum_g(grad_ckeys_part).astype(BF).astype(F32)
    grad_cvals = sum_g(grad_cvals_part).astype(BF).reshape(text_count, wq)
    grad_g_ckey = gather_z(jnp.sum(grad_ckeys * ckey_hat, axis=0).reshape(-1)).reshape(-1)
    grad_ckey_raw = (
        normed_back(grad_ckeys * gain_ckey, ckey_hat, ckey_recip).astype(BF).reshape(text_count, wq)
    )
    cap_grads = gather_z(jnp.stack([grad_ckey_raw, grad_cvals])).transpose(1, 2, 0, 3)
    cap_grads = cap_grads.reshape(2, text_count, SPLIT * wq)
    grad_mod = token_sums[0]
    grad_b_ada = jnp.sum(grad_mod, axis=0)
    grad_w_ada = jnp.dot(cond_low.astype(F32).T, grad_mod, precision=HIGH)
    grad_cond_act = jnp.dot(grad_mod, w_ada.astype(F32).T, precision=HIGH)
    grad_cond_pre = grad_cond_act * cond_sig * (1.0 + cond_pre * (1.0 - cond_sig))
    grad_band_table = jnp.dot(band_hot.T, grad_cond_pre, precision=HIGH)
    return (
        lax.all_gather(output, "tp", axis=0, tiled=True),
        lax.all_gather(grad_patches, "tp", axis=0, tiled=True),
        shard_query,
        shard_key,
        shard_value,
        shard_out.T,
        shard_gate,
        shard_up,
        shard_down.T,
        t_dot(text_local, cap_grads[0]),
        t_dot(text_local, cap_grads[1]),
        grad_w_ada,
        grad_b_ada,
        token_sums[1],
        token_sums[2],
        token_sums[3],
        token_sums[4],
        head_sums[:, :wq].reshape(-1),
        head_sums[:, wq : 2 * wq].reshape(-1),
        grad_g_ckey,
        head_sums[:, 2 * wq :].reshape(-1),
        grad_band_table,
    )


def local(
    patches,
    caption,
    band_table,
    block_item,
    item_band,
    positions,
    out_grad,
    w_query,
    w_key,
    w_value,
    w_out,
    w_gate,
    w_up,
    w_down,
    w_ckey,
    w_cvalue,
    w_ada,
    b_ada,
    g_attn_in,
    g_attn_out,
    g_ffn_in,
    g_ffn_out,
    g_query,
    g_key,
    g_ckey,
    cross_gate,
):
    scale = 1.0 / math.sqrt(HEAD)
    rank = lax.axis_index("sp")
    half = lax.axis_index("tp")
    cycle = lax.axis_size("sp")
    halves = lax.axis_size("tp")
    lanes = cycle // SPLIT
    along_z, along_g = groups_of(cycle)
    my_z, my_g = rank // lanes, rank % lanes
    tok_rows, width = patches.shape
    own_rows = tok_rows // halves
    text_count = caption.shape[0]
    blocks_dev = tok_rows // BLK
    wq, wf = w_query.shape[1] // SPLIT, w_gate.shape[1] // SPLIT
    heads = wq // HEAD
    sizes = (wq, wq, wq, wq, wf, wf, wf)
    starts = [sum(sizes[:i]) for i in range(8)]

    def gather_z(block):
        return lax.all_gather(block, "sp", axis_index_groups=along_z, axis=0, tiled=False)

    def gather_g(block):
        return lax.all_gather(block, "sp", axis_index_groups=along_g, axis=0, tiled=False)

    def scatter_z(block):
        return lax.psum_scatter(
            block, "sp", axis_index_groups=along_z, scatter_dimension=0, tiled=False
        )

    def scatter_g(block):
        return lax.psum_scatter(
            block, "sp", axis_index_groups=along_g, scatter_dimension=0, tiled=False
        )

    def turn_z(block):
        return lax.all_to_all(
            block, "sp", 0, 0, axis_index_groups=along_z, tiled=True
        )

    def sum_g(block):
        return lax.psum(block, "sp", axis_index_groups=along_g)

    def gather_tokens(own):
        both = lax.all_gather(own, "tp", axis=0, tiled=True)
        return gather_z(both).reshape(SPLIT * tok_rows, -1)

    def scatter_tokens(part):
        part = part.astype(BF).reshape(SPLIT, halves, own_rows, width)
        mine = lax.psum_scatter(part, "tp", scatter_dimension=1, tiled=False)
        return scatter_z(mine.astype(BF)).astype(F32)

    def by_z(block):
        rows, cols = block.shape
        return block.reshape(rows, SPLIT, cols // SPLIT).transpose(1, 0, 2)

    qkvo_in = jnp.concatenate([by_z(m) for m in (w_key, w_query, w_out.T, w_value)], axis=2)
    ffn_in = jnp.concatenate([by_z(m) for m in (w_gate, w_up, w_down.T)], axis=2)
    rows_dev = ffn_in.shape[1]

    items_all = block_item.reshape(SPLIT, lanes, blocks_dev)
    grp_items = jnp.repeat(
        lax.dynamic_index_in_dim(items_all, my_g, 1, keepdims=False).reshape(-1), BLK
    )
    key_items = jnp.repeat(items_all.transpose(1, 0, 2).reshape(-1), BLK)
    row0 = half * own_rows

    def own_part(block):
        return lax.dynamic_slice_in_dim(block, row0, own_rows, 0)

    own_items = own_part(
        jnp.repeat(lax.dynamic_slice_in_dim(block_item, rank * blocks_dev, blocks_dev), BLK)
    )

    band_hot = (item_band[:, None] == jnp.arange(BANDS, dtype=jnp.int32)[None, :]).astype(F32)
    cond_pre = jnp.dot(band_hot, band_table, precision=HIGH)
    cond_sig = jax.nn.sigmoid(cond_pre)
    cond_low = (cond_pre * cond_sig).astype(BF)
    text_rows = w_ckey.shape[0]
    text_local = lax.dynamic_slice_in_dim(caption, rank * text_rows, text_rows, 1)
    cap_part = jnp.concatenate(
        [by_z(bdot(text_local, w_ckey)), by_z(bdot(text_local, w_cvalue))], axis=2
    ).astype(BF)
    cap_part = cap_part.reshape(SPLIT, 2, 2, text_count // lanes, 2 * wq).transpose(2, 1, 0, 3, 4)

    def per_head(vector):
        return lax.dynamic_slice_in_dim(vector, my_z * wq, wq, 0).reshape(heads, HEAD)

    gain_query, gain_key, gain_ckey = per_head(g_query), per_head(g_key), per_head(g_ckey)
    gate_tanh = jnp.tanh(lax.dynamic_slice_in_dim(cross_gate, my_z * heads, heads, 0))
    def of_items(rows, items):
        return jnp.where(items[:, None] == 0, rows[0], rows[1])

    group_rows = SPLIT * tok_rows

    row = lambda vector: vector.reshape(1, -1)
    lane = jnp.arange(2 * HEAD)
    freqs = FREQ_BASE ** (-(lane % (HEAD // 4)).astype(F32) / (HEAD // 4))
    att = attention_call(
        own_part(patches),
        bdot(cond_low, w_ada),
        row(b_ada),
        jnp.pad(positions.astype(F32), ((0, 6), (0, 0))),
        row(freqs),
        cap_part,
        qkvo_in,
        ffn_in,
        grp_items[:, None],
        row(key_items),
        row(g_attn_in),
        jnp.concatenate([row(gain_key), row(gain_query)], axis=1),
        jnp.concatenate([row(gain_ckey), jnp.ones((1, wq), F32)], axis=1),
        row(jnp.repeat(gate_tanh, HEAD)),
    )
    attn_branch = att["branch"]
    modulation = att["mod"]
    ffn_w = att["ffn"].reshape(width, -1)
    f_gate, f_up, f_down = (ffn_w[:, i * wf : (i + 1) * wf] for i in range(3))
    qkvo = att["qkvo"].reshape(width, -1)
    f_key, f_query, f_out, f_value = (qkvo[:, i * wq : (i + 1) * wq] for i in range(4))
    norm_in = att["norm_in"].reshape(group_rows, width)
    split_heads = (group_rows, heads, HEAD)
    queries = att["queries"].reshape(split_heads)
    all_keys, all_values = (att[n].reshape(-1, heads, HEAD) for n in ("k_all", "v_all"))
    kq_hat = att["kq_hat"].reshape(group_rows, 2, heads, HEAD)
    kq_recip = att["kq_recip"].reshape(group_rows, 2, heads, HEAD)
    key_hat, query_hat = kq_hat[:, 0], kq_hat[:, 1]
    key_recip, query_recip = kq_recip[:, 0], kq_recip[:, 1]
    attn_self, attn_cross = (att[n].reshape(split_heads) for n in ("attn_self", "attn_cross"))
    mixed = att["mixed"]
    cap_keys, cap_values = (att[n].reshape(text_count, heads, HEAD) for n in ("cap_k", "cap_v"))
    ckey_hat, ckey_recip = (
        gather_g(att[n][:, :wq]).reshape(text_count, heads, HEAD) for n in ("cap_hat", "cap_recip")
    )
    log_total = att["totals"][:, :heads].T
    cross_log = att["totals"][:, heads : 2 * heads].T
    cos64, sin64 = (att[n].reshape(group_rows, 2 * HEAD)[:, None, :HEAD] for n in ("cos", "sin"))
    quarter = HEAD // 4
    cos_row, cos_col = cos64[..., :quarter], cos64[..., 2 * quarter : 3 * quarter]
    sin_row, sin_col = sin64[..., quarter : 2 * quarter], sin64[..., 3 * quarter :]
    mod_own = of_items(modulation, own_items)
    scale_attn = mod_own[:, :width]
    hat_one, recip_one = normed_pair(own_part(patches).astype(F32))
    factor_one = g_attn_in * (1.0 + scale_attn)
    same = (grp_items[:, None] == key_items[None, :])[None]
    scores = jnp.einsum("qhd,khd->hqk", queries, all_keys, preferred_element_type=F32) * scale
    probs = jnp.where(same, jnp.exp(scores - log_total[..., None]), 0.0)
    probs_low = probs.astype(BF)
    cross_scores = (
        jnp.einsum("qhd,khd->hqk", queries, cap_keys, preferred_element_type=F32) * scale
    )
    cross_probs = jnp.exp(cross_scores - cross_log[..., None])
    cross_low = cross_probs.astype(BF)

    output, grad_resid, grad_attn, ffn_sums, ffn_grads = ffn_call(
        attn_branch,
        own_part(patches),
        own_part(out_grad),
        modulation,
        own_items[:, None],
        row(g_attn_out),
        row(g_ffn_in),
        row(g_ffn_out),
        f_gate,
        f_up,
        f_down,
    )

    grad_attn = gather_tokens(grad_attn)
    grad_mixed = bdot(grad_attn, f_out).astype(BF).reshape(split_heads)
    grad_mixed_f = grad_mixed.astype(F32)
    grad_cross_gate = jnp.sum(grad_mixed_f * attn_cross, axis=(0, 2)) * (
        1.0 - gate_tanh * gate_tanh
    )
    grad_cross = (gate_tanh[None, :, None] * grad_mixed_f).astype(BF)
    grad_cprobs = jnp.einsum("qhd,khd->hqk", grad_cross, cap_values, preferred_element_type=F32)
    grad_cscores = (
        cross_probs * (grad_cprobs - jnp.sum(cross_probs * grad_cprobs, axis=-1, keepdims=True))
    ).astype(BF)
    query_grad = jnp.einsum("hqk,khd->qhd", grad_cscores, cap_keys, preferred_element_type=F32)
    grad_ckeys_part = (
        jnp.einsum("hqk,qhd->khd", grad_cscores, queries, preferred_element_type=F32) * scale
    )
    grad_cvals_part = jnp.einsum(
        "hqk,qhd->khd", cross_low, grad_cross, preferred_element_type=F32
    )
    row_delta = jnp.sum(grad_mixed_f * attn_self, axis=-1).T
    grad_probs = jnp.einsum("qhd,khd->hqk", grad_mixed, all_values, preferred_element_type=F32)
    grad_scores = (probs * (grad_probs - row_delta[..., None])).astype(BF)
    query_grad = query_grad + jnp.einsum(
        "hqk,khd->qhd", grad_scores, all_keys, preferred_element_type=F32
    )
    key_part = (
        jnp.einsum("hqk,qhd->khd", grad_scores, queries, preferred_element_type=F32) * scale
    )
    value_part = jnp.einsum("hqk,qhd->khd", probs_low, grad_mixed, preferred_element_type=F32)
    key_grad, value_grad = (
        scatter_g(block.astype(BF).reshape(lanes, group_rows, wq)) for block in (key_part, value_part)
    )
    grad_queries = (query_grad * scale).astype(BF).astype(F32)
    grad_qnorm = rotate(grad_queries, cos_row, -sin_row, cos_col, -sin_col)
    grad_g_query = jnp.sum(grad_qnorm * query_hat, axis=0).reshape(-1)
    grad_query_raw = (
        normed_back(grad_qnorm * gain_query, query_hat, query_recip).astype(BF).reshape(-1, wq)
    )
    grad_keys = key_grad.astype(F32).reshape(split_heads)
    grad_knorm = rotate(grad_keys, cos_row, -sin_row, cos_col, -sin_col)
    grad_g_key = jnp.sum(grad_knorm * key_hat, axis=0).reshape(-1)
    grad_key_raw = (
        normed_back(grad_knorm * gain_key, key_hat, key_recip).astype(BF).reshape(-1, wq)
    )
    grad_values = value_grad.astype(BF)
    grad_norm_in = scatter_tokens(
        dot_t(grad_query_raw, f_query) + dot_t(grad_key_raw, f_key) + dot_t(grad_values, f_value)
    )
    grad_scale_attn = grad_norm_in * hat_one * g_attn_in
    grad_g_attn_in = jnp.sum(grad_norm_in * hat_one * (1.0 + scale_attn), axis=0)
    grad_patches = grad_resid + normed_back(grad_norm_in * factor_one, hat_one, recip_one)

    grad_merged = jnp.concatenate(
        [
            t_dot(norm_in, grad_query_raw),
            t_dot(norm_in, grad_key_raw),
            t_dot(norm_in, grad_values),
            t_dot(grad_attn, mixed),
        ],
        axis=1,
    ).astype(BF)
    grad_merged = jnp.concatenate([grad_merged, ffn_grads], axis=1)
    grad_merged = grad_merged.reshape(SPLIT, lanes, rows_dev, -1).transpose(1, 0, 2, 3)
    shard_grads = turn_z(scatter_g(grad_merged)).astype(F32)
    (shard_query, shard_key, shard_value, shard_out, shard_gate, shard_up, shard_down) = (
        shard_grads[:, :, starts[i] : starts[i + 1]].transpose(1, 0, 2).reshape(rows_dev, -1)
        for i in range(7)
    )

    scale_sums = jnp.stack(item_sums(grad_scale_attn, own_items[:, None])).reshape(ITEMS, width)
    mod_sums = jnp.concatenate(
        [scale_sums, ffn_sums[4:6], ffn_sums[6:8], ffn_sums[8:10]], axis=1
    )
    token_sums = lax.psum(
        (mod_sums, grad_g_attn_in, ffn_sums[0], ffn_sums[1], ffn_sums[2]), ("sp", "tp")
    )
    head_sums = jnp.concatenate([grad_g_query, grad_g_key, grad_cross_gate])
    head_sums = gather_z(sum_g(head_sums))
    grad_ckeys = sum_g(grad_ckeys_part).astype(BF).astype(F32)
    grad_cvals = sum_g(grad_cvals_part).astype(BF).reshape(text_count, wq)
    grad_g_ckey = gather_z(jnp.sum(grad_ckeys * ckey_hat, axis=0).reshape(-1)).reshape(-1)
    grad_ckey_raw = (
        normed_back(grad_ckeys * gain_ckey, ckey_hat, ckey_recip).astype(BF).reshape(text_count, wq)
    )
    cap_grads = gather_z(jnp.stack([grad_ckey_raw, grad_cvals])).transpose(1, 2, 0, 3)
    cap_grads = cap_grads.reshape(2, text_count, SPLIT * wq)
    grad_mod = token_sums[0]
    grad_b_ada = jnp.sum(grad_mod, axis=0)
    grad_w_ada = jnp.dot(cond_low.astype(F32).T, grad_mod, precision=HIGH)
    grad_cond_act = jnp.dot(grad_mod, w_ada.astype(F32).T, precision=HIGH)
    grad_cond_pre = grad_cond_act * cond_sig * (1.0 + cond_pre * (1.0 - cond_sig))
    grad_band_table = jnp.dot(band_hot.T, grad_cond_pre, precision=HIGH)
    return (
        output.reshape(tok_rows, width),
        lax.all_gather(grad_patches, "tp", axis=0, tiled=True),
        shard_query,
        shard_key,
        shard_value,
        shard_out.T,
        shard_gate,
        shard_up,
        shard_down.T,
        t_dot(text_local, cap_grads[0]),
        t_dot(text_local, cap_grads[1]),
        grad_w_ada,
        grad_b_ada,
        token_sums[1],
        token_sums[2],
        token_sums[3],
        token_sums[4],
        head_sums[:, :wq].reshape(-1),
        head_sums[:, wq : 2 * wq].reshape(-1),
        grad_g_ckey,
        head_sums[:, 2 * wq :].reshape(-1),
        grad_band_table,
    )


def solution(mesh):
    lanes = mesh.shape["sp"] // SPLIT
    body = local if lanes == 4 and mesh.shape["tp"] == 2 else local_any
    in_specs = (
        P("sp", None),
        P(),
        P(None, "sp"),
        P(),
        P(),
        P(None, "sp"),
        P("sp", None),
        P("sp", "tp"),
        P("sp", "tp"),
        P("sp", "tp"),
        P("tp", "sp"),
        P("sp", "tp"),
        P("sp", "tp"),
        P("tp", "sp"),
        P("sp", "tp"),
        P("sp", "tp"),
        P("sp", None),
        P(),
        P(),
        P(),
        P(),
        P(),
        P("tp"),
        P("tp"),
        P("tp"),
        P("tp"),
    )
    out_specs = (
        P("sp", None),
        P("sp", None),
        P("sp", "tp"),
        P("sp", "tp"),
        P("sp", "tp"),
        P("tp", "sp"),
        P("sp", "tp"),
        P("sp", "tp"),
        P("tp", "sp"),
        P("sp", "tp"),
        P("sp", "tp"),
        P("sp", None),
        P(),
        P(),
        P(),
        P(),
        P(),
        P("tp"),
        P("tp"),
        P("tp"),
        P("tp"),
        P(None, "sp"),
    )
    return jax.shard_map(body, mesh=mesh, in_specs=in_specs, out_specs=out_specs, check_vma=False)
```

```python
import math

import jax
import jax.numpy as jnp
from jax import lax
from jax.experimental import pallas as pl
from jax.experimental.pallas import tpu as pltpu
from jax.sharding import PartitionSpec as P

BANDS = 16
ITEMS = 2
BLK = 32
HEAD = 64
EPS = 1e-06
NEG = -1e30
FREQ_BASE = 10000.0
HIGH = lax.Precision.HIGHEST
BF = jnp.bfloat16
F32 = jnp.float32
SPLIT = 4


def groups_of(cycle_size):
    lanes = cycle_size // SPLIT
    along_z = [[z * lanes + g for z in range(SPLIT)] for g in range(lanes)]
    along_g = [[z * lanes + g for g in range(lanes)] for z in range(SPLIT)]
    return along_z, along_g


def normed_pair(value):
    recip = lax.rsqrt(jnp.mean(value * value, axis=-1, keepdims=True) + EPS)
    return value * recip, recip


def normed_back(grad_hat, normal, recip):
    return recip * (grad_hat - normal * jnp.mean(grad_hat * normal, axis=-1, keepdims=True))


def rotate(value, cos_row, sin_row, cos_col, sin_col):
    quarter = value.shape[-1] // 4
    part_a = value[..., :quarter]
    part_b = value[..., quarter : 2 * quarter]
    part_c = value[..., 2 * quarter : 3 * quarter]
    part_e = value[..., 3 * quarter :]
    return jnp.concatenate(
        [
            part_a * cos_row - part_b * sin_row,
            part_a * sin_row + part_b * cos_row,
            part_c * cos_col - part_e * sin_col,
            part_c * sin_col + part_e * cos_col,
        ],
        axis=-1,
    )


def angles(positions):
    quarter = HEAD // 4
    freqs = FREQ_BASE ** (-jnp.arange(quarter, dtype=F32) / quarter)
    row_angle = positions[0].astype(F32)[:, None] * freqs[None, :]
    col_angle = positions[1].astype(F32)[:, None] * freqs[None, :]
    return (
        jnp.cos(row_angle)[:, None, :],
        jnp.sin(row_angle)[:, None, :],
        jnp.cos(col_angle)[:, None, :],
        jnp.sin(col_angle)[:, None, :],
    )


def bdot(left, right):
    return jnp.dot(left, right, preferred_element_type=F32)


def dot_t(left, right):
    return lax.dot_general(left, right, (((1,), (1,)), ((), ())), preferred_element_type=F32)


def t_dot(left, right):
    return lax.dot_general(left, right, (((0,), (0,)), ((), ())), preferred_element_type=F32)


MESH = pl.DeviceIdType.MESH
VMEM_LIMIT = 60 * 2**20


class Place:
    def __init__(self):
        rank = lax.axis_index("sp")
        self.lanes = lax.axis_size("sp") // SPLIT
        self.x = lax.axis_index("tp")
        self.z = rank // self.lanes
        self.g = rank % self.lanes
        self.x_peer = (rank, 1 - self.x)
        self.z_peer = {
            d: (lax.rem(self.z + d, SPLIT) * self.lanes + self.g, self.x) for d in (1, 2, 3)
        }
        self.y, self.c = self.g // 2, self.g % 2
        self.g_y = (1 - self.y) * 2 + self.c
        self.g_c = self.y * 2 + 1 - self.c
        self.g_yc = (1 - self.y) * 2 + 1 - self.c
        self.y_peer = (self.z * self.lanes + self.g_y, self.x)
        self.c_peer = (self.z * self.lanes + self.g_c, self.x)

    def z_from(self, d):
        return lax.rem(self.z + SPLIT - d, SPLIT)

    def z_to(self, d):
        return lax.rem(self.z + d, SPLIT)


def enter(peers):
    barrier = pltpu.get_barrier_semaphore()
    for peer in peers:
        pl.semaphore_signal(barrier, inc=1, device_id=peer, device_id_type=MESH)
    pl.semaphore_wait(barrier, len(peers))


def remote(src, dst, send, recv, peer):
    return pltpu.make_async_remote_copy(
        src_ref=src, dst_ref=dst, send_sem=send, recv_sem=recv, device_id=peer, device_id_type=MESH
    )


NEAR = (1, 3, 2)


class Gather:
    def __init__(self, place, buf, send, recv):
        self.place, self.buf = place, buf
        own = buf.at[place.z * 2 + place.x]
        self.own = own
        self.along_z = [
            remote(own, own, send.at[i], recv.at[i], place.z_peer[d]) for i, d in enumerate(NEAR)
        ]
        self.to_x = remote(own, own, send.at[3], recv.at[3], place.x_peer)
        self.landed = []
        self.forward = []
        for i, d in enumerate(NEAR):
            block = buf.at[place.z_from(d) * 2 + place.x]
            self.landed.append(remote(block, block, send.at[i], recv.at[i], place.z_peer[d]))
            self.forward.append(remote(block, block, send.at[4 + i], recv.at[4 + i], place.x_peer))
        self.other = [buf.at[place.z * 2 + 1 - place.x]] + [
            buf.at[place.z_from(d) * 2 + 1 - place.x] for d in NEAR
        ]
        self.arrive_x = [
            remote(block, block, send.at[3 + i], recv.at[3 + i], place.x_peer)
            for i, block in enumerate(self.other)
        ]

    def start(self):
        for copy in self.along_z:
            copy.start()
        self.to_x.start()

    def pass_on(self):
        for landed, forward in zip(self.landed, self.forward):
            landed.wait_recv()
            forward.start()

    def finish(self):
        for copy in self.arrive_x:
            copy.wait_recv()
        for copy in self.along_z + [self.to_x] + self.forward:
            copy.wait_send()


class Scatter:
    def __init__(self, place, part, from_x, to_z, from_z, send, recv):
        self.place, self.part, self.from_x = place, part, from_x
        self.to_z, self.from_z = to_z, from_z
        self.order = [place.z_to(d) for d in NEAR] + [place.z]
        self.across = [
            remote(
                part.at[target, 1 - place.x], from_x.at[i], send.at[i], recv.at[i], place.x_peer
            )
            for i, target in enumerate(self.order)
        ]
        self.along = [
            remote(to_z.at[i], from_z.at[i], send.at[4 + i], recv.at[4 + i], place.z_peer[d])
            for i, d in enumerate(NEAR)
        ]

    def send_x(self, i):
        self.across[i].start()

    def pass_on(self):
        for i in range(3):
            self.across[i].wait_recv()
            self.to_z[i] = (
                self.part[self.order[i], self.place.x].astype(F32) + self.from_x[i].astype(F32)
            ).astype(BF)
            self.along[i].start()

    def finish(self):
        self.across[3].wait_recv()
        total = self.part[self.place.z, self.place.x].astype(F32) + self.from_x[3].astype(F32)
        for i in range(3):
            self.along[i].wait_recv()
            total = total + self.from_z[i].astype(F32)
        for copy in self.across + self.along:
            copy.wait_send()
        return total


def gather_scratch(rows, width):
    return [
        pltpu.VMEM((2 * SPLIT, rows, width), BF),
        pltpu.SemaphoreType.DMA((7,)),
        pltpu.SemaphoreType.DMA((7,)),
    ]


def scatter_scratch(rows, width):
    return [
        pltpu.VMEM((SPLIT, 2, rows, width), BF),
        pltpu.VMEM((SPLIT, rows, width), BF),
        pltpu.VMEM((3, rows, width), BF),
        pltpu.VMEM((3, rows, width), BF),
        pltpu.SemaphoreType.DMA((7,)),
        pltpu.SemaphoreType.DMA((7,)),
    ]


def item_rows(mod, items, index, width):
    first = mod[0:1, index * width : (index + 1) * width]
    second = mod[1:2, index * width : (index + 1) * width]
    return jnp.where(items == 0, first, second)


def item_sums(value, items):
    return [
        jnp.sum(jnp.where(items == item, value, 0.0), axis=0, keepdims=True)
        for item in range(ITEMS)
    ]


def ffn_kernel(
    branch, patches, out_grad, mod, items, gain_out, gain_in, gain_ffn, w_gate, w_up, w_down,
    output, grad_resid, grad_attn, sums, grad_w,
    n_buf, n_send, n_recv, g_buf, g_send, g_recv,
    p1, fx1, tz1, fz1, s1, r1, p2, fx2, tz2, fz2, s2, r2,
    gate_s, up_s, hid_s, gg_s, gu_s, out_send, out_recv,
):
    place = Place()
    rows, width = branch.shape
    item = items[...]
    enter([place.x_peer] + [place.z_peer[d] for d in (1, 2, 3)])
    norms = Gather(place, n_buf, n_send, n_recv)
    grads = Gather(place, g_buf, g_send, g_recv)
    down = Scatter(place, p1, fx1, tz1, fz1, s1, r1)
    back = Scatter(place, p2, fx2, tz2, fz2, s2, r2)

    hat_two, recip_two = normed_pair(branch[...])
    tanh_one = jnp.tanh(item_rows(mod, item, 1, width))
    resid = patches[...].astype(F32) + tanh_one * hat_two * gain_out[...]
    hat_three, recip_three = normed_pair(resid)
    factor_three = gain_in[...] * (1.0 + item_rows(mod, item, 2, width))
    norms.own[...] = (hat_three * factor_three).astype(BF)
    norms.start()
    norms.pass_on()
    norms.finish()

    def forward(i, carry):
        target = lax.rem(place.z + 1 + i, SPLIT)
        block = n_buf[pl.ds(target * 2, 2)].reshape(2 * rows, width)
        gate_val = bdot(block, w_gate[...])
        up_val = bdot(block, w_up[...])
        gate_s[target] = gate_val
        up_s[target] = up_val
        hidden = (gate_val * jax.nn.sigmoid(gate_val) * up_val).astype(BF)
        hid_s[target] = hidden
        p1[target] = dot_t(hidden, w_down[...]).astype(BF).reshape(2, rows, width)
        return carry

    lax.fori_loop(0, SPLIT, forward, 0)
    for i in range(4):
        down.send_x(i)
    down.pass_on()
    ffn = down.finish()

    hat_four, recip_four = normed_pair(ffn)
    tanh_two = jnp.tanh(item_rows(mod, item, 3, width))
    output[place.x] = resid + tanh_two * hat_four * gain_ffn[...]
    out_copy = remote(output.at[place.x], output.at[place.x], out_send, out_recv, place.x_peer)
    grad_out = out_grad[...].astype(F32)
    grad_four = grad_out * tanh_two
    grads.own[...] = normed_back(grad_four * gain_ffn[...], hat_four, recip_four).astype(BF)
    grads.start()
    out_copy.start()
    gate_sums = item_sums(
        grad_out * hat_four * gain_ffn[...] * (1.0 - tanh_two * tanh_two), item
    )
    sum_ffn_out = jnp.sum(grad_four * hat_four, axis=0, keepdims=True)
    sums[...] = jnp.zeros_like(sums)
    sums[2:3] = sum_ffn_out
    sums[8:9] = gate_sums[0]
    sums[9:10] = gate_sums[1]
    grads.pass_on()
    grads.finish()

    def backward(i, carry):
        target = lax.rem(place.z + 1 + i, SPLIT)
        block = g_buf[pl.ds(target * 2, 2)].reshape(2 * rows, width)
        grad_hidden = bdot(block, w_down[...])
        gate_val = gate_s[target]
        gate_sig = jax.nn.sigmoid(gate_val)
        grad_gate = (
            grad_hidden * up_s[target] * gate_sig * (1.0 + gate_val * (1.0 - gate_sig))
        ).astype(BF)
        grad_up = (grad_hidden * gate_val * gate_sig).astype(BF)
        gg_s[target] = grad_gate
        gu_s[target] = grad_up
        p2[target] = (
            (dot_t(grad_gate, w_gate[...]) + dot_t(grad_up, w_up[...]))
            .astype(BF)
            .reshape(2, rows, width)
        )
        return carry

    lax.fori_loop(0, SPLIT, backward, 0)
    for i in range(4):
        back.send_x(i)
    back.pass_on()

    hid = w_gate.shape[1]
    block_rows = grad_w.shape[3]
    step = 4 * block_rows

    def weights(i, carry):
        cols = pl.ds(pl.multiple_of(i * step, step), step)
        norm = n_buf[:, :, cols].reshape(SPLIT * 2 * rows, step)
        grad = g_buf[:, :, cols].reshape(SPLIT * 2 * rows, step)
        for j, (left, right) in enumerate(((norm, gg_s), (norm, gu_s), (grad, hid_s))):
            block = t_dot(left, right[...].reshape(-1, hid)).astype(BF)
            block = block.reshape(4, block_rows, hid)
            for g in range(4):
                grad_w[g % 2, g // 2, i, :, j * hid : (j + 1) * hid] = block[g]
        return carry

    lax.fori_loop(0, SPLIT, weights, 0)

    grad_norm = back.finish()
    scale_sums = item_sums(grad_norm * hat_three * gain_in[...], item)
    sums[1:2] = jnp.sum(
        grad_norm * hat_three * (1.0 + item_rows(mod, item, 2, width)), axis=0, keepdims=True
    )
    sums[6:7] = scale_sums[0]
    sums[7:8] = scale_sums[1]
    grad_res = grad_out + normed_back(grad_norm * factor_three, hat_three, recip_three)
    grad_resid[...] = grad_res
    gate_sums = item_sums(
        grad_res * hat_two * gain_out[...] * (1.0 - tanh_one * tanh_one), item
    )
    grad_two = grad_res * tanh_one
    sums[0:1] = jnp.sum(grad_two * hat_two, axis=0, keepdims=True)
    sums[4:5] = gate_sums[0]
    sums[5:6] = gate_sums[1]
    grad_attn[...] = normed_back(grad_two * gain_out[...], hat_two, recip_two).astype(BF)
    out_copy.wait_send()
    remote(
        output.at[1 - place.x], output.at[1 - place.x], out_send, out_recv, place.x_peer
    ).wait_recv()


def ffn_call(branch, patches, out_grad, mod, items, gain_out, gain_in, gain_ffn, wg, wu, wd):
    rows, width = branch.shape
    hid = wg.shape[1]
    vmem = pl.BlockSpec(memory_space=pltpu.VMEM)
    shape = jax.ShapeDtypeStruct
    return pl.pallas_call(
        ffn_kernel,
        out_shape=(
            shape((2, rows, width), F32),
            shape((rows, width), F32),
            shape((rows, width), BF),
            shape((16, width), F32),
            shape((2, 2, SPLIT, width // (4 * SPLIT), 3 * hid), BF),
        ),
        in_specs=[vmem] * 11,
        out_specs=[vmem] * 5,
        scratch_shapes=gather_scratch(rows, width)
        + gather_scratch(rows, width)
        + scatter_scratch(rows, width)
        + scatter_scratch(rows, width)
        + [
            pltpu.VMEM((SPLIT, 2 * rows, hid), F32),
            pltpu.VMEM((SPLIT, 2 * rows, hid), F32),
            pltpu.VMEM((SPLIT, 2 * rows, hid), BF),
            pltpu.VMEM((SPLIT, 2 * rows, hid), BF),
            pltpu.VMEM((SPLIT, 2 * rows, hid), BF),
            pltpu.SemaphoreType.DMA,
            pltpu.SemaphoreType.DMA,
        ],
        compiler_params=pltpu.CompilerParams(
            collective_id=2, has_side_effects=True, vmem_limit_bytes=VMEM_LIMIT
        ),
        name="feed_forward",
    )(branch, patches, out_grad, mod, items, gain_out, gain_in, gain_ffn, wg, wu, wd)


class LaneGather:
    def __init__(self, place, buf, send, recv):
        own = buf.at[place.g]
        self.own = own
        self.to_y = remote(own, own, send.at[0], recv.at[0], place.y_peer)
        self.to_c = remote(own, own, send.at[1], recv.at[1], place.c_peer)
        across = buf.at[place.g_y]
        self.from_y = remote(across, across, send.at[2], recv.at[0], place.c_peer)
        self.on = remote(across, across, send.at[2], recv.at[2], place.c_peer)
        pair = buf.at[place.g_c]
        self.from_c = remote(pair, pair, send.at[1], recv.at[1], place.c_peer)
        diagonal = buf.at[place.g_yc]
        self.from_diagonal = remote(diagonal, diagonal, send.at[2], recv.at[2], place.c_peer)

    def start(self):
        self.to_y.start()
        self.to_c.start()

    def pass_on(self):
        self.from_y.wait_recv()
        self.on.start()

    def finish(self):
        self.from_c.wait_recv()
        self.from_diagonal.wait_recv()
        self.to_y.wait_send()
        self.to_c.wait_send()
        self.on.wait_send()


class WeightGather:
    def __init__(self, place, shards, buf, send, recv):
        self.place = place
        lanes = place.lanes
        order = [place.z] + [place.z_from(d) for d in NEAR]
        own = buf.at[place.z * lanes + place.g]
        self.keep = pltpu.make_async_copy(shards.at[place.z], own, recv.at[3])
        self.along_z = [
            remote(shards.at[place.z_to(d)], own, send.at[i], recv.at[i], place.z_peer[d])
            for i, d in enumerate(NEAR)
        ]
        self.blocks, self.to_y, self.to_c, self.from_y, self.on = [], [], [], [], []
        self.from_c, self.from_diagonal = [], []
        for i, z in enumerate(order):
            block = buf.at[z * lanes + place.g]
            self.blocks.append(block)
            self.to_y.append(remote(block, block, send.at[4 + i], recv.at[4 + i], place.y_peer))
            self.to_c.append(remote(block, block, send.at[8 + i], recv.at[8 + i], place.c_peer))
            across = buf.at[z * lanes + place.g_y]
            self.from_y.append(
                remote(across, across, send.at[12 + i], recv.at[4 + i], place.c_peer)
            )
            self.on.append(
                remote(across, across, send.at[12 + i], recv.at[12 + i], place.c_peer)
            )
            pair = buf.at[z * lanes + place.g_c]
            self.from_c.append(remote(pair, pair, send.at[8 + i], recv.at[8 + i], place.c_peer))
            diagonal = buf.at[z * lanes + place.g_yc]
            self.from_diagonal.append(
                remote(diagonal, diagonal, send.at[12 + i], recv.at[12 + i], place.c_peer)
            )
        self.landed = [
            remote(self.blocks[1 + i], self.blocks[1 + i], send.at[i], recv.at[i], place.z_peer[d])
            for i, d in enumerate(NEAR)
        ]

    def start(self):
        for copy in self.along_z:
            copy.start()
        self.keep.start()

    def pass_own(self):
        self.keep.wait()
        self.to_y[0].start()
        self.to_c[0].start()

    def pass_z(self, i):
        self.landed[i].wait_recv()
        self.to_y[1 + i].start()
        self.to_c[1 + i].start()

    def pass_y(self, i):
        self.from_y[i].wait_recv()
        self.on[i].start()

    def finish(self):
        for copy in self.from_c + self.from_diagonal:
            copy.wait_recv()
        for copy in self.along_z + self.to_y + self.to_c + self.on:
            copy.wait_send()


class AllSum:
    def __init__(self, place, acc, land, slots, send, recv, over_x):
        self.place, self.acc, self.land, self.slots = place, acc, land, slots
        peers = [place.c_peer, place.y_peer] + ([place.x_peer] if over_x else [])
        self.steps = len(peers)
        self.pairs = [
            remote(acc.at[i], land.at[i], send.at[i], recv.at[i], peer)
            for i, peer in enumerate(peers)
        ]
        own = slots.at[place.z]
        self.own = own
        self.along_z = [
            remote(own, own, send.at[3 + i], recv.at[3 + i], place.z_peer[d])
            for i, d in enumerate(NEAR)
        ]
        self.landed = []
        for i, d in enumerate(NEAR):
            slot = slots.at[place.z_from(d)]
            self.landed.append(remote(slot, slot, send.at[3 + i], recv.at[3 + i], place.z_peer[d]))

    def start(self):
        self.pairs[0].start()

    def step(self, i):
        self.pairs[i].wait_recv()
        total = self.acc[i] + self.land[i]
        if i + 1 < self.steps:
            self.acc[i + 1] = total
            self.pairs[i + 1].start()
        else:
            self.own[...] = total
            for copy in self.along_z:
                copy.start()

    def finish(self):
        for copy in self.landed:
            copy.wait_recv()
        for copy in self.pairs + self.along_z:
            copy.wait_send()
        return (self.slots[0] + self.slots[1]) + (self.slots[2] + self.slots[3])


class LaneScatter:
    def __init__(self, place, part, from_c, acc, from_y, send, recv):
        self.place, self.part, self.from_c = place, part, from_c
        self.acc, self.from_y = acc, from_y
        self.to_c = remote(part.at[1 - place.c], from_c, send.at[0], recv.at[0], place.c_peer)
        self.to_y = remote(acc.at[1 - place.y], from_y, send.at[1], recv.at[1], place.y_peer)

    def start(self):
        self.to_c.start()

    def step(self):
        self.to_c.wait_recv()
        c, y = self.place.c, self.place.y
        self.acc[1 - y] = (
            self.part[c, 1 - y].astype(F32) + self.from_c[1 - y].astype(F32)
        ).astype(BF)
        self.to_y.start()

    def finish(self):
        c, y = self.place.c, self.place.y
        near = self.part[c, y].astype(F32) + self.from_c[y].astype(F32)
        self.to_y.wait_recv()
        self.to_c.wait_send()
        self.to_y.wait_send()
        return near + self.from_y[...].astype(F32)


def segments(lanes):
    row = lax.broadcasted_iota(jnp.int32, (lanes, lanes), 0) // HEAD
    col = lax.broadcasted_iota(jnp.int32, (lanes, lanes), 1) // HEAD
    return jnp.where(row == col, 1.0 / HEAD, 0.0).astype(F32)


def head_mean(value, mean):
    return jnp.dot(value, mean, precision=HIGH, preferred_element_type=F32)


def swap_quarters(value):
    lanes = value.shape[1]
    lane = lax.broadcasted_iota(jnp.int32, value.shape, 1)
    even = (lane // (HEAD // 4)) % 2 == 0
    return jnp.where(
        even, pltpu.roll(value, lanes - HEAD // 4, 1), pltpu.roll(value, HEAD // 4, 1)
    )


def head_lanes(shape, head):
    lane = lax.broadcasted_iota(jnp.int32, shape, 1)
    return (lane >= head * HEAD) & (lane < (head + 1) * HEAD)


def of_head(value, head):
    return jnp.where(head_lanes(value.shape, head), value, jnp.zeros_like(value))


def attention_kernel(
    patches, mod_in, b_ada, pos_in, freqs, cap_in, qkvo_in, ffn_in, grp_items, key_items,
    gain_in, gain_kq, gain_ckey, gate_row,
    branch, norm_in, qkvo, ffn, mod, queries, kv, k_all, v_all, kq_hat, kq_recip,
    cos_t, sin_t, totals, attn_self, attn_cross, mixed, cap_k, cap_v, cap_hat, cap_recip,
    x_buf, x_send, x_recv, w_send, w_recv, f_send, f_recv,
    m_acc, m_land, m_slots, m_send, m_recv,
    pos_buf, pos_send, pos_recv,
    cap_fc, cap_acc, cap_fy, cap_s, cap_r, cap_out, cap_z, cz_send, cz_recv,
    cap_kv, ckv_send, ckv_recv, kv_send, kv_recv, p1, fx1, tz1, fz1, s1, r1,
):
    place = Place()
    rows, width = patches.shape
    wq = queries.shape[1]
    heads = wq // HEAD
    both = 2 * rows
    enter([place.x_peer, place.c_peer, place.y_peer] + [place.z_peer[d] for d in (1, 2, 3)])

    weights = WeightGather(place, qkvo_in, qkvo, w_send, w_recv)
    weights.start()
    tokens = Gather(place, x_buf, x_send, x_recv)
    tokens.own[...] = patches[...]
    tokens.start()
    sums = AllSum(place, m_acc, m_land, m_slots, m_send, m_recv, False)
    m_acc[0] = mod_in[...]
    sums.start()
    caption = LaneScatter(place, cap_in, cap_fc, cap_acc, cap_fy, cap_s, cap_r)
    caption.start()
    pos_buf[place.z] = pos_in[...]
    own_pos = pos_buf.at[place.z]
    pos_out = [
        remote(own_pos, own_pos, pos_send.at[i], pos_recv.at[i], place.z_peer[d])
        for i, d in enumerate(NEAR)
    ]
    for copy in pos_out:
        copy.start()
    weights.pass_own()
    sums.step(0)
    sums.step(1)
    caption.step()
    mean = segments(2 * wq)
    lane = lax.broadcasted_iota(jnp.int32, (1, 2 * wq), 1)

    for i, d in enumerate(NEAR):
        slot = pos_buf.at[place.z_from(d)]
        remote(slot, slot, pos_send.at[i], pos_recv.at[i], place.z_peer[d]).wait_recv()
    lane_row = lax.broadcasted_iota(jnp.int32, (1, 2 * HEAD), 1)
    by_row = (lane_row // (HEAD // 2)) % 2 == 0
    sign = jnp.where((lane_row // (HEAD // 4)) % 2 == 0, -1.0, 1.0)
    for i in range(SPLIT):
        cols = pos_buf[i].T
        angle = jnp.where(by_row, cols[:, 0:1], cols[:, 1:2]) * freqs[...]
        cos_t[i] = jnp.cos(angle)
        sin_t[i] = jnp.sin(angle) * sign

    cap_out[...] = caption.finish().astype(BF)
    cap_sends = [
        remote(
            cap_out.at[place.z_to(d)], cap_z.at[place.z], cz_send.at[i], cz_recv.at[i],
            place.z_peer[d],
        )
        for i, d in enumerate(NEAR)
    ]
    for copy in cap_sends:
        copy.start()
    cap_z[place.z] = cap_out[place.z]
    tokens.pass_on()
    for i in range(3):
        weights.pass_z(i)
    for i in range(4):
        weights.pass_y(i)
    feed = WeightGather(place, ffn_in, ffn, f_send, f_recv)
    feed.start()
    feed.pass_own()
    mod[...] = sums.finish() + b_ada[...]
    for i, d in enumerate(NEAR):
        slot = cap_z.at[place.z_from(d)]
        remote(slot, slot, cz_send.at[i], cz_recv.at[i], place.z_peer[d]).wait_recv()
    cap_raw = (cap_z[0].astype(F32) + cap_z[1].astype(F32)) + (
        cap_z[2].astype(F32) + cap_z[3].astype(F32)
    )
    recip = lax.rsqrt(head_mean(cap_raw * cap_raw, mean) + EPS)
    hat = cap_raw * recip
    cap_hat[...] = hat
    cap_recip[...] = recip
    cap_gather = LaneGather(place, cap_kv, ckv_send, ckv_recv)
    cap_gather.own[...] = jnp.where(lane < wq, hat * gain_ckey[...], cap_raw).astype(BF)
    cap_gather.start()
    tokens.finish()
    cap_gather.pass_on()
    weights.finish()

    keep = LaneGather(place, kv, kv_send, kv_recv)

    def project(i, carry):
        at = pl.ds(pl.multiple_of(i * both, both), both)
        block = x_buf[pl.ds(i * 2, 2)].reshape(both, width).astype(F32)
        unit, _ = normed_pair(block)
        factor = gain_in[...] * (1.0 + item_rows(mod, grp_items[at], 0, width))
        norm = (unit * factor).astype(BF)
        norm_in[i] = norm
        raw = bdot(norm, qkvo[:, :, 0 : 2 * wq].reshape(width, 2 * wq))
        own_v = bdot(norm, qkvo[:, :, 2 * wq : 4 * wq].reshape(width, 2 * wq))
        recip = lax.rsqrt(head_mean(raw * raw, mean) + EPS)
        hat = raw * recip
        kq_hat[i] = hat
        kq_recip[i] = recip
        cos = jnp.concatenate([cos_t[i]] * heads, axis=1)
        sin = jnp.concatenate([sin_t[i]] * heads, axis=1)
        gained = hat * gain_kq[...]
        turned = gained * cos + swap_quarters(gained) * sin
        kv[place.g, at] = jnp.where(lane < wq, turned, own_v).astype(BF)
        queries[at] = turned[:, wq:].astype(BF)
        return carry

    lax.fori_loop(0, SPLIT, project, 0)
    keep.start()
    for i in range(3):
        feed.pass_z(i)
    cap_gather.finish()
    kv_text = cap_kv[...].reshape(SPLIT * cap_kv.shape[1], 2 * wq)
    cap_k[...] = kv_text[:, :wq]
    cap_v[...] = kv_text[:, wq:]
    scale = 1.0 / math.sqrt(HEAD)
    gates = gate_row[...]

    def one_head(block, keys, vals, head, same):
        scores = dot_t(of_head(block, head), keys)
        if same is not None:
            scores = jnp.where(same, scores, NEG)
        most = jnp.max(scores, axis=1, keepdims=True)
        weight = jnp.exp(scores - most)
        total = jnp.sum(weight, axis=1, keepdims=True)
        out = bdot((weight * (1.0 / total)).astype(BF), vals)
        return of_head(out, head), most + jnp.log(total)

    slot_lane = lax.broadcasted_iota(jnp.int32, (1, totals.shape[1]), 1)

    def cross(i, carry):
        at = pl.ds(pl.multiple_of(i * both, both), both)
        block = (queries[at].astype(F32) * scale).astype(BF)
        out = jnp.zeros((both, wq), F32)
        logs = jnp.zeros((both, totals.shape[1]), F32)
        for head in range(heads):
            part, log = one_head(block, cap_k[...], cap_v[...], head, None)
            out = out + part
            logs = logs + jnp.where(slot_lane == heads + head, log, 0.0)
        attn_cross[at] = out
        totals[at] = logs
        return carry

    lax.fori_loop(0, SPLIT, cross, 0)
    keep.pass_on()
    keep.finish()
    for i in range(SPLIT):
        lump = kv[i]
        at = pl.ds(i * lump.shape[0], lump.shape[0])
        k_all[at] = lump[:, :wq]
        v_all[at] = lump[:, wq:]
    for i in range(4):
        feed.pass_y(i)

    def attend(i, carry):
        at = pl.ds(pl.multiple_of(i * both, both), both)
        block = (queries[at].astype(F32) * scale).astype(BF)
        same = grp_items[at] == key_items[...]
        out = jnp.zeros((both, wq), F32)
        logs = totals[at]
        for head in range(heads):
            part, log = one_head(block, k_all[...], v_all[...], head, same)
            out = out + part
            logs = logs + jnp.where(slot_lane == head, log, 0.0)
        attn_self[at] = out
        totals[at] = logs
        blend = (out + gates * attn_cross[at]).astype(BF)
        mixed[at] = blend
        wide = jnp.concatenate([blend, jnp.zeros_like(blend)], axis=1)
        p1[i] = (
            dot_t(wide, qkvo[:, :, 2 * wq : 4 * wq].reshape(width, 2 * wq))
            .astype(BF)
            .reshape(2, rows, width)
        )
        return carry

    lax.fori_loop(0, SPLIT, attend, 0)
    out = Scatter(place, p1, fx1, tz1, fz1, s1, r1)
    for i in range(4):
        out.send_x(i)
    out.pass_on()
    feed.finish()
    branch[...] = out.finish()
    for copy in pos_out + cap_sends:
        copy.wait_send()


def attention_call(
    patches, mod_in, b_ada, pos_in, freqs, cap_in, qkvo_in, ffn_in, grp_items, key_items,
    gain_in, gain_kq, gain_ckey, gate_row,
):
    rows, width = patches.shape
    wq = qkvo_in.shape[2] // 4
    lanes = cap_in.shape[0] * cap_in.shape[1]
    text = cap_in.shape[3]
    both = 2 * rows
    group = SPLIT * both
    vmem = pl.BlockSpec(memory_space=pltpu.VMEM)
    hbm = pl.BlockSpec(memory_space=pl.ANY)
    shape = jax.ShapeDtypeStruct
    dma = pltpu.SemaphoreType.DMA
    outs = {
        "branch": shape((rows, width), F32),
        "norm_in": shape((SPLIT, both, width), BF),
        "qkvo": shape((SPLIT * lanes,) + qkvo_in.shape[1:], BF),
        "ffn": shape((SPLIT * lanes,) + ffn_in.shape[1:], BF),
        "mod": shape(mod_in.shape, F32),
        "queries": shape((group, wq), BF),
        "kv": shape((lanes, group, 2 * wq), BF),
        "k_all": shape((lanes * group, wq), BF),
        "v_all": shape((lanes * group, wq), BF),
        "kq_hat": shape((SPLIT, both, 2 * wq), F32),
        "kq_recip": shape((SPLIT, both, 2 * wq), F32),
        "cos": shape((SPLIT, both, 2 * HEAD), F32),
        "sin": shape((SPLIT, both, 2 * HEAD), F32),
        "totals": shape((group, 128), F32),
        "attn_self": shape((group, wq), F32),
        "attn_cross": shape((group, wq), F32),
        "mixed": shape((group, wq), BF),
        "cap_k": shape((lanes * text, wq), BF),
        "cap_v": shape((lanes * text, wq), BF),
        "cap_hat": shape((text, 2 * wq), F32),
        "cap_recip": shape((text, 2 * wq), F32),
    }
    results = pl.pallas_call(
        attention_kernel,
        out_shape=tuple(outs.values()),
        in_specs=[vmem] * 7 + [hbm] + [vmem] * 6,
        out_specs=[hbm if name == "ffn" else vmem for name in outs],
        scratch_shapes=gather_scratch(rows, width)
        + [dma((16,)), dma((16,)), dma((16,)), dma((16,))]
        + [
            pltpu.VMEM((2,) + mod_in.shape, F32),
            pltpu.VMEM((2,) + mod_in.shape, F32),
            pltpu.VMEM((SPLIT,) + mod_in.shape, F32),
            dma((6,)),
            dma((6,)),
        ]
        + [pltpu.VMEM((SPLIT,) + pos_in.shape, F32), dma((3,)), dma((3,))]
        + [
            pltpu.VMEM(cap_in.shape[1:], BF),
            pltpu.VMEM(cap_in.shape[1:], BF),
            pltpu.VMEM(cap_in.shape[2:], BF),
            dma((2,)),
            dma((2,)),
            pltpu.VMEM(cap_in.shape[2:], BF),
            pltpu.VMEM(cap_in.shape[2:], BF),
            dma((3,)),
            dma((3,)),
            pltpu.VMEM((lanes, text, 2 * wq), BF),
            dma((3,)),
            dma((3,)),
        ]
        + [dma((3,)), dma((3,))]
        + scatter_scratch(rows, width),
        compiler_params=pltpu.CompilerParams(
            collective_id=1, has_side_effects=True, vmem_limit_bytes=VMEM_LIMIT
        ),
        name="attention",
    )(
        patches, mod_in, b_ada, pos_in, freqs, cap_in, qkvo_in, ffn_in, grp_items, key_items,
        gain_in, gain_kq, gain_ckey, gate_row,
    )
    return dict(zip(outs, results))


class TurnZ:
    def __init__(self, place, out, land, send, recv):
        self.place, self.out, self.land = place, out, land
        self.sends = [
            remote(
                out.at[place.z_to(d)], land.at[place.z], send.at[i], recv.at[i], place.z_peer[d]
            )
            for i, d in enumerate(NEAR)
        ]
        self.landed = []
        for i, d in enumerate(NEAR):
            slot = land.at[place.z_from(d)]
            self.landed.append(remote(slot, slot, send.at[i], recv.at[i], place.z_peer[d]))

    def start(self):
        for copy in self.sends:
            copy.start()
        self.land[self.place.z] = self.out[self.place.z]

    def finish(self):
        for copy in self.landed:
            copy.wait_recv()
        for copy in self.sends:
            copy.wait_send()


class SpreadZ:
    def __init__(self, place, buf, send, recv):
        own = buf.at[place.z]
        self.own = own
        self.sends = [
            remote(own, own, send.at[i], recv.at[i], place.z_peer[d]) for i, d in enumerate(NEAR)
        ]
        self.landed = []
        for i, d in enumerate(NEAR):
            slot = buf.at[place.z_from(d)]
            self.landed.append(remote(slot, slot, send.at[i], recv.at[i], place.z_peer[d]))

    def start(self):
        for copy in self.sends:
            copy.start()

    def finish(self):
        for copy in self.landed:
            copy.wait_recv()
        for copy in self.sends:
            copy.wait_send()


def backward_kernel(
    patches, grad_resid, grad_attn, ffn_sums, ffn_part,
    norm_in, qkvo, mod, queries, k_all, v_all, kq_hat, kq_recip, cos_t, sin_t, totals,
    attn_self, attn_cross, mixed, cap_k, cap_v, cap_hat, cap_recip, text,
    items, grp_items, key_items, gain_in, gain_kq, gain_ckey, gate_row,
    d_patches, d_query, d_key, d_value, d_out, d_gate, d_up, d_down, d_ckey, d_cvalue,
    early_out, late_out, head_out,
    g_buf, g_send, g_recv,
    e_acc, e_land, e_slots, e_send, e_recv, l_acc, l_land, l_slots, l_send, l_recv,
    h_acc, h_land, h_slots, h_send, h_recv,
    f_fc, f_acc, f_fy, f_s, f_r, f_out, f_land, fz_s, fz_r,
    w_part, w_fc, w_acc, w_fy, w_s, w_r, w_out, w_land, wz_s, wz_r,
    t_part, t_fc, t_acc, t_fy, t_s, t_r, t_z, tz_s, tz_r, t_all, ta_s, ta_r,
    kv_part, kv_fc, kv_acc, kv_fy, kv_s, kv_r, kv_sum,
    dk_acc, dv_acc, dq_s, dkq_s, ov_s, mix_s, dck_acc, dcv_acc,
    p1, fx1, tz1, fz1, s1, r1, out_send, out_recv,
):
    place = Place()
    rows, width = patches.shape
    wq = queries.shape[1]
    heads = wq // HEAD
    both = 2 * rows
    scale = 1.0 / math.sqrt(HEAD)
    enter([place.x_peer, place.c_peer, place.y_peer] + [place.z_peer[d] for d in (1, 2, 3)])
    ffn = LaneScatter(place, ffn_part, f_fc, f_acc, f_fy, f_s, f_r)
    grads = Gather(place, g_buf, g_send, g_recv)
    grads.own[...] = grad_attn[...]
    grads.start()
    early = AllSum(place, e_acc, e_land, e_slots, e_send, e_recv, True)
    e_acc[0] = ffn_sums[...]
    early.start()
    ffn.start()
    mean = segments(2 * wq)
    mean_q = segments(wq)
    lane = lax.broadcasted_iota(jnp.int32, (1, 2 * wq), 1)
    dk_acc[...] = jnp.zeros_like(dk_acc)
    dv_acc[...] = jnp.zeros_like(dv_acc)
    dck_acc[...] = jnp.zeros_like(dck_acc)
    dcv_acc[...] = jnp.zeros_like(dcv_acc)
    early.step(0)
    early.step(1)
    grads.pass_on()
    early.step(2)
    ffn.step()
    grads.finish()
    gates = gate_row[...]

    def attend(i, gate_sum):
        at = pl.ds(pl.multiple_of(i * both, both), both)
        block = g_buf[pl.ds(i * 2, 2)].reshape(both, width)
        d_mix = bdot(block, qkvo[:, :, 2 * wq : 4 * wq].reshape(width, 2 * wq))[:, :wq].astype(BF)
        mix_f = d_mix.astype(F32)
        d_cross = (gates * mix_f).astype(BF)
        delta = head_mean(mix_f * attn_self[at], mean_q) * HEAD
        gate_sum = gate_sum + jnp.sum(mix_f * attn_cross[at], axis=0, keepdims=True)
        query = (queries[at].astype(F32) * scale).astype(BF)
        logs = totals[at]
        same = grp_items[at] == key_items[...]
        dq = jnp.zeros((both, wq), F32)
        for head in range(heads):
            query_h = of_head(query, head)
            cross_h = of_head(d_cross, head)
            probs = jnp.exp(dot_t(query_h, cap_k[...]) - logs[:, heads + head : heads + head + 1])
            d_probs = dot_t(cross_h, cap_v[...])
            inner = jnp.sum(probs * d_probs, axis=1, keepdims=True)
            d_scores = (probs * (d_probs - inner)).astype(BF)
            part = bdot(d_scores, cap_k[...])
            dck_acc[...] += t_dot(d_scores, query_h)
            dcv_acc[...] += t_dot(probs.astype(BF), cross_h)
            mix_h = of_head(d_mix, head)
            scores = jnp.where(same, dot_t(query_h, k_all[...]), NEG)
            probs = jnp.exp(scores - logs[:, head : head + 1])
            d_probs = dot_t(mix_h, v_all[...])
            d_scores = (probs * (d_probs - delta[:, head * HEAD : head * HEAD + 1])).astype(BF)
            part = part + bdot(d_scores, k_all[...])
            dq = dq + of_head(part, head)
            dk_acc[...] += t_dot(d_scores, query_h)
            dv_acc[...] += t_dot(probs.astype(BF), mix_h)
        dq = (dq * scale).astype(BF).astype(F32)
        dq_s[at] = jnp.concatenate([jnp.zeros_like(dq), dq], axis=1)
        mix_s[at] = jnp.concatenate([mixed[at], jnp.zeros_like(mixed[at])], axis=1)
        return gate_sum

    gate_sum = lax.fori_loop(0, SPLIT, attend, jnp.zeros((1, wq), F32))

    keys = LaneScatter(place, kv_part, kv_fc, kv_acc, kv_fy, kv_s, kv_r)
    owned = SPLIT * both
    for g in range(4):
        at = slice(g * owned, (g + 1) * owned)
        kv_part[g % 2, g // 2] = jnp.concatenate([dk_acc[at], dv_acc[at]], axis=1).astype(BF)
    keys.start()
    words = cap_hat.shape[0]
    caption = LaneScatter(place, t_part, t_fc, t_acc, t_fy, t_s, t_r)
    for g in range(4):
        at = slice(g * words, (g + 1) * words)
        t_part[g % 2, g // 2] = jnp.concatenate([dck_acc[at], dcv_acc[at]], axis=1).astype(BF)
    caption.start()
    f_out[...] = ffn.finish().astype(BF)
    turn_f = TurnZ(place, f_out, f_land, fz_s, fz_r)
    turn_f.start()
    keys.step()
    caption.step()
    d_cap = caption.finish()
    d_cap_low = d_cap.astype(BF).astype(F32)
    cap_gain = jnp.where(lane < wq, gain_ckey[...], 0.0)
    gck_sum = jnp.sum(jnp.where(lane < wq, d_cap_low * cap_hat[...], 0.0), axis=0, keepdims=True)
    hat = cap_hat[...]
    d_hat = d_cap_low * cap_gain
    d_raw = cap_recip[...] * (d_hat - hat * head_mean(d_hat * hat, mean))
    cap_spread = SpreadZ(place, t_z, tz_s, tz_r)
    cap_spread.own[...] = jnp.where(lane < wq, d_raw, d_cap).astype(BF)
    cap_spread.start()
    kv_sum[...] = keys.finish().astype(BF).reshape(kv_sum.shape)

    def raw(i, head_sum):
        at = pl.ds(pl.multiple_of(i * both, both), both)
        total = kv_sum[at].astype(F32)
        d_kq = jnp.where(lane < wq, total, dq_s[at])
        cos = jnp.concatenate([cos_t[i]] * heads, axis=1)
        sin = jnp.concatenate([sin_t[i]] * heads, axis=1)
        d_norm = d_kq * cos - swap_quarters(d_kq) * sin
        hat = kq_hat[i]
        head_sum = head_sum + jnp.sum(d_norm * hat, axis=0, keepdims=True)
        d_hat = d_norm * gain_kq[...]
        d_kq = (kq_recip[i] * (d_hat - hat * head_mean(d_hat * hat, mean))).astype(BF)
        dkq_s[at] = d_kq
        d_ov = jnp.where(lane < wq, 0.0, total).astype(BF)
        ov_s[at] = d_ov
        p1[i] = (
            (
                dot_t(d_kq, qkvo[:, :, 0 : 2 * wq].reshape(width, 2 * wq))
                + dot_t(d_ov, qkvo[:, :, 2 * wq : 4 * wq].reshape(width, 2 * wq))
            )
            .astype(BF)
            .reshape(2, rows, width)
        )
        return head_sum

    head_sum = lax.fori_loop(0, SPLIT, raw, jnp.zeros((1, 2 * wq), F32))
    back = Scatter(place, p1, fx1, tz1, fz1, s1, r1)
    for i in range(4):
        back.send_x(i)
    heads_sum = AllSum(place, h_acc, h_land, h_slots, h_send, h_recv, False)
    h_acc[0] = jnp.zeros(h_acc.shape[1:], F32)
    h_acc[0, 0:1] = head_sum
    h_acc[0, 1:2] = gck_sum
    h_acc[0, 2:3] = jnp.concatenate([gate_sum, jnp.zeros_like(gate_sum)], axis=1)
    heads_sum.start()

    block_rows = qkvo.shape[1]
    step = 4 * block_rows

    def matrices(i, carry):
        cols = pl.ds(pl.multiple_of(i * step, step), step)
        left = norm_in[:, :, cols].reshape(SPLIT * both, step)
        above = g_buf[:, :, cols].reshape(SPLIT * both, step)
        d_kq = t_dot(left, dkq_s[...]).astype(BF).reshape(4, block_rows, 2 * wq)
        d_ov = t_dot(left, ov_s[...]) + t_dot(above, mix_s[...])
        d_ov = d_ov.astype(BF).reshape(4, block_rows, 2 * wq)
        for g in range(4):
            w_part[g % 2, g // 2, i, :, 0 : 2 * wq] = d_kq[g]
            w_part[g % 2, g // 2, i, :, 2 * wq : 4 * wq] = d_ov[g]
        return carry

    back.pass_on()
    lax.fori_loop(0, SPLIT, matrices, 0)
    attn = LaneScatter(place, w_part, w_fc, w_acc, w_fy, w_s, w_r)
    attn.start()
    cap_spread.finish()
    cap_all = LaneGather(place, t_all, ta_s, ta_r)
    cap_all.own[...] = t_z[...]
    cap_all.start()
    heads_sum.step(0)
    heads_sum.step(1)
    attn.step()
    cap_all.pass_on()

    item = items[...]
    d_norm = back.finish()
    hat, recip = normed_pair(patches[...].astype(F32))
    factor = 1.0 + item_rows(mod, item, 0, width)
    scale_sums = item_sums(d_norm * hat * gain_in[...], item)
    late = AllSum(place, l_acc, l_land, l_slots, l_send, l_recv, True)
    l_acc[0] = jnp.zeros(l_acc.shape[1:], F32)
    l_acc[0, 0:1] = jnp.sum(d_norm * hat * factor, axis=0, keepdims=True)
    l_acc[0, 1:2] = scale_sums[0]
    l_acc[0, 2:3] = scale_sums[1]
    late.start()
    d_patches[place.x] = grad_resid[...] + normed_back(d_norm * gain_in[...] * factor, hat, recip)
    own_d = d_patches.at[place.x]
    out_copy = remote(own_d, own_d, out_send, out_recv, place.x_peer)
    out_copy.start()
    late.step(0)
    w_out[...] = attn.finish().astype(BF)
    turn_w = TurnZ(place, w_out, w_land, wz_s, wz_r)
    turn_w.start()
    late.step(1)
    late.step(2)
    turn_f.finish()
    wf = f_land.shape[2] // 3
    for z in range(SPLIT):
        at = slice(z * wf, (z + 1) * wf)
        d_gate[:, at] = f_land[z, :, 0:wf].astype(F32)
        d_up[:, at] = f_land[z, :, wf : 2 * wf].astype(F32)
        d_down[at] = f_land[z, :, 2 * wf : 3 * wf].astype(F32).T
    cap_all.finish()
    for z in range(SPLIT):
        at = slice(z * wq, (z + 1) * wq)
        d_cap = t_dot(text[...], t_all[:, z].reshape(4 * words, 2 * wq))
        d_ckey[:, at] = d_cap[:, :wq]
        d_cvalue[:, at] = d_cap[:, wq:]
    early_out[...] = early.finish()
    heads_sum.finish()
    head_out[...] = h_slots[...]
    late_out[...] = late.finish()
    turn_w.finish()
    for z in range(SPLIT):
        at = slice(z * wq, (z + 1) * wq)
        d_key[:, at] = w_land[z, :, 0:wq].astype(F32)
        d_query[:, at] = w_land[z, :, wq : 2 * wq].astype(F32)
        d_out[at] = w_land[z, :, 2 * wq : 3 * wq].astype(F32).T
        d_value[:, at] = w_land[z, :, 3 * wq : 4 * wq].astype(F32)
    other = d_patches.at[1 - place.x]
    remote(other, other, out_send, out_recv, place.x_peer).wait_recv()
    out_copy.wait_send()


def backward_call(
    patches, grad_resid, grad_attn, ffn_sums, ffn_part, att, text,
    items, grp_items, key_items, gain_in, gain_kq, gain_ckey, gate_row,
):
    rows, width = patches.shape
    names = (
        "norm_in", "qkvo", "mod", "queries", "k_all", "v_all", "kq_hat", "kq_recip", "cos", "sin",
        "totals", "attn_self", "attn_cross", "mixed", "cap_k", "cap_v", "cap_hat", "cap_recip",
    )
    group, wq = att["queries"].shape
    lanes = group // rows // 2
    lanes = att["qkvo"].shape[0] // SPLIT
    row_dev = att["qkvo"].shape[1]
    words = att["cap_hat"].shape[0]
    wf = ffn_part.shape[4] // 3
    vmem = pl.BlockSpec(memory_space=pltpu.VMEM)
    shape = jax.ShapeDtypeStruct
    dma = pltpu.SemaphoreType.DMA
    tile = pltpu.VMEM

    def all_sum(size, steps):
        return [
            tile((steps,) + size, F32), tile((steps,) + size, F32), tile((SPLIT,) + size, F32),
            dma((6,)), dma((6,)),
        ]

    def lane_scatter(size):
        return [tile((2,) + size, BF), tile((2,) + size, BF), tile(size, BF), dma((2,)), dma((2,))]

    def turn_z(size):
        return [tile(size, BF), tile(size, BF), dma((3,)), dma((3,))]

    ffn_size = ffn_part.shape[2:]
    attn_size = (SPLIT, row_dev, 4 * wq)
    cap_size = (words, 2 * wq)
    kv_size = (group, 2 * wq)
    outs = (
        shape((2, rows, width), F32),
        shape((row_dev, SPLIT * wq), F32),
        shape((row_dev, SPLIT * wq), F32),
        shape((row_dev, SPLIT * wq), F32),
        shape((SPLIT * wq, row_dev), F32),
        shape((row_dev, SPLIT * wf), F32),
        shape((row_dev, SPLIT * wf), F32),
        shape((SPLIT * wf, row_dev), F32),
        shape((text.shape[1], SPLIT * wq), F32),
        shape((text.shape[1], SPLIT * wq), F32),
        shape(ffn_sums.shape, F32),
        shape((8, width), F32),
        shape((SPLIT, 8, 2 * wq), F32),
    )
    args = (
        [patches, grad_resid, grad_attn, ffn_sums, ffn_part]
        + [att[name] for name in names]
        + [text, items, grp_items, key_items, gain_in, gain_kq, gain_ckey, gate_row]
    )
    return pl.pallas_call(
        backward_kernel,
        out_shape=outs,
        in_specs=[vmem] * len(args),
        out_specs=[vmem] * len(outs),
        scratch_shapes=gather_scratch(rows, width)
        + all_sum(ffn_sums.shape, 3)
        + all_sum((8, width), 3)
        + all_sum((8, 2 * wq), 2)
        + lane_scatter(ffn_size)
        + turn_z(ffn_size)
        + [tile((2, 2) + attn_size, BF)]
        + lane_scatter(attn_size)
        + turn_z(attn_size)
        + [tile((2, 2) + cap_size, BF)]
        + lane_scatter(cap_size)
        + [tile((SPLIT,) + cap_size, BF), dma((3,)), dma((3,))]
        + [tile((lanes, SPLIT) + cap_size, BF), dma((3,)), dma((3,))]
        + [tile((2, 2) + kv_size, BF)]
        + lane_scatter(kv_size)
        + [tile(kv_size, BF)]
        + [
            tile((lanes * group, wq), F32),
            tile((lanes * group, wq), F32),
            tile((group, 2 * wq), F32),
            tile((group, 2 * wq), BF),
            tile((group, 2 * wq), BF),
            tile((group, 2 * wq), BF),
            tile((lanes * words, wq), F32),
            tile((lanes * words, wq), F32),
        ]
        + scatter_scratch(rows, width)
        + [dma, dma],
        compiler_params=pltpu.CompilerParams(
            collective_id=3, has_side_effects=True, vmem_limit_bytes=VMEM_LIMIT
        ),
        name="attention_backward",
    )(*args)


def local_any(
    patches,
    caption,
    band_table,
    block_item,
    item_band,
    positions,
    out_grad,
    w_query,
    w_key,
    w_value,
    w_out,
    w_gate,
    w_up,
    w_down,
    w_ckey,
    w_cvalue,
    w_ada,
    b_ada,
    g_attn_in,
    g_attn_out,
    g_ffn_in,
    g_ffn_out,
    g_query,
    g_key,
    g_ckey,
    cross_gate,
):
    scale = 1.0 / math.sqrt(HEAD)
    rank = lax.axis_index("sp")
    half = lax.axis_index("tp")
    cycle = lax.axis_size("sp")
    halves = lax.axis_size("tp")
    lanes = cycle // SPLIT
    along_z, along_g = groups_of(cycle)
    my_z, my_g = rank // lanes, rank % lanes
    tok_rows, width = patches.shape
    own_rows = tok_rows // halves
    text_count = caption.shape[0]
    blocks_dev = tok_rows // BLK
    wq, wf = w_query.shape[1] // SPLIT, w_gate.shape[1] // SPLIT
    heads = wq // HEAD
    sizes = (wq, wq, wq, wq, wf, wf, wf)
    starts = [sum(sizes[:i]) for i in range(8)]

    def gather_z(block):
        return lax.all_gather(block, "sp", axis_index_groups=along_z, axis=0, tiled=False)

    def gather_g(block):
        return lax.all_gather(block, "sp", axis_index_groups=along_g, axis=0, tiled=False)

    def scatter_z(block):
        return lax.psum_scatter(
            block, "sp", axis_index_groups=along_z, scatter_dimension=0, tiled=False
        )

    def scatter_g(block):
        return lax.psum_scatter(
            block, "sp", axis_index_groups=along_g, scatter_dimension=0, tiled=False
        )

    def turn_z(block):
        return lax.all_to_all(
            block, "sp", 0, 0, axis_index_groups=along_z, tiled=True
        )

    def sum_g(block):
        return lax.psum(block, "sp", axis_index_groups=along_g)

    def gather_tokens(own):
        both = lax.all_gather(own, "tp", axis=0, tiled=True)
        return gather_z(both).reshape(SPLIT * tok_rows, -1)

    def scatter_tokens(part):
        part = part.astype(BF).reshape(SPLIT, halves, own_rows, width)
        mine = lax.psum_scatter(part, "tp", scatter_dimension=1, tiled=False)
        return scatter_z(mine.astype(BF)).astype(F32)

    def by_z(block):
        rows, cols = block.shape
        return block.reshape(rows, SPLIT, cols // SPLIT).transpose(1, 0, 2)

    shards = jnp.concatenate(
        [by_z(m) for m in (w_query, w_key, w_value, w_out.T, w_gate, w_up, w_down.T)], axis=2
    )
    rows_dev = shards.shape[1]
    merged = gather_g(turn_z(shards)).transpose(1, 0, 2, 3).reshape(cycle * rows_dev, -1)
    f_query, f_key, f_value, f_out, f_gate, f_up, f_down = (
        merged[:, starts[i] : starts[i + 1]] for i in range(7)
    )

    items_all = block_item.reshape(SPLIT, lanes, blocks_dev)
    grp_items = jnp.repeat(
        lax.dynamic_index_in_dim(items_all, my_g, 1, keepdims=False).reshape(-1), BLK
    )
    key_items = jnp.repeat(items_all.transpose(1, 0, 2).reshape(-1), BLK)
    row0 = half * own_rows

    def own_part(block):
        return lax.dynamic_slice_in_dim(block, row0, own_rows, 0)

    own_items = own_part(
        jnp.repeat(lax.dynamic_slice_in_dim(block_item, rank * blocks_dev, blocks_dev), BLK)
    )

    band_hot = (item_band[:, None] == jnp.arange(BANDS, dtype=jnp.int32)[None, :]).astype(F32)
    cond_pre = jnp.dot(band_hot, band_table, precision=HIGH)
    cond_sig = jax.nn.sigmoid(cond_pre)
    cond_low = (cond_pre * cond_sig).astype(BF)
    text_rows = w_ckey.shape[0]
    text_local = lax.dynamic_slice_in_dim(caption, rank * text_rows, text_rows, 1)
    modulation = lax.psum(bdot(cond_low, w_ada), "sp") + b_ada
    cap_part = jnp.stack([by_z(bdot(text_local, w_ckey)), by_z(bdot(text_local, w_cvalue))], 1)
    cap_raw = sum_g(scatter_z(cap_part))
    ckey_hat, ckey_recip = normed_pair(cap_raw[0].reshape(text_count, heads, HEAD))

    def per_head(vector):
        return lax.dynamic_slice_in_dim(vector, my_z * wq, wq, 0).reshape(heads, HEAD)

    gain_query, gain_key, gain_ckey = per_head(g_query), per_head(g_key), per_head(g_ckey)
    gate_tanh = jnp.tanh(lax.dynamic_slice_in_dim(cross_gate, my_z * heads, heads, 0))
    cap_keys = (ckey_hat * gain_ckey).astype(BF)
    cap_values = cap_raw[1].astype(BF).reshape(text_count, heads, HEAD)

    def of_items(rows, items):
        return jnp.where(items[:, None] == 0, rows[0], rows[1])

    mod_own = of_items(modulation, own_items)
    scale_attn, gate_attn, scale_ffn, gate_ffn = (
        mod_own[:, i * width : (i + 1) * width] for i in range(4)
    )
    group_rows = SPLIT * tok_rows

    patch_f = own_part(patches).astype(F32)
    grad_out = own_part(out_grad).astype(F32)
    hat_one, recip_one = normed_pair(patch_f)
    factor_one = g_attn_in * (1.0 + scale_attn)
    norm_in = gather_tokens((hat_one * factor_one).astype(BF))
    pos_all = gather_z(positions).transpose(1, 0, 2).reshape(2, group_rows)
    cos_row, sin_row, cos_col, sin_col = angles(pos_all)
    split_heads = (group_rows, heads, HEAD)
    query_raw = bdot(norm_in, f_query).reshape(split_heads)
    key_raw = bdot(norm_in, f_key).reshape(split_heads)
    values_low = bdot(norm_in, f_value).astype(BF)
    query_hat, query_recip = normed_pair(query_raw)
    queries = rotate(query_hat * gain_query, cos_row, sin_row, cos_col, sin_col).astype(BF)
    key_hat, key_recip = normed_pair(key_raw)
    keys_low = rotate(key_hat * gain_key, cos_row, sin_row, cos_col, sin_col).astype(BF)
    all_keys, all_values = (
        gather_g(block).reshape(lanes * group_rows, heads, HEAD)
        for block in (keys_low.reshape(group_rows, wq), values_low)
    )
    same = (grp_items[:, None] == key_items[None, :])[None]
    scores = jnp.einsum("qhd,khd->hqk", queries, all_keys, preferred_element_type=F32) * scale
    scores = jnp.where(same, scores, NEG)
    exps = jnp.exp(scores - jnp.max(scores, axis=-1, keepdims=True))
    probs = exps / jnp.sum(exps, axis=-1, keepdims=True)
    probs_low = probs.astype(BF)
    attn_self = jnp.einsum("hqk,khd->qhd", probs_low, all_values, preferred_element_type=F32)
    cross_scores = (
        jnp.einsum("qhd,khd->hqk", queries, cap_keys, preferred_element_type=F32) * scale
    )
    cross_exp = jnp.exp(cross_scores - jnp.max(cross_scores, axis=-1, keepdims=True))
    cross_probs = cross_exp / jnp.sum(cross_exp, axis=-1, keepdims=True)
    cross_low = cross_probs.astype(BF)
    attn_cross = jnp.einsum("hqk,khd->qhd", cross_low, cap_values, preferred_element_type=F32)
    mixed = (attn_self + gate_tanh[None, :, None] * attn_cross).astype(BF).reshape(group_rows, wq)
    attn_branch = scatter_tokens(dot_t(mixed, f_out))

    hat_two, recip_two = normed_pair(attn_branch)
    tanh_one = jnp.tanh(gate_attn)
    resid = patch_f + tanh_one * hat_two * g_attn_out
    hat_three, recip_three = normed_pair(resid)
    factor_three = g_ffn_in * (1.0 + scale_ffn)
    norm_ffn = gather_tokens((hat_three * factor_three).astype(BF))
    gate_val = bdot(norm_ffn, f_gate)
    up_val = bdot(norm_ffn, f_up)
    gate_sig = jax.nn.sigmoid(gate_val)
    hidden = (gate_val * gate_sig * up_val).astype(BF)
    ffn_branch = scatter_tokens(dot_t(hidden, f_down))
    hat_four, recip_four = normed_pair(ffn_branch)
    tanh_two = jnp.tanh(gate_ffn)
    output = resid + tanh_two * hat_four * g_ffn_out

    grad_gate_ffn = grad_out * hat_four * g_ffn_out * (1.0 - tanh_two * tanh_two)
    grad_four = grad_out * tanh_two
    grad_g_ffn_out = jnp.sum(grad_four * hat_four, axis=0)
    grad_ffn = gather_tokens(
        normed_back(grad_four * g_ffn_out, hat_four, recip_four).astype(BF)
    )
    grad_hidden = bdot(grad_ffn, f_down)
    grad_gate = (grad_hidden * up_val * gate_sig * (1.0 + gate_val * (1.0 - gate_sig))).astype(BF)
    grad_up = (grad_hidden * gate_val * gate_sig).astype(BF)
    grad_norm_ffn = scatter_tokens(dot_t(grad_gate, f_gate) + dot_t(grad_up, f_up))
    grad_scale_ffn = grad_norm_ffn * hat_three * g_ffn_in
    grad_g_ffn_in = jnp.sum(grad_norm_ffn * hat_three * (1.0 + scale_ffn), axis=0)
    grad_resid = grad_out + normed_back(grad_norm_ffn * factor_three, hat_three, recip_three)

    grad_gate_attn = grad_resid * hat_two * g_attn_out * (1.0 - tanh_one * tanh_one)
    grad_two = grad_resid * tanh_one
    grad_g_attn_out = jnp.sum(grad_two * hat_two, axis=0)
    grad_attn = gather_tokens(normed_back(grad_two * g_attn_out, hat_two, recip_two).astype(BF))
    grad_mixed = bdot(grad_attn, f_out).astype(BF).reshape(split_heads)
    grad_mixed_f = grad_mixed.astype(F32)
    grad_cross_gate = jnp.sum(grad_mixed_f * attn_cross, axis=(0, 2)) * (
        1.0 - gate_tanh * gate_tanh
    )
    grad_cross = (gate_tanh[None, :, None] * grad_mixed_f).astype(BF)
    grad_cprobs = jnp.einsum("qhd,khd->hqk", grad_cross, cap_values, preferred_element_type=F32)
    grad_cscores = (
        cross_probs * (grad_cprobs - jnp.sum(cross_probs * grad_cprobs, axis=-1, keepdims=True))
    ).astype(BF)
    query_grad = jnp.einsum("hqk,khd->qhd", grad_cscores, cap_keys, preferred_element_type=F32)
    grad_ckeys_part = (
        jnp.einsum("hqk,qhd->khd", grad_cscores, queries, preferred_element_type=F32) * scale
    )
    grad_cvals_part = jnp.einsum(
        "hqk,qhd->khd", cross_low, grad_cross, preferred_element_type=F32
    )
    row_delta = jnp.sum(grad_mixed_f * attn_self, axis=-1).T
    grad_probs = jnp.einsum("qhd,khd->hqk", grad_mixed, all_values, preferred_element_type=F32)
    grad_scores = (probs * (grad_probs - row_delta[..., None])).astype(BF)
    query_grad = query_grad + jnp.einsum(
        "hqk,khd->qhd", grad_scores, all_keys, preferred_element_type=F32
    )
    key_part = (
        jnp.einsum("hqk,qhd->khd", grad_scores, queries, preferred_element_type=F32) * scale
    )
    value_part = jnp.einsum("hqk,qhd->khd", probs_low, grad_mixed, preferred_element_type=F32)
    key_grad, value_grad = (
        scatter_g(block.astype(BF).reshape(lanes, group_rows, wq)) for block in (key_part, value_part)
    )
    grad_queries = (query_grad * scale).astype(BF).astype(F32)
    grad_qnorm = rotate(grad_queries, cos_row, -sin_row, cos_col, -sin_col)
    grad_g_query = jnp.sum(grad_qnorm * query_hat, axis=0).reshape(-1)
    grad_query_raw = (
        normed_back(grad_qnorm * gain_query, query_hat, query_recip).astype(BF).reshape(-1, wq)
    )
    grad_keys = key_grad.astype(F32).reshape(split_heads)
    grad_knorm = rotate(grad_keys, cos_row, -sin_row, cos_col, -sin_col)
    grad_g_key = jnp.sum(grad_knorm * key_hat, axis=0).reshape(-1)
    grad_key_raw = (
        normed_back(grad_knorm * gain_key, key_hat, key_recip).astype(BF).reshape(-1, wq)
    )
    grad_values = value_grad.astype(BF)
    grad_norm_in = scatter_tokens(
        dot_t(grad_query_raw, f_query) + dot_t(grad_key_raw, f_key) + dot_t(grad_values, f_value)
    )
    grad_scale_attn = grad_norm_in * hat_one * g_attn_in
    grad_g_attn_in = jnp.sum(grad_norm_in * hat_one * (1.0 + scale_attn), axis=0)
    grad_patches = grad_resid + normed_back(grad_norm_in * factor_one, hat_one, recip_one)

    grad_merged = jnp.concatenate(
        [
            t_dot(norm_in, grad_query_raw),
            t_dot(norm_in, grad_key_raw),
            t_dot(norm_in, grad_values),
            t_dot(grad_attn, mixed),
            t_dot(norm_ffn, grad_gate),
            t_dot(norm_ffn, grad_up),
            t_dot(grad_ffn, hidden),
        ],
        axis=1,
    ).astype(BF)
    grad_merged = grad_merged.reshape(SPLIT, lanes, rows_dev, -1).transpose(1, 0, 2, 3)
    shard_grads = turn_z(scatter_g(grad_merged)).astype(F32)
    (shard_query, shard_key, shard_value, shard_out, shard_gate, shard_up, shard_down) = (
        shard_grads[:, :, starts[i] : starts[i + 1]].transpose(1, 0, 2).reshape(rows_dev, -1)
        for i in range(7)
    )

    token_sums = lax.psum(
        (
            jnp.stack(
                [
                    jnp.concatenate(
                        [
                            jnp.sum(
                                jnp.where((own_items == item)[:, None], block, 0.0), axis=0
                            )
                            for block in (
                                grad_scale_attn,
                                grad_gate_attn,
                                grad_scale_ffn,
                                grad_gate_ffn,
                            )
                        ]
                    )
                    for item in range(ITEMS)
                ]
            ),
            grad_g_attn_in,
            grad_g_attn_out,
            grad_g_ffn_in,
            grad_g_ffn_out,
        ),
        ("sp", "tp"),
    )
    head_sums = jnp.concatenate([grad_g_query, grad_g_key, grad_cross_gate])
    head_sums = gather_z(sum_g(head_sums))
    grad_ckeys = sum_g(grad_ckeys_part).astype(BF).astype(F32)
    grad_cvals = sum_g(grad_cvals_part).astype(BF).reshape(text_count, wq)
    grad_g_ckey = gather_z(jnp.sum(grad_ckeys * ckey_hat, axis=0).reshape(-1)).reshape(-1)
    grad_ckey_raw = (
        normed_back(grad_ckeys * gain_ckey, ckey_hat, ckey_recip).astype(BF).reshape(text_count, wq)
    )
    cap_grads = gather_z(jnp.stack([grad_ckey_raw, grad_cvals])).transpose(1, 2, 0, 3)
    cap_grads = cap_grads.reshape(2, text_count, SPLIT * wq)
    grad_mod = token_sums[0]
    grad_b_ada = jnp.sum(grad_mod, axis=0)
    grad_w_ada = jnp.dot(cond_low.astype(F32).T, grad_mod, precision=HIGH)
    grad_cond_act = jnp.dot(grad_mod, w_ada.astype(F32).T, precision=HIGH)
    grad_cond_pre = grad_cond_act * cond_sig * (1.0 + cond_pre * (1.0 - cond_sig))
    grad_band_table = jnp.dot(band_hot.T, grad_cond_pre, precision=HIGH)
    return (
        lax.all_gather(output, "tp", axis=0, tiled=True),
        lax.all_gather(grad_patches, "tp", axis=0, tiled=True),
        shard_query,
        shard_key,
        shard_value,
        shard_out.T,
        shard_gate,
        shard_up,
        shard_down.T,
        t_dot(text_local, cap_grads[0]),
        t_dot(text_local, cap_grads[1]),
        grad_w_ada,
        grad_b_ada,
        token_sums[1],
        token_sums[2],
        token_sums[3],
        token_sums[4],
        head_sums[:, :wq].reshape(-1),
        head_sums[:, wq : 2 * wq].reshape(-1),
        grad_g_ckey,
        head_sums[:, 2 * wq :].reshape(-1),
        grad_band_table,
    )


def local(
    patches,
    caption,
    band_table,
    block_item,
    item_band,
    positions,
    out_grad,
    w_query,
    w_key,
    w_value,
    w_out,
    w_gate,
    w_up,
    w_down,
    w_ckey,
    w_cvalue,
    w_ada,
    b_ada,
    g_attn_in,
    g_attn_out,
    g_ffn_in,
    g_ffn_out,
    g_query,
    g_key,
    g_ckey,
    cross_gate,
):
    scale = 1.0 / math.sqrt(HEAD)
    rank = lax.axis_index("sp")
    half = lax.axis_index("tp")
    cycle = lax.axis_size("sp")
    halves = lax.axis_size("tp")
    lanes = cycle // SPLIT
    along_z, along_g = groups_of(cycle)
    my_z, my_g = rank // lanes, rank % lanes
    tok_rows, width = patches.shape
    own_rows = tok_rows // halves
    text_count = caption.shape[0]
    blocks_dev = tok_rows // BLK
    wq, wf = w_query.shape[1] // SPLIT, w_gate.shape[1] // SPLIT
    heads = wq // HEAD
    sizes = (wq, wq, wq, wq, wf, wf, wf)
    starts = [sum(sizes[:i]) for i in range(8)]

    def by_z(block):
        rows, cols = block.shape
        return block.reshape(rows, SPLIT, cols // SPLIT).transpose(1, 0, 2)

    qkvo_in = jnp.concatenate([by_z(m) for m in (w_key, w_query, w_out.T, w_value)], axis=2)
    ffn_in = jnp.concatenate([by_z(m) for m in (w_gate, w_up, w_down.T)], axis=2)
    rows_dev = ffn_in.shape[1]

    items_all = block_item.reshape(SPLIT, lanes, blocks_dev)
    grp_items = jnp.repeat(
        lax.dynamic_index_in_dim(items_all, my_g, 1, keepdims=False).reshape(-1), BLK
    )
    key_items = jnp.repeat(items_all.transpose(1, 0, 2).reshape(-1), BLK)
    row0 = half * own_rows

    def own_part(block):
        return lax.dynamic_slice_in_dim(block, row0, own_rows, 0)

    own_items = own_part(
        jnp.repeat(lax.dynamic_slice_in_dim(block_item, rank * blocks_dev, blocks_dev), BLK)
    )

    band_hot = (item_band[:, None] == jnp.arange(BANDS, dtype=jnp.int32)[None, :]).astype(F32)
    cond_pre = jnp.dot(band_hot, band_table, precision=HIGH)
    cond_sig = jax.nn.sigmoid(cond_pre)
    cond_low = (cond_pre * cond_sig).astype(BF)
    text_rows = w_ckey.shape[0]
    text_local = lax.dynamic_slice_in_dim(caption, rank * text_rows, text_rows, 1)
    cap_part = jnp.concatenate(
        [by_z(bdot(text_local, w_ckey)), by_z(bdot(text_local, w_cvalue))], axis=2
    ).astype(BF)
    cap_part = cap_part.reshape(SPLIT, 2, 2, text_count // lanes, 2 * wq).transpose(2, 1, 0, 3, 4)

    def per_head(vector):
        return lax.dynamic_slice_in_dim(vector, my_z * wq, wq, 0).reshape(heads, HEAD)

    gain_query, gain_key, gain_ckey = per_head(g_query), per_head(g_key), per_head(g_ckey)
    gate_tanh = jnp.tanh(lax.dynamic_slice_in_dim(cross_gate, my_z * heads, heads, 0))
    def of_items(rows, items):
        return jnp.where(items[:, None] == 0, rows[0], rows[1])

    group_rows = SPLIT * tok_rows

    row = lambda vector: vector.reshape(1, -1)
    lane = jnp.arange(2 * HEAD)
    freqs = FREQ_BASE ** (-(lane % (HEAD // 4)).astype(F32) / (HEAD // 4))
    gain_kq_row = jnp.concatenate([row(gain_key), row(gain_query)], axis=1)
    gain_ckey_row = jnp.concatenate([row(gain_ckey), jnp.ones((1, wq), F32)], axis=1)
    gate_tanh_row = row(jnp.repeat(gate_tanh, HEAD))
    att = attention_call(
        own_part(patches),
        bdot(cond_low, w_ada),
        row(b_ada),
        jnp.pad(positions.astype(F32), ((0, 6), (0, 0))),
        row(freqs),
        cap_part,
        qkvo_in,
        ffn_in,
        grp_items[:, None],
        row(key_items),
        row(g_attn_in),
        gain_kq_row,
        gain_ckey_row,
        gate_tanh_row,
    )
    attn_branch = att["branch"]
    modulation = att["mod"]
    ffn_w = att["ffn"].reshape(width, -1)
    f_gate, f_up, f_down = (ffn_w[:, i * wf : (i + 1) * wf] for i in range(3))

    output, grad_resid, grad_attn, ffn_sums, ffn_part = ffn_call(
        attn_branch,
        own_part(patches),
        own_part(out_grad),
        modulation,
        own_items[:, None],
        row(g_attn_out),
        row(g_ffn_in),
        row(g_ffn_out),
        f_gate,
        f_up,
        f_down,
    )

    (
        grad_patches, shard_query, shard_key, shard_value, shard_out, shard_gate, shard_up,
        shard_down, grad_w_ckey, grad_w_cvalue, early, late, head_rows,
    ) = backward_call(
        own_part(patches),
        grad_resid,
        grad_attn,
        ffn_sums,
        ffn_part,
        att,
        text_local,
        own_items[:, None],
        grp_items[:, None],
        row(key_items),
        row(g_attn_in),
        gain_kq_row,
        gain_ckey_row,
        gate_tanh_row,
    )
    grad_mod = jnp.concatenate([late[1:3], early[4:6], early[6:8], early[8:10]], axis=1)
    grad_g_query = head_rows[:, 0, wq:].reshape(-1)
    grad_g_key = head_rows[:, 0, :wq].reshape(-1)
    grad_g_ckey = head_rows[:, 1, :wq].reshape(-1)
    grad_cross_gate = jnp.sum(head_rows[:, 2, :wq].reshape(-1, HEAD), axis=1)
    all_tanh = jnp.tanh(cross_gate)
    grad_cross_gate = grad_cross_gate * (1.0 - all_tanh * all_tanh)
    grad_b_ada = jnp.sum(grad_mod, axis=0)
    grad_w_ada = jnp.dot(cond_low.astype(F32).T, grad_mod, precision=HIGH)
    grad_cond_act = jnp.dot(grad_mod, w_ada.astype(F32).T, precision=HIGH)
    grad_cond_pre = grad_cond_act * cond_sig * (1.0 + cond_pre * (1.0 - cond_sig))
    grad_band_table = jnp.dot(band_hot.T, grad_cond_pre, precision=HIGH)
    return (
        output.reshape(tok_rows, width),
        grad_patches.reshape(tok_rows, width),
        shard_query,
        shard_key,
        shard_value,
        shard_out,
        shard_gate,
        shard_up,
        shard_down,
        grad_w_ckey,
        grad_w_cvalue,
        grad_w_ada,
        grad_b_ada,
        late[0],
        early[0],
        early[1],
        early[2],
        grad_g_query,
        grad_g_key,
        grad_g_ckey,
        grad_cross_gate,
        grad_band_table,
    )


def solution(mesh):
    lanes = mesh.shape["sp"] // SPLIT
    body = local if lanes == 4 and mesh.shape["tp"] == 2 else local_any
    in_specs = (
        P("sp", None),
        P(),
        P(None, "sp"),
        P(),
        P(),
        P(None, "sp"),
        P("sp", None),
        P("sp", "tp"),
        P("sp", "tp"),
        P("sp", "tp"),
        P("tp", "sp"),
        P("sp", "tp"),
        P("sp", "tp"),
        P("tp", "sp"),
        P("sp", "tp"),
        P("sp", "tp"),
        P("sp", None),
        P(),
        P(),
        P(),
        P(),
        P(),
        P("tp"),
        P("tp"),
        P("tp"),
        P("tp"),
    )
    out_specs = (
        P("sp", None),
        P("sp", None),
        P("sp", "tp"),
        P("sp", "tp"),
        P("sp", "tp"),
        P("tp", "sp"),
        P("sp", "tp"),
        P("sp", "tp"),
        P("tp", "sp"),
        P("sp", "tp"),
        P("sp", "tp"),
        P("sp", None),
        P(),
        P(),
        P(),
        P(),
        P(),
        P("tp"),
        P("tp"),
        P("tp"),
        P("tp"),
        P(None, "sp"),
    )
    return jax.shard_map(body, mesh=mesh, in_specs=in_specs, out_specs=out_specs, check_vma=False)
```

```python
import functools
import math
from types import SimpleNamespace

import jax
import jax.numpy as jnp
from jax import lax
from jax.experimental import pallas as pl
from jax.experimental.pallas import tpu as pltpu
from jax.sharding import PartitionSpec as P

BANDS = 16
ITEMS = 2
BLK = 32
HEAD = 64
EPS = 1e-06
NEG = -1e30
FREQ_BASE = 10000.0
HIGH = lax.Precision.HIGHEST
BF = jnp.bfloat16
F32 = jnp.float32
SPLIT = 4


def groups_of(cycle_size):
    lanes = cycle_size // SPLIT
    along_z = [[z * lanes + g for z in range(SPLIT)] for g in range(lanes)]
    along_g = [[z * lanes + g for g in range(lanes)] for z in range(SPLIT)]
    return along_z, along_g


def normed_pair(value):
    recip = lax.rsqrt(jnp.mean(value * value, axis=-1, keepdims=True) + EPS)
    return value * recip, recip


def normed_back(grad_hat, normal, recip):
    return recip * (grad_hat - normal * jnp.mean(grad_hat * normal, axis=-1, keepdims=True))


def rotate(value, cos_row, sin_row, cos_col, sin_col):
    quarter = value.shape[-1] // 4
    part_a = value[..., :quarter]
    part_b = value[..., quarter : 2 * quarter]
    part_c = value[..., 2 * quarter : 3 * quarter]
    part_e = value[..., 3 * quarter :]
    return jnp.concatenate(
        [
            part_a * cos_row - part_b * sin_row,
            part_a * sin_row + part_b * cos_row,
            part_c * cos_col - part_e * sin_col,
            part_c * sin_col + part_e * cos_col,
        ],
        axis=-1,
    )


def angles(positions):
    quarter = HEAD // 4
    freqs = FREQ_BASE ** (-jnp.arange(quarter, dtype=F32) / quarter)
    row_angle = positions[0].astype(F32)[:, None] * freqs[None, :]
    col_angle = positions[1].astype(F32)[:, None] * freqs[None, :]
    return (
        jnp.cos(row_angle)[:, None, :],
        jnp.sin(row_angle)[:, None, :],
        jnp.cos(col_angle)[:, None, :],
        jnp.sin(col_angle)[:, None, :],
    )


def bdot(left, right):
    return jnp.dot(left, right, preferred_element_type=F32)


def dot_t(left, right):
    return lax.dot_general(left, right, (((1,), (1,)), ((), ())), preferred_element_type=F32)


def t_dot(left, right):
    return lax.dot_general(left, right, (((0,), (0,)), ((), ())), preferred_element_type=F32)


MESH = pl.DeviceIdType.MESH
VMEM_LIMIT = 63 * 2**20
NEAR = (1, 3, 2)


class Place:
    def __init__(self):
        rank = lax.axis_index("sp")
        self.lanes = lax.axis_size("sp") // SPLIT
        self.x = lax.axis_index("tp")
        self.z = rank // self.lanes
        self.g = rank % self.lanes
        self.x_peer = (rank, 1 - self.x)
        self.z_peer = {
            d: (lax.rem(self.z + d, SPLIT) * self.lanes + self.g, self.x) for d in (1, 2, 3)
        }
        self.z_pair = self.at_z(self.z + 1 - 2 * lax.rem(self.z, 2))
        self.z_far = self.z_peer[2]
        self.y, self.c = self.g // 2, self.g % 2
        self.g_y = (1 - self.y) * 2 + self.c
        self.g_c = self.y * 2 + 1 - self.c
        self.g_yc = (1 - self.y) * 2 + 1 - self.c
        self.y_peer = (self.z * self.lanes + self.g_y, self.x)
        self.c_peer = (self.z * self.lanes + self.g_c, self.x)

    def z_from(self, d):
        return lax.rem(self.z + SPLIT - d, SPLIT)

    def z_to(self, d):
        return lax.rem(self.z + d, SPLIT)


    def block(self, i):
        middle = lax.div(self.z * (3 - self.z), 2)
        near = i + middle * (1 - 2 * i) * (1 - lax.div(i, 2))
        return near + lax.div(self.z, 2) * (3 - 2 * near)

    def at_z(self, z):
        return (z * self.lanes + self.g, self.x)


def remote(src, dst, send, recv, peer):
    return pltpu.make_async_remote_copy(
        src_ref=src, dst_ref=dst, send_sem=send, recv_sem=recv, device_id=peer, device_id_type=MESH
    )


def as_index(i):
    return jnp.int32(i) if isinstance(i, int) else i


class Gather:
    def __init__(self, place, buf, send, recv):
        self.place, self.buf, self.send, self.recv = place, buf, send, recv
        self.own = buf.at[place.z * 2 + place.x]

    def to_right(self, z):
        place = self.place
        block = self.buf.at[z * 2 + place.x]
        steps = place.z - z
        return remote(
            block, block, self.send.at[steps], self.recv.at[3 + steps], place.at_z(place.z + 1)
        )

    def to_left(self, z):
        place = self.place
        block = self.buf.at[z * 2 + place.x]
        steps = z - place.z
        return remote(
            block, block, self.send.at[3 + steps], self.recv.at[steps], place.at_z(place.z - 1)
        )

    def to_x(self, z):
        block = self.buf.at[z * 2 + self.place.x]
        return remote(
            block, block, self.send.at[6 + z], self.recv.at[6 + z], self.place.x_peer
        )

    def landed(self, z, index):
        block = self.buf.at[z * 2 + self.place.x]
        return remote(block, block, self.send.at[index], self.recv.at[index], self.place.x_peer)

    def start(self):
        place = self.place

        @pl.when(place.z < 3)
        def _():
            self.to_right(place.z).start()

        @pl.when(place.z > 0)
        def _():
            self.to_left(place.z).start()

        self.to_x(place.z).start()

    def pass_on(self, i):
        place = self.place
        z = place.block(as_index(i))

        @pl.when(z < place.z)
        def _():
            self.landed(z, 2 + place.z - z).wait_recv()

            @pl.when(place.z < 3)
            def _():
                self.to_right(z).start()

        @pl.when(z > place.z)
        def _():
            self.landed(z, z - place.z - 1).wait_recv()

            @pl.when(place.z > 0)
            def _():
                self.to_left(z).start()

        self.to_x(z).start()

    def arrive(self, i):
        z = self.place.block(as_index(i))
        block = self.buf.at[z * 2 + 1 - self.place.x]
        remote(
            block, block, self.send.at[6 + z], self.recv.at[6 + z], self.place.x_peer
        ).wait_recv()

    def finish(self):
        place = self.place
        for z in range(SPLIT):

            @pl.when((z <= place.z) & (place.z < 3))
            def _():
                self.to_right(z).wait_send()

            @pl.when((z >= place.z) & (place.z > 0))
            def _():
                self.to_left(z).wait_send()

            self.to_x(z).wait_send()


class Scatter:
    def __init__(self, place, part, from_x, from_z, send, recv):
        self.place, self.part, self.from_x = place, part, from_x
        self.from_z, self.send, self.recv = from_z, send, recv

    def across(self, z):
        return remote(
            self.part.at[z, 1 - self.place.x],
            self.from_x.at[z],
            self.send.at[z],
            self.recv.at[z],
            self.place.x_peer,
        )

    def along(self, z):
        return remote(
            self.part.at[z, self.place.x],
            self.from_z.at[self.place.z],
            self.send.at[4 + z],
            self.recv.at[4 + self.place.z],
            self.place.at_z(z),
        )

    def pass_on(self, z):
        self.across(z).wait_recv()
        own = self.part[z, self.place.x].astype(F32)
        self.part[z, self.place.x] = (own + self.from_x[z].astype(F32)).astype(BF)
        self.along(z).start()

    def finish(self):
        place = self.place
        self.across(place.z).wait_recv()
        total = self.part[place.z, place.x].astype(F32) + self.from_x[place.z].astype(F32)
        for d in (1, 2, 3):
            z = place.z_to(d)
            block = self.from_z.at[z]
            remote(
                block, block, self.send.at[4 + z], self.recv.at[4 + z], place.at_z(z)
            ).wait_recv()
            total = total + self.from_z[z].astype(F32)
        for z in range(SPLIT):
            self.across(z).wait_send()
        for d in (1, 2, 3):
            self.along(place.z_to(d)).wait_send()
        return total


def flow(place, gather, scatter, work, carry, between=None):
    def order(i):
        return place.block(i if gather is not None else 3 - i)

    def step(i, carry):
        if gather is not None:

            @pl.when((i >= 1) & (i < 3))
            def _():
                gather.pass_on(i + 1)

            gather.arrive(i)
        if between is not None:
            pl.when(i == 2)(between)
        z = order(i)
        carry = work(z, carry)
        if scatter is not None:
            scatter.across(z).start()
        if gather is not None:

            @pl.when(i == 0)
            def _():
                gather.pass_on(1)

        if scatter is not None:
            first = 2 if gather is not None else 1

            @pl.when(i >= first)
            def _():
                scatter.pass_on(order(i - 1))

        return carry

    carry = lax.fori_loop(0, SPLIT, step, carry)
    if scatter is not None and gather is not None:
        scatter.pass_on(order(jnp.int32(3)))
    return carry


class LaneGather:
    def __init__(self, place, buf, send, recv):
        own = buf.at[place.g]
        self.own = own
        self.to_y = remote(own, own, send.at[0], recv.at[0], place.y_peer)
        self.to_c = remote(own, own, send.at[1], recv.at[1], place.c_peer)
        across = buf.at[place.g_y]
        self.from_y = remote(across, across, send.at[2], recv.at[0], place.c_peer)
        self.on = remote(across, across, send.at[2], recv.at[2], place.c_peer)
        pair = buf.at[place.g_c]
        self.from_c = remote(pair, pair, send.at[1], recv.at[1], place.c_peer)
        diagonal = buf.at[place.g_yc]
        self.from_diagonal = remote(diagonal, diagonal, send.at[2], recv.at[2], place.c_peer)

    def start(self):
        self.to_y.start()
        self.to_c.start()

    def pass_on(self):
        self.from_y.wait_recv()
        self.on.start()

    def finish(self):
        self.from_c.wait_recv()
        self.from_diagonal.wait_recv()
        self.sent()

    def sent(self):
        self.to_y.wait_send()
        self.to_c.wait_send()
        self.on.wait_send()


class WeightGather:
    def __init__(self, place, shards, buf, send, recv):
        self.place, self.shards, self.buf = place, shards, buf
        self.send, self.recv = send, recv
        self.keep = pltpu.make_async_copy(
            shards.at[place.z], buf.at[place.z * place.lanes + place.g], recv.at[place.z]
        )

    def copy(self, z, g, sent, landed, peer):
        block = self.buf.at[z * self.place.lanes + g]
        return remote(block, block, self.send.at[sent + z], self.recv.at[landed + z], peer)

    def along(self, z):
        place = self.place
        return remote(
            self.shards.at[z],
            self.buf.at[place.z * place.lanes + place.g],
            self.send.at[z],
            self.recv.at[place.z],
            place.at_z(z),
        )

    def to_y(self, z):
        return self.copy(z, self.place.g, 4, 4, self.place.y_peer)

    def to_c(self, z):
        return self.copy(z, self.place.g, 8, 8, self.place.c_peer)

    def on(self, z):
        return self.copy(z, self.place.g_y, 12, 12, self.place.c_peer)

    def start(self, i):
        self.along(self.place.block(as_index(i))).start()

    def pass_own(self):
        self.keep.start()
        self.keep.wait()
        self.to_y(self.place.z).start()
        self.to_c(self.place.z).start()

    def pass_z(self, i):
        z = self.place.block(as_index(i))
        self.copy(z, self.place.g, 0, 0, self.place.x_peer).wait_recv()
        self.to_y(z).start()
        self.to_c(z).start()

    def pass_y(self, i):
        z = self.place.block(as_index(i))
        self.copy(z, self.place.g_y, 12, 4, self.place.c_peer).wait_recv()
        self.on(z).start()

    def finish(self):
        place = self.place
        for z in range(SPLIT):
            self.copy(z, place.g_c, 8, 8, place.c_peer).wait_recv()
            self.copy(z, place.g_yc, 12, 12, place.c_peer).wait_recv()
        for d in (1, 2, 3):
            self.along(place.z_to(d)).wait_send()
        for z in range(SPLIT):
            self.to_y(z).wait_send()
            self.to_c(z).wait_send()
            self.on(z).wait_send()


class AllSum:
    def __init__(self, peers, acc, land, send, recv):
        self.acc, self.land = acc, land
        self.pairs = [
            remote(acc.at[i], land.at[i], send.at[i], recv.at[i], peer)
            for i, peer in enumerate(peers)
        ]

    def start(self):
        self.pairs[0].start()

    def step(self):
        pair, *rest = self.pairs
        pair.wait_recv()
        pair.wait_send()
        i = self.acc.shape[0] - len(self.pairs)
        total = self.acc[i] + self.land[i]
        self.pairs = rest
        if rest:
            self.acc[i + 1] = total
            rest[0].start()
        return total


class LaneScatter:
    def __init__(self, place, part, from_c, from_y, send, recv):
        self.part, self.from_c, self.from_y = part, from_c, from_y
        self.count = count = from_y.shape[0]
        self.base = (place.c * 2 + place.y) * count
        self.away = (place.c * 2 + 1 - place.y) * count
        self.base_c, self.away_c = place.y * count, (1 - place.y) * count
        self.to_c = remote(
            part.at[pl.ds((1 - place.c) * 2 * count, 2 * count)],
            from_c,
            send.at[0],
            recv.at[0],
            place.c_peer,
        )
        self.to_y = remote(
            part.at[pl.ds(self.away, count)], from_y, send.at[1], recv.at[1], place.y_peer
        )
        self.own = part.at[pl.ds(self.base, count)]

    def start(self):
        self.to_c.start()

    def step(self):
        self.to_c.wait_recv()

        def add(i, carry):
            at = self.away + i
            near = self.part[at].astype(F32) + self.from_c[self.away_c + i].astype(F32)
            self.part[at] = near.astype(BF)
            return carry

        lax.fori_loop(0, self.count, add, 0)
        self.to_y.start()

    def finish(self):
        self.to_y.wait_recv()
        self.to_c.wait_send()

        def add(i, carry):
            at = self.base + i
            near = self.part[at].astype(F32) + self.from_c[self.base_c + i].astype(F32)
            self.part[at] = (near + self.from_y[i].astype(F32)).astype(BF)
            return carry

        lax.fori_loop(0, self.count, add, 0)
        self.to_y.wait_send()


class TurnZ:
    def __init__(self, place, out, base, land, send, recv):
        self.keep = pltpu.make_async_copy(
            out.at[base + place.z], land.at[place.z], send.at[3]
        )
        self.sends = [
            remote(
                out.at[base + place.z_to(d)],
                land.at[place.z],
                send.at[i],
                recv.at[i],
                place.z_peer[d],
            )
            for i, d in enumerate(NEAR)
        ]
        self.landed = []
        for i, d in enumerate(NEAR):
            slot = land.at[place.z_from(d)]
            self.landed.append(remote(slot, slot, send.at[i], recv.at[i], place.z_peer[d]))

    def start(self):
        for copy in self.sends:
            copy.start()
        self.keep.start()

    def finish(self):
        for copy in self.landed:
            copy.wait_recv()
        for copy in self.sends:
            copy.wait_send()
        self.keep.wait()


class SpreadZ:
    def __init__(self, place, buf, send, recv):
        own = buf.at[place.z]
        self.own = own
        self.sends = [
            remote(own, own, send.at[i], recv.at[i], place.z_peer[d]) for i, d in enumerate(NEAR)
        ]
        self.landed = []
        for i, d in enumerate(NEAR):
            slot = buf.at[place.z_from(d)]
            self.landed.append(remote(slot, slot, send.at[i], recv.at[i], place.z_peer[d]))

    def start(self):
        for copy in self.sends:
            copy.start()

    def finish(self):
        for copy in self.landed:
            copy.wait_recv()
        for copy in self.sends:
            copy.wait_send()


def item_rows(mod, items, index, width):
    first = mod[0:1, index * width : (index + 1) * width]
    second = mod[1:2, index * width : (index + 1) * width]
    return jnp.where(items == 0, first, second)


def item_sums(value, items):
    return [
        jnp.sum(jnp.where(items == item, value, 0.0), axis=0, keepdims=True)
        for item in range(ITEMS)
    ]


def segments(lanes):
    row = lax.broadcasted_iota(jnp.int32, (lanes, lanes), 0) // HEAD
    col = lax.broadcasted_iota(jnp.int32, (lanes, lanes), 1) // HEAD
    return jnp.where(row == col, 1.0 / HEAD, 0.0).astype(F32)


def head_mean(value, mean):
    return jnp.dot(value, mean, precision=HIGH, preferred_element_type=F32)


def swap_quarters(value):
    lanes = value.shape[1]
    lane = lax.broadcasted_iota(jnp.int32, value.shape, 1)
    even = (lane // (HEAD // 4)) % 2 == 0
    return jnp.where(
        even, pltpu.roll(value, lanes - HEAD // 4, 1), pltpu.roll(value, HEAD // 4, 1)
    )


def head_lanes(shape, head):
    lane = lax.broadcasted_iota(jnp.int32, shape, 1)
    return (lane >= head * HEAD) & (lane < (head + 1) * HEAD)


def of_head(value, head):
    return jnp.where(head_lanes(value.shape, head), value, jnp.zeros_like(value))


def lane_order(g):
    return (g % 2) * 2 + g // 2


def layer_kernel(names, *refs):
    r = SimpleNamespace(**dict(zip(names, refs)))
    place = Place()
    z, g, x = place.z, place.g, place.x
    tok_rows, width = r.patches.shape
    rows = tok_rows // 2
    wq, wf = r.w_query.shape[1] // SPLIT, r.w_gate.shape[1] // SPLIT
    two = 2 * wq
    heads = wq // HEAD
    group = SPLIT * tok_rows
    scale = 1.0 / math.sqrt(HEAD)
    peers = [place.x_peer, place.c_peer, place.y_peer] + [place.z_peer[d] for d in (1, 2, 3)]
    barrier = pltpu.get_barrier_semaphore()
    for peer in peers:
        pl.semaphore_signal(barrier, inc=1, device_id=peer, device_id_type=MESH)

    text_cols = pl.ds(pl.multiple_of((z * place.lanes + g) * r.text.shape[1], 128), r.text.shape[1])
    text_copy = pltpu.make_async_copy(r.caption.at[:, text_cols], r.text, r.text_sem)
    text_copy.start()
    for i in range(SPLIT):
        at = slice(i * wq, (i + 1) * wq)
        r.qkvo_in[i, :, 0:wq] = r.w_key[:, at]
        r.qkvo_in[i, :, wq:two] = r.w_query[:, at]
        r.qkvo_in[i, :, two : two + wq] = r.w_out[at, :].T
        r.qkvo_in[i, :, two + wq : 2 * two] = r.w_value[:, at]
    pl.semaphore_wait(barrier, len(peers))

    weights = WeightGather(place, r.qkvo_in, r.qkvo, r.w_send, r.w_recv)
    weights.start(1)
    mine = pl.ds(pl.multiple_of(x * rows, rows), rows)
    tokens = Gather(place, r.x_buf, r.x_send, r.x_recv)
    tokens.own[...] = r.patches[mine]
    tokens.start()
    along = [place.c_peer, place.y_peer, place.z_pair, place.z_far]
    sums = AllSum(along, r.m_acc, r.m_land, r.m_send, r.m_recv)
    pre, sig = conditioning(r.band_table, r.item_band)
    act = jnp.concatenate([pre * sig, jnp.zeros((6, pre.shape[1]), F32)], axis=0).astype(BF)
    r.m_acc[0] = bdot(act, r.w_ada[...])[:ITEMS]
    sums.start()
    spots = SpreadZ(place, r.pos_buf, r.pos_send, r.pos_recv)
    spots.own[...] = jnp.concatenate(
        [r.positions[...].astype(F32), jnp.zeros((6, tok_rows), F32)], axis=0
    )
    spots.start()
    weights.pass_own()
    weights.start(2)
    text_copy.wait()
    words = r.cap_part.shape[1]
    caption = LaneScatter(place, r.cap_part, r.cap_fc, r.cap_fy, r.cap_s, r.cap_r)
    for kind, matrix in enumerate((r.w_ckey, r.w_cvalue)):
        full = bdot(r.text[...], matrix[...]).astype(BF)
        for i in range(SPLIT):
            for lane_g in range(4):
                block = lane_order(lane_g) * SPLIT + i
                r.cap_part[block, :, kind * wq : (kind + 1) * wq] = full[
                    lane_g * words : (lane_g + 1) * words, i * wq : (i + 1) * wq
                ]
    caption.start()
    for i in range(SPLIT):
        at = slice(i * wf, (i + 1) * wf)
        r.ffn_in[i, :, 0:wf] = r.w_gate[:, at]
        r.ffn_in[i, :, wf : 2 * wf] = r.w_up[:, at]
        r.ffn_in[i, :, 2 * wf : 3 * wf] = r.w_down[at, :].T
    sums.step()
    sums.step()
    caption.step()
    weights.start(3)
    tokens.pass_on(1)
    weights.pass_z(1)
    sums.step()

    blocks = tok_rows // BLK
    token = lax.broadcasted_iota(jnp.int32, (group, 1), 0) // BLK
    key = lax.broadcasted_iota(jnp.int32, (1, 4 * group), 1) // BLK
    token_item = jnp.zeros((group, 1), jnp.int32)
    key_item = jnp.zeros((1, 4 * group), jnp.int32)
    for i in range(SPLIT):
        for j in range(blocks):
            own = r.block_item[(i * place.lanes + g) * blocks + j]
            token_item = jnp.where(token == i * blocks + j, own, token_item)
            for other in range(4):
                value = r.block_item[(i * place.lanes + other) * blocks + j]
                key_item = jnp.where(key == (other * SPLIT + i) * blocks + j, value, key_item)
    r.items[...] = token_item
    for i in range(4):
        r.key_items[i] = key_item[:, i * group : (i + 1) * group]
    own_at = pl.ds(pl.multiple_of(z * tok_rows + x * rows, rows), rows)

    mean = segments(two)
    mean_q = segments(wq)
    lane = lax.broadcasted_iota(jnp.int32, (1, two), 1)
    gain_kq = r.head_rows[z, 0:1]
    gain_ckey = r.head_rows[z, 1:2]
    gates = jnp.tanh(r.head_rows[z, 2:3])[:, :wq]
    freqs = r.head_rows[z, 3:4][:, : 2 * HEAD]
    gain_in, gain_attn = r.rows_in[0:1], r.rows_in[1:2]
    gain_ffn, gain_out = r.rows_in[2:3], r.rows_in[3:4]

    spots.finish()
    lane_row = lax.broadcasted_iota(jnp.int32, (1, 2 * HEAD), 1)
    by_row = (lane_row // (HEAD // 2)) % 2 == 0
    sign = jnp.where((lane_row // (HEAD // 4)) % 2 == 0, -1.0, 1.0)
    for i in range(SPLIT):
        cols = r.pos_buf[i].T
        angle = jnp.where(by_row, cols[:, 0:1], cols[:, 1:2]) * freqs
        r.cos_t[i] = jnp.cos(angle)
        r.sin_t[i] = jnp.sin(angle) * sign

    caption.finish()
    cap_turn = TurnZ(place, r.cap_part, caption.base, r.cap_z, r.cz_send, r.cz_recv)
    cap_turn.start()
    for i in (2, 3):
        tokens.pass_on(i)
        weights.pass_z(i)
    for i in range(4):
        weights.pass_y(i)
    feed = WeightGather(place, r.ffn_in, r.ffn, r.f_send, r.f_recv)
    for i in (1, 2, 3):
        feed.start(i)
    feed.pass_own()
    r.mod[...] = sums.step() + jnp.concatenate(
        [r.rows_in[4 + i : 5 + i] for i in range(4)], axis=1
    )
    cap_turn.finish()
    cap_raw = (r.cap_z[0].astype(F32) + r.cap_z[1].astype(F32)) + (
        r.cap_z[2].astype(F32) + r.cap_z[3].astype(F32)
    )
    cap_recip = lax.rsqrt(head_mean(cap_raw * cap_raw, mean) + EPS)
    cap_hat = cap_raw * cap_recip
    r.cap_hat[...] = cap_hat
    r.cap_recip[...] = cap_recip
    cap_gather = LaneGather(place, r.cap_kv, r.ckv_send, r.ckv_recv)
    cap_gather.own[...] = jnp.where(lane < wq, cap_hat * gain_ckey, cap_raw).astype(BF)
    cap_gather.start()
    for i in range(4):
        tokens.arrive(i)
    cap_gather.pass_on()
    weights.finish()

    keep = LaneGather(place, r.kv, r.kv_send, r.kv_recv)

    def span(i):
        return pl.ds(pl.multiple_of(i * tok_rows, tok_rows), tok_rows)

    def w_kq():
        return r.qkvo[:, :, 0:two].reshape(width, two)

    def w_ov():
        return r.qkvo[:, :, two : 2 * two].reshape(width, two)

    def project(i, carry):
        block = r.x_buf[pl.ds(i * 2, 2)].reshape(tok_rows, width).astype(F32)
        unit, _ = normed_pair(block)
        factor = gain_in * (1.0 + item_rows(r.mod, r.items[span(i)], 0, width))
        norm = (unit * factor).astype(BF)
        r.norm_in[i] = norm
        raw = bdot(norm, w_kq())
        own_v = bdot(norm, w_ov())
        recip = lax.rsqrt(head_mean(raw * raw, mean) + EPS)
        hat = raw * recip
        r.kq_hat[i] = hat
        r.kq_recip[i] = recip
        cos = jnp.concatenate([r.cos_t[i]] * heads, axis=1)
        sin = jnp.concatenate([r.sin_t[i]] * heads, axis=1)
        gained = hat * gain_kq
        turned = gained * cos + swap_quarters(gained) * sin
        r.kv[g, span(i)] = jnp.where(lane < wq, turned, own_v).astype(BF)
        r.queries[span(i)] = (turned[:, wq:].astype(BF).astype(F32) * scale).astype(BF)
        return carry

    lax.fori_loop(0, SPLIT, project, 0)
    keep.start()
    slot_lane = lax.broadcasted_iota(jnp.int32, (1, r.totals.shape[1]), 1)
    ones = jnp.where(lax.broadcasted_iota(jnp.int32, (1, HEAD), 1) == 0, 1.0, 0.0).astype(BF)

    def with_ones(values):
        return jnp.concatenate([values, jnp.broadcast_to(ones, (values.shape[0], HEAD))], axis=1)

    def split_lump(index):
        lump = r.kv[index]
        r.k_all[index] = lump[:, :wq]
        r.v_all[index] = with_ones(lump[:, wq:])

    def attend(head, keys, values, same):
        scores = dot_t(of_head(r.queries[...], head), keys)
        if same is not None:
            scores = jnp.where(same, scores, NEG)
        out = bdot(jnp.exp(scores).astype(BF), values)
        return of_head(out[:, :wq], head), jnp.where(slot_lane == head, out[:, wq : wq + 1], 0.0)

    def cross(head, carry):
        out, total = attend(head, r.cap_k[...], r.cap_v[...], None)
        r.attn_cross[...] += out
        r.cross_logs[...] += total
        return carry

    def attend_into(index):
        def step(head, carry):
            same = r.items[...] == r.key_items[index]
            out, total = attend(head, r.k_all[index], r.v_all[index], same)
            r.attn_self[...] += out
            r.totals[...] += total
            return carry

        lax.fori_loop(0, heads, step, 0)

    for ref in (r.attn_self, r.attn_cross, r.totals, r.cross_logs):
        ref[...] = jnp.zeros_like(ref)
    split_lump(g)
    attend_into(g)
    cap_gather.finish()
    kv_text = r.cap_kv[...].reshape(4 * words, two)
    r.cap_k[...] = kv_text[:, :wq]
    r.cap_v[...] = with_ones(kv_text[:, wq:])
    feed.pass_z(1)
    keep.from_c.wait_recv()
    split_lump(place.g_c)
    attend_into(place.g_c)
    feed.pass_z(2)
    keep.pass_on()
    split_lump(place.g_y)
    attend_into(place.g_y)
    feed.pass_z(3)
    lax.fori_loop(0, heads, cross, 0)
    keep.from_diagonal.wait_recv()
    split_lump(place.g_yc)
    attend_into(place.g_yc)

    def by_total(out, totals):
        shares = jnp.zeros_like(out)
        for head in range(heads):
            share = 1.0 / totals[:, head : head + 1]
            shares = shares + of_head(jnp.broadcast_to(share, out.shape), head)
        return out * shares

    def blend(i, carry):
        at = span(i)
        self_part = by_total(r.attn_self[at], r.totals[at])
        cross_part = by_total(r.attn_cross[at], r.cross_logs[at])
        r.attn_self[at] = self_part
        r.attn_cross[at] = cross_part
        r.totals[at] = jnp.log(r.totals[at])
        r.cross_logs[at] = jnp.log(r.cross_logs[at])
        mixed = (self_part + gates * cross_part).astype(BF)
        wide = jnp.concatenate([mixed, jnp.zeros_like(mixed)], axis=1)
        r.mix_s[at] = wide
        r.part[i] = dot_t(wide, w_ov()).astype(BF).reshape(2, rows, width)
        return carry

    def scatter_of(send, recv):
        return Scatter(place, r.part, r.from_x, r.from_z, send, recv)

    out_sum = scatter_of(r.s1, r.r1)
    flow(place, None, out_sum, blend, 0)
    for i in range(4):
        feed.pass_y(i)
    branch = out_sum.finish()

    item = r.items[own_at]
    hat_two, recip_two = normed_pair(branch)
    tanh_one = jnp.tanh(item_rows(r.mod, item, 1, width))
    resid = r.patches[mine].astype(F32) + tanh_one * hat_two * gain_attn
    hat_three, recip_three = normed_pair(resid)
    factor_three = gain_ffn * (1.0 + item_rows(r.mod, item, 2, width))
    norms = Gather(place, r.n_buf, r.n_send, r.n_recv)
    norms.own[...] = (hat_three * factor_three).astype(BF)
    norms.start()
    tokens.finish()
    keep.sent()
    feed.finish()

    def f_weights(index):
        return r.ffn[:, :, index * wf : (index + 1) * wf].reshape(width, wf)

    def forward(i, carry):
        block = r.n_buf[pl.ds(i * 2, 2)].reshape(tok_rows, width)
        gate_val = bdot(block, f_weights(0))
        up_val = bdot(block, f_weights(1))
        r.gate_s[i] = gate_val
        r.up_s[i] = up_val
        hidden = (gate_val * jax.nn.sigmoid(gate_val) * up_val).astype(BF)
        r.hid_s[i] = hidden
        r.part[i] = dot_t(hidden, f_weights(2)).astype(BF).reshape(2, rows, width)
        return carry

    down = scatter_of(r.s2, r.r2)
    flow(place, norms, down, forward, 0)
    ffn = down.finish()
    norms.finish()

    hat_four, recip_four = normed_pair(ffn)
    tanh_two = jnp.tanh(item_rows(r.mod, item, 3, width))
    grad_out = r.out_grad[mine].astype(F32)
    grad_four = grad_out * tanh_two
    grads = Gather(place, r.g_buf, r.g_send, r.g_recv)
    grads.own[...] = normed_back(grad_four * gain_out, hat_four, recip_four).astype(BF)
    grads.start()
    output = resid + tanh_two * hat_four * gain_out
    r.out_own[...] = output
    r.out_half[0] = output.astype(BF)
    out_copy = remote(r.out_half.at[0], r.out_half.at[1], r.o_send, r.o_recv, place.x_peer)
    out_copy.start()
    everywhere = along[:2] + [place.x_peer] + along[2:]
    early = AllSum(everywhere, r.e_acc, r.e_land, r.e_send, r.e_recv)
    r.e_acc[0] = jnp.zeros(r.e_acc.shape[1:], F32)
    gate_sums = item_sums(grad_out * hat_four * gain_out * (1.0 - tanh_two * tanh_two), item)
    r.e_acc[0, 2:3] = jnp.sum(grad_four * hat_four, axis=0, keepdims=True)
    r.e_acc[0, 8:9] = gate_sums[0]
    r.e_acc[0, 9:10] = gate_sums[1]

    def backward(i, carry):
        block = r.g_buf[pl.ds(i * 2, 2)].reshape(tok_rows, width)
        grad_hidden = bdot(block, f_weights(2))
        gate_val = r.gate_s[i]
        gate_sig = jax.nn.sigmoid(gate_val)
        grad_gate = (
            grad_hidden * r.up_s[i] * gate_sig * (1.0 + gate_val * (1.0 - gate_sig))
        ).astype(BF)
        grad_up = (grad_hidden * gate_val * gate_sig).astype(BF)
        r.gg_s[i] = grad_gate
        r.gu_s[i] = grad_up
        r.part[i] = (
            (dot_t(grad_gate, f_weights(0)) + dot_t(grad_up, f_weights(1)))
            .astype(BF)
            .reshape(2, rows, width)
        )
        return carry

    back = scatter_of(r.s3, r.r3)
    flow(place, grads, back, backward, 0)

    block_rows = r.ffn.shape[1]
    step_cols = 4 * block_rows

    def ffn_matrices(i, carry):
        cols = pl.ds(pl.multiple_of(i * step_cols, step_cols), step_cols)
        norm = r.n_buf[:, :, cols].reshape(group, step_cols)
        grad = r.g_buf[:, :, cols].reshape(group, step_cols)
        for j, (left, right) in enumerate(((norm, r.gg_s), (norm, r.gu_s), (grad, r.hid_s))):
            block = t_dot(left, right[...].reshape(group, wf)).astype(BF)
            block = block.reshape(4, block_rows, wf)
            for other in range(4):
                r.ffn[lane_order(other) * SPLIT + i, :, j * wf : (j + 1) * wf] = block[other]
        return carry

    lax.fori_loop(0, SPLIT, ffn_matrices, 0)
    f_home = LaneScatter(place, r.ffn, r.f_fc, r.f_fy, r.fh_s, r.fh_r)
    f_home.start()
    grad_norm = back.finish()
    grads.finish()
    d_resid = grad_out + normed_back(grad_norm * factor_three, hat_three, recip_three)
    grad_two = d_resid * tanh_one
    attn_grads = Gather(place, r.x_buf, r.a_send, r.a_recv)
    attn_grads.own[...] = normed_back(grad_two * gain_attn, hat_two, recip_two).astype(BF)
    attn_grads.start()
    r.dp_own[...] = d_resid
    scale_sums = item_sums(grad_norm * hat_three * gain_ffn, item)
    gate_sums = item_sums(d_resid * hat_two * gain_attn * (1.0 - tanh_one * tanh_one), item)
    r.e_acc[0, 0:1] = jnp.sum(grad_two * hat_two, axis=0, keepdims=True)
    r.e_acc[0, 1:2] = jnp.sum(
        grad_norm * hat_three * (1.0 + item_rows(r.mod, item, 2, width)), axis=0, keepdims=True
    )
    r.e_acc[0, 4:5] = gate_sums[0]
    r.e_acc[0, 5:6] = gate_sums[1]
    r.e_acc[0, 6:7] = scale_sums[0]
    r.e_acc[0, 7:8] = scale_sums[1]

    r.dk_acc[...] = jnp.zeros_like(r.dk_acc)
    r.dv_acc[...] = jnp.zeros_like(r.dv_acc)
    r.dck_acc[...] = jnp.zeros_like(r.dck_acc)
    r.dcv_acc[...] = jnp.zeros_like(r.dcv_acc)
    f_home.step()

    def attend_back(i, gate_sum):
        at = span(i)
        block = r.x_buf[pl.ds(i * 2, 2)].reshape(tok_rows, width)
        d_mix = bdot(block, w_ov())[:, :wq].astype(BF)
        mix_f = d_mix.astype(F32)
        d_cross = (gates * mix_f).astype(BF)
        delta = head_mean(mix_f * r.attn_self[at], mean_q) * HEAD
        gate_sum = gate_sum + jnp.sum(mix_f * r.attn_cross[at], axis=0, keepdims=True)
        query = r.queries[at]
        logs = r.totals[at]
        cross_logs = r.cross_logs[at]
        dq = jnp.zeros((tok_rows, wq), F32)
        for head in range(heads):
            stack = slice(head * tok_rows, (head + 1) * tok_rows)
            query_h = of_head(query, head)
            cross_h = of_head(d_cross, head)
            r.q_stack[stack] = query_h
            r.c_stack[stack] = cross_h
            r.m_stack[stack] = of_head(d_mix, head)
            probs = jnp.exp(dot_t(query_h, r.cap_k[...]) - cross_logs[:, head : head + 1])
            d_probs = dot_t(cross_h, r.cap_v[:, :wq])
            inner = jnp.sum(probs * d_probs, axis=1, keepdims=True)
            d_scores = (probs * (d_probs - inner)).astype(BF)
            r.cp_stack[stack] = probs.astype(BF)
            r.cs_stack[stack] = d_scores
            dq = dq + of_head(bdot(d_scores, r.cap_k[...]), head)
        r.dck_acc[...] += t_dot(r.cs_stack[...], r.q_stack[...])
        r.dcv_acc[...] += t_dot(r.cp_stack[...], r.c_stack[...])
        for j in range(4):
            same = r.items[at] == r.key_items[j]
            for head in range(heads):
                stack = slice(head * tok_rows, (head + 1) * tok_rows)
                scores = jnp.where(same, dot_t(r.q_stack[stack], r.k_all[j]), NEG)
                probs = jnp.exp(scores - logs[:, head : head + 1])
                d_probs = dot_t(r.m_stack[stack], r.v_all[j, :, :wq])
                d_scores = (probs * (d_probs - delta[:, head * HEAD : head * HEAD + 1])).astype(BF)
                r.p_stack[stack] = probs.astype(BF)
                r.s_stack[stack] = d_scores
                dq = dq + of_head(bdot(d_scores, r.k_all[j]), head)
            r.dk_acc[j] += t_dot(r.s_stack[...], r.q_stack[...])
            r.dv_acc[j] += t_dot(r.p_stack[...], r.m_stack[...])
        r.dq_s[at] = (dq * scale).astype(BF)
        return gate_sum

    f_turn = TurnZ(place, r.ffn, f_home.base, r.f_land, r.fz_s, r.fz_r)

    def turn_ffn():
        f_home.finish()
        f_turn.start()

    gate_sum = flow(place, attn_grads, None, attend_back, jnp.zeros((1, wq), F32), turn_ffn)
    early.start()

    keys_home = LaneScatter(place, r.kv, r.kv_fc, r.kv_fy, r.kvh_s, r.kvh_r)
    for i in range(4):
        r.kv[lane_order(i)] = jnp.concatenate([r.dk_acc[i], r.dv_acc[i]], axis=1).astype(BF)
    keys_home.start()
    cap_home = LaneScatter(place, r.t_part, r.t_fc, r.t_fy, r.t_s, r.t_r)
    for i in range(4):
        at = slice(i * words, (i + 1) * words)
        d_cap = jnp.concatenate([r.dck_acc[at], r.dcv_acc[at]], axis=1)
        r.t_part[lane_order(i)] = d_cap.astype(BF)
    cap_home.start()

    def turn_back(i, grad):
        cos = jnp.concatenate([r.cos_t[i]] * heads, axis=1)
        sin = jnp.concatenate([r.sin_t[i]] * heads, axis=1)
        d_norm = grad * cos - swap_quarters(grad) * sin
        hat = r.kq_hat[i]
        gain_sum = jnp.sum(d_norm * hat, axis=0, keepdims=True)
        d_hat = d_norm * gain_kq
        grad = (r.kq_recip[i] * (d_hat - hat * head_mean(d_hat * hat, mean))).astype(BF)
        return grad, gain_sum

    def raw_queries(i, query_sum):
        d_query = r.dq_s[span(i)].astype(F32)
        d_query = jnp.concatenate([jnp.zeros_like(d_query), d_query], axis=1)
        grad, gain_sum = turn_back(i, d_query)
        r.dq_raw[span(i)] = grad
        return query_sum + gain_sum

    keys_home.step()
    early.step()
    cap_home.step()
    query_sum = lax.fori_loop(0, SPLIT, raw_queries, jnp.zeros((1, two), F32))

    def store_part(part, i, block):
        block = block.astype(BF).reshape(4, block_rows, two)
        for other in range(4):
            part[lane_order(other) * SPLIT + i] = block[other]

    def matrices_oq(i, carry):
        cols = pl.ds(pl.multiple_of(i * step_cols, step_cols), step_cols)
        above = r.x_buf[:, :, cols].reshape(group, step_cols)
        left = r.norm_in[:, :, cols].reshape(group, step_cols)
        store_part(r.a_part, i, t_dot(above, r.mix_s[...]) + t_dot(left, r.dq_raw[...]))
        return carry

    lax.fori_loop(0, SPLIT, matrices_oq, 0)
    a_home = LaneScatter(place, r.a_part, r.a_fc, r.a_fy, r.ah_s, r.ah_r)
    a_home.start()
    early.step()
    a_home.step()

    cap_home.finish()
    d_cap = r.t_part[cap_home.base].astype(F32)
    hat = r.cap_hat[...]
    key_lanes = lane < wq
    cap_sum = jnp.sum(jnp.where(key_lanes, d_cap * hat, 0.0), axis=0, keepdims=True)
    d_hat = d_cap * jnp.where(key_lanes, gain_ckey, 0.0)
    d_raw = r.cap_recip[...] * (d_hat - hat * head_mean(d_hat * hat, mean))
    cap_spread = SpreadZ(place, r.t_z, r.tz_s, r.tz_r)
    cap_spread.own[...] = jnp.where(key_lanes, d_raw, d_cap).astype(BF)
    cap_spread.start()
    keys_home.finish()

    def raw_keys(i, key_sum):
        total = r.kv[keys_home.base, span(i)].astype(F32)
        grad, gain_sum = turn_back(i, jnp.where(key_lanes, total, 0.0))
        r.dkv_raw[span(i)] = jnp.where(key_lanes, grad.astype(F32), total).astype(BF)
        d_kq = jnp.where(key_lanes, grad.astype(F32), r.dq_raw[span(i)].astype(F32)).astype(BF)
        d_ov = jnp.where(key_lanes, 0.0, total).astype(BF)
        r.part[i] = (
            (dot_t(d_kq, w_kq()) + dot_t(d_ov, w_ov())).astype(BF).reshape(2, rows, width)
        )
        return key_sum + gain_sum

    in_sum = scatter_of(r.s4, r.r4)
    key_sum = flow(place, None, in_sum, raw_keys, jnp.zeros((1, two), F32))

    def matrices_kv(i, carry):
        cols = pl.ds(pl.multiple_of(i * step_cols, step_cols), step_cols)
        left = r.norm_in[:, :, cols].reshape(group, step_cols)
        store_part(r.b_part, i, t_dot(left, r.dkv_raw[...]))
        return carry

    lax.fori_loop(0, SPLIT, matrices_kv, 0)
    b_home = LaneScatter(place, r.b_part, r.b_fc, r.b_fy, r.bh_s, r.bh_r)
    b_home.start()
    heads_sum = AllSum(along[:2], r.h_acc, r.h_land, r.h_send, r.h_recv)
    r.h_acc[0] = jnp.zeros(r.h_acc.shape[1:], F32)
    r.h_acc[0, 0:1] = jnp.where(key_lanes, key_sum, query_sum)
    r.h_acc[0, 1:2] = cap_sum
    r.h_acc[0, 2:3] = jnp.concatenate([gate_sum, jnp.zeros_like(gate_sum)], axis=1)
    heads_sum.start()
    a_home.finish()
    a_turn = TurnZ(place, r.a_part, a_home.base, r.a_land, r.az_s, r.az_r)
    a_turn.start()
    cap_spread.finish()
    cap_all = LaneGather(place, r.t_all, r.ta_s, r.ta_r)
    cap_all.own[...] = r.t_z[...]
    cap_all.start()
    b_home.step()
    heads_sum.step()
    heads_spread = SpreadZ(place, r.h_slots, r.hz_send, r.hz_recv)
    heads_spread.own[...] = heads_sum.step()
    heads_spread.start()
    early.step()
    early.step()
    cap_all.pass_on()

    d_norm = in_sum.finish()
    hat, recip = normed_pair(r.patches[mine].astype(F32))
    factor = 1.0 + item_rows(r.mod, item, 0, width)
    d_patches = r.dp_own[...] + normed_back(d_norm * gain_in * factor, hat, recip)
    r.dp_own[...] = d_patches
    r.dp_half[0] = d_patches.astype(BF)
    dp_copy = remote(r.dp_half.at[0], r.dp_half.at[1], r.dp_send, r.dp_recv, place.x_peer)
    dp_copy.start()
    scale_sums = item_sums(d_norm * hat * gain_in, item)
    late = AllSum(everywhere, r.l_acc, r.l_land, r.l_send, r.l_recv)
    r.l_acc[0] = jnp.zeros(r.l_acc.shape[1:], F32)
    r.l_acc[0, 0:1] = jnp.sum(d_norm * hat * factor, axis=0, keepdims=True)
    r.l_acc[0, 1:2] = scale_sums[0]
    r.l_acc[0, 2:3] = scale_sums[1]
    late.start()
    b_home.finish()
    b_turn = TurnZ(place, r.b_part, b_home.base, r.b_land, r.bz_s, r.bz_r)
    b_turn.start()
    for _ in range(4):
        late.step()
    out_copy.wait()
    attn_grads.finish()
    r.early[...] = early.step()
    heads_spread.finish()
    f_turn.finish()
    a_turn.finish()
    cap_all.finish()
    dp_copy.wait()
    r.late[...] = late.step()
    b_turn.finish()


def finish_kernel(
    out_own, out_half, dp_own, dp_half, f_land, a_land, b_land, t_all, early, late, heads_in, text,
    head_rows, band_table, item_band, w_ada,
    output, d_patches, d_query, d_key, d_value, d_out, d_gate, d_up, d_down, d_ckey, d_cvalue,
    d_ada, d_b_ada, d_attn_in, d_attn_out, d_ffn_in, d_ffn_out, d_g_query, d_g_key, d_g_ckey,
    d_cross, d_band,
):
    x = lax.axis_index("tp")
    rows, width = out_own.shape
    wf = f_land.shape[2] // 3
    wq = a_land.shape[2] // 2
    words = t_all.shape[2]
    mine = pl.ds(pl.multiple_of(x * rows, rows), rows)
    other = pl.ds(pl.multiple_of((1 - x) * rows, rows), rows)
    output[mine] = out_own[...]
    output[other] = out_half[1].astype(F32)
    d_patches[mine] = dp_own[...]
    d_patches[other] = dp_half[1].astype(F32)
    for z in range(SPLIT):
        at = slice(z * wf, (z + 1) * wf)
        d_gate[:, at] = f_land[z, :, 0:wf].astype(F32)
        d_up[:, at] = f_land[z, :, wf : 2 * wf].astype(F32)
        d_down[at] = f_land[z, :, 2 * wf : 3 * wf].astype(F32).T
        at = slice(z * wq, (z + 1) * wq)
        d_out[at] = a_land[z, :, 0:wq].astype(F32).T
        d_query[:, at] = a_land[z, :, wq : 2 * wq].astype(F32)
        d_key[:, at] = b_land[z, :, 0:wq].astype(F32)
        d_value[:, at] = b_land[z, :, wq : 2 * wq].astype(F32)
        d_cap = t_dot(text[...], t_all[:, z].reshape(4 * words, 2 * wq))
        d_ckey[:, at] = d_cap[:, :wq]
        d_cvalue[:, at] = d_cap[:, wq:]
    grad_mod = jnp.concatenate([late[1:3], early[4:6], early[6:8], early[8:10]], axis=1)
    pre, sig = conditioning(band_table, item_band)
    low = (pre * sig).astype(BF).astype(F32)
    cols = jnp.concatenate([low, jnp.zeros((6, low.shape[1]), F32)], axis=0).T
    d_ada[...] = cols[:, 0:1] * grad_mod[0:1] + cols[:, 1:2] * grad_mod[1:2]
    d_act = lax.dot_general(
        grad_mod,
        w_ada[...].astype(F32),
        (((1,), (1,)), ((), ())),
        precision=HIGH,
        preferred_element_type=F32,
    )
    d_pre = d_act * sig * (1.0 + pre * (1.0 - sig))
    band = lax.broadcasted_iota(jnp.int32, (BANDS, 1), 0)
    d_band[...] = sum(
        jnp.where(band == item_band[i], d_pre[i : i + 1], 0.0) for i in range(ITEMS)
    )
    d_b_ada[...] = (grad_mod[0:1] + grad_mod[1:2]).reshape(d_b_ada.shape)
    d_attn_in[...] = late[0:1].reshape(d_attn_in.shape)
    d_attn_out[...] = early[0:1].reshape(d_attn_out.shape)
    d_ffn_in[...] = early[1:2].reshape(d_ffn_in.shape)
    d_ffn_out[...] = early[2:3].reshape(d_ffn_out.shape)

    def joined(row, part):
        return jnp.concatenate(
            [heads_in[z, row : row + 1, part * wq : (part + 1) * wq] for z in range(SPLIT)], axis=1
        ).reshape(d_g_key.shape)

    d_g_key[...] = joined(0, 0)
    d_g_query[...] = joined(0, 1)
    d_g_ckey[...] = joined(1, 0)
    heads = wq // HEAD
    lane = lax.broadcasted_iota(jnp.int32, (wq, 128), 0) // HEAD
    col = lax.broadcasted_iota(jnp.int32, (wq, 128), 1)
    total = jnp.zeros((8, 128), F32)
    for z in range(SPLIT):
        gate = jnp.tanh(head_rows[z, 2:3, :wq])
        terms = heads_in[z, 2:3, :wq] * (1.0 - gate * gate)
        terms = jnp.concatenate([terms, jnp.zeros((7, wq), F32)], axis=0)
        pick = jnp.where(col == lane + z * heads, 1.0, 0.0)
        total = total + jnp.dot(terms, pick, precision=HIGH, preferred_element_type=F32)
    d_cross[...] = total[0:1]


def conditioning(band_table, item_band):
    band = lax.broadcasted_iota(jnp.int32, (BANDS, 1), 0)
    table = band_table[...]
    pre = jnp.concatenate(
        [
            jnp.sum(jnp.where(band == item_band[i], table, 0.0), axis=0, keepdims=True)
            for i in range(ITEMS)
        ],
        axis=0,
    )
    return pre, jax.nn.sigmoid(pre)


def layer_call(ins):
    tok_rows, width = ins["patches"].shape
    rows = tok_rows // 2
    row_dev, q_cols = ins["w_query"].shape
    wq, wf = q_cols // SPLIT, ins["w_gate"].shape[1] // SPLIT
    two = 2 * wq
    heads = wq // HEAD
    lanes = 4
    group = SPLIT * tok_rows
    text, features = ins["caption"].shape
    words = text // lanes
    feat_dev = ins["w_ckey"].shape[0]
    mod = (ITEMS, 4 * width)
    tile, sem = pltpu.VMEM, lambda count: pltpu.SemaphoreType.DMA((count,))
    cap = (words, two)
    shard = (SPLIT, row_dev)
    both, half = (SPLIT, tok_rows), (rows, width)

    def sum_tile(size, steps):
        return tile((steps,) + size, F32)

    scratch = dict(
        text_sem=pltpu.SemaphoreType.DMA,
        qkvo_in=tile(shard + (2 * two,), BF),
        ffn_in=tile(shard + (3 * wf,), BF),
        qkvo=tile((SPLIT * lanes, row_dev, 2 * two), BF),
        ffn=tile((SPLIT * lanes, row_dev, 3 * wf), BF),
        w_send=sem(16),
        w_recv=sem(16),
        f_send=sem(16),
        f_recv=sem(16),
        x_buf=tile((2 * SPLIT,) + half, BF),
        n_buf=tile((2 * SPLIT,) + half, BF),
        g_buf=tile((2 * SPLIT,) + half, BF),
        x_send=sem(10),
        x_recv=sem(10),
        n_send=sem(10),
        n_recv=sem(10),
        g_send=sem(10),
        g_recv=sem(10),
        a_send=sem(10),
        a_recv=sem(10),
        part=tile((SPLIT, 2) + half, BF),
        from_x=tile((SPLIT,) + half, BF),
        from_z=tile((SPLIT,) + half, BF),
        s1=sem(8),
        r1=sem(8),
        s2=sem(8),
        r2=sem(8),
        s3=sem(8),
        r3=sem(8),
        s4=sem(8),
        r4=sem(8),
        m_acc=sum_tile((ITEMS, 4 * width), 4),
        m_land=sum_tile((ITEMS, 4 * width), 4),
        m_send=sem(6),
        m_recv=sem(6),
        e_acc=sum_tile((16, width), 5),
        e_land=sum_tile((16, width), 5),
        e_send=sem(6),
        e_recv=sem(6),
        l_acc=sum_tile((8, width), 5),
        l_land=sum_tile((8, width), 5),
        l_send=sem(6),
        l_recv=sem(6),
        h_acc=sum_tile((8, two), 2),
        h_land=sum_tile((8, two), 2),
        hz_send=sem(3),
        hz_recv=sem(3),
        h_send=sem(6),
        h_recv=sem(6),
        mod=tile((ITEMS, 4 * width), F32),
        pos_buf=tile((SPLIT, 8, tok_rows), F32),
        pos_send=sem(3),
        pos_recv=sem(3),
        cap_part=tile((4 * SPLIT,) + cap, BF),
        cap_fc=tile((2 * SPLIT,) + cap, BF),
        cap_fy=tile((SPLIT,) + cap, BF),
        cap_s=sem(2),
        cap_r=sem(2),
        cap_z=tile((SPLIT,) + cap, BF),
        cz_send=sem(4),
        cz_recv=sem(4),
        cap_kv=tile((lanes,) + cap, BF),
        ckv_send=sem(3),
        ckv_recv=sem(3),
        cap_hat=tile(cap, F32),
        cap_recip=tile(cap, F32),
        cap_k=tile((text, wq), BF),
        cap_v=tile((text, wq + HEAD), BF),
        items=tile((group, 1), jnp.int32),
        key_items=tile((lanes, 1, group), jnp.int32),
        cos_t=tile(both + (2 * HEAD,), F32),
        sin_t=tile(both + (2 * HEAD,), F32),
        norm_in=tile(both + (width,), BF),
        kq_hat=tile(both + (two,), F32),
        kq_recip=tile(both + (two,), F32),
        kv=tile((lanes, group, two), BF),
        kv_send=sem(3),
        kv_recv=sem(3),
        k_all=tile((lanes, group, wq), BF),
        v_all=tile((lanes, group, wq + HEAD), BF),
        queries=tile((group, wq), BF),
        totals=tile((group, 128), F32),
        cross_logs=tile((group, 128), F32),
        attn_self=tile((group, wq), F32),
        attn_cross=tile((group, wq), F32),
        mix_s=tile((group, two), BF),
        gate_s=tile(both + (wf,), F32),
        up_s=tile(both + (wf,), F32),
        hid_s=tile(both + (wf,), BF),
        gg_s=tile(both + (wf,), BF),
        gu_s=tile(both + (wf,), BF),
        o_send=pltpu.SemaphoreType.DMA,
        o_recv=pltpu.SemaphoreType.DMA,
        dp_send=pltpu.SemaphoreType.DMA,
        dp_recv=pltpu.SemaphoreType.DMA,
        f_fc=tile((2 * SPLIT, row_dev, 3 * wf), BF),
        f_fy=tile((SPLIT, row_dev, 3 * wf), BF),
        fh_s=sem(2),
        fh_r=sem(2),
        fz_s=sem(4),
        fz_r=sem(4),
        a_part=tile((4 * SPLIT, row_dev, two), BF),
        a_fc=tile((2 * SPLIT, row_dev, two), BF),
        a_fy=tile((SPLIT, row_dev, two), BF),
        ah_s=sem(2),
        ah_r=sem(2),
        az_s=sem(4),
        az_r=sem(4),
        b_part=tile((4 * SPLIT, row_dev, two), BF),
        b_fc=tile((2 * SPLIT, row_dev, two), BF),
        b_fy=tile((SPLIT, row_dev, two), BF),
        bh_s=sem(2),
        bh_r=sem(2),
        bz_s=sem(4),
        bz_r=sem(4),
        kv_fc=tile((2, group, two), BF),
        kv_fy=tile((1, group, two), BF),
        kvh_s=sem(2),
        kvh_r=sem(2),
        t_part=tile((4,) + cap, BF),
        t_fc=tile((2,) + cap, BF),
        t_fy=tile((1,) + cap, BF),
        t_s=sem(2),
        t_r=sem(2),
        t_z=tile((SPLIT,) + cap, BF),
        tz_s=sem(3),
        tz_r=sem(3),
        ta_s=sem(3),
        ta_r=sem(3),
        dk_acc=tile((lanes, group, wq), F32),
        dv_acc=tile((lanes, group, wq), F32),
        dck_acc=tile((text, wq), F32),
        dcv_acc=tile((text, wq), F32),
        q_stack=tile((heads * tok_rows, wq), BF),
        c_stack=tile((heads * tok_rows, wq), BF),
        m_stack=tile((heads * tok_rows, wq), BF),
        cp_stack=tile((heads * tok_rows, text), BF),
        cs_stack=tile((heads * tok_rows, text), BF),
        p_stack=tile((heads * tok_rows, group), BF),
        s_stack=tile((heads * tok_rows, group), BF),
        dq_s=tile((group, wq), BF),
        dq_raw=tile((group, two), BF),
        dkv_raw=tile((group, two), BF),
    )
    shape = jax.ShapeDtypeStruct
    outs = dict(
        out_own=shape((rows, width), F32),
        out_half=shape((2, rows, width), BF),
        dp_own=shape((rows, width), F32),
        dp_half=shape((2, rows, width), BF),
        f_land=shape((SPLIT, row_dev, 3 * wf), BF),
        a_land=shape((SPLIT, row_dev, two), BF),
        b_land=shape((SPLIT, row_dev, two), BF),
        t_all=shape((lanes, SPLIT) + cap, BF),
        early=shape((16, width), F32),
        late=shape((8, width), F32),
        h_slots=shape((SPLIT, 8, two), F32),
        text=shape((text, feat_dev), BF),
    )
    vmem = pl.BlockSpec(memory_space=pltpu.VMEM)
    hbm = pl.BlockSpec(memory_space=pl.ANY)
    smem = pl.BlockSpec(memory_space=pltpu.SMEM)
    places = dict(caption=hbm, block_item=smem, item_band=smem)
    names = list(ins) + list(outs) + list(scratch)
    results = pl.pallas_call(
        functools.partial(layer_kernel, names),
        out_shape=tuple(outs.values()),
        in_specs=[places.get(name, vmem) for name in ins],
        out_specs=[hbm if name.endswith("_land") else vmem for name in outs],
        scratch_shapes=list(scratch.values()),
        compiler_params=pltpu.CompilerParams(
            collective_id=1, has_side_effects=True, vmem_limit_bytes=VMEM_LIMIT
        ),
        name="layer",
    )(*ins.values())
    return dict(zip(outs, results))


def local_any(
    patches,
    caption,
    band_table,
    block_item,
    item_band,
    positions,
    out_grad,
    w_query,
    w_key,
    w_value,
    w_out,
    w_gate,
    w_up,
    w_down,
    w_ckey,
    w_cvalue,
    w_ada,
    b_ada,
    g_attn_in,
    g_attn_out,
    g_ffn_in,
    g_ffn_out,
    g_query,
    g_key,
    g_ckey,
    cross_gate,
):
    scale = 1.0 / math.sqrt(HEAD)
    rank = lax.axis_index("sp")
    half = lax.axis_index("tp")
    cycle = lax.axis_size("sp")
    halves = lax.axis_size("tp")
    lanes = cycle // SPLIT
    along_z, along_g = groups_of(cycle)
    my_z, my_g = rank // lanes, rank % lanes
    tok_rows, width = patches.shape
    own_rows = tok_rows // halves
    text_count = caption.shape[0]
    blocks_dev = tok_rows // BLK
    wq, wf = w_query.shape[1] // SPLIT, w_gate.shape[1] // SPLIT
    heads = wq // HEAD
    sizes = (wq, wq, wq, wq, wf, wf, wf)
    starts = [sum(sizes[:i]) for i in range(8)]

    def gather_z(block):
        return lax.all_gather(block, "sp", axis_index_groups=along_z, axis=0, tiled=False)

    def gather_g(block):
        return lax.all_gather(block, "sp", axis_index_groups=along_g, axis=0, tiled=False)

    def scatter_z(block):
        return lax.psum_scatter(
            block, "sp", axis_index_groups=along_z, scatter_dimension=0, tiled=False
        )

    def scatter_g(block):
        return lax.psum_scatter(
            block, "sp", axis_index_groups=along_g, scatter_dimension=0, tiled=False
        )

    def turn_z(block):
        return lax.all_to_all(
            block, "sp", 0, 0, axis_index_groups=along_z, tiled=True
        )

    def sum_g(block):
        return lax.psum(block, "sp", axis_index_groups=along_g)

    def gather_tokens(own):
        both = lax.all_gather(own, "tp", axis=0, tiled=True)
        return gather_z(both).reshape(SPLIT * tok_rows, -1)

    def scatter_tokens(part):
        part = part.astype(BF).reshape(SPLIT, halves, own_rows, width)
        mine = lax.psum_scatter(part, "tp", scatter_dimension=1, tiled=False)
        return scatter_z(mine.astype(BF)).astype(F32)

    def by_z(block):
        rows, cols = block.shape
        return block.reshape(rows, SPLIT, cols // SPLIT).transpose(1, 0, 2)

    shards = jnp.concatenate(
        [by_z(m) for m in (w_query, w_key, w_value, w_out.T, w_gate, w_up, w_down.T)], axis=2
    )
    rows_dev = shards.shape[1]
    merged = gather_g(turn_z(shards)).transpose(1, 0, 2, 3).reshape(cycle * rows_dev, -1)
    f_query, f_key, f_value, f_out, f_gate, f_up, f_down = (
        merged[:, starts[i] : starts[i + 1]] for i in range(7)
    )

    items_all = block_item.reshape(SPLIT, lanes, blocks_dev)
    grp_items = jnp.repeat(
        lax.dynamic_index_in_dim(items_all, my_g, 1, keepdims=False).reshape(-1), BLK
    )
    key_items = jnp.repeat(items_all.transpose(1, 0, 2).reshape(-1), BLK)
    row0 = half * own_rows

    def own_part(block):
        return lax.dynamic_slice_in_dim(block, row0, own_rows, 0)

    own_items = own_part(
        jnp.repeat(lax.dynamic_slice_in_dim(block_item, rank * blocks_dev, blocks_dev), BLK)
    )

    band_hot = (item_band[:, None] == jnp.arange(BANDS, dtype=jnp.int32)[None, :]).astype(F32)
    cond_pre = jnp.dot(band_hot, band_table, precision=HIGH)
    cond_sig = jax.nn.sigmoid(cond_pre)
    cond_low = (cond_pre * cond_sig).astype(BF)
    text_rows = w_ckey.shape[0]
    text_local = lax.dynamic_slice_in_dim(caption, rank * text_rows, text_rows, 1)
    modulation = lax.psum(bdot(cond_low, w_ada), "sp") + b_ada
    cap_part = jnp.stack([by_z(bdot(text_local, w_ckey)), by_z(bdot(text_local, w_cvalue))], 1)
    cap_raw = sum_g(scatter_z(cap_part))
    ckey_hat, ckey_recip = normed_pair(cap_raw[0].reshape(text_count, heads, HEAD))

    def per_head(vector):
        return lax.dynamic_slice_in_dim(vector, my_z * wq, wq, 0).reshape(heads, HEAD)

    gain_query, gain_key, gain_ckey = per_head(g_query), per_head(g_key), per_head(g_ckey)
    gate_tanh = jnp.tanh(lax.dynamic_slice_in_dim(cross_gate, my_z * heads, heads, 0))
    cap_keys = (ckey_hat * gain_ckey).astype(BF)
    cap_values = cap_raw[1].astype(BF).reshape(text_count, heads, HEAD)

    def of_items(rows, items):
        return jnp.where(items[:, None] == 0, rows[0], rows[1])

    mod_own = of_items(modulation, own_items)
    scale_attn, gate_attn, scale_ffn, gate_ffn = (
        mod_own[:, i * width : (i + 1) * width] for i in range(4)
    )
    group_rows = SPLIT * tok_rows

    patch_f = own_part(patches).astype(F32)
    grad_out = own_part(out_grad).astype(F32)
    hat_one, recip_one = normed_pair(patch_f)
    factor_one = g_attn_in * (1.0 + scale_attn)
    norm_in = gather_tokens((hat_one * factor_one).astype(BF))
    pos_all = gather_z(positions).transpose(1, 0, 2).reshape(2, group_rows)
    cos_row, sin_row, cos_col, sin_col = angles(pos_all)
    split_heads = (group_rows, heads, HEAD)
    query_raw = bdot(norm_in, f_query).reshape(split_heads)
    key_raw = bdot(norm_in, f_key).reshape(split_heads)
    values_low = bdot(norm_in, f_value).astype(BF)
    query_hat, query_recip = normed_pair(query_raw)
    queries = rotate(query_hat * gain_query, cos_row, sin_row, cos_col, sin_col).astype(BF)
    key_hat, key_recip = normed_pair(key_raw)
    keys_low = rotate(key_hat * gain_key, cos_row, sin_row, cos_col, sin_col).astype(BF)
    all_keys, all_values = (
        gather_g(block).reshape(lanes * group_rows, heads, HEAD)
        for block in (keys_low.reshape(group_rows, wq), values_low)
    )
    same = (grp_items[:, None] == key_items[None, :])[None]
    scores = jnp.einsum("qhd,khd->hqk", queries, all_keys, preferred_element_type=F32) * scale
    scores = jnp.where(same, scores, NEG)
    exps = jnp.exp(scores - jnp.max(scores, axis=-1, keepdims=True))
    probs = exps / jnp.sum(exps, axis=-1, keepdims=True)
    probs_low = probs.astype(BF)
    attn_self = jnp.einsum("hqk,khd->qhd", probs_low, all_values, preferred_element_type=F32)
    cross_scores = (
        jnp.einsum("qhd,khd->hqk", queries, cap_keys, preferred_element_type=F32) * scale
    )
    cross_exp = jnp.exp(cross_scores - jnp.max(cross_scores, axis=-1, keepdims=True))
    cross_probs = cross_exp / jnp.sum(cross_exp, axis=-1, keepdims=True)
    cross_low = cross_probs.astype(BF)
    attn_cross = jnp.einsum("hqk,khd->qhd", cross_low, cap_values, preferred_element_type=F32)
    mixed = (attn_self + gate_tanh[None, :, None] * attn_cross).astype(BF).reshape(group_rows, wq)
    attn_branch = scatter_tokens(dot_t(mixed, f_out))

    hat_two, recip_two = normed_pair(attn_branch)
    tanh_one = jnp.tanh(gate_attn)
    resid = patch_f + tanh_one * hat_two * g_attn_out
    hat_three, recip_three = normed_pair(resid)
    factor_three = g_ffn_in * (1.0 + scale_ffn)
    norm_ffn = gather_tokens((hat_three * factor_three).astype(BF))
    gate_val = bdot(norm_ffn, f_gate)
    up_val = bdot(norm_ffn, f_up)
    gate_sig = jax.nn.sigmoid(gate_val)
    hidden = (gate_val * gate_sig * up_val).astype(BF)
    ffn_branch = scatter_tokens(dot_t(hidden, f_down))
    hat_four, recip_four = normed_pair(ffn_branch)
    tanh_two = jnp.tanh(gate_ffn)
    output = resid + tanh_two * hat_four * g_ffn_out

    grad_gate_ffn = grad_out * hat_four * g_ffn_out * (1.0 - tanh_two * tanh_two)
    grad_four = grad_out * tanh_two
    grad_g_ffn_out = jnp.sum(grad_four * hat_four, axis=0)
    grad_ffn = gather_tokens(
        normed_back(grad_four * g_ffn_out, hat_four, recip_four).astype(BF)
    )
    grad_hidden = bdot(grad_ffn, f_down)
    grad_gate = (grad_hidden * up_val * gate_sig * (1.0 + gate_val * (1.0 - gate_sig))).astype(BF)
    grad_up = (grad_hidden * gate_val * gate_sig).astype(BF)
    grad_norm_ffn = scatter_tokens(dot_t(grad_gate, f_gate) + dot_t(grad_up, f_up))
    grad_scale_ffn = grad_norm_ffn * hat_three * g_ffn_in
    grad_g_ffn_in = jnp.sum(grad_norm_ffn * hat_three * (1.0 + scale_ffn), axis=0)
    grad_resid = grad_out + normed_back(grad_norm_ffn * factor_three, hat_three, recip_three)

    grad_gate_attn = grad_resid * hat_two * g_attn_out * (1.0 - tanh_one * tanh_one)
    grad_two = grad_resid * tanh_one
    grad_g_attn_out = jnp.sum(grad_two * hat_two, axis=0)
    grad_attn = gather_tokens(normed_back(grad_two * g_attn_out, hat_two, recip_two).astype(BF))
    grad_mixed = bdot(grad_attn, f_out).astype(BF).reshape(split_heads)
    grad_mixed_f = grad_mixed.astype(F32)
    grad_cross_gate = jnp.sum(grad_mixed_f * attn_cross, axis=(0, 2)) * (
        1.0 - gate_tanh * gate_tanh
    )
    grad_cross = (gate_tanh[None, :, None] * grad_mixed_f).astype(BF)
    grad_cprobs = jnp.einsum("qhd,khd->hqk", grad_cross, cap_values, preferred_element_type=F32)
    grad_cscores = (
        cross_probs * (grad_cprobs - jnp.sum(cross_probs * grad_cprobs, axis=-1, keepdims=True))
    ).astype(BF)
    query_grad = jnp.einsum("hqk,khd->qhd", grad_cscores, cap_keys, preferred_element_type=F32)
    grad_ckeys_part = (
        jnp.einsum("hqk,qhd->khd", grad_cscores, queries, preferred_element_type=F32) * scale
    )
    grad_cvals_part = jnp.einsum(
        "hqk,qhd->khd", cross_low, grad_cross, preferred_element_type=F32
    )
    row_delta = jnp.sum(grad_mixed_f * attn_self, axis=-1).T
    grad_probs = jnp.einsum("qhd,khd->hqk", grad_mixed, all_values, preferred_element_type=F32)
    grad_scores = (probs * (grad_probs - row_delta[..., None])).astype(BF)
    query_grad = query_grad + jnp.einsum(
        "hqk,khd->qhd", grad_scores, all_keys, preferred_element_type=F32
    )
    key_part = (
        jnp.einsum("hqk,qhd->khd", grad_scores, queries, preferred_element_type=F32) * scale
    )
    value_part = jnp.einsum("hqk,qhd->khd", probs_low, grad_mixed, preferred_element_type=F32)
    key_grad, value_grad = (
        scatter_g(block.astype(BF).reshape(lanes, group_rows, wq)) for block in (key_part, value_part)
    )
    grad_queries = (query_grad * scale).astype(BF).astype(F32)
    grad_qnorm = rotate(grad_queries, cos_row, -sin_row, cos_col, -sin_col)
    grad_g_query = jnp.sum(grad_qnorm * query_hat, axis=0).reshape(-1)
    grad_query_raw = (
        normed_back(grad_qnorm * gain_query, query_hat, query_recip).astype(BF).reshape(-1, wq)
    )
    grad_keys = key_grad.astype(F32).reshape(split_heads)
    grad_knorm = rotate(grad_keys, cos_row, -sin_row, cos_col, -sin_col)
    grad_g_key = jnp.sum(grad_knorm * key_hat, axis=0).reshape(-1)
    grad_key_raw = (
        normed_back(grad_knorm * gain_key, key_hat, key_recip).astype(BF).reshape(-1, wq)
    )
    grad_values = value_grad.astype(BF)
    grad_norm_in = scatter_tokens(
        dot_t(grad_query_raw, f_query) + dot_t(grad_key_raw, f_key) + dot_t(grad_values, f_value)
    )
    grad_scale_attn = grad_norm_in * hat_one * g_attn_in
    grad_g_attn_in = jnp.sum(grad_norm_in * hat_one * (1.0 + scale_attn), axis=0)
    grad_patches = grad_resid + normed_back(grad_norm_in * factor_one, hat_one, recip_one)

    grad_merged = jnp.concatenate(
        [
            t_dot(norm_in, grad_query_raw),
            t_dot(norm_in, grad_key_raw),
            t_dot(norm_in, grad_values),
            t_dot(grad_attn, mixed),
            t_dot(norm_ffn, grad_gate),
            t_dot(norm_ffn, grad_up),
            t_dot(grad_ffn, hidden),
        ],
        axis=1,
    ).astype(BF)
    grad_merged = grad_merged.reshape(SPLIT, lanes, rows_dev, -1).transpose(1, 0, 2, 3)
    shard_grads = turn_z(scatter_g(grad_merged)).astype(F32)
    (shard_query, shard_key, shard_value, shard_out, shard_gate, shard_up, shard_down) = (
        shard_grads[:, :, starts[i] : starts[i + 1]].transpose(1, 0, 2).reshape(rows_dev, -1)
        for i in range(7)
    )

    token_sums = lax.psum(
        (
            jnp.stack(
                [
                    jnp.concatenate(
                        [
                            jnp.sum(
                                jnp.where((own_items == item)[:, None], block, 0.0), axis=0
                            )
                            for block in (
                                grad_scale_attn,
                                grad_gate_attn,
                                grad_scale_ffn,
                                grad_gate_ffn,
                            )
                        ]
                    )
                    for item in range(ITEMS)
                ]
            ),
            grad_g_attn_in,
            grad_g_attn_out,
            grad_g_ffn_in,
            grad_g_ffn_out,
        ),
        ("sp", "tp"),
    )
    head_sums = jnp.concatenate([grad_g_query, grad_g_key, grad_cross_gate])
    head_sums = gather_z(sum_g(head_sums))
    grad_ckeys = sum_g(grad_ckeys_part).astype(BF).astype(F32)
    grad_cvals = sum_g(grad_cvals_part).astype(BF).reshape(text_count, wq)
    grad_g_ckey = gather_z(jnp.sum(grad_ckeys * ckey_hat, axis=0).reshape(-1)).reshape(-1)
    grad_ckey_raw = (
        normed_back(grad_ckeys * gain_ckey, ckey_hat, ckey_recip).astype(BF).reshape(text_count, wq)
    )
    cap_grads = gather_z(jnp.stack([grad_ckey_raw, grad_cvals])).transpose(1, 2, 0, 3)
    cap_grads = cap_grads.reshape(2, text_count, SPLIT * wq)
    grad_mod = token_sums[0]
    grad_b_ada = jnp.sum(grad_mod, axis=0)
    grad_w_ada = jnp.dot(cond_low.astype(F32).T, grad_mod, precision=HIGH)
    grad_cond_act = jnp.dot(grad_mod, w_ada.astype(F32).T, precision=HIGH)
    grad_cond_pre = grad_cond_act * cond_sig * (1.0 + cond_pre * (1.0 - cond_sig))
    grad_band_table = jnp.dot(band_hot.T, grad_cond_pre, precision=HIGH)
    return (
        lax.all_gather(output, "tp", axis=0, tiled=True),
        lax.all_gather(grad_patches, "tp", axis=0, tiled=True),
        shard_query,
        shard_key,
        shard_value,
        shard_out.T,
        shard_gate,
        shard_up,
        shard_down.T,
        t_dot(text_local, cap_grads[0]),
        t_dot(text_local, cap_grads[1]),
        grad_w_ada,
        grad_b_ada,
        token_sums[1],
        token_sums[2],
        token_sums[3],
        token_sums[4],
        head_sums[:, :wq].reshape(-1),
        head_sums[:, wq : 2 * wq].reshape(-1),
        grad_g_ckey,
        head_sums[:, 2 * wq :].reshape(-1),
        grad_band_table,
    )


def local(
    patches,
    caption,
    band_table,
    block_item,
    item_band,
    positions,
    out_grad,
    w_query,
    w_key,
    w_value,
    w_out,
    w_gate,
    w_up,
    w_down,
    w_ckey,
    w_cvalue,
    w_ada,
    b_ada,
    g_attn_in,
    g_attn_out,
    g_ffn_in,
    g_ffn_out,
    g_query,
    g_key,
    g_ckey,
    cross_gate,
):
    width = patches.shape[1]
    wq = w_query.shape[1] // SPLIT
    rows_in = jnp.concatenate(
        [jnp.stack([g_attn_in, g_attn_out, g_ffn_in, g_ffn_out]), b_ada.reshape(4, width)]
    )
    gains = [vector.reshape(SPLIT, wq) for vector in (g_key, g_query, g_ckey)]
    pad = jnp.zeros((SPLIT, wq), F32)
    freqs = FREQ_BASE ** (-(jnp.arange(2 * wq) % (HEAD // 4)).astype(F32) / (HEAD // 4))
    head_rows = jnp.stack(
        [
            jnp.concatenate([gains[0], gains[1]], axis=1),
            jnp.concatenate([gains[2], pad], axis=1),
            jnp.concatenate([jnp.repeat(cross_gate, HEAD).reshape(SPLIT, wq), pad], axis=1),
            jnp.broadcast_to(freqs, (SPLIT, 2 * wq)),
        ]
        + [jnp.zeros((SPLIT, 2 * wq), F32)] * 4,
        axis=1,
    )
    done = layer_call(
        dict(
            patches=patches,
            caption=caption,
            band_table=band_table,
            block_item=block_item,
            item_band=item_band,
            positions=positions,
            out_grad=out_grad,
            w_query=w_query,
            w_key=w_key,
            w_value=w_value,
            w_out=w_out,
            w_gate=w_gate,
            w_up=w_up,
            w_down=w_down,
            w_ckey=w_ckey,
            w_cvalue=w_cvalue,
            w_ada=w_ada,
            rows_in=rows_in,
            head_rows=head_rows,
        )
    )
    shape = jax.ShapeDtypeStruct
    like = lambda array: shape(array.shape, F32)
    vmem = pl.BlockSpec(memory_space=pltpu.VMEM)
    smem = pl.BlockSpec(memory_space=pltpu.SMEM)
    results = pl.pallas_call(
        finish_kernel,
        out_shape=(
            like(patches), like(patches), like(w_query), like(w_key), like(w_value), like(w_out),
            like(w_gate), like(w_up), like(w_down), like(w_ckey), like(w_cvalue), like(w_ada),
            like(b_ada), like(g_attn_in), like(g_attn_out), like(g_ffn_in), like(g_ffn_out),
            like(g_query), like(g_key), like(g_ckey), shape((1, 128), F32), like(band_table),
        ),
        in_specs=[vmem] * 14 + [smem, vmem],
        out_specs=[vmem] * 22,
        compiler_params=pltpu.CompilerParams(vmem_limit_bytes=VMEM_LIMIT),
        name="finish",
    )(*done.values(), head_rows, band_table, item_band, w_ada)
    results = list(results)
    results[20] = results[20][0, : cross_gate.shape[0]]
    return tuple(results)


def solution(mesh):
    lanes = mesh.shape["sp"] // SPLIT
    body = local if lanes == 4 and mesh.shape["tp"] == 2 else local_any
    in_specs = (
        P("sp", None),
        P(),
        P(None, "sp"),
        P(),
        P(),
        P(None, "sp"),
        P("sp", None),
        P("sp", "tp"),
        P("sp", "tp"),
        P("sp", "tp"),
        P("tp", "sp"),
        P("sp", "tp"),
        P("sp", "tp"),
        P("tp", "sp"),
        P("sp", "tp"),
        P("sp", "tp"),
        P("sp", None),
        P(),
        P(),
        P(),
        P(),
        P(),
        P("tp"),
        P("tp"),
        P("tp"),
        P("tp"),
    )
    out_specs = (
        P("sp", None),
        P("sp", None),
        P("sp", "tp"),
        P("sp", "tp"),
        P("sp", "tp"),
        P("tp", "sp"),
        P("sp", "tp"),
        P("sp", "tp"),
        P("tp", "sp"),
        P("sp", "tp"),
        P("sp", "tp"),
        P("sp", None),
        P(),
        P(),
        P(),
        P(),
        P(),
        P("tp"),
        P("tp"),
        P("tp"),
        P("tp"),
        P(None, "sp"),
    )
    return jax.shard_map(body, mesh=mesh, in_specs=in_specs, out_specs=out_specs, check_vma=False)
```

```python
import functools
import math
from types import SimpleNamespace

import jax
import jax.numpy as jnp
from jax import lax
from jax.experimental import pallas as pl
from jax.experimental.pallas import tpu as pltpu
from jax.sharding import PartitionSpec as P

BANDS = 16
ITEMS = 2
BLK = 32
HEAD = 64
EPS = 1e-06
NEG = -1e30
FREQ_BASE = 10000.0
HIGH = lax.Precision.HIGHEST
BF = jnp.bfloat16
F32 = jnp.float32
SPLIT = 4


def groups_of(cycle_size):
    lanes = cycle_size // SPLIT
    along_z = [[z * lanes + g for z in range(SPLIT)] for g in range(lanes)]
    along_g = [[z * lanes + g for g in range(lanes)] for z in range(SPLIT)]
    return along_z, along_g


def normed_pair(value):
    recip = lax.rsqrt(jnp.mean(value * value, axis=-1, keepdims=True) + EPS)
    return value * recip, recip


def normed_back(grad_hat, normal, recip):
    return recip * (grad_hat - normal * jnp.mean(grad_hat * normal, axis=-1, keepdims=True))


def rotate(value, cos_row, sin_row, cos_col, sin_col):
    quarter = value.shape[-1] // 4
    part_a = value[..., :quarter]
    part_b = value[..., quarter : 2 * quarter]
    part_c = value[..., 2 * quarter : 3 * quarter]
    part_e = value[..., 3 * quarter :]
    return jnp.concatenate(
        [
            part_a * cos_row - part_b * sin_row,
            part_a * sin_row + part_b * cos_row,
            part_c * cos_col - part_e * sin_col,
            part_c * sin_col + part_e * cos_col,
        ],
        axis=-1,
    )


def angles(positions):
    quarter = HEAD // 4
    freqs = FREQ_BASE ** (-jnp.arange(quarter, dtype=F32) / quarter)
    row_angle = positions[0].astype(F32)[:, None] * freqs[None, :]
    col_angle = positions[1].astype(F32)[:, None] * freqs[None, :]
    return (
        jnp.cos(row_angle)[:, None, :],
        jnp.sin(row_angle)[:, None, :],
        jnp.cos(col_angle)[:, None, :],
        jnp.sin(col_angle)[:, None, :],
    )


def bdot(left, right):
    return jnp.dot(left, right, preferred_element_type=F32)


def dot_t(left, right):
    return lax.dot_general(left, right, (((1,), (1,)), ((), ())), preferred_element_type=F32)


def t_dot(left, right):
    return lax.dot_general(left, right, (((0,), (0,)), ((), ())), preferred_element_type=F32)


MESH = pl.DeviceIdType.MESH
VMEM_LIMIT = 63 * 2**20
NEAR = (1, 3, 2)


class Place:
    def __init__(self):
        rank = lax.axis_index("sp")
        self.lanes = lax.axis_size("sp") // SPLIT
        self.x = lax.axis_index("tp")
        self.z = rank // self.lanes
        self.g = rank % self.lanes
        self.x_peer = (rank, 1 - self.x)
        self.z_peer = {
            d: (lax.rem(self.z + d, SPLIT) * self.lanes + self.g, self.x) for d in (1, 2, 3)
        }
        self.z_pair = self.at_z(self.z + 1 - 2 * lax.rem(self.z, 2))
        self.z_far = self.z_peer[2]
        self.y, self.c = self.g // 2, self.g % 2
        self.g_y = (1 - self.y) * 2 + self.c
        self.g_c = self.y * 2 + 1 - self.c
        self.g_yc = (1 - self.y) * 2 + 1 - self.c
        self.y_peer = (self.z * self.lanes + self.g_y, self.x)
        self.c_peer = (self.z * self.lanes + self.g_c, self.x)

    def z_from(self, d):
        return lax.rem(self.z + SPLIT - d, SPLIT)

    def z_to(self, d):
        return lax.rem(self.z + d, SPLIT)


    def block(self, i):
        middle = lax.div(self.z * (3 - self.z), 2)
        near = i + middle * (1 - 2 * i) * (1 - lax.div(i, 2))
        return near + lax.div(self.z, 2) * (3 - 2 * near)

    def at_z(self, z):
        return (z * self.lanes + self.g, self.x)


def remote(src, dst, send, recv, peer):
    return pltpu.make_async_remote_copy(
        src_ref=src, dst_ref=dst, send_sem=send, recv_sem=recv, device_id=peer, device_id_type=MESH
    )


def as_index(i):
    return jnp.int32(i) if isinstance(i, int) else i


class Gather:
    def __init__(self, place, buf, send, recv):
        self.place, self.buf, self.send, self.recv = place, buf, send, recv
        self.own = buf.at[place.z * 2 + place.x]

    def to_right(self, z):
        place = self.place
        block = self.buf.at[z * 2 + place.x]
        steps = place.z - z
        return remote(
            block, block, self.send.at[steps], self.recv.at[3 + steps], place.at_z(place.z + 1)
        )

    def to_left(self, z):
        place = self.place
        block = self.buf.at[z * 2 + place.x]
        steps = z - place.z
        return remote(
            block, block, self.send.at[3 + steps], self.recv.at[steps], place.at_z(place.z - 1)
        )

    def to_x(self, z):
        block = self.buf.at[z * 2 + self.place.x]
        return remote(
            block, block, self.send.at[6 + z], self.recv.at[6 + z], self.place.x_peer
        )

    def landed(self, z, index):
        block = self.buf.at[z * 2 + self.place.x]
        return remote(block, block, self.send.at[index], self.recv.at[index], self.place.x_peer)

    def start(self):
        place = self.place

        @pl.when(place.z < 3)
        def _():
            self.to_right(place.z).start()

        @pl.when(place.z > 0)
        def _():
            self.to_left(place.z).start()

        self.to_x(place.z).start()

    def pass_on(self, i):
        place = self.place
        z = place.block(as_index(i))

        @pl.when(z < place.z)
        def _():
            self.landed(z, 2 + place.z - z).wait_recv()

            @pl.when(place.z < 3)
            def _():
                self.to_right(z).start()

        @pl.when(z > place.z)
        def _():
            self.landed(z, z - place.z - 1).wait_recv()

            @pl.when(place.z > 0)
            def _():
                self.to_left(z).start()

        self.to_x(z).start()

    def arrive(self, i):
        z = self.place.block(as_index(i))
        block = self.buf.at[z * 2 + 1 - self.place.x]
        remote(
            block, block, self.send.at[6 + z], self.recv.at[6 + z], self.place.x_peer
        ).wait_recv()

    def finish(self):
        place = self.place
        for z in range(SPLIT):

            @pl.when((z <= place.z) & (place.z < 3))
            def _():
                self.to_right(z).wait_send()

            @pl.when((z >= place.z) & (place.z > 0))
            def _():
                self.to_left(z).wait_send()

            self.to_x(z).wait_send()


class Scatter:
    def __init__(self, place, part, from_x, from_z, send, recv):
        self.place, self.part, self.from_x = place, part, from_x
        self.from_z, self.send, self.recv = from_z, send, recv

    def across(self, z):
        return remote(
            self.part.at[z, 1 - self.place.x],
            self.from_x.at[z],
            self.send.at[z],
            self.recv.at[z],
            self.place.x_peer,
        )

    def along(self, z):
        return remote(
            self.part.at[z, self.place.x],
            self.from_z.at[self.place.z],
            self.send.at[4 + z],
            self.recv.at[4 + self.place.z],
            self.place.at_z(z),
        )

    def pass_on(self, z):
        self.across(z).wait_recv()
        own = self.part[z, self.place.x].astype(F32)
        self.part[z, self.place.x] = (own + self.from_x[z].astype(F32)).astype(BF)
        self.along(z).start()

    def finish(self):
        place = self.place
        self.across(place.z).wait_recv()
        total = self.part[place.z, place.x].astype(F32) + self.from_x[place.z].astype(F32)
        for d in (1, 2, 3):
            z = place.z_to(d)
            block = self.from_z.at[z]
            remote(
                block, block, self.send.at[4 + z], self.recv.at[4 + z], place.at_z(z)
            ).wait_recv()
            total = total + self.from_z[z].astype(F32)
        for z in range(SPLIT):
            self.across(z).wait_send()
        for d in (1, 2, 3):
            self.along(place.z_to(d)).wait_send()
        return total


def flow(place, gather, work, carry, between=None):
    def step(i, carry):
        @pl.when(i < 3)
        def _():
            gather.pass_on(i + 1)

        gather.arrive(i)
        if between is not None:
            between(i)
        return work(place.block(i), carry)

    return lax.fori_loop(0, SPLIT, step, carry)


def flow_and_sum(place, gather, scatter, work, before=None):
    def start(i):
        scatter.across(place.block(jnp.int32(i))).start()

    def pass_on(i):
        scatter.pass_on(place.block(jnp.int32(i)))

    def begin(i):
        if before is not None:
            pl.when(i == 0)(before)

        @pl.when(i == 3)
        def _():
            start(2)
            start(1)

    def step(z, carry):
        work(z, carry)
        return carry

    flow(place, gather, step, 0, begin)
    start(3)
    pass_on(2)
    start(0)
    pass_on(1)
    pass_on(3)


def work_and_sum(place, scatter, work, carry):
    def step(i, carry):
        z = place.block(3 - i)
        carry = work(z, carry)
        scatter.across(z).start()

        @pl.when(i >= 1)
        def _():
            scatter.pass_on(place.block(4 - i))

        return carry

    return lax.fori_loop(0, SPLIT, step, carry)


class LaneGather:
    def __init__(self, place, buf, send, recv):
        own = buf.at[place.g]
        self.own = own
        self.to_y = remote(own, own, send.at[0], recv.at[0], place.y_peer)
        self.to_c = remote(own, own, send.at[1], recv.at[1], place.c_peer)
        across = buf.at[place.g_y]
        self.from_y = remote(across, across, send.at[2], recv.at[0], place.c_peer)
        self.on = remote(across, across, send.at[2], recv.at[2], place.c_peer)
        pair = buf.at[place.g_c]
        self.from_c = remote(pair, pair, send.at[1], recv.at[1], place.c_peer)
        diagonal = buf.at[place.g_yc]
        self.from_diagonal = remote(diagonal, diagonal, send.at[2], recv.at[2], place.c_peer)

    def start(self):
        self.to_y.start()
        self.to_c.start()

    def pass_on(self):
        self.from_y.wait_recv()
        self.on.start()

    def finish(self):
        self.from_c.wait_recv()
        self.from_diagonal.wait_recv()
        self.sent()

    def sent(self):
        self.to_y.wait_send()
        self.to_c.wait_send()
        self.on.wait_send()


class WeightGather:
    def __init__(self, place, shards, buf, send, recv):
        self.place, self.shards, self.buf = place, shards, buf
        self.send, self.recv = send, recv
        self.keep = pltpu.make_async_copy(
            shards.at[place.z], buf.at[place.z * place.lanes + place.g], recv.at[place.z]
        )

    def copy(self, z, g, sent, landed, peer):
        block = self.buf.at[z * self.place.lanes + g]
        return remote(block, block, self.send.at[sent + z], self.recv.at[landed + z], peer)

    def along(self, z):
        place = self.place
        return remote(
            self.shards.at[z],
            self.buf.at[place.z * place.lanes + place.g],
            self.send.at[z],
            self.recv.at[place.z],
            place.at_z(z),
        )

    def to_y(self, z):
        return self.copy(z, self.place.g, 4, 4, self.place.y_peer)

    def to_c(self, z):
        return self.copy(z, self.place.g, 8, 8, self.place.c_peer)

    def on(self, z):
        return self.copy(z, self.place.g_y, 12, 12, self.place.c_peer)

    def start(self, i):
        self.along(self.place.block(as_index(i))).start()

    def pass_own(self):
        self.keep.start()
        self.keep.wait()
        self.to_y(self.place.z).start()
        self.to_c(self.place.z).start()

    def pass_z(self, i):
        z = self.place.block(as_index(i))
        self.copy(z, self.place.g, 0, 0, self.place.x_peer).wait_recv()
        self.to_y(z).start()
        self.to_c(z).start()

    def pass_y(self, i):
        z = self.place.block(as_index(i))
        self.copy(z, self.place.g_y, 12, 4, self.place.c_peer).wait_recv()
        self.on(z).start()

    def finish(self):
        place = self.place
        for z in range(SPLIT):
            self.copy(z, place.g_c, 8, 8, place.c_peer).wait_recv()
            self.copy(z, place.g_yc, 12, 12, place.c_peer).wait_recv()
        for d in (1, 2, 3):
            self.along(place.z_to(d)).wait_send()
        for z in range(SPLIT):
            self.to_y(z).wait_send()
            self.to_c(z).wait_send()
            self.on(z).wait_send()


class AllSum:
    def __init__(self, peers, acc, land, send, recv):
        self.acc, self.land = acc, land
        self.pairs = [
            remote(acc.at[i], land.at[i], send.at[i], recv.at[i], peer)
            for i, peer in enumerate(peers)
        ]

    def start(self):
        self.pairs[0].start()

    def step(self):
        pair, *rest = self.pairs
        pair.wait_recv()
        pair.wait_send()
        i = self.acc.shape[0] - len(self.pairs)
        total = self.acc[i] + self.land[i]
        self.pairs = rest
        if rest:
            self.acc[i + 1] = total
            rest[0].start()
        return total


class LaneScatter:
    def __init__(self, place, part, from_c, from_y, send, recv):
        self.part, self.from_c, self.from_y = part, from_c, from_y
        self.count = count = from_y.shape[0]
        self.base = (place.c * 2 + place.y) * count
        self.away = (place.c * 2 + 1 - place.y) * count
        self.base_c, self.away_c = place.y * count, (1 - place.y) * count
        self.to_c = remote(
            part.at[pl.ds((1 - place.c) * 2 * count, 2 * count)],
            from_c,
            send.at[0],
            recv.at[0],
            place.c_peer,
        )
        self.to_y = remote(
            part.at[pl.ds(self.away, count)], from_y, send.at[1], recv.at[1], place.y_peer
        )
        self.own = part.at[pl.ds(self.base, count)]

    def start(self):
        self.to_c.start()

    def step(self):
        self.to_c.wait_recv()

        def add(i, carry):
            at = self.away + i
            near = self.part[at].astype(F32) + self.from_c[self.away_c + i].astype(F32)
            self.part[at] = near.astype(BF)
            return carry

        lax.fori_loop(0, self.count, add, 0)
        self.to_y.start()

    def finish(self):
        self.to_y.wait_recv()
        self.to_c.wait_send()

        def add(i, carry):
            at = self.base + i
            near = self.part[at].astype(F32) + self.from_c[self.base_c + i].astype(F32)
            self.part[at] = (near + self.from_y[i].astype(F32)).astype(BF)
            return carry

        lax.fori_loop(0, self.count, add, 0)
        self.to_y.wait_send()


class TurnZ:
    def __init__(self, place, out, base, land, send, recv):
        self.keep = pltpu.make_async_copy(
            out.at[base + place.z], land.at[place.z], send.at[3]
        )
        self.sends = [
            remote(
                out.at[base + place.z_to(d)],
                land.at[place.z],
                send.at[i],
                recv.at[i],
                place.z_peer[d],
            )
            for i, d in enumerate(NEAR)
        ]
        self.landed = []
        for i, d in enumerate(NEAR):
            slot = land.at[place.z_from(d)]
            self.landed.append(remote(slot, slot, send.at[i], recv.at[i], place.z_peer[d]))

    def start(self):
        for copy in self.sends:
            copy.start()
        self.keep.start()

    def finish(self):
        for copy in self.landed:
            copy.wait_recv()
        for copy in self.sends:
            copy.wait_send()
        self.keep.wait()


class HomeByZ:
    def __init__(self, place, part, from_c, from_y, land, send, recv):
        self.place, self.part, self.from_c, self.from_y = place, part, from_c, from_y
        self.land, self.send, self.recv = land, send, recv

    def blocks(self, at):
        return self.part.at[at, :, pl.ds(0, self.from_y.shape[2])]

    def to_c(self, z):
        place = self.place
        return remote(
            self.blocks(pl.ds(z * 4 + (1 - place.c) * 2, 2)),
            self.from_c.at[pl.ds(z * 2, 2)],
            self.send.at[z],
            self.recv.at[z],
            place.c_peer,
        )

    def to_y(self, z):
        place = self.place
        return remote(
            self.blocks(z * 4 + place.c * 2 + 1 - place.y),
            self.from_y.at[z],
            self.send.at[4 + z],
            self.recv.at[4 + z],
            place.y_peer,
        )

    def to_z(self, z):
        place = self.place
        return remote(
            self.blocks(z * 4 + place.c * 2 + place.y),
            self.land.at[place.z],
            self.send.at[8 + z],
            self.recv.at[8 + place.z],
            place.at_z(z),
        )

    def keep(self):
        place = self.place
        return pltpu.make_async_copy(
            self.blocks(place.z * 4 + place.c * 2 + place.y),
            self.land.at[place.z],
            self.recv.at[8 + place.z],
        )

    def start(self, z):
        self.to_c(z).start()

    def step(self, z):
        self.to_c(z).wait_recv()
        place = self.place
        at = z * 4 + place.c * 2 + 1 - place.y
        near = self.blocks(at)[...].astype(F32) + self.from_c[z * 2 + 1 - place.y].astype(F32)
        self.blocks(at)[...] = near.astype(BF)
        self.to_y(z).start()

    def leave(self, z):
        place = self.place
        self.to_y(z).wait_recv()
        at = z * 4 + place.c * 2 + place.y
        near = self.blocks(at)[...].astype(F32) + self.from_c[z * 2 + place.y].astype(F32)
        self.blocks(at)[...] = (near + self.from_y[z].astype(F32)).astype(BF)

        @pl.when(z == place.z)
        def _():
            self.keep().start()

        @pl.when(z != place.z)
        def _():
            self.to_z(z).start()

    def finish(self):
        place = self.place
        self.keep().wait()
        for d in (1, 2, 3):
            z = place.z_to(d)
            block = self.land.at[z]
            remote(
                block, block, self.send.at[8 + z], self.recv.at[8 + z], place.at_z(z)
            ).wait_recv()
            self.to_z(z).wait_send()
        for z in range(SPLIT):
            self.to_c(z).wait_send()
            self.to_y(z).wait_send()


class SpreadZ:
    def __init__(self, place, buf, send, recv):
        own = buf.at[place.z]
        self.own = own
        self.sends = [
            remote(own, own, send.at[i], recv.at[i], place.z_peer[d]) for i, d in enumerate(NEAR)
        ]
        self.landed = []
        for i, d in enumerate(NEAR):
            slot = buf.at[place.z_from(d)]
            self.landed.append(remote(slot, slot, send.at[i], recv.at[i], place.z_peer[d]))

    def start(self):
        for copy in self.sends:
            copy.start()

    def finish(self):
        for copy in self.landed:
            copy.wait_recv()
        for copy in self.sends:
            copy.wait_send()


def item_rows(mod, items, index, width):
    first = mod[0:1, index * width : (index + 1) * width]
    second = mod[1:2, index * width : (index + 1) * width]
    return jnp.where(items == 0, first, second)


def item_sums(value, items):
    return [
        jnp.sum(jnp.where(items == item, value, 0.0), axis=0, keepdims=True)
        for item in range(ITEMS)
    ]


def segments(lanes):
    row = lax.broadcasted_iota(jnp.int32, (lanes, lanes), 0) // HEAD
    col = lax.broadcasted_iota(jnp.int32, (lanes, lanes), 1) // HEAD
    return jnp.where(row == col, 1.0 / HEAD, 0.0).astype(F32)


def head_mean(value, mean):
    return jnp.dot(value, mean, precision=HIGH, preferred_element_type=F32)


def swap_quarters(value):
    lanes = value.shape[1]
    lane = lax.broadcasted_iota(jnp.int32, value.shape, 1)
    even = (lane // (HEAD // 4)) % 2 == 0
    return jnp.where(
        even, pltpu.roll(value, lanes - HEAD // 4, 1), pltpu.roll(value, HEAD // 4, 1)
    )


def head_lanes(shape, head):
    lane = lax.broadcasted_iota(jnp.int32, shape, 1)
    return (lane >= head * HEAD) & (lane < (head + 1) * HEAD)


def of_head(value, head):
    return jnp.where(head_lanes(value.shape, head), value, jnp.zeros_like(value))


def gate_lanes(cross_gate, z, wq):
    heads = wq // HEAD
    lane = lax.broadcasted_iota(jnp.int32, (1, wq), 1) // HEAD
    gates = jnp.zeros((1, wq), F32)
    for head in range(heads):
        gates = jnp.where(lane == head, cross_gate[z * heads + head], gates)
    return gates


def lane_order(g):
    return (g % 2) * 2 + g // 2


def layer_kernel(names, *refs):
    r = SimpleNamespace(**dict(zip(names, refs)))
    place = Place()
    z, g, x = place.z, place.g, place.x
    tok_rows, width = r.patches.shape
    rows = tok_rows // 2
    wq, wf = r.w_query.shape[1] // SPLIT, r.w_gate.shape[1] // SPLIT
    two = 2 * wq
    heads = wq // HEAD
    group = SPLIT * tok_rows
    scale = 1.0 / math.sqrt(HEAD)
    peers = [place.x_peer, place.c_peer, place.y_peer] + [place.z_peer[d] for d in (1, 2, 3)]
    barrier = pltpu.get_barrier_semaphore()
    for peer in peers:
        pl.semaphore_signal(barrier, inc=1, device_id=peer, device_id_type=MESH)

    text_cols = pl.ds(pl.multiple_of((z * place.lanes + g) * r.text.shape[1], 128), r.text.shape[1])
    text_copy = pltpu.make_async_copy(r.caption.at[:, text_cols], r.text, r.text_sem)
    text_copy.start()
    for i in range(SPLIT):
        at = slice(i * wq, (i + 1) * wq)
        r.qkvo_in[i, :, 0:wq] = r.w_key[:, at]
        r.qkvo_in[i, :, wq:two] = r.w_query[:, at]
        r.qkvo_in[i, :, two : two + wq] = r.w_out[:, at]
        r.qkvo_in[i, :, two + wq : 2 * two] = r.w_value[:, at]
    pl.semaphore_wait(barrier, len(peers))

    pre, sig = conditioning(r.band_table, r.item_band)
    act = jnp.concatenate([pre * sig, jnp.zeros((6, pre.shape[1]), F32)], axis=0).astype(BF)
    r.m_acc[0] = bdot(act, r.w_ada[...])[:ITEMS]
    along = [place.c_peer, place.y_peer, place.z_pair, place.z_far]
    sums = AllSum(along, r.m_acc, r.m_land, r.m_send, r.m_recv)
    sums.start()
    weights = WeightGather(place, r.qkvo_in, r.qkvo, r.w_send, r.w_recv)
    weights.start(1)
    mine = pl.ds(pl.multiple_of(x * rows, rows), rows)
    tokens = Gather(place, r.x_buf, r.x_send, r.x_recv)
    tokens.own[...] = r.patches[mine]
    tokens.start()
    for i in (2, 3):
        weights.start(i)
    spots = SpreadZ(place, r.pos_buf, r.pos_send, r.pos_recv)
    spots.own[...] = jnp.concatenate(
        [r.positions[...].astype(F32), jnp.zeros((6, tok_rows), F32)], axis=0
    )
    spots.start()
    weights.pass_own()
    sums.step()
    text_copy.wait()
    words = r.cap_part.shape[1]
    caption = LaneScatter(place, r.cap_part, r.cap_fc, r.cap_fy, r.cap_s, r.cap_r)
    for kind, matrix in enumerate((r.w_ckey, r.w_cvalue)):
        full = bdot(r.text[...], matrix[...]).astype(BF)
        for i in range(SPLIT):
            for lane_g in range(4):
                block = lane_order(lane_g) * SPLIT + i
                r.cap_part[block, :, kind * wq : (kind + 1) * wq] = full[
                    lane_g * words : (lane_g + 1) * words, i * wq : (i + 1) * wq
                ]
    caption.start()
    tokens.pass_on(1)
    weights.pass_z(1)
    sums.step()

    blocks = tok_rows // BLK
    token = lax.broadcasted_iota(jnp.int32, (group, 1), 0) // BLK
    key = lax.broadcasted_iota(jnp.int32, (1, 4 * group), 1) // BLK
    token_item = jnp.zeros((group, 1), jnp.int32)
    key_item = jnp.zeros((1, 4 * group), jnp.int32)
    for i in range(SPLIT):
        for j in range(blocks):
            own = r.block_item[(i * place.lanes + g) * blocks + j]
            token_item = jnp.where(token == i * blocks + j, own, token_item)
            for other in range(4):
                value = r.block_item[(i * place.lanes + other) * blocks + j]
                key_item = jnp.where(key == (other * SPLIT + i) * blocks + j, value, key_item)
    r.items[...] = token_item
    for i in range(4):
        r.key_items[i] = key_item[:, i * group : (i + 1) * group]
        column = jnp.zeros((group, 1), jnp.int32)
        for j in range(SPLIT * blocks):
            value = r.block_item[(j // blocks * place.lanes + i) * blocks + j % blocks]
            column = jnp.where(token == j, value, column)
        r.key_cols[i] = column
    for i in range(SPLIT):
        at = slice(i * wf, (i + 1) * wf)
        r.ffn_in[i, :, 0:wf] = r.w_gate[:, at]
        r.ffn_in[i, :, wf : 2 * wf] = r.w_up[:, at]
        r.ffn_in[i, :, 2 * wf : 3 * wf] = r.w_down[:, at]
    tokens.pass_on(2)
    weights.pass_z(2)
    sums.step()

    own_at = pl.ds(pl.multiple_of(z * tok_rows + x * rows, rows), rows)

    mean = segments(two)
    mean_q = segments(wq)
    lane = lax.broadcasted_iota(jnp.int32, (1, two), 1)
    gain_in, gain_attn, gain_ffn, gain_out = (
        ref[...].reshape(1, width) for ref in (r.g_attn_in, r.g_attn_out, r.g_ffn_in, r.g_ffn_out)
    )

    def own_heads(ref):
        whole = ref[...].reshape(1, SPLIT * wq)
        part = whole[:, 0:wq]
        for i in range(1, SPLIT):
            part = jnp.where(z == i, whole[:, i * wq : (i + 1) * wq], part)
        return part

    gain_kq = jnp.concatenate([own_heads(r.g_key), own_heads(r.g_query)], axis=1)
    gain_ckey = own_heads(r.g_ckey)
    gain_ckey = jnp.concatenate([gain_ckey, jnp.zeros_like(gain_ckey)], axis=1)
    gates = jnp.tanh(gate_lanes(r.cross_gate, z, wq))
    lane_row = lax.broadcasted_iota(jnp.int32, (1, 2 * HEAD), 1)
    quarter = HEAD // 4
    freqs = jnp.ones((1, 2 * HEAD), F32)
    for i in range(1, quarter):
        freqs = jnp.where(lane_row % quarter == i, FREQ_BASE ** (-i / quarter), freqs)

    spots.finish()
    by_row = (lane_row // (HEAD // 2)) % 2 == 0
    sign = jnp.where((lane_row // (HEAD // 4)) % 2 == 0, -1.0, 1.0)
    for i in range(SPLIT):
        cols = r.pos_buf[i].T
        angle = jnp.where(by_row, cols[:, 0:1], cols[:, 1:2]) * freqs
        r.cos_t[i] = jnp.cos(angle)
        r.sin_t[i] = jnp.sin(angle) * sign

    tokens.pass_on(3)
    weights.pass_z(3)
    feed = WeightGather(place, r.ffn_in, r.ffn, r.f_send, r.f_recv)
    for i in (1, 2, 3):
        feed.start(i)
    for i in range(4):
        weights.pass_y(i)
    r.mod[...] = sums.step() + r.b_ada[...].reshape(1, 4 * width)
    for i in range(4):
        tokens.arrive(i)
    caption.step()
    weights.finish()
    feed.pass_own()

    keep = LaneGather(place, r.kv, r.kv_send, r.kv_recv)

    def span(i):
        return pl.ds(pl.multiple_of(i * tok_rows, tok_rows), tok_rows)

    def w_kq():
        return r.qkvo[:, :, 0:two].reshape(width, two)

    def w_ov():
        return r.qkvo[:, :, two : 2 * two].reshape(width, two)

    def project(i, carry):
        block = r.x_buf[pl.ds(i * 2, 2)].reshape(tok_rows, width).astype(F32)
        unit, _ = normed_pair(block)
        factor = gain_in * (1.0 + item_rows(r.mod, r.items[span(i)], 0, width))
        norm = (unit * factor).astype(BF)
        r.norm_in[i] = norm
        r.hat_in[i] = unit.astype(BF)
        raw = bdot(norm, w_kq())
        own_v = bdot(norm, w_ov())
        recip = lax.rsqrt(head_mean(raw * raw, mean) + EPS)
        hat = raw * recip
        r.kq_hat[i] = hat
        r.kq_recip[i] = recip
        cos = jnp.concatenate([r.cos_t[i]] * heads, axis=1)
        sin = jnp.concatenate([r.sin_t[i]] * heads, axis=1)
        gained = hat * gain_kq
        turned = gained * cos + swap_quarters(gained) * sin
        r.kv[g, span(i)] = jnp.where(lane < wq, turned, own_v).astype(BF)
        r.queries[span(i)] = (turned[:, wq:].astype(BF).astype(F32) * scale).astype(BF)
        return carry

    lax.fori_loop(0, SPLIT, project, 0)
    keep.start()

    caption.finish()
    cap_turn = TurnZ(place, r.cap_part, caption.base, r.cap_z, r.cz_send, r.cz_recv)
    cap_turn.start()
    slot_lane = lax.broadcasted_iota(jnp.int32, (1, r.totals.shape[1]), 1)
    ones = jnp.where(lax.broadcasted_iota(jnp.int32, (1, HEAD), 1) == 0, 1.0, 0.0).astype(BF)

    def with_ones(values):
        return jnp.concatenate([values, jnp.broadcast_to(ones, (values.shape[0], HEAD))], axis=1)

    def split_lump(index):
        lump = r.kv[index]
        r.k_all[index] = lump[:, :wq]
        r.v_all[index] = with_ones(lump[:, wq:])

    def attend(head, keys, values, same):
        scores = dot_t(of_head(r.queries[...], head), keys)
        if same is not None:
            scores = jnp.where(same, scores, NEG)
        out = bdot(jnp.exp(scores).astype(BF), values)
        return of_head(out[:, :wq], head), jnp.where(slot_lane == head, out[:, wq : wq + 1], 0.0)

    def cross(head, carry):
        out, total = attend(head, r.cap_k[...], r.cap_v[...], None)
        r.attn_cross[...] += out
        r.cross_logs[...] += total
        return carry

    def attend_into(index):
        def step(head, carry):
            same = r.items[...] == r.key_items[index]
            out, total = attend(head, r.k_all[index], r.v_all[index], same)
            r.attn_self[...] += out
            r.totals[...] += total
            return carry

        lax.fori_loop(0, heads, step, 0)

    for ref in (r.attn_self, r.attn_cross, r.totals, r.cross_logs):
        ref[...] = jnp.zeros_like(ref)
    split_lump(g)
    attend_into(g)
    cap_turn.finish()
    cap_raw = (r.cap_z[0].astype(F32) + r.cap_z[1].astype(F32)) + (
        r.cap_z[2].astype(F32) + r.cap_z[3].astype(F32)
    )
    cap_recip = lax.rsqrt(head_mean(cap_raw * cap_raw, mean) + EPS)
    cap_hat = cap_raw * cap_recip
    r.cap_hat[...] = cap_hat
    r.cap_recip[...] = cap_recip
    cap_gather = LaneGather(place, r.cap_kv, r.ckv_send, r.ckv_recv)
    cap_gather.own[...] = jnp.where(lane < wq, cap_hat * gain_ckey, cap_raw).astype(BF)
    cap_gather.start()
    keep.from_c.wait_recv()
    split_lump(place.g_c)
    attend_into(place.g_c)
    cap_gather.pass_on()
    keep.pass_on()
    feed.pass_z(1)
    split_lump(place.g_y)
    attend_into(place.g_y)
    feed.pass_z(2)
    feed.pass_y(0)
    cap_gather.finish()
    kv_text = r.cap_kv[...].reshape(4 * words, two)
    r.cap_k[...] = kv_text[:, :wq]
    r.cap_v[...] = with_ones(kv_text[:, wq:])
    lax.fori_loop(0, heads, cross, 0)
    feed.pass_z(3)
    feed.pass_y(1)
    keep.from_diagonal.wait_recv()
    split_lump(place.g_yc)
    attend_into(place.g_yc)

    def by_total(out, totals):
        shares = jnp.zeros_like(out)
        for head in range(heads):
            share = 1.0 / totals[:, head : head + 1]
            shares = shares + of_head(jnp.broadcast_to(share, out.shape), head)
        return out * shares

    def blend(i, carry):
        at = span(i)
        self_part = by_total(r.attn_self[at], r.totals[at])
        cross_part = by_total(r.attn_cross[at], r.cross_logs[at])
        r.attn_self[at] = self_part
        r.attn_cross[at] = cross_part
        r.totals[at] = jnp.log(r.totals[at])
        r.cross_logs[at] = jnp.log(r.cross_logs[at])
        mixed = (self_part + gates * cross_part).astype(BF)
        wide = jnp.concatenate([mixed, jnp.zeros_like(mixed)], axis=1)
        r.mix_s[at] = wide
        r.part[i] = dot_t(wide, w_ov()).astype(BF).reshape(2, rows, width)
        return carry

    def scatter_of(send, recv):
        return Scatter(place, r.part, r.from_x, r.from_z, send, recv)

    out_sum = scatter_of(r.s1, r.r1)
    work_and_sum(place, out_sum, blend, 0)
    for i in (2, 3):
        feed.pass_y(i)
    branch = out_sum.finish()

    item = r.items[own_at]
    hat_two, recip_two = normed_pair(branch)
    tanh_one = jnp.tanh(item_rows(r.mod, item, 1, width))
    resid = r.patches[mine].astype(F32) + tanh_one * hat_two * gain_attn
    hat_three, recip_three = normed_pair(resid)
    factor_three = gain_ffn * (1.0 + item_rows(r.mod, item, 2, width))
    norms = Gather(place, r.n_buf, r.n_send, r.n_recv)
    norms.own[...] = (hat_three * factor_three).astype(BF)
    norms.start()
    tokens.finish()
    keep.sent()

    def f_weights(index):
        return r.ffn[:, :, index * wf : (index + 1) * wf].reshape(width, wf)

    def forward(i, carry):
        block = r.n_buf[pl.ds(i * 2, 2)].reshape(tok_rows, width)
        gate_val = bdot(block, f_weights(0))
        up_val = bdot(block, f_weights(1))
        r.gate_s[i] = gate_val
        r.up_s[i] = up_val
        hidden = (gate_val * jax.nn.sigmoid(gate_val) * up_val).astype(BF)
        r.hid_s[i] = hidden
        r.part[i] = dot_t(hidden, f_weights(2)).astype(BF).reshape(2, rows, width)
        return carry

    down = scatter_of(r.s2, r.r2)
    flow_and_sum(place, norms, down, forward, feed.finish)
    ffn = down.finish()
    norms.finish()

    hat_four, recip_four = normed_pair(ffn)
    tanh_two = jnp.tanh(item_rows(r.mod, item, 3, width))
    grad_out = r.out_grad[mine].astype(F32)
    grad_four = grad_out * tanh_two
    grads = Gather(place, r.g_buf, r.g_send, r.g_recv)
    grads.own[...] = normed_back(grad_four * gain_out, hat_four, recip_four).astype(BF)
    grads.start()
    output = resid + tanh_two * hat_four * gain_out
    r.out_own[...] = output
    r.out_half[0] = output.astype(BF)
    out_copy = remote(r.out_half.at[0], r.out_half.at[1], r.o_send, r.o_recv, place.x_peer)
    out_copy.start()
    everywhere = along[:2] + [place.x_peer] + along[2:]
    early = AllSum(everywhere, r.e_acc, r.e_land, r.e_send, r.e_recv)
    r.e_acc[0] = jnp.zeros(r.e_acc.shape[1:], F32)
    gate_sums = item_sums(grad_out * hat_four * gain_out * (1.0 - tanh_two * tanh_two), item)
    r.e_acc[0, 2:3] = jnp.sum(grad_four * hat_four, axis=0, keepdims=True)
    r.e_acc[0, 8:9] = gate_sums[0]
    r.e_acc[0, 9:10] = gate_sums[1]

    def backward(i, carry):
        block = r.g_buf[pl.ds(i * 2, 2)].reshape(tok_rows, width)
        grad_hidden = bdot(block, f_weights(2))
        gate_val = r.gate_s[i]
        gate_sig = jax.nn.sigmoid(gate_val)
        grad_gate = (
            grad_hidden * r.up_s[i] * gate_sig * (1.0 + gate_val * (1.0 - gate_sig))
        ).astype(BF)
        grad_up = (grad_hidden * gate_val * gate_sig).astype(BF)
        r.gg_s[i] = grad_gate
        r.gu_s[i] = grad_up
        r.part[i] = (
            (dot_t(grad_gate, f_weights(0)) + dot_t(grad_up, f_weights(1)))
            .astype(BF)
            .reshape(2, rows, width)
        )
        return carry

    back = scatter_of(r.s3, r.r3)
    flow_and_sum(place, grads, back, backward)

    block_rows = r.ffn.shape[1]
    step_cols = 4 * block_rows

    f_home = HomeByZ(place, r.ffn, r.f_fc, r.f_fy, r.f_land, r.f_s, r.f_r)

    def ffn_matrices(i, carry):
        target = place.block(3 - i)
        cols = pl.ds(pl.multiple_of(target * step_cols, step_cols), step_cols)
        norm = r.n_buf[:, :, cols].reshape(group, step_cols)
        grad = r.g_buf[:, :, cols].reshape(group, step_cols)
        for j, (left, right) in enumerate(((norm, r.gg_s), (norm, r.gu_s), (grad, r.hid_s))):
            block = t_dot(left, right[...].reshape(group, wf)).astype(BF)
            block = block.reshape(4, block_rows, wf)
            for other in range(4):
                at = target * 4 + lane_order(other)
                r.ffn[at, :, j * wf : (j + 1) * wf] = block[other]
        f_home.start(target)
        return carry

    lax.fori_loop(0, SPLIT, ffn_matrices, 0)
    f_home.step(place.block(jnp.int32(3)))
    f_home.step(place.block(jnp.int32(2)))
    grad_norm = back.finish()
    grads.finish()
    d_resid = grad_out + normed_back(grad_norm * factor_three, hat_three, recip_three)
    grad_two = d_resid * tanh_one
    attn_grads = Gather(place, r.x_buf, r.a_send, r.a_recv)
    attn_grads.own[...] = normed_back(grad_two * gain_attn, hat_two, recip_two).astype(BF)
    attn_grads.start()
    r.dp_own[...] = d_resid
    scale_sums = item_sums(grad_norm * hat_three * gain_ffn, item)
    gate_sums = item_sums(d_resid * hat_two * gain_attn * (1.0 - tanh_one * tanh_one), item)
    r.e_acc[0, 0:1] = jnp.sum(grad_two * hat_two, axis=0, keepdims=True)
    r.e_acc[0, 1:2] = jnp.sum(
        grad_norm * hat_three * (1.0 + item_rows(r.mod, item, 2, width)), axis=0, keepdims=True
    )
    r.e_acc[0, 4:5] = gate_sums[0]
    r.e_acc[0, 5:6] = gate_sums[1]
    r.e_acc[0, 6:7] = scale_sums[0]
    r.e_acc[0, 7:8] = scale_sums[1]
    early.start()

    r.dk_acc[...] = jnp.zeros_like(r.dk_acc)
    r.dv_acc[...] = jnp.zeros_like(r.dv_acc)
    r.dck_acc[...] = jnp.zeros_like(r.dck_acc)
    r.dcv_acc[...] = jnp.zeros_like(r.dcv_acc)

    def attend_back(i, gate_sum):
        at = span(i)
        block = r.x_buf[pl.ds(i * 2, 2)].reshape(tok_rows, width)
        d_mix = bdot(block, w_ov())[:, :wq].astype(BF)
        mix_f = d_mix.astype(F32)
        d_cross = (gates * mix_f).astype(BF)
        delta = head_mean(mix_f * r.attn_self[at], mean_q) * HEAD
        gate_sum = gate_sum + jnp.sum(mix_f * r.attn_cross[at], axis=0, keepdims=True)
        query = r.queries[at]
        per_row = jnp.zeros((tok_rows, 128), F32)
        for head in range(heads):
            stack = slice(head * tok_rows, (head + 1) * tok_rows)
            r.q_stack[stack] = of_head(query, head)
            r.c_stack[stack] = of_head(d_cross, head)
            r.m_stack[stack] = of_head(d_mix, head)
            for part, column in enumerate(
                (
                    r.totals[at][:, head : head + 1],
                    delta[:, head * HEAD : head * HEAD + 1],
                    r.cross_logs[at][:, head : head + 1],
                )
            ):
                per_row = per_row + jnp.where(slot_lane == part * heads + head, column, 0.0)
        per_row = per_row.T
        logs, deltas, cross_logs = (
            jnp.concatenate(
                [per_row[part * heads + head : part * heads + head + 1] for head in range(heads)],
                axis=1,
            )
            for part in range(3)
        )
        item_row = jnp.concatenate(
            [r.key_items[g, :, pl.ds(pl.multiple_of(i * tok_rows, 128), tok_rows)]] * heads, axis=1
        )
        query_s, cross_s, mix_s = r.q_stack[...], r.c_stack[...], r.m_stack[...]
        probs = jnp.exp(dot_t(r.cap_k[...], query_s) - cross_logs)
        d_probs = dot_t(r.cap_v[:, :wq], cross_s)
        inner = jnp.sum(probs * d_probs, axis=0, keepdims=True)
        d_scores = (probs * (d_probs - inner)).astype(BF)
        r.dck_acc[...] += bdot(d_scores, query_s)
        r.dcv_acc[...] += bdot(probs.astype(BF), cross_s)
        r.dq_stack[...] = t_dot(d_scores, r.cap_k[...])

        def keys(j, carry):
            same = r.key_cols[j] == item_row
            scores = jnp.where(same, dot_t(r.k_all[j], query_s), NEG)
            probs = jnp.exp(scores - logs)
            d_probs = dot_t(r.v_all[j, :, :wq], mix_s)
            d_scores = (probs * (d_probs - deltas)).astype(BF)
            r.dk_acc[j] += bdot(d_scores, query_s)
            r.dv_acc[j] += bdot(probs.astype(BF), mix_s)
            r.dq_stack[...] += t_dot(d_scores, r.k_all[j])
            return carry

        lax.fori_loop(0, 4, keys, 0)
        dq = jnp.zeros((tok_rows, wq), F32)
        for head in range(heads):
            stack = slice(head * tok_rows, (head + 1) * tok_rows)
            dq = dq + of_head(r.dq_stack[stack], head)
        r.dq_s[at] = (dq * scale).astype(BF)
        return gate_sum

    def ffn_home(i):
        for step in range(4):

            @pl.when(i == step)
            def _():
                early.step()

        @pl.when(i < 2)
        def _():
            f_home.step(place.block(1 - i))

        @pl.when(i >= 1)
        def _():
            f_home.leave(place.block(4 - i))

    gate_sum = flow(place, attn_grads, attend_back, jnp.zeros((1, wq), F32), ffn_home)
    keys_home = LaneScatter(place, r.kv, r.kv_fc, r.kv_fy, r.kvh_s, r.kvh_r)

    def store_keys(i, carry):
        lane_c, lane_y = lax.rem(place.c + 1 + lax.div(i, 2), 2), lax.rem(i, 2)
        both = [r.dk_acc[lane_y * 2 + lane_c], r.dv_acc[lane_y * 2 + lane_c]]
        r.kv[lane_c * 2 + lane_y] = jnp.concatenate(both, axis=1).astype(BF)

        @pl.when(i == 1)
        def _():
            keys_home.start()

        return carry

    lax.fori_loop(0, 4, store_keys, 0)
    cap_home = LaneScatter(place, r.t_part, r.t_fc, r.t_fy, r.t_s, r.t_r)
    for i in range(4):
        at = slice(i * words, (i + 1) * words)
        d_cap = jnp.concatenate([r.dck_acc[at], r.dcv_acc[at]], axis=1)
        r.t_part[lane_order(i)] = d_cap.astype(BF)
    cap_home.start()

    key_lanes = lane < wq

    def turn_back(i, grad):
        cos = jnp.concatenate([r.cos_t[i]] * heads, axis=1)
        sin = jnp.concatenate([r.sin_t[i]] * heads, axis=1)
        d_norm = grad * cos - swap_quarters(grad) * sin
        hat = r.kq_hat[i]
        gain_sum = jnp.sum(d_norm * hat, axis=0, keepdims=True)
        d_hat = d_norm * gain_kq
        grad = (r.kq_recip[i] * (d_hat - hat * head_mean(d_hat * hat, mean))).astype(BF)
        return grad, gain_sum

    def raw_queries(i, query_sum):
        d_query = r.dq_s[span(i)].astype(F32)
        d_query = jnp.concatenate([jnp.zeros_like(d_query), d_query], axis=1)
        grad, gain_sum = turn_back(i, d_query)
        r.dq_raw[span(i)] = grad
        return query_sum + gain_sum

    query_sum = lax.fori_loop(0, SPLIT, raw_queries, jnp.zeros((1, two), F32))
    keys_home.step()
    f_home.leave(place.block(jnp.int32(0)))

    def store_part(home, target, block):
        block = block.astype(BF).reshape(4, block_rows, two)
        for other in range(4):
            home.blocks(target * 4 + lane_order(other))[...] = block[other]
        home.start(target)

    a_home = HomeByZ(place, r.a_part, r.a_fc, r.a_fy, r.a_land, r.a_s, r.a_r)
    b_home = HomeByZ(place, r.qkvo, r.b_fc, r.b_fy, r.b_land, r.b_s, r.b_r)

    def matrices_oq(i, carry):
        target = place.block(3 - i)
        cols = pl.ds(pl.multiple_of(target * step_cols, step_cols), step_cols)
        above = r.x_buf[:, :, cols].reshape(group, step_cols)
        left = r.norm_in[:, :, cols].reshape(group, step_cols)
        store_part(a_home, target, t_dot(above, r.mix_s[...]) + t_dot(left, r.dq_raw[...]))
        return carry

    lax.fori_loop(0, SPLIT, matrices_oq, 0)
    cap_home.step()
    keys_home.finish()

    def raw_keys(i, carry):
        key_sum, first, second = carry
        total = r.kv[keys_home.base, span(i)].astype(F32)
        grad, gain_sum = turn_back(i, jnp.where(key_lanes, total, 0.0))
        r.dkv_raw[span(i)] = jnp.where(key_lanes, grad.astype(F32), total).astype(BF)
        d_kq = jnp.where(key_lanes, grad.astype(F32), r.dq_raw[span(i)].astype(F32)).astype(BF)
        d_ov = jnp.where(key_lanes, 0.0, total).astype(BF)
        d_norm = dot_t(d_kq, w_kq()) + dot_t(d_ov, w_ov())
        r.part[i] = d_norm.astype(BF).reshape(2, rows, width)
        by_item = item_sums(d_norm * r.hat_in[i].astype(F32), r.items[span(i)])
        return key_sum + gain_sum, first + by_item[0], second + by_item[1]

    in_sum = scatter_of(r.s4, r.r4)
    zeros = jnp.zeros((1, width), F32)
    key_sum, *item_parts = work_and_sum(
        place, in_sum, raw_keys, (jnp.zeros((1, two), F32), zeros, zeros)
    )
    late = AllSum(everywhere, r.l_acc, r.l_land, r.l_send, r.l_recv)
    r.l_acc[0] = jnp.concatenate(item_parts, axis=0)
    late.start()

    cap_home.finish()
    d_cap = r.t_part[cap_home.base].astype(F32)
    hat = r.cap_hat[...]
    cap_sum = jnp.sum(jnp.where(key_lanes, d_cap * hat, 0.0), axis=0, keepdims=True)
    d_hat = d_cap * jnp.where(key_lanes, gain_ckey, 0.0)
    d_raw = r.cap_recip[...] * (d_hat - hat * head_mean(d_hat * hat, mean))
    cap_spread = SpreadZ(place, r.t_z, r.tz_s, r.tz_r)
    cap_spread.own[...] = jnp.where(key_lanes, d_raw, d_cap).astype(BF)
    cap_spread.start()
    for i in range(4):
        a_home.step(place.block(jnp.int32(3 - i)))

    def matrices_kv(i, carry):
        target = place.block(3 - i)
        cols = pl.ds(pl.multiple_of(target * step_cols, step_cols), step_cols)
        left = r.norm_in[:, :, cols].reshape(group, step_cols)
        store_part(b_home, target, t_dot(left, r.dkv_raw[...]))
        return carry

    lax.fori_loop(0, SPLIT, matrices_kv, 0)
    heads_sum = AllSum(along[:2], r.h_acc, r.h_land, r.h_send, r.h_recv)
    r.h_acc[0] = jnp.zeros(r.h_acc.shape[1:], F32)
    r.h_acc[0, 0:1] = jnp.where(key_lanes, key_sum, query_sum)
    r.h_acc[0, 1:2] = cap_sum
    r.h_acc[0, 2:3] = jnp.concatenate([gate_sum, jnp.zeros_like(gate_sum)], axis=1)
    heads_sum.start()
    late.step()
    for i in range(4):
        b_home.step(place.block(jnp.int32(3 - i)))
    late.step()
    for i in range(4):
        a_home.leave(place.block(jnp.int32(3 - i)))

    d_norm = in_sum.finish()
    hat, recip = normed_pair(r.patches[mine].astype(F32))
    factor = 1.0 + item_rows(r.mod, item, 0, width)
    d_patches = r.dp_own[...] + normed_back(d_norm * gain_in * factor, hat, recip)
    r.dp_own[...] = d_patches
    r.dp_half[0] = d_patches.astype(BF)
    dp_copy = remote(r.dp_half.at[0], r.dp_half.at[1], r.dp_send, r.dp_recv, place.x_peer)
    dp_copy.start()
    late.step()
    heads_sum.step()
    for i in range(4):
        b_home.leave(place.block(jnp.int32(3 - i)))
    late.step()
    cap_spread.finish()
    cap_all = LaneGather(place, r.t_all, r.ta_s, r.ta_r)
    cap_all.own[...] = r.t_z[...]
    cap_all.start()
    heads_spread = SpreadZ(place, r.h_slots, r.hz_send, r.hz_recv)
    heads_spread.own[...] = heads_sum.step()
    heads_spread.start()
    total = late.step()
    cap_all.pass_on()
    factors = 1.0 + r.mod[:, 0:width]
    r.late[...] = jnp.concatenate(
        [
            jnp.sum(total * factors, axis=0, keepdims=True),
            total * gain_in,
            jnp.zeros((5, width), F32),
        ],
        axis=0,
    )
    out_copy.wait()
    attn_grads.finish()
    r.early[...] = early.step()
    heads_spread.finish()
    f_home.finish()
    a_home.finish()
    cap_all.finish()
    dp_copy.wait()
    b_home.finish()


def finish_kernel(
    out_own, out_half, dp_own, dp_half, f_land, a_land, b_land, t_all, early, late, heads_in, text,
    cross_gate, band_table, item_band, w_ada,
    output, d_patches, d_query, d_key, d_value, d_out, d_gate, d_up, d_down, d_ckey, d_cvalue,
    d_ada, d_b_ada, d_attn_in, d_attn_out, d_ffn_in, d_ffn_out, d_g_query, d_g_key, d_g_ckey,
    d_cross, d_band,
):
    x = lax.axis_index("tp")
    rows, width = out_own.shape
    wf = f_land.shape[2] // 3
    wq = a_land.shape[2] // 2
    words = t_all.shape[2]
    mine = pl.ds(pl.multiple_of(x * rows, rows), rows)
    other = pl.ds(pl.multiple_of((1 - x) * rows, rows), rows)
    output[mine] = out_own[...]
    output[other] = out_half[1].astype(F32)
    d_patches[mine] = dp_own[...]
    d_patches[other] = dp_half[1].astype(F32)
    for z in range(SPLIT):
        at = slice(z * wf, (z + 1) * wf)
        d_gate[:, at] = f_land[z, :, 0:wf].astype(F32)
        d_up[:, at] = f_land[z, :, wf : 2 * wf].astype(F32)
        d_down[:, at] = f_land[z, :, 2 * wf : 3 * wf].astype(F32)
        at = slice(z * wq, (z + 1) * wq)
        d_out[:, at] = a_land[z, :, 0:wq].astype(F32)
        d_query[:, at] = a_land[z, :, wq : 2 * wq].astype(F32)
        d_key[:, at] = b_land[z, :, 0:wq].astype(F32)
        d_value[:, at] = b_land[z, :, wq : 2 * wq].astype(F32)
        d_cap = t_dot(text[...], t_all[:, z].reshape(4 * words, 2 * wq))
        d_ckey[:, at] = d_cap[:, :wq]
        d_cvalue[:, at] = d_cap[:, wq:]
    grad_mod = jnp.concatenate([late[1:3], early[4:6], early[6:8], early[8:10]], axis=1)
    pre, sig = conditioning(band_table, item_band)
    low = (pre * sig).astype(BF).astype(F32)
    cols = jnp.concatenate([low, jnp.zeros((6, low.shape[1]), F32)], axis=0).T
    d_ada[...] = cols[:, 0:1] * grad_mod[0:1] + cols[:, 1:2] * grad_mod[1:2]
    d_act = lax.dot_general(
        grad_mod,
        w_ada[...].astype(F32),
        (((1,), (1,)), ((), ())),
        precision=HIGH,
        preferred_element_type=F32,
    )
    d_pre = d_act * sig * (1.0 + pre * (1.0 - sig))
    band = lax.broadcasted_iota(jnp.int32, (BANDS, 1), 0)
    d_band[...] = sum(
        jnp.where(band == item_band[i], d_pre[i : i + 1], 0.0) for i in range(ITEMS)
    )
    d_b_ada[...] = (grad_mod[0:1] + grad_mod[1:2]).reshape(d_b_ada.shape)
    d_attn_in[...] = late[0:1].reshape(d_attn_in.shape)
    d_attn_out[...] = early[0:1].reshape(d_attn_out.shape)
    d_ffn_in[...] = early[1:2].reshape(d_ffn_in.shape)
    d_ffn_out[...] = early[2:3].reshape(d_ffn_out.shape)

    def joined(row, part):
        return jnp.concatenate(
            [heads_in[z, row : row + 1, part * wq : (part + 1) * wq] for z in range(SPLIT)], axis=1
        ).reshape(d_g_key.shape)

    d_g_key[...] = joined(0, 0)
    d_g_query[...] = joined(0, 1)
    d_g_ckey[...] = joined(1, 0)
    heads = wq // HEAD
    lane = lax.broadcasted_iota(jnp.int32, (wq, 128), 0) // HEAD
    col = lax.broadcasted_iota(jnp.int32, (wq, 128), 1)
    total = jnp.zeros((8, 128), F32)
    for z in range(SPLIT):
        gate = jnp.tanh(gate_lanes(cross_gate, z, wq))
        terms = heads_in[z, 2:3, :wq] * (1.0 - gate * gate)
        terms = jnp.concatenate([terms, jnp.zeros((7, wq), F32)], axis=0)
        pick = jnp.where(col == lane + z * heads, 1.0, 0.0)
        total = total + jnp.dot(terms, pick, precision=HIGH, preferred_element_type=F32)
    d_cross[...] = total[0:1, : d_cross.shape[0]].reshape(d_cross.shape)


def conditioning(band_table, item_band):
    band = lax.broadcasted_iota(jnp.int32, (BANDS, 1), 0)
    table = band_table[...]
    pre = jnp.concatenate(
        [
            jnp.sum(jnp.where(band == item_band[i], table, 0.0), axis=0, keepdims=True)
            for i in range(ITEMS)
        ],
        axis=0,
    )
    return pre, jax.nn.sigmoid(pre)


def layer_call(ins):
    tok_rows, width = ins["patches"].shape
    rows = tok_rows // 2
    row_dev, q_cols = ins["w_query"].shape
    wq, wf = q_cols // SPLIT, ins["w_gate"].shape[1] // SPLIT
    two = 2 * wq
    heads = wq // HEAD
    lanes = 4
    group = SPLIT * tok_rows
    text, features = ins["caption"].shape
    words = text // lanes
    feat_dev = ins["w_ckey"].shape[0]
    mod = (ITEMS, 4 * width)
    tile, sem = pltpu.VMEM, lambda count: pltpu.SemaphoreType.DMA((count,))
    cap = (words, two)
    shard = (SPLIT, row_dev)
    both, half = (SPLIT, tok_rows), (rows, width)

    def sum_tile(size, steps):
        return tile((steps,) + size, F32)

    scratch = dict(
        text_sem=pltpu.SemaphoreType.DMA,
        qkvo_in=tile(shard + (2 * two,), BF),
        ffn_in=tile(shard + (3 * wf,), BF),
        qkvo=tile((SPLIT * lanes, row_dev, 2 * two), BF),
        ffn=tile((SPLIT * lanes, row_dev, 3 * wf), BF),
        w_send=sem(16),
        w_recv=sem(16),
        f_send=sem(16),
        f_recv=sem(16),
        x_buf=tile((2 * SPLIT,) + half, BF),
        n_buf=tile((2 * SPLIT,) + half, BF),
        g_buf=tile((2 * SPLIT,) + half, BF),
        x_send=sem(10),
        x_recv=sem(10),
        n_send=sem(10),
        n_recv=sem(10),
        g_send=sem(10),
        g_recv=sem(10),
        a_send=sem(10),
        a_recv=sem(10),
        part=tile((SPLIT, 2) + half, BF),
        from_x=tile((SPLIT,) + half, BF),
        from_z=tile((SPLIT,) + half, BF),
        s1=sem(8),
        r1=sem(8),
        s2=sem(8),
        r2=sem(8),
        s3=sem(8),
        r3=sem(8),
        s4=sem(8),
        r4=sem(8),
        m_acc=sum_tile((ITEMS, 4 * width), 4),
        m_land=sum_tile((ITEMS, 4 * width), 4),
        m_send=sem(6),
        m_recv=sem(6),
        e_acc=sum_tile((16, width), 5),
        e_land=sum_tile((16, width), 5),
        e_send=sem(6),
        e_recv=sem(6),
        l_acc=sum_tile((ITEMS, width), 5),
        l_land=sum_tile((ITEMS, width), 5),
        l_send=sem(6),
        l_recv=sem(6),
        h_acc=sum_tile((8, two), 2),
        h_land=sum_tile((8, two), 2),
        hz_send=sem(3),
        hz_recv=sem(3),
        h_send=sem(6),
        h_recv=sem(6),
        mod=tile((ITEMS, 4 * width), F32),
        pos_buf=tile((SPLIT, 8, tok_rows), F32),
        pos_send=sem(3),
        pos_recv=sem(3),
        cap_part=tile((4 * SPLIT,) + cap, BF),
        cap_fc=tile((2 * SPLIT,) + cap, BF),
        cap_fy=tile((SPLIT,) + cap, BF),
        cap_s=sem(2),
        cap_r=sem(2),
        cap_z=tile((SPLIT,) + cap, BF),
        cz_send=sem(4),
        cz_recv=sem(4),
        cap_kv=tile((lanes,) + cap, BF),
        ckv_send=sem(3),
        ckv_recv=sem(3),
        cap_hat=tile(cap, F32),
        cap_recip=tile(cap, F32),
        cap_k=tile((text, wq), BF),
        cap_v=tile((text, wq + HEAD), BF),
        items=tile((group, 1), jnp.int32),
        key_items=tile((lanes, 1, group), jnp.int32),
        key_cols=tile((lanes, group, 1), jnp.int32),
        cos_t=tile(both + (2 * HEAD,), F32),
        sin_t=tile(both + (2 * HEAD,), F32),
        norm_in=tile(both + (width,), BF),
        hat_in=tile(both + (width,), BF),
        kq_hat=tile(both + (two,), F32),
        kq_recip=tile(both + (two,), F32),
        kv=tile((lanes, group, two), BF),
        kv_send=sem(3),
        kv_recv=sem(3),
        k_all=tile((lanes, group, wq), BF),
        v_all=tile((lanes, group, wq + HEAD), BF),
        queries=tile((group, wq), BF),
        totals=tile((group, 128), F32),
        cross_logs=tile((group, 128), F32),
        attn_self=tile((group, wq), F32),
        attn_cross=tile((group, wq), F32),
        mix_s=tile((group, two), BF),
        gate_s=tile(both + (wf,), F32),
        up_s=tile(both + (wf,), F32),
        hid_s=tile(both + (wf,), BF),
        gg_s=tile(both + (wf,), BF),
        gu_s=tile(both + (wf,), BF),
        o_send=pltpu.SemaphoreType.DMA,
        o_recv=pltpu.SemaphoreType.DMA,
        dp_send=pltpu.SemaphoreType.DMA,
        dp_recv=pltpu.SemaphoreType.DMA,
        f_fc=tile((2 * SPLIT, row_dev, 3 * wf), BF),
        f_fy=tile((SPLIT, row_dev, 3 * wf), BF),
        f_s=sem(12),
        f_r=sem(12),
        a_part=tile((4 * SPLIT, row_dev, two), BF),
        a_fc=tile((2 * SPLIT, row_dev, two), BF),
        a_fy=tile((SPLIT, row_dev, two), BF),
        a_s=sem(12),
        a_r=sem(12),
        b_fc=tile((2 * SPLIT, row_dev, two), BF),
        b_fy=tile((SPLIT, row_dev, two), BF),
        b_s=sem(12),
        b_r=sem(12),
        kv_fc=tile((2, group, two), BF),
        kv_fy=tile((1, group, two), BF),
        kvh_s=sem(2),
        kvh_r=sem(2),
        t_part=tile((4,) + cap, BF),
        t_fc=tile((2,) + cap, BF),
        t_fy=tile((1,) + cap, BF),
        t_s=sem(2),
        t_r=sem(2),
        t_z=tile((SPLIT,) + cap, BF),
        tz_s=sem(3),
        tz_r=sem(3),
        ta_s=sem(3),
        ta_r=sem(3),
        dk_acc=tile((lanes, group, wq), F32),
        dv_acc=tile((lanes, group, wq), F32),
        dck_acc=tile((text, wq), F32),
        dcv_acc=tile((text, wq), F32),
        q_stack=tile((heads * tok_rows, wq), BF),
        c_stack=tile((heads * tok_rows, wq), BF),
        m_stack=tile((heads * tok_rows, wq), BF),
        dq_stack=tile((heads * tok_rows, wq), F32),
        dq_s=tile((group, wq), BF),
        dq_raw=tile((group, two), BF),
        dkv_raw=tile((group, two), BF),
    )
    shape = jax.ShapeDtypeStruct
    outs = dict(
        out_own=shape((rows, width), F32),
        out_half=shape((2, rows, width), BF),
        dp_own=shape((rows, width), F32),
        dp_half=shape((2, rows, width), BF),
        f_land=shape((SPLIT, row_dev, 3 * wf), BF),
        a_land=shape((SPLIT, row_dev, two), BF),
        b_land=shape((SPLIT, row_dev, two), BF),
        t_all=shape((lanes, SPLIT) + cap, BF),
        early=shape((16, width), F32),
        late=shape((8, width), F32),
        h_slots=shape((SPLIT, 8, two), F32),
        text=shape((text, feat_dev), BF),
    )
    vmem = pl.BlockSpec(memory_space=pltpu.VMEM)
    hbm = pl.BlockSpec(memory_space=pl.ANY)
    smem = pl.BlockSpec(memory_space=pltpu.SMEM)
    places = dict(caption=hbm, block_item=smem, item_band=smem, cross_gate=smem)
    names = list(ins) + list(outs) + list(scratch)
    results = pl.pallas_call(
        functools.partial(layer_kernel, names),
        out_shape=tuple(outs.values()),
        in_specs=[places.get(name, vmem) for name in ins],
        out_specs=[hbm if name.endswith("_land") else vmem for name in outs],
        scratch_shapes=list(scratch.values()),
        compiler_params=pltpu.CompilerParams(
            collective_id=1, has_side_effects=True, vmem_limit_bytes=VMEM_LIMIT
        ),
        name="layer",
    )(*ins.values())
    return dict(zip(outs, results))


def local_any(
    patches,
    caption,
    band_table,
    block_item,
    item_band,
    positions,
    out_grad,
    w_query,
    w_key,
    w_value,
    w_out,
    w_gate,
    w_up,
    w_down,
    w_ckey,
    w_cvalue,
    w_ada,
    b_ada,
    g_attn_in,
    g_attn_out,
    g_ffn_in,
    g_ffn_out,
    g_query,
    g_key,
    g_ckey,
    cross_gate,
):
    scale = 1.0 / math.sqrt(HEAD)
    rank = lax.axis_index("sp")
    half = lax.axis_index("tp")
    cycle = lax.axis_size("sp")
    halves = lax.axis_size("tp")
    lanes = cycle // SPLIT
    along_z, along_g = groups_of(cycle)
    my_z, my_g = rank // lanes, rank % lanes
    tok_rows, width = patches.shape
    own_rows = tok_rows // halves
    text_count = caption.shape[0]
    blocks_dev = tok_rows // BLK
    wq, wf = w_query.shape[1] // SPLIT, w_gate.shape[1] // SPLIT
    heads = wq // HEAD
    sizes = (wq, wq, wq, wq, wf, wf, wf)
    starts = [sum(sizes[:i]) for i in range(8)]

    def gather_z(block):
        return lax.all_gather(block, "sp", axis_index_groups=along_z, axis=0, tiled=False)

    def gather_g(block):
        return lax.all_gather(block, "sp", axis_index_groups=along_g, axis=0, tiled=False)

    def scatter_z(block):
        return lax.psum_scatter(
            block, "sp", axis_index_groups=along_z, scatter_dimension=0, tiled=False
        )

    def scatter_g(block):
        return lax.psum_scatter(
            block, "sp", axis_index_groups=along_g, scatter_dimension=0, tiled=False
        )

    def turn_z(block):
        return lax.all_to_all(
            block, "sp", 0, 0, axis_index_groups=along_z, tiled=True
        )

    def sum_g(block):
        return lax.psum(block, "sp", axis_index_groups=along_g)

    def gather_tokens(own):
        both = lax.all_gather(own, "tp", axis=0, tiled=True)
        return gather_z(both).reshape(SPLIT * tok_rows, -1)

    def scatter_tokens(part):
        part = part.astype(BF).reshape(SPLIT, halves, own_rows, width)
        mine = lax.psum_scatter(part, "tp", scatter_dimension=1, tiled=False)
        return scatter_z(mine.astype(BF)).astype(F32)

    def by_z(block):
        rows, cols = block.shape
        return block.reshape(rows, SPLIT, cols // SPLIT).transpose(1, 0, 2)

    shards = jnp.concatenate(
        [by_z(m) for m in (w_query, w_key, w_value, w_out.T, w_gate, w_up, w_down.T)], axis=2
    )
    rows_dev = shards.shape[1]
    merged = gather_g(turn_z(shards)).transpose(1, 0, 2, 3).reshape(cycle * rows_dev, -1)
    f_query, f_key, f_value, f_out, f_gate, f_up, f_down = (
        merged[:, starts[i] : starts[i + 1]] for i in range(7)
    )

    items_all = block_item.reshape(SPLIT, lanes, blocks_dev)
    grp_items = jnp.repeat(
        lax.dynamic_index_in_dim(items_all, my_g, 1, keepdims=False).reshape(-1), BLK
    )
    key_items = jnp.repeat(items_all.transpose(1, 0, 2).reshape(-1), BLK)
    row0 = half * own_rows

    def own_part(block):
        return lax.dynamic_slice_in_dim(block, row0, own_rows, 0)

    own_items = own_part(
        jnp.repeat(lax.dynamic_slice_in_dim(block_item, rank * blocks_dev, blocks_dev), BLK)
    )

    band_hot = (item_band[:, None] == jnp.arange(BANDS, dtype=jnp.int32)[None, :]).astype(F32)
    cond_pre = jnp.dot(band_hot, band_table, precision=HIGH)
    cond_sig = jax.nn.sigmoid(cond_pre)
    cond_low = (cond_pre * cond_sig).astype(BF)
    text_rows = w_ckey.shape[0]
    text_local = lax.dynamic_slice_in_dim(caption, rank * text_rows, text_rows, 1)
    modulation = lax.psum(bdot(cond_low, w_ada), "sp") + b_ada
    cap_part = jnp.stack([by_z(bdot(text_local, w_ckey)), by_z(bdot(text_local, w_cvalue))], 1)
    cap_raw = sum_g(scatter_z(cap_part))
    ckey_hat, ckey_recip = normed_pair(cap_raw[0].reshape(text_count, heads, HEAD))

    def per_head(vector):
        return lax.dynamic_slice_in_dim(vector, my_z * wq, wq, 0).reshape(heads, HEAD)

    gain_query, gain_key, gain_ckey = per_head(g_query), per_head(g_key), per_head(g_ckey)
    gate_tanh = jnp.tanh(lax.dynamic_slice_in_dim(cross_gate, my_z * heads, heads, 0))
    cap_keys = (ckey_hat * gain_ckey).astype(BF)
    cap_values = cap_raw[1].astype(BF).reshape(text_count, heads, HEAD)

    def of_items(rows, items):
        return jnp.where(items[:, None] == 0, rows[0], rows[1])

    mod_own = of_items(modulation, own_items)
    scale_attn, gate_attn, scale_ffn, gate_ffn = (
        mod_own[:, i * width : (i + 1) * width] for i in range(4)
    )
    group_rows = SPLIT * tok_rows

    patch_f = own_part(patches).astype(F32)
    grad_out = own_part(out_grad).astype(F32)
    hat_one, recip_one = normed_pair(patch_f)
    factor_one = g_attn_in * (1.0 + scale_attn)
    norm_in = gather_tokens((hat_one * factor_one).astype(BF))
    pos_all = gather_z(positions).transpose(1, 0, 2).reshape(2, group_rows)
    cos_row, sin_row, cos_col, sin_col = angles(pos_all)
    split_heads = (group_rows, heads, HEAD)
    query_raw = bdot(norm_in, f_query).reshape(split_heads)
    key_raw = bdot(norm_in, f_key).reshape(split_heads)
    values_low = bdot(norm_in, f_value).astype(BF)
    query_hat, query_recip = normed_pair(query_raw)
    queries = rotate(query_hat * gain_query, cos_row, sin_row, cos_col, sin_col).astype(BF)
    key_hat, key_recip = normed_pair(key_raw)
    keys_low = rotate(key_hat * gain_key, cos_row, sin_row, cos_col, sin_col).astype(BF)
    all_keys, all_values = (
        gather_g(block).reshape(lanes * group_rows, heads, HEAD)
        for block in (keys_low.reshape(group_rows, wq), values_low)
    )
    same = (grp_items[:, None] == key_items[None, :])[None]
    scores = jnp.einsum("qhd,khd->hqk", queries, all_keys, preferred_element_type=F32) * scale
    scores = jnp.where(same, scores, NEG)
    exps = jnp.exp(scores - jnp.max(scores, axis=-1, keepdims=True))
    probs = exps / jnp.sum(exps, axis=-1, keepdims=True)
    probs_low = probs.astype(BF)
    attn_self = jnp.einsum("hqk,khd->qhd", probs_low, all_values, preferred_element_type=F32)
    cross_scores = (
        jnp.einsum("qhd,khd->hqk", queries, cap_keys, preferred_element_type=F32) * scale
    )
    cross_exp = jnp.exp(cross_scores - jnp.max(cross_scores, axis=-1, keepdims=True))
    cross_probs = cross_exp / jnp.sum(cross_exp, axis=-1, keepdims=True)
    cross_low = cross_probs.astype(BF)
    attn_cross = jnp.einsum("hqk,khd->qhd", cross_low, cap_values, preferred_element_type=F32)
    mixed = (attn_self + gate_tanh[None, :, None] * attn_cross).astype(BF).reshape(group_rows, wq)
    attn_branch = scatter_tokens(dot_t(mixed, f_out))

    hat_two, recip_two = normed_pair(attn_branch)
    tanh_one = jnp.tanh(gate_attn)
    resid = patch_f + tanh_one * hat_two * g_attn_out
    hat_three, recip_three = normed_pair(resid)
    factor_three = g_ffn_in * (1.0 + scale_ffn)
    norm_ffn = gather_tokens((hat_three * factor_three).astype(BF))
    gate_val = bdot(norm_ffn, f_gate)
    up_val = bdot(norm_ffn, f_up)
    gate_sig = jax.nn.sigmoid(gate_val)
    hidden = (gate_val * gate_sig * up_val).astype(BF)
    ffn_branch = scatter_tokens(dot_t(hidden, f_down))
    hat_four, recip_four = normed_pair(ffn_branch)
    tanh_two = jnp.tanh(gate_ffn)
    output = resid + tanh_two * hat_four * g_ffn_out

    grad_gate_ffn = grad_out * hat_four * g_ffn_out * (1.0 - tanh_two * tanh_two)
    grad_four = grad_out * tanh_two
    grad_g_ffn_out = jnp.sum(grad_four * hat_four, axis=0)
    grad_ffn = gather_tokens(
        normed_back(grad_four * g_ffn_out, hat_four, recip_four).astype(BF)
    )
    grad_hidden = bdot(grad_ffn, f_down)
    grad_gate = (grad_hidden * up_val * gate_sig * (1.0 + gate_val * (1.0 - gate_sig))).astype(BF)
    grad_up = (grad_hidden * gate_val * gate_sig).astype(BF)
    grad_norm_ffn = scatter_tokens(dot_t(grad_gate, f_gate) + dot_t(grad_up, f_up))
    grad_scale_ffn = grad_norm_ffn * hat_three * g_ffn_in
    grad_g_ffn_in = jnp.sum(grad_norm_ffn * hat_three * (1.0 + scale_ffn), axis=0)
    grad_resid = grad_out + normed_back(grad_norm_ffn * factor_three, hat_three, recip_three)

    grad_gate_attn = grad_resid * hat_two * g_attn_out * (1.0 - tanh_one * tanh_one)
    grad_two = grad_resid * tanh_one
    grad_g_attn_out = jnp.sum(grad_two * hat_two, axis=0)
    grad_attn = gather_tokens(normed_back(grad_two * g_attn_out, hat_two, recip_two).astype(BF))
    grad_mixed = bdot(grad_attn, f_out).astype(BF).reshape(split_heads)
    grad_mixed_f = grad_mixed.astype(F32)
    grad_cross_gate = jnp.sum(grad_mixed_f * attn_cross, axis=(0, 2)) * (
        1.0 - gate_tanh * gate_tanh
    )
    grad_cross = (gate_tanh[None, :, None] * grad_mixed_f).astype(BF)
    grad_cprobs = jnp.einsum("qhd,khd->hqk", grad_cross, cap_values, preferred_element_type=F32)
    grad_cscores = (
        cross_probs * (grad_cprobs - jnp.sum(cross_probs * grad_cprobs, axis=-1, keepdims=True))
    ).astype(BF)
    query_grad = jnp.einsum("hqk,khd->qhd", grad_cscores, cap_keys, preferred_element_type=F32)
    grad_ckeys_part = (
        jnp.einsum("hqk,qhd->khd", grad_cscores, queries, preferred_element_type=F32) * scale
    )
    grad_cvals_part = jnp.einsum(
        "hqk,qhd->khd", cross_low, grad_cross, preferred_element_type=F32
    )
    row_delta = jnp.sum(grad_mixed_f * attn_self, axis=-1).T
    grad_probs = jnp.einsum("qhd,khd->hqk", grad_mixed, all_values, preferred_element_type=F32)
    grad_scores = (probs * (grad_probs - row_delta[..., None])).astype(BF)
    query_grad = query_grad + jnp.einsum(
        "hqk,khd->qhd", grad_scores, all_keys, preferred_element_type=F32
    )
    key_part = (
        jnp.einsum("hqk,qhd->khd", grad_scores, queries, preferred_element_type=F32) * scale
    )
    value_part = jnp.einsum("hqk,qhd->khd", probs_low, grad_mixed, preferred_element_type=F32)
    key_grad, value_grad = (
        scatter_g(block.astype(BF).reshape(lanes, group_rows, wq)) for block in (key_part, value_part)
    )
    grad_queries = (query_grad * scale).astype(BF).astype(F32)
    grad_qnorm = rotate(grad_queries, cos_row, -sin_row, cos_col, -sin_col)
    grad_g_query = jnp.sum(grad_qnorm * query_hat, axis=0).reshape(-1)
    grad_query_raw = (
        normed_back(grad_qnorm * gain_query, query_hat, query_recip).astype(BF).reshape(-1, wq)
    )
    grad_keys = key_grad.astype(F32).reshape(split_heads)
    grad_knorm = rotate(grad_keys, cos_row, -sin_row, cos_col, -sin_col)
    grad_g_key = jnp.sum(grad_knorm * key_hat, axis=0).reshape(-1)
    grad_key_raw = (
        normed_back(grad_knorm * gain_key, key_hat, key_recip).astype(BF).reshape(-1, wq)
    )
    grad_values = value_grad.astype(BF)
    grad_norm_in = scatter_tokens(
        dot_t(grad_query_raw, f_query) + dot_t(grad_key_raw, f_key) + dot_t(grad_values, f_value)
    )
    grad_scale_attn = grad_norm_in * hat_one * g_attn_in
    grad_g_attn_in = jnp.sum(grad_norm_in * hat_one * (1.0 + scale_attn), axis=0)
    grad_patches = grad_resid + normed_back(grad_norm_in * factor_one, hat_one, recip_one)

    grad_merged = jnp.concatenate(
        [
            t_dot(norm_in, grad_query_raw),
            t_dot(norm_in, grad_key_raw),
            t_dot(norm_in, grad_values),
            t_dot(grad_attn, mixed),
            t_dot(norm_ffn, grad_gate),
            t_dot(norm_ffn, grad_up),
            t_dot(grad_ffn, hidden),
        ],
        axis=1,
    ).astype(BF)
    grad_merged = grad_merged.reshape(SPLIT, lanes, rows_dev, -1).transpose(1, 0, 2, 3)
    shard_grads = turn_z(scatter_g(grad_merged)).astype(F32)
    (shard_query, shard_key, shard_value, shard_out, shard_gate, shard_up, shard_down) = (
        shard_grads[:, :, starts[i] : starts[i + 1]].transpose(1, 0, 2).reshape(rows_dev, -1)
        for i in range(7)
    )

    token_sums = lax.psum(
        (
            jnp.stack(
                [
                    jnp.concatenate(
                        [
                            jnp.sum(
                                jnp.where((own_items == item)[:, None], block, 0.0), axis=0
                            )
                            for block in (
                                grad_scale_attn,
                                grad_gate_attn,
                                grad_scale_ffn,
                                grad_gate_ffn,
                            )
                        ]
                    )
                    for item in range(ITEMS)
                ]
            ),
            grad_g_attn_in,
            grad_g_attn_out,
            grad_g_ffn_in,
            grad_g_ffn_out,
        ),
        ("sp", "tp"),
    )
    head_sums = jnp.concatenate([grad_g_query, grad_g_key, grad_cross_gate])
    head_sums = gather_z(sum_g(head_sums))
    grad_ckeys = sum_g(grad_ckeys_part).astype(BF).astype(F32)
    grad_cvals = sum_g(grad_cvals_part).astype(BF).reshape(text_count, wq)
    grad_g_ckey = gather_z(jnp.sum(grad_ckeys * ckey_hat, axis=0).reshape(-1)).reshape(-1)
    grad_ckey_raw = (
        normed_back(grad_ckeys * gain_ckey, ckey_hat, ckey_recip).astype(BF).reshape(text_count, wq)
    )
    cap_grads = gather_z(jnp.stack([grad_ckey_raw, grad_cvals])).transpose(1, 2, 0, 3)
    cap_grads = cap_grads.reshape(2, text_count, SPLIT * wq)
    grad_mod = token_sums[0]
    grad_b_ada = jnp.sum(grad_mod, axis=0)
    grad_w_ada = jnp.dot(cond_low.astype(F32).T, grad_mod, precision=HIGH)
    grad_cond_act = jnp.dot(grad_mod, w_ada.astype(F32).T, precision=HIGH)
    grad_cond_pre = grad_cond_act * cond_sig * (1.0 + cond_pre * (1.0 - cond_sig))
    grad_band_table = jnp.dot(band_hot.T, grad_cond_pre, precision=HIGH)
    return (
        lax.all_gather(output, "tp", axis=0, tiled=True),
        lax.all_gather(grad_patches, "tp", axis=0, tiled=True),
        shard_query,
        shard_key,
        shard_value,
        shard_out.T,
        shard_gate,
        shard_up,
        shard_down.T,
        t_dot(text_local, cap_grads[0]),
        t_dot(text_local, cap_grads[1]),
        grad_w_ada,
        grad_b_ada,
        token_sums[1],
        token_sums[2],
        token_sums[3],
        token_sums[4],
        head_sums[:, :wq].reshape(-1),
        head_sums[:, wq : 2 * wq].reshape(-1),
        grad_g_ckey,
        head_sums[:, 2 * wq :].reshape(-1),
        grad_band_table,
    )


def local(
    patches,
    caption,
    band_table,
    block_item,
    item_band,
    positions,
    out_grad,
    w_query,
    w_key,
    w_value,
    w_out,
    w_gate,
    w_up,
    w_down,
    w_ckey,
    w_cvalue,
    w_ada,
    b_ada,
    g_attn_in,
    g_attn_out,
    g_ffn_in,
    g_ffn_out,
    g_query,
    g_key,
    g_ckey,
    cross_gate,
):
    done = layer_call(
        dict(
            patches=patches,
            caption=caption,
            band_table=band_table,
            block_item=block_item,
            item_band=item_band,
            positions=positions,
            out_grad=out_grad,
            w_query=w_query,
            w_key=w_key,
            w_value=w_value,
            w_out=w_out.T,
            w_gate=w_gate,
            w_up=w_up,
            w_down=w_down.T,
            w_ckey=w_ckey,
            w_cvalue=w_cvalue,
            w_ada=w_ada,
            b_ada=b_ada,
            g_attn_in=g_attn_in,
            g_attn_out=g_attn_out,
            g_ffn_in=g_ffn_in,
            g_ffn_out=g_ffn_out,
            g_query=g_query,
            g_key=g_key,
            g_ckey=g_ckey,
            cross_gate=cross_gate,
        )
    )
    shape = jax.ShapeDtypeStruct
    like = lambda array: shape(array.shape, F32)
    vmem = pl.BlockSpec(memory_space=pltpu.VMEM)
    smem = pl.BlockSpec(memory_space=pltpu.SMEM)
    results = pl.pallas_call(
        finish_kernel,
        out_shape=(
            like(patches), like(patches), like(w_query), like(w_key), like(w_value), like(w_out.T),
            like(w_gate), like(w_up), like(w_down.T), like(w_ckey), like(w_cvalue), like(w_ada),
            like(b_ada), like(g_attn_in), like(g_attn_out), like(g_ffn_in), like(g_ffn_out),
            like(g_query), like(g_key), like(g_ckey), like(cross_gate), like(band_table),
        ),
        in_specs=[vmem] * 12 + [smem, vmem, smem, vmem],
        out_specs=[vmem] * 22,
        compiler_params=pltpu.CompilerParams(vmem_limit_bytes=VMEM_LIMIT),
        name="finish",
    )(*done.values(), cross_gate, band_table, item_band, w_ada)
    results = list(results)
    results[5], results[8] = results[5].T, results[8].T
    return tuple(results)


def solution(mesh):
    lanes = mesh.shape["sp"] // SPLIT
    body = local if lanes == 4 and mesh.shape["tp"] == 2 else local_any
    in_specs = (
        P("sp", None),
        P(),
        P(None, "sp"),
        P(),
        P(),
        P(None, "sp"),
        P("sp", None),
        P("sp", "tp"),
        P("sp", "tp"),
        P("sp", "tp"),
        P("tp", "sp"),
        P("sp", "tp"),
        P("sp", "tp"),
        P("tp", "sp"),
        P("sp", "tp"),
        P("sp", "tp"),
        P("sp", None),
        P(),
        P(),
        P(),
        P(),
        P(),
        P("tp"),
        P("tp"),
        P("tp"),
        P("tp"),
    )
    out_specs = (
        P("sp", None),
        P("sp", None),
        P("sp", "tp"),
        P("sp", "tp"),
        P("sp", "tp"),
        P("tp", "sp"),
        P("sp", "tp"),
        P("sp", "tp"),
        P("tp", "sp"),
        P("sp", "tp"),
        P("sp", "tp"),
        P("sp", None),
        P(),
        P(),
        P(),
        P(),
        P(),
        P("tp"),
        P("tp"),
        P("tp"),
        P("tp"),
        P(None, "sp"),
    )
    return jax.shard_map(body, mesh=mesh, in_specs=in_specs, out_specs=out_specs, check_vma=False)
```

```python
import functools
import math
from types import SimpleNamespace

import jax
import jax.numpy as jnp
from jax import lax
from jax.experimental import pallas as pl
from jax.experimental.pallas import tpu as pltpu
from jax.sharding import PartitionSpec as P

BANDS = 16
ITEMS = 2
BLK = 32
HEAD = 64
EPS = 1e-06
NEG = -1e30
FREQ_BASE = 10000.0
HIGH = lax.Precision.HIGHEST
BF = jnp.bfloat16
F32 = jnp.float32
SPLIT = 4


def groups_of(cycle_size):
    lanes = cycle_size // SPLIT
    along_z = [[z * lanes + g for z in range(SPLIT)] for g in range(lanes)]
    along_g = [[z * lanes + g for g in range(lanes)] for z in range(SPLIT)]
    return along_z, along_g


def normed_pair(value):
    recip = lax.rsqrt(jnp.mean(value * value, axis=-1, keepdims=True) + EPS)
    return value * recip, recip


def normed_back(grad_hat, normal, recip):
    return recip * (grad_hat - normal * jnp.mean(grad_hat * normal, axis=-1, keepdims=True))


def rotate(value, cos_row, sin_row, cos_col, sin_col):
    quarter = value.shape[-1] // 4
    part_a = value[..., :quarter]
    part_b = value[..., quarter : 2 * quarter]
    part_c = value[..., 2 * quarter : 3 * quarter]
    part_e = value[..., 3 * quarter :]
    return jnp.concatenate(
        [
            part_a * cos_row - part_b * sin_row,
            part_a * sin_row + part_b * cos_row,
            part_c * cos_col - part_e * sin_col,
            part_c * sin_col + part_e * cos_col,
        ],
        axis=-1,
    )


def angles(positions):
    quarter = HEAD // 4
    freqs = FREQ_BASE ** (-jnp.arange(quarter, dtype=F32) / quarter)
    row_angle = positions[0].astype(F32)[:, None] * freqs[None, :]
    col_angle = positions[1].astype(F32)[:, None] * freqs[None, :]
    return (
        jnp.cos(row_angle)[:, None, :],
        jnp.sin(row_angle)[:, None, :],
        jnp.cos(col_angle)[:, None, :],
        jnp.sin(col_angle)[:, None, :],
    )


def bdot(left, right):
    return jnp.dot(left, right, preferred_element_type=F32)


def dot_t(left, right):
    return lax.dot_general(left, right, (((1,), (1,)), ((), ())), preferred_element_type=F32)


def t_dot(left, right):
    return lax.dot_general(left, right, (((0,), (0,)), ((), ())), preferred_element_type=F32)


MESH = pl.DeviceIdType.MESH
VMEM_LIMIT = 63 * 2**20
NEAR = (1, 3, 2)


class Place:
    def __init__(self):
        rank = lax.axis_index("sp")
        self.lanes = lax.axis_size("sp") // SPLIT
        self.x = lax.axis_index("tp")
        self.z = rank // self.lanes
        self.g = rank % self.lanes
        self.x_peer = (rank, 1 - self.x)
        self.z_peer = {
            d: (lax.rem(self.z + d, SPLIT) * self.lanes + self.g, self.x) for d in (1, 2, 3)
        }
        self.z_pair = self.at_z(self.z + 1 - 2 * lax.rem(self.z, 2))
        self.z_far = self.z_peer[2]
        self.y, self.c = self.g // 2, self.g % 2
        self.g_y = (1 - self.y) * 2 + self.c
        self.g_c = self.y * 2 + 1 - self.c
        self.g_yc = (1 - self.y) * 2 + 1 - self.c
        self.y_peer = (self.z * self.lanes + self.g_y, self.x)
        self.c_peer = (self.z * self.lanes + self.g_c, self.x)

    def z_from(self, d):
        return lax.rem(self.z + SPLIT - d, SPLIT)

    def z_to(self, d):
        return lax.rem(self.z + d, SPLIT)


    def block(self, i):
        middle = lax.div(self.z * (3 - self.z), 2)
        near = i + middle * (1 - 2 * i) * (1 - lax.div(i, 2))
        return near + lax.div(self.z, 2) * (3 - 2 * near)

    def at_z(self, z):
        return (z * self.lanes + self.g, self.x)


def remote(src, dst, send, recv, peer):
    return pltpu.make_async_remote_copy(
        src_ref=src, dst_ref=dst, send_sem=send, recv_sem=recv, device_id=peer, device_id_type=MESH
    )


def as_index(i):
    return jnp.int32(i) if isinstance(i, int) else i


class Gather:
    def __init__(self, place, buf, send, recv):
        self.place, self.buf, self.send, self.recv = place, buf, send, recv
        self.own = buf.at[place.z * 2 + place.x]

    def to_right(self, z):
        place = self.place
        block = self.buf.at[z * 2 + place.x]
        steps = place.z - z
        return remote(
            block, block, self.send.at[steps], self.recv.at[3 + steps], place.at_z(place.z + 1)
        )

    def to_left(self, z):
        place = self.place
        block = self.buf.at[z * 2 + place.x]
        steps = z - place.z
        return remote(
            block, block, self.send.at[3 + steps], self.recv.at[steps], place.at_z(place.z - 1)
        )

    def to_x(self, z):
        block = self.buf.at[z * 2 + self.place.x]
        return remote(
            block, block, self.send.at[6 + z], self.recv.at[6 + z], self.place.x_peer
        )

    def landed(self, z, index):
        block = self.buf.at[z * 2 + self.place.x]
        return remote(block, block, self.send.at[index], self.recv.at[index], self.place.x_peer)

    def start(self):
        place = self.place

        @pl.when(place.z < 3)
        def _():
            self.to_right(place.z).start()

        @pl.when(place.z > 0)
        def _():
            self.to_left(place.z).start()

        self.to_x(place.z).start()

    def pass_on(self, i):
        place = self.place
        z = place.block(as_index(i))

        @pl.when(z < place.z)
        def _():
            self.landed(z, 2 + place.z - z).wait_recv()

            @pl.when(place.z < 3)
            def _():
                self.to_right(z).start()

        @pl.when(z > place.z)
        def _():
            self.landed(z, z - place.z - 1).wait_recv()

            @pl.when(place.z > 0)
            def _():
                self.to_left(z).start()

        self.to_x(z).start()

    def arrive(self, i):
        z = self.place.block(as_index(i))
        block = self.buf.at[z * 2 + 1 - self.place.x]
        remote(
            block, block, self.send.at[6 + z], self.recv.at[6 + z], self.place.x_peer
        ).wait_recv()

    def finish(self):
        place = self.place
        for z in range(SPLIT):

            @pl.when((z <= place.z) & (place.z < 3))
            def _():
                self.to_right(z).wait_send()

            @pl.when((z >= place.z) & (place.z > 0))
            def _():
                self.to_left(z).wait_send()

            self.to_x(z).wait_send()


class Scatter:
    def __init__(self, place, part, from_x, from_z, send, recv):
        self.place, self.part, self.from_x = place, part, from_x
        self.from_z, self.send, self.recv = from_z, send, recv

    def across(self, z):
        return remote(
            self.part.at[z, 1 - self.place.x],
            self.from_x.at[z],
            self.send.at[z],
            self.recv.at[z],
            self.place.x_peer,
        )

    def along(self, z):
        return remote(
            self.part.at[z, self.place.x],
            self.from_z.at[self.place.z],
            self.send.at[4 + z],
            self.recv.at[4 + self.place.z],
            self.place.at_z(z),
        )

    def pass_on(self, z):
        self.across(z).wait_recv()
        own = self.part[z, self.place.x].astype(F32)
        self.part[z, self.place.x] = (own + self.from_x[z].astype(F32)).astype(BF)
        self.along(z).start()

    def finish(self):
        place = self.place
        self.across(place.z).wait_recv()
        total = self.part[place.z, place.x].astype(F32) + self.from_x[place.z].astype(F32)
        for d in (1, 2, 3):
            z = place.z_to(d)
            block = self.from_z.at[z]
            remote(
                block, block, self.send.at[4 + z], self.recv.at[4 + z], place.at_z(z)
            ).wait_recv()
            total = total + self.from_z[z].astype(F32)
        return total

    def sent(self):
        for z in range(SPLIT):
            self.across(z).wait_send()
        for d in (1, 2, 3):
            self.along(self.place.z_to(d)).wait_send()


def flow(place, gather, work, carry, between=None):
    def step(i, carry):
        @pl.when(i < 3)
        def _():
            gather.pass_on(i + 1)

        gather.arrive(i)
        if between is not None:
            between(i)
        return work(place.block(i), carry)

    return lax.fori_loop(0, SPLIT, step, carry)


def flow_and_sum(place, gather, scatter, work, before=None):
    def start(i):
        scatter.across(place.block(jnp.int32(i))).start()

    def pass_on(i):
        scatter.pass_on(place.block(jnp.int32(i)))

    def begin(i):
        if before is not None:
            pl.when(i == 0)(before)

        @pl.when(i == 3)
        def _():
            start(2)
            start(1)

    def step(z, carry):
        work(z, carry)
        return carry

    flow(place, gather, step, 0, begin)
    start(3)
    pass_on(2)
    start(0)
    pass_on(1)
    pass_on(3)


def work_and_sum(place, scatter, work, carry):
    def step(i, carry):
        z = place.block(3 - i)
        carry = work(z, carry)
        scatter.across(z).start()

        @pl.when(i >= 1)
        def _():
            scatter.pass_on(place.block(4 - i))

        return carry

    return lax.fori_loop(0, SPLIT, step, carry)


class LaneGather:
    def __init__(self, place, buf, send, recv):
        own = buf.at[place.g]
        self.own = own
        self.to_y = remote(own, own, send.at[0], recv.at[0], place.y_peer)
        self.to_c = remote(own, own, send.at[1], recv.at[1], place.c_peer)
        across = buf.at[place.g_y]
        self.from_y = remote(across, across, send.at[2], recv.at[0], place.c_peer)
        self.on = remote(across, across, send.at[2], recv.at[2], place.c_peer)
        pair = buf.at[place.g_c]
        self.from_c = remote(pair, pair, send.at[1], recv.at[1], place.c_peer)
        diagonal = buf.at[place.g_yc]
        self.from_diagonal = remote(diagonal, diagonal, send.at[2], recv.at[2], place.c_peer)

    def start(self):
        self.to_y.start()
        self.to_c.start()

    def pass_on(self):
        self.from_y.wait_recv()
        self.on.start()

    def finish(self):
        self.from_c.wait_recv()
        self.from_diagonal.wait_recv()
        self.sent()

    def sent(self):
        self.to_y.wait_send()
        self.to_c.wait_send()
        self.on.wait_send()


class WeightGather:
    def __init__(self, place, shards, buf, send, recv):
        self.place, self.shards, self.buf = place, shards, buf
        self.send, self.recv = send, recv
        self.keep = pltpu.make_async_copy(
            shards.at[place.z], buf.at[place.z * place.lanes + place.g], recv.at[place.z]
        )

    def copy(self, z, g, sent, landed, peer):
        block = self.buf.at[z * self.place.lanes + g]
        return remote(block, block, self.send.at[sent + z], self.recv.at[landed + z], peer)

    def along(self, z):
        place = self.place
        return remote(
            self.shards.at[z],
            self.buf.at[place.z * place.lanes + place.g],
            self.send.at[z],
            self.recv.at[place.z],
            place.at_z(z),
        )

    def to_y(self, z):
        return self.copy(z, self.place.g, 4, 4, self.place.y_peer)

    def to_c(self, z):
        return self.copy(z, self.place.g, 8, 8, self.place.c_peer)

    def on(self, z):
        return self.copy(z, self.place.g_y, 12, 12, self.place.c_peer)

    def start(self, i):
        self.along(self.place.block(as_index(i))).start()

    def pass_own(self):
        self.keep.start()
        self.keep.wait()
        self.to_y(self.place.z).start()
        self.to_c(self.place.z).start()

    def pass_z(self, i):
        z = self.place.block(as_index(i))
        self.copy(z, self.place.g, 0, 0, self.place.x_peer).wait_recv()
        self.to_y(z).start()
        self.to_c(z).start()

    def pass_y(self, i):
        z = self.place.block(as_index(i))
        self.copy(z, self.place.g_y, 12, 4, self.place.c_peer).wait_recv()
        self.on(z).start()

    def finish(self):
        place = self.place
        for z in range(SPLIT):
            self.copy(z, place.g_c, 8, 8, place.c_peer).wait_recv()
            self.copy(z, place.g_yc, 12, 12, place.c_peer).wait_recv()
        for d in (1, 2, 3):
            self.along(place.z_to(d)).wait_send()
        for z in range(SPLIT):
            self.to_y(z).wait_send()
            self.to_c(z).wait_send()
            self.on(z).wait_send()


class AllSum:
    def __init__(self, peers, acc, land, send, recv):
        self.acc, self.land = acc, land
        self.pairs = [
            remote(acc.at[i], land.at[i], send.at[i], recv.at[i], peer)
            for i, peer in enumerate(peers)
        ]

    def start(self):
        self.pairs[0].start()

    def step(self):
        pair, *rest = self.pairs
        pair.wait_recv()
        pair.wait_send()
        i = self.acc.shape[0] - len(self.pairs)
        total = self.acc[i] + self.land[i]
        self.pairs = rest
        if rest:
            self.acc[i + 1] = total
            rest[0].start()
        return total


class LaneScatter:
    def __init__(self, place, part, from_c, from_y, send, recv):
        self.part, self.from_c, self.from_y = part, from_c, from_y
        self.count = count = from_y.shape[0]
        self.base = (place.c * 2 + place.y) * count
        self.away = (place.c * 2 + 1 - place.y) * count
        self.base_c, self.away_c = place.y * count, (1 - place.y) * count
        self.to_c = remote(
            part.at[pl.ds((1 - place.c) * 2 * count, 2 * count)],
            from_c,
            send.at[0],
            recv.at[0],
            place.c_peer,
        )
        self.to_y = remote(
            part.at[pl.ds(self.away, count)], from_y, send.at[1], recv.at[1], place.y_peer
        )
        self.own = part.at[pl.ds(self.base, count)]

    def start(self):
        self.to_c.start()

    def step(self):
        self.to_c.wait_recv()

        def add(i, carry):
            at = self.away + i
            near = self.part[at].astype(F32) + self.from_c[self.away_c + i].astype(F32)
            self.part[at] = near.astype(BF)
            return carry

        lax.fori_loop(0, self.count, add, 0)
        self.to_y.start()

    def finish(self):
        self.to_y.wait_recv()
        self.to_c.wait_send()

        def add(i, carry):
            at = self.base + i
            near = self.part[at].astype(F32) + self.from_c[self.base_c + i].astype(F32)
            self.part[at] = (near + self.from_y[i].astype(F32)).astype(BF)
            return carry

        lax.fori_loop(0, self.count, add, 0)
        self.to_y.wait_send()


class TurnZ:
    def __init__(self, place, out, base, land, send, recv):
        self.keep = pltpu.make_async_copy(
            out.at[base + place.z], land.at[place.z], send.at[3]
        )
        self.sends = [
            remote(
                out.at[base + place.z_to(d)],
                land.at[place.z],
                send.at[i],
                recv.at[i],
                place.z_peer[d],
            )
            for i, d in enumerate(NEAR)
        ]
        self.landed = []
        for i, d in enumerate(NEAR):
            slot = land.at[place.z_from(d)]
            self.landed.append(remote(slot, slot, send.at[i], recv.at[i], place.z_peer[d]))

    def start(self):
        for copy in self.sends:
            copy.start()
        self.keep.start()

    def finish(self):
        for copy in self.landed:
            copy.wait_recv()
        for copy in self.sends:
            copy.wait_send()
        self.keep.wait()


class HomeByZ:
    def __init__(self, place, part, from_c, from_y, land, send, recv):
        self.place, self.part, self.from_c, self.from_y = place, part, from_c, from_y
        self.land, self.send, self.recv = land, send, recv

    def blocks(self, at):
        return self.part.at[at, :, pl.ds(0, self.from_y.shape[2])]

    def to_c(self, z):
        place = self.place
        return remote(
            self.blocks(pl.ds(z * 4 + (1 - place.c) * 2, 2)),
            self.from_c.at[pl.ds(z * 2, 2)],
            self.send.at[z],
            self.recv.at[z],
            place.c_peer,
        )

    def to_y(self, z):
        place = self.place
        return remote(
            self.blocks(z * 4 + place.c * 2 + 1 - place.y),
            self.from_y.at[z],
            self.send.at[4 + z],
            self.recv.at[4 + z],
            place.y_peer,
        )

    def to_z(self, z):
        place = self.place
        return remote(
            self.blocks(z * 4 + place.c * 2 + place.y),
            self.land.at[place.z],
            self.send.at[8 + z],
            self.recv.at[8 + place.z],
            place.at_z(z),
        )

    def keep(self):
        place = self.place
        return pltpu.make_async_copy(
            self.blocks(place.z * 4 + place.c * 2 + place.y),
            self.land.at[place.z],
            self.recv.at[8 + place.z],
        )

    def start(self, z):
        self.to_c(z).start()

    def step(self, z):
        self.to_c(z).wait_recv()
        place = self.place
        at = z * 4 + place.c * 2 + 1 - place.y
        near = self.blocks(at)[...].astype(F32) + self.from_c[z * 2 + 1 - place.y].astype(F32)
        self.blocks(at)[...] = near.astype(BF)
        self.to_y(z).start()

    def leave(self, z):
        place = self.place
        self.to_y(z).wait_recv()
        at = z * 4 + place.c * 2 + place.y
        near = self.blocks(at)[...].astype(F32) + self.from_c[z * 2 + place.y].astype(F32)
        self.blocks(at)[...] = (near + self.from_y[z].astype(F32)).astype(BF)

        @pl.when(z == place.z)
        def _():
            self.keep().start()

        @pl.when(z != place.z)
        def _():
            self.to_z(z).start()

    def finish(self):
        place = self.place
        self.keep().wait()
        for d in (1, 2, 3):
            z = place.z_to(d)
            block = self.land.at[z]
            remote(
                block, block, self.send.at[8 + z], self.recv.at[8 + z], place.at_z(z)
            ).wait_recv()
            self.to_z(z).wait_send()
        for z in range(SPLIT):
            self.to_c(z).wait_send()
            self.to_y(z).wait_send()


class SpreadZ:
    def __init__(self, place, buf, send, recv):
        own = buf.at[place.z]
        self.own = own
        self.sends = [
            remote(own, own, send.at[i], recv.at[i], place.z_peer[d]) for i, d in enumerate(NEAR)
        ]
        self.landed = []
        for i, d in enumerate(NEAR):
            slot = buf.at[place.z_from(d)]
            self.landed.append(remote(slot, slot, send.at[i], recv.at[i], place.z_peer[d]))

    def start(self):
        for copy in self.sends:
            copy.start()

    def finish(self):
        for copy in self.landed:
            copy.wait_recv()
        for copy in self.sends:
            copy.wait_send()


def item_rows(mod, items, index, width):
    first = mod[0:1, index * width : (index + 1) * width]
    second = mod[1:2, index * width : (index + 1) * width]
    return jnp.where(items == 0, first, second)


def item_sums(value, items):
    return [
        jnp.sum(jnp.where(items == item, value, 0.0), axis=0, keepdims=True)
        for item in range(ITEMS)
    ]


def segments(lanes):
    row = lax.broadcasted_iota(jnp.int32, (lanes, lanes), 0) // HEAD
    col = lax.broadcasted_iota(jnp.int32, (lanes, lanes), 1) // HEAD
    return jnp.where(row == col, 1.0 / HEAD, 0.0).astype(F32)


def head_mean(value, mean):
    return jnp.dot(value, mean, precision=HIGH, preferred_element_type=F32)


def swap_quarters(value):
    lanes = value.shape[1]
    lane = lax.broadcasted_iota(jnp.int32, value.shape, 1)
    even = (lane // (HEAD // 4)) % 2 == 0
    return jnp.where(
        even, pltpu.roll(value, lanes - HEAD // 4, 1), pltpu.roll(value, HEAD // 4, 1)
    )


def head_lanes(shape, head):
    lane = lax.broadcasted_iota(jnp.int32, shape, 1)
    return (lane >= head * HEAD) & (lane < (head + 1) * HEAD)


def of_head(value, head):
    return jnp.where(head_lanes(value.shape, head), value, jnp.zeros_like(value))


def gate_lanes(cross_gate, z, wq):
    heads = wq // HEAD
    lane = lax.broadcasted_iota(jnp.int32, (1, wq), 1) // HEAD
    gates = jnp.zeros((1, wq), F32)
    for head in range(heads):
        gates = jnp.where(lane == head, cross_gate[z * heads + head], gates)
    return gates


def lane_order(g):
    return (g % 2) * 2 + g // 2


def layer_kernel(names, *refs):
    r = SimpleNamespace(**dict(zip(names, refs)))
    place = Place()
    z, g, x = place.z, place.g, place.x
    tok_rows, width = r.patches.shape
    rows = tok_rows // 2
    wq, wf = r.w_query.shape[1] // SPLIT, r.w_gate.shape[1] // SPLIT
    two = 2 * wq
    heads = wq // HEAD
    group = SPLIT * tok_rows
    scale = 1.0 / math.sqrt(HEAD)
    peers = [place.x_peer, place.c_peer, place.y_peer] + [place.z_peer[d] for d in (1, 2, 3)]
    barrier = pltpu.get_barrier_semaphore()
    for peer in peers:
        pl.semaphore_signal(barrier, inc=1, device_id=peer, device_id_type=MESH)

    text_cols = pl.ds(pl.multiple_of((z * place.lanes + g) * r.text.shape[1], 128), r.text.shape[1])
    text_copy = pltpu.make_async_copy(r.caption.at[:, text_cols], r.text, r.text_sem)
    text_copy.start()
    for i in range(SPLIT):
        at = slice(i * wq, (i + 1) * wq)
        r.qkvo_in[i, :, 0:wq] = r.w_key[:, at]
        r.qkvo_in[i, :, wq:two] = r.w_query[:, at]
        r.qkvo_in[i, :, two : two + wq] = r.w_out[:, at]
        r.qkvo_in[i, :, two + wq : 2 * two] = r.w_value[:, at]
    pl.semaphore_wait(barrier, len(peers))

    pre, sig = conditioning(r.band_table, r.item_band)
    act = jnp.concatenate([pre * sig, jnp.zeros((6, pre.shape[1]), F32)], axis=0).astype(BF)
    r.m_acc[0] = bdot(act, r.w_ada[...])[:ITEMS]
    along = [place.c_peer, place.y_peer, place.z_pair, place.z_far]
    sums = AllSum(along, r.m_acc, r.m_land, r.m_send, r.m_recv)
    sums.start()
    weights = WeightGather(place, r.qkvo_in, r.qkvo, r.w_send, r.w_recv)
    weights.start(1)
    mine = pl.ds(pl.multiple_of(x * rows, rows), rows)
    tokens = Gather(place, r.x_buf, r.x_send, r.x_recv)
    tokens.own[...] = r.patches[mine]
    tokens.start()
    for i in (2, 3):
        weights.start(i)
    spots = SpreadZ(place, r.pos_buf, r.pos_send, r.pos_recv)
    spots.own[...] = jnp.concatenate(
        [r.positions[...].astype(F32), jnp.zeros((6, tok_rows), F32)], axis=0
    )
    spots.start()
    weights.pass_own()
    sums.step()
    text_copy.wait()
    words = r.cap_part.shape[1]
    caption = LaneScatter(place, r.cap_part, r.cap_fc, r.cap_fy, r.cap_s, r.cap_r)
    for kind, matrix in enumerate((r.w_ckey, r.w_cvalue)):
        full = bdot(r.text[...], matrix[...]).astype(BF)
        for i in range(SPLIT):
            for lane_g in range(4):
                block = lane_order(lane_g) * SPLIT + i
                r.cap_part[block, :, kind * wq : (kind + 1) * wq] = full[
                    lane_g * words : (lane_g + 1) * words, i * wq : (i + 1) * wq
                ]
    caption.start()
    tokens.pass_on(1)
    weights.pass_z(1)
    sums.step()

    blocks = tok_rows // BLK
    token = lax.broadcasted_iota(jnp.int32, (group, 1), 0) // BLK
    key = lax.broadcasted_iota(jnp.int32, (1, 4 * group), 1) // BLK
    token_item = jnp.zeros((group, 1), jnp.int32)
    key_item = jnp.zeros((1, 4 * group), jnp.int32)
    for i in range(SPLIT):
        for j in range(blocks):
            own = r.block_item[(i * place.lanes + g) * blocks + j]
            token_item = jnp.where(token == i * blocks + j, own, token_item)
            for other in range(4):
                value = r.block_item[(i * place.lanes + other) * blocks + j]
                key_item = jnp.where(key == (other * SPLIT + i) * blocks + j, value, key_item)
    r.items[...] = token_item
    for i in range(4):
        r.key_items[i] = key_item[:, i * group : (i + 1) * group]
        column = jnp.zeros((group, 1), jnp.int32)
        for j in range(SPLIT * blocks):
            value = r.block_item[(j // blocks * place.lanes + i) * blocks + j % blocks]
            column = jnp.where(token == j, value, column)
        r.key_cols[i] = column
    for i in range(SPLIT):
        at = slice(i * wf, (i + 1) * wf)
        r.ffn_in[i, :, 0:wf] = r.w_gate[:, at]
        r.ffn_in[i, :, wf : 2 * wf] = r.w_up[:, at]
        r.ffn_in[i, :, 2 * wf : 3 * wf] = r.w_down[:, at]
    feed = WeightGather(place, r.ffn_in, r.ffn, r.f_send, r.f_recv)
    feed.start(1)
    tokens.pass_on(2)
    weights.pass_z(2)
    sums.step()

    own_at = pl.ds(pl.multiple_of(z * tok_rows + x * rows, rows), rows)

    mean = segments(two)
    mean_q = segments(wq)
    lane = lax.broadcasted_iota(jnp.int32, (1, two), 1)
    gain_in, gain_attn, gain_ffn, gain_out = (
        ref[...].reshape(1, width) for ref in (r.g_attn_in, r.g_attn_out, r.g_ffn_in, r.g_ffn_out)
    )

    def own_heads(ref):
        whole = ref[...].reshape(1, SPLIT * wq)
        part = whole[:, 0:wq]
        for i in range(1, SPLIT):
            part = jnp.where(z == i, whole[:, i * wq : (i + 1) * wq], part)
        return part

    gain_kq = jnp.concatenate([own_heads(r.g_key), own_heads(r.g_query)], axis=1)
    gain_ckey = own_heads(r.g_ckey)
    gain_ckey = jnp.concatenate([gain_ckey, jnp.zeros_like(gain_ckey)], axis=1)
    gates = jnp.tanh(gate_lanes(r.cross_gate, z, wq))
    lane_row = lax.broadcasted_iota(jnp.int32, (1, 2 * HEAD), 1)
    quarter = HEAD // 4
    freqs = jnp.ones((1, 2 * HEAD), F32)
    for i in range(1, quarter):
        freqs = jnp.where(lane_row % quarter == i, FREQ_BASE ** (-i / quarter), freqs)

    spots.finish()
    by_row = (lane_row // (HEAD // 2)) % 2 == 0
    sign = jnp.where((lane_row // (HEAD // 4)) % 2 == 0, -1.0, 1.0)
    for i in range(SPLIT):
        cols = r.pos_buf[i].T
        angle = jnp.where(by_row, cols[:, 0:1], cols[:, 1:2]) * freqs
        r.cos_t[i] = jnp.cos(angle)
        r.sin_t[i] = jnp.sin(angle) * sign

    tokens.pass_on(3)
    weights.pass_z(3)
    feed.start(2)
    feed.pass_own()
    for i in range(4):
        weights.pass_y(i)
    r.mod[...] = sums.step() + r.b_ada[...].reshape(1, 4 * width)
    for i in range(4):
        tokens.arrive(i)
    caption.step()
    weights.finish()

    keep = LaneGather(place, r.kv, r.kv_send, r.kv_recv)

    def span(i):
        return pl.ds(pl.multiple_of(i * tok_rows, tok_rows), tok_rows)

    def w_kq():
        return r.qkvo[:, :, 0:two].reshape(width, two)

    def w_ov():
        return r.qkvo[:, :, two : 2 * two].reshape(width, two)

    def project(i, carry):
        block = r.x_buf[pl.ds(i * 2, 2)].reshape(tok_rows, width).astype(F32)
        unit, _ = normed_pair(block)
        factor = gain_in * (1.0 + item_rows(r.mod, r.items[span(i)], 0, width))
        norm = (unit * factor).astype(BF)
        r.norm_in[i] = norm
        r.hat_in[i] = unit.astype(BF)
        raw = bdot(norm, w_kq())
        own_v = bdot(norm, w_ov())
        recip = lax.rsqrt(head_mean(raw * raw, mean) + EPS)
        hat = raw * recip
        r.kq_hat[i] = hat
        r.kq_recip[i] = recip
        cos = jnp.concatenate([r.cos_t[i]] * heads, axis=1)
        sin = jnp.concatenate([r.sin_t[i]] * heads, axis=1)
        gained = hat * gain_kq
        turned = gained * cos + swap_quarters(gained) * sin
        r.kv[g, span(i)] = jnp.where(lane < wq, turned, own_v).astype(BF)
        r.queries[span(i)] = (turned[:, wq:].astype(BF).astype(F32) * scale).astype(BF)
        return carry

    lax.fori_loop(0, SPLIT, project, 0)
    keep.start()

    caption.finish()
    cap_turn = TurnZ(place, r.cap_part, caption.base, r.cap_z, r.cz_send, r.cz_recv)
    cap_turn.start()
    slot_lane = lax.broadcasted_iota(jnp.int32, (1, r.totals.shape[1]), 1)
    ones = jnp.where(lax.broadcasted_iota(jnp.int32, (1, HEAD), 1) == 0, 1.0, 0.0).astype(BF)

    def with_ones(values):
        return jnp.concatenate([values, jnp.broadcast_to(ones, (values.shape[0], HEAD))], axis=1)

    def split_lump(index):
        lump = r.kv[index]
        r.k_all[index] = lump[:, :wq]
        r.v_all[index] = with_ones(lump[:, wq:])

    def attend(head, keys, values, same):
        scores = dot_t(of_head(r.queries[...], head), keys)
        if same is not None:
            scores = jnp.where(same, scores, NEG)
        out = bdot(jnp.exp(scores).astype(BF), values)
        return of_head(out[:, :wq], head), jnp.where(slot_lane == head, out[:, wq : wq + 1], 0.0)

    def cross(head, carry):
        out, total = attend(head, r.cap_k[...], r.cap_v[...], None)
        r.attn_cross[...] += out
        r.cross_logs[...] += total
        return carry

    def attend_into(index):
        def step(head, carry):
            same = r.items[...] == r.key_items[index]
            out, total = attend(head, r.k_all[index], r.v_all[index], same)
            r.attn_self[...] += out
            r.totals[...] += total
            return carry

        lax.fori_loop(0, heads, step, 0)

    for ref in (r.attn_self, r.attn_cross, r.totals, r.cross_logs):
        ref[...] = jnp.zeros_like(ref)
    split_lump(g)
    attend_into(g)
    feed.start(3)
    cap_turn.finish()
    cap_raw = (r.cap_z[0].astype(F32) + r.cap_z[1].astype(F32)) + (
        r.cap_z[2].astype(F32) + r.cap_z[3].astype(F32)
    )
    cap_recip = lax.rsqrt(head_mean(cap_raw * cap_raw, mean) + EPS)
    cap_hat = cap_raw * cap_recip
    r.cap_hat[...] = cap_hat
    r.cap_recip[...] = cap_recip
    cap_gather = LaneGather(place, r.cap_kv, r.ckv_send, r.ckv_recv)
    cap_gather.own[...] = jnp.where(lane < wq, cap_hat * gain_ckey, cap_raw).astype(BF)
    cap_gather.start()
    keep.from_c.wait_recv()
    split_lump(place.g_c)
    attend_into(place.g_c)
    cap_gather.pass_on()
    keep.pass_on()
    feed.pass_z(1)
    split_lump(place.g_y)
    attend_into(place.g_y)
    feed.pass_z(2)
    feed.pass_y(0)
    cap_gather.finish()
    kv_text = r.cap_kv[...].reshape(4 * words, two)
    r.cap_k[...] = kv_text[:, :wq]
    r.cap_v[...] = with_ones(kv_text[:, wq:])
    lax.fori_loop(0, heads, cross, 0)
    feed.pass_z(3)
    feed.pass_y(1)
    keep.from_diagonal.wait_recv()
    split_lump(place.g_yc)
    attend_into(place.g_yc)

    def by_total(out, totals):
        shares = jnp.zeros_like(out)
        for head in range(heads):
            share = 1.0 / totals[:, head : head + 1]
            shares = shares + of_head(jnp.broadcast_to(share, out.shape), head)
        return out * shares

    def blend(i, carry):
        at = span(i)
        self_part = by_total(r.attn_self[at], r.totals[at])
        cross_part = by_total(r.attn_cross[at], r.cross_logs[at])
        r.attn_self[at] = self_part
        r.attn_cross[at] = cross_part
        r.totals[at] = jnp.log(r.totals[at])
        r.cross_logs[at] = jnp.log(r.cross_logs[at])
        mixed = (self_part + gates * cross_part).astype(BF)
        wide = jnp.concatenate([mixed, jnp.zeros_like(mixed)], axis=1)
        r.mix_s[at] = wide
        r.part[i] = dot_t(wide, w_ov()).astype(BF).reshape(2, rows, width)
        return carry

    def scatter_of(send, recv):
        return Scatter(place, r.part, r.from_x, r.from_z, send, recv)

    out_sum = scatter_of(r.s1, r.r1)
    work_and_sum(place, out_sum, blend, 0)
    for i in (2, 3):
        feed.pass_y(i)
    branch = out_sum.finish()

    item = r.items[own_at]
    hat_two, recip_two = normed_pair(branch)
    tanh_one = jnp.tanh(item_rows(r.mod, item, 1, width))
    resid = r.patches[mine].astype(F32) + tanh_one * hat_two * gain_attn
    hat_three, recip_three = normed_pair(resid)
    factor_three = gain_ffn * (1.0 + item_rows(r.mod, item, 2, width))
    norms = Gather(place, r.n_buf, r.n_send, r.n_recv)
    norms.own[...] = (hat_three * factor_three).astype(BF)
    norms.start()
    out_sum.sent()
    tokens.finish()
    keep.sent()

    def f_weights(index):
        return r.ffn[:, :, index * wf : (index + 1) * wf].reshape(width, wf)

    def forward(i, carry):
        block = r.n_buf[pl.ds(i * 2, 2)].reshape(tok_rows, width)
        gate_val = bdot(block, f_weights(0))
        up_val = bdot(block, f_weights(1))
        r.gate_s[i] = gate_val
        r.up_s[i] = up_val
        hidden = (gate_val * jax.nn.sigmoid(gate_val) * up_val).astype(BF)
        r.hid_s[i] = hidden
        r.part[i] = dot_t(hidden, f_weights(2)).astype(BF).reshape(2, rows, width)
        return carry

    down = scatter_of(r.s2, r.r2)
    flow_and_sum(place, norms, down, forward, feed.finish)
    ffn = down.finish()
    norms.finish()

    hat_four, recip_four = normed_pair(ffn)
    tanh_two = jnp.tanh(item_rows(r.mod, item, 3, width))
    grad_out = r.out_grad[mine].astype(F32)
    grad_four = grad_out * tanh_two
    grads = Gather(place, r.g_buf, r.g_send, r.g_recv)
    grads.own[...] = normed_back(grad_four * gain_out, hat_four, recip_four).astype(BF)
    grads.start()
    down.sent()
    output = resid + tanh_two * hat_four * gain_out
    r.out_own[...] = output
    r.out_half[0] = output.astype(BF)
    out_copy = remote(r.out_half.at[0], r.out_half.at[1], r.o_send, r.o_recv, place.x_peer)
    everywhere = along[:2] + [place.x_peer] + along[2:]
    early = AllSum(everywhere, r.e_acc, r.e_land, r.e_send, r.e_recv)
    r.e_acc[0] = jnp.zeros(r.e_acc.shape[1:], F32)
    gate_sums = item_sums(grad_out * hat_four * gain_out * (1.0 - tanh_two * tanh_two), item)
    r.e_acc[0, 2:3] = jnp.sum(grad_four * hat_four, axis=0, keepdims=True)
    r.e_acc[0, 8:9] = gate_sums[0]
    r.e_acc[0, 9:10] = gate_sums[1]

    def backward(i, carry):
        block = r.g_buf[pl.ds(i * 2, 2)].reshape(tok_rows, width)
        grad_hidden = bdot(block, f_weights(2))
        gate_val = r.gate_s[i]
        gate_sig = jax.nn.sigmoid(gate_val)
        grad_gate = (
            grad_hidden * r.up_s[i] * gate_sig * (1.0 + gate_val * (1.0 - gate_sig))
        ).astype(BF)
        grad_up = (grad_hidden * gate_val * gate_sig).astype(BF)
        r.gg_s[i] = grad_gate
        r.gu_s[i] = grad_up
        r.part[i] = (
            (dot_t(grad_gate, f_weights(0)) + dot_t(grad_up, f_weights(1)))
            .astype(BF)
            .reshape(2, rows, width)
        )
        return carry

    back = scatter_of(r.s3, r.r3)
    flow_and_sum(place, grads, back, backward)

    block_rows = r.ffn.shape[1]
    step_cols = 4 * block_rows

    f_home = HomeByZ(place, r.ffn, r.f_fc, r.f_fy, r.f_land, r.f_s, r.f_r)

    def ffn_matrices(i, carry):
        target = place.block(3 - i)
        cols = pl.ds(pl.multiple_of(target * step_cols, step_cols), step_cols)
        norm = r.n_buf[:, :, cols].reshape(group, step_cols)
        grad = r.g_buf[:, :, cols].reshape(group, step_cols)
        for j, (left, right) in enumerate(((norm, r.gg_s), (norm, r.gu_s), (grad, r.hid_s))):
            block = t_dot(left, right[...].reshape(group, wf)).astype(BF)
            block = block.reshape(4, block_rows, wf)
            for other in range(4):
                at = target * 4 + lane_order(other)
                r.ffn[at, :, j * wf : (j + 1) * wf] = block[other]
        f_home.start(target)
        return carry

    lax.fori_loop(0, SPLIT, ffn_matrices, 0)
    f_home.step(place.block(jnp.int32(3)))
    grad_norm = back.finish()
    grads.finish()
    d_resid = grad_out + normed_back(grad_norm * factor_three, hat_three, recip_three)
    grad_two = d_resid * tanh_one
    attn_grads = Gather(place, r.x_buf, r.a_send, r.a_recv)
    attn_grads.own[...] = normed_back(grad_two * gain_attn, hat_two, recip_two).astype(BF)
    attn_grads.start()
    back.sent()
    r.dp_own[...] = d_resid
    scale_sums = item_sums(grad_norm * hat_three * gain_ffn, item)
    gate_sums = item_sums(d_resid * hat_two * gain_attn * (1.0 - tanh_one * tanh_one), item)
    r.e_acc[0, 0:1] = jnp.sum(grad_two * hat_two, axis=0, keepdims=True)
    r.e_acc[0, 1:2] = jnp.sum(
        grad_norm * hat_three * (1.0 + item_rows(r.mod, item, 2, width)), axis=0, keepdims=True
    )
    r.e_acc[0, 4:5] = gate_sums[0]
    r.e_acc[0, 5:6] = gate_sums[1]
    r.e_acc[0, 6:7] = scale_sums[0]
    r.e_acc[0, 7:8] = scale_sums[1]
    early.start()

    r.dk_acc[...] = jnp.zeros_like(r.dk_acc)
    r.dv_acc[...] = jnp.zeros_like(r.dv_acc)
    r.dck_acc[...] = jnp.zeros_like(r.dck_acc)
    r.dcv_acc[...] = jnp.zeros_like(r.dcv_acc)

    def attend_back(i, gate_sum):
        at = span(i)
        block = r.x_buf[pl.ds(i * 2, 2)].reshape(tok_rows, width)
        d_mix = bdot(block, w_ov())[:, :wq].astype(BF)
        mix_f = d_mix.astype(F32)
        d_cross = (gates * mix_f).astype(BF)
        delta = head_mean(mix_f * r.attn_self[at], mean_q) * HEAD
        gate_sum = gate_sum + jnp.sum(mix_f * r.attn_cross[at], axis=0, keepdims=True)
        query = r.queries[at]
        per_row = jnp.zeros((tok_rows, 128), F32)
        for head in range(heads):
            stack = slice(head * tok_rows, (head + 1) * tok_rows)
            r.q_stack[stack] = of_head(query, head)
            r.c_stack[stack] = of_head(d_cross, head)
            r.m_stack[stack] = of_head(d_mix, head)
            for part, column in enumerate(
                (
                    r.totals[at][:, head : head + 1],
                    delta[:, head * HEAD : head * HEAD + 1],
                    r.cross_logs[at][:, head : head + 1],
                )
            ):
                per_row = per_row + jnp.where(slot_lane == part * heads + head, column, 0.0)
        per_row = per_row.T
        logs, deltas, cross_logs = (
            jnp.concatenate(
                [per_row[part * heads + head : part * heads + head + 1] for head in range(heads)],
                axis=1,
            )
            for part in range(3)
        )
        item_row = jnp.concatenate(
            [r.key_items[g, :, pl.ds(pl.multiple_of(i * tok_rows, 128), tok_rows)]] * heads, axis=1
        )
        query_s, cross_s, mix_s = r.q_stack[...], r.c_stack[...], r.m_stack[...]
        probs = jnp.exp(dot_t(r.cap_k[...], query_s) - cross_logs)
        d_probs = dot_t(r.cap_v[:, :wq], cross_s)
        inner = jnp.sum(probs * d_probs, axis=0, keepdims=True)
        d_scores = (probs * (d_probs - inner)).astype(BF)
        r.dck_acc[...] += bdot(d_scores, query_s)
        r.dcv_acc[...] += bdot(probs.astype(BF), cross_s)
        r.dq_stack[...] = t_dot(d_scores, r.cap_k[...])

        def keys(j, carry):
            same = r.key_cols[j] == item_row
            scores = jnp.where(same, dot_t(r.k_all[j], query_s), NEG)
            probs = jnp.exp(scores - logs)
            d_probs = dot_t(r.v_all[j, :, :wq], mix_s)
            d_scores = (probs * (d_probs - deltas)).astype(BF)
            r.dk_acc[j] += bdot(d_scores, query_s)
            r.dv_acc[j] += bdot(probs.astype(BF), mix_s)
            r.dq_stack[...] += t_dot(d_scores, r.k_all[j])
            return carry

        lax.fori_loop(0, 4, keys, 0)
        dq = jnp.zeros((tok_rows, wq), F32)
        for head in range(heads):
            stack = slice(head * tok_rows, (head + 1) * tok_rows)
            dq = dq + of_head(r.dq_stack[stack], head)
        r.dq_s[at] = (dq * scale).astype(BF)
        return gate_sum

    def ffn_home(i):
        for step in range(4):

            @pl.when(i == step)
            def _():
                early.step()

        @pl.when(i < 3)
        def _():
            f_home.step(place.block(2 - i))

        @pl.when(i >= 1)
        def _():
            f_home.leave(place.block(4 - i))

    gate_sum = flow(place, attn_grads, attend_back, jnp.zeros((1, wq), F32), ffn_home)
    keys_home = LaneScatter(place, r.kv, r.kv_fc, r.kv_fy, r.kvh_s, r.kvh_r)

    def store_keys(i, carry):
        lane_c, lane_y = lax.rem(place.c + 1 + lax.div(i, 2), 2), lax.rem(i, 2)
        both = [r.dk_acc[lane_y * 2 + lane_c], r.dv_acc[lane_y * 2 + lane_c]]
        r.kv[lane_c * 2 + lane_y] = jnp.concatenate(both, axis=1).astype(BF)

        @pl.when(i == 1)
        def _():
            keys_home.start()

        return carry

    lax.fori_loop(0, 4, store_keys, 0)
    out_copy.start()
    cap_home = LaneScatter(place, r.t_part, r.t_fc, r.t_fy, r.t_s, r.t_r)
    for i in range(4):
        at = slice(i * words, (i + 1) * words)
        d_cap = jnp.concatenate([r.dck_acc[at], r.dcv_acc[at]], axis=1)
        r.t_part[lane_order(i)] = d_cap.astype(BF)
    cap_home.start()

    key_lanes = lane < wq

    def turn_back(i, grad):
        cos = jnp.concatenate([r.cos_t[i]] * heads, axis=1)
        sin = jnp.concatenate([r.sin_t[i]] * heads, axis=1)
        d_norm = grad * cos - swap_quarters(grad) * sin
        hat = r.kq_hat[i]
        gain_sum = jnp.sum(d_norm * hat, axis=0, keepdims=True)
        d_hat = d_norm * gain_kq
        grad = (r.kq_recip[i] * (d_hat - hat * head_mean(d_hat * hat, mean))).astype(BF)
        return grad, gain_sum

    def raw_queries(i, query_sum):
        d_query = r.dq_s[span(i)].astype(F32)
        d_query = jnp.concatenate([jnp.zeros_like(d_query), d_query], axis=1)
        grad, gain_sum = turn_back(i, d_query)
        r.dq_raw[span(i)] = grad
        return query_sum + gain_sum

    query_sum = lax.fori_loop(0, SPLIT, raw_queries, jnp.zeros((1, two), F32))
    keys_home.step()
    f_home.leave(place.block(jnp.int32(0)))

    def store_part(home, target, block):
        block = block.astype(BF).reshape(4, block_rows, two)
        for other in range(4):
            home.blocks(target * 4 + lane_order(other))[...] = block[other]
        home.start(target)

    a_home = HomeByZ(place, r.a_part, r.a_fc, r.a_fy, r.a_land, r.a_s, r.a_r)
    b_home = HomeByZ(place, r.qkvo, r.b_fc, r.b_fy, r.b_land, r.b_s, r.b_r)

    def matrices_oq(i, carry):
        target = place.block(3 - i)
        cols = pl.ds(pl.multiple_of(target * step_cols, step_cols), step_cols)
        above = r.x_buf[:, :, cols].reshape(group, step_cols)
        left = r.norm_in[:, :, cols].reshape(group, step_cols)
        store_part(a_home, target, t_dot(above, r.mix_s[...]) + t_dot(left, r.dq_raw[...]))
        return carry

    lax.fori_loop(0, SPLIT, matrices_oq, 0)
    cap_home.step()
    keys_home.finish()

    def raw_keys(i, carry):
        key_sum, first, second = carry
        total = r.kv[keys_home.base, span(i)].astype(F32)
        grad, gain_sum = turn_back(i, jnp.where(key_lanes, total, 0.0))
        r.dkv_raw[span(i)] = jnp.where(key_lanes, grad.astype(F32), total).astype(BF)
        d_kq = jnp.where(key_lanes, grad.astype(F32), r.dq_raw[span(i)].astype(F32)).astype(BF)
        d_ov = jnp.where(key_lanes, 0.0, total).astype(BF)
        d_norm = dot_t(d_kq, w_kq()) + dot_t(d_ov, w_ov())
        r.part[i] = d_norm.astype(BF).reshape(2, rows, width)
        by_item = item_sums(d_norm * r.hat_in[i].astype(F32), r.items[span(i)])
        return key_sum + gain_sum, first + by_item[0], second + by_item[1]

    in_sum = scatter_of(r.s4, r.r4)
    zeros = jnp.zeros((1, width), F32)
    key_sum, *item_parts = work_and_sum(
        place, in_sum, raw_keys, (jnp.zeros((1, two), F32), zeros, zeros)
    )
    late = AllSum(everywhere, r.l_acc, r.l_land, r.l_send, r.l_recv)
    r.l_acc[0] = jnp.concatenate(item_parts, axis=0)
    late.start()

    cap_home.finish()
    d_cap = r.t_part[cap_home.base].astype(F32)
    hat = r.cap_hat[...]
    cap_sum = jnp.sum(jnp.where(key_lanes, d_cap * hat, 0.0), axis=0, keepdims=True)
    d_hat = d_cap * jnp.where(key_lanes, gain_ckey, 0.0)
    d_raw = r.cap_recip[...] * (d_hat - hat * head_mean(d_hat * hat, mean))
    cap_spread = SpreadZ(place, r.t_z, r.tz_s, r.tz_r)
    cap_spread.own[...] = jnp.where(key_lanes, d_raw, d_cap).astype(BF)
    cap_spread.start()
    for i in range(4):
        a_home.step(place.block(jnp.int32(3 - i)))

    def matrices_kv(i, carry):
        target = place.block(3 - i)
        cols = pl.ds(pl.multiple_of(target * step_cols, step_cols), step_cols)
        left = r.norm_in[:, :, cols].reshape(group, step_cols)
        store_part(b_home, target, t_dot(left, r.dkv_raw[...]))
        return carry

    lax.fori_loop(0, SPLIT, matrices_kv, 0)
    heads_sum = AllSum(along[:2], r.h_acc, r.h_land, r.h_send, r.h_recv)
    r.h_acc[0] = jnp.zeros(r.h_acc.shape[1:], F32)
    r.h_acc[0, 0:1] = jnp.where(key_lanes, key_sum, query_sum)
    r.h_acc[0, 1:2] = cap_sum
    r.h_acc[0, 2:3] = jnp.concatenate([gate_sum, jnp.zeros_like(gate_sum)], axis=1)
    heads_sum.start()
    late.step()
    for i in range(4):
        b_home.step(place.block(jnp.int32(3 - i)))
    late.step()
    for i in range(4):
        a_home.leave(place.block(jnp.int32(3 - i)))

    d_norm = in_sum.finish()
    hat, recip = normed_pair(r.patches[mine].astype(F32))
    factor = 1.0 + item_rows(r.mod, item, 0, width)
    d_patches = r.dp_own[...] + normed_back(d_norm * gain_in * factor, hat, recip)
    r.dp_own[...] = d_patches
    r.dp_half[0] = d_patches.astype(BF)
    dp_copy = remote(r.dp_half.at[0], r.dp_half.at[1], r.dp_send, r.dp_recv, place.x_peer)
    dp_copy.start()
    in_sum.sent()
    late.step()
    heads_sum.step()
    for i in range(4):
        b_home.leave(place.block(jnp.int32(3 - i)))
    late.step()
    cap_spread.finish()
    cap_all = LaneGather(place, r.t_all, r.ta_s, r.ta_r)
    cap_all.own[...] = r.t_z[...]
    cap_all.start()
    heads_spread = SpreadZ(place, r.h_slots, r.hz_send, r.hz_recv)
    heads_spread.own[...] = heads_sum.step()
    heads_spread.start()
    total = late.step()
    cap_all.pass_on()
    factors = 1.0 + r.mod[:, 0:width]
    r.late[...] = jnp.concatenate(
        [
            jnp.sum(total * factors, axis=0, keepdims=True),
            total * gain_in,
            jnp.zeros((5, width), F32),
        ],
        axis=0,
    )
    out_copy.wait()
    attn_grads.finish()
    r.early[...] = early.step()
    heads_spread.finish()
    f_home.finish()
    a_home.finish()
    cap_all.finish()
    dp_copy.wait()
    b_home.finish()


def finish_kernel(
    out_own, out_half, dp_own, dp_half, f_land, a_land, b_land, t_all, early, late, heads_in, text,
    cross_gate, band_table, item_band, w_ada,
    output, d_patches, d_query, d_key, d_value, d_out, d_gate, d_up, d_down, d_ckey, d_cvalue,
    d_ada, d_b_ada, d_attn_in, d_attn_out, d_ffn_in, d_ffn_out, d_g_query, d_g_key, d_g_ckey,
    d_cross, d_band,
):
    x = lax.axis_index("tp")
    rows, width = out_own.shape
    wf = f_land.shape[2] // 3
    wq = a_land.shape[2] // 2
    words = t_all.shape[2]
    mine = pl.ds(pl.multiple_of(x * rows, rows), rows)
    other = pl.ds(pl.multiple_of((1 - x) * rows, rows), rows)
    output[mine] = out_own[...]
    output[other] = out_half[1].astype(F32)
    d_patches[mine] = dp_own[...]
    d_patches[other] = dp_half[1].astype(F32)
    for z in range(SPLIT):
        at = slice(z * wf, (z + 1) * wf)
        d_gate[:, at] = f_land[z, :, 0:wf].astype(F32)
        d_up[:, at] = f_land[z, :, wf : 2 * wf].astype(F32)
        d_down[:, at] = f_land[z, :, 2 * wf : 3 * wf].astype(F32)
        at = slice(z * wq, (z + 1) * wq)
        d_out[:, at] = a_land[z, :, 0:wq].astype(F32)
        d_query[:, at] = a_land[z, :, wq : 2 * wq].astype(F32)
        d_key[:, at] = b_land[z, :, 0:wq].astype(F32)
        d_value[:, at] = b_land[z, :, wq : 2 * wq].astype(F32)
        d_cap = t_dot(text[...], t_all[:, z].reshape(4 * words, 2 * wq))
        d_ckey[:, at] = d_cap[:, :wq]
        d_cvalue[:, at] = d_cap[:, wq:]
    grad_mod = jnp.concatenate([late[1:3], early[4:6], early[6:8], early[8:10]], axis=1)
    pre, sig = conditioning(band_table, item_band)
    low = (pre * sig).astype(BF).astype(F32)
    cols = jnp.concatenate([low, jnp.zeros((6, low.shape[1]), F32)], axis=0).T
    d_ada[...] = cols[:, 0:1] * grad_mod[0:1] + cols[:, 1:2] * grad_mod[1:2]
    d_act = lax.dot_general(
        grad_mod,
        w_ada[...].astype(F32),
        (((1,), (1,)), ((), ())),
        precision=HIGH,
        preferred_element_type=F32,
    )
    d_pre = d_act * sig * (1.0 + pre * (1.0 - sig))
    band = lax.broadcasted_iota(jnp.int32, (BANDS, 1), 0)
    d_band[...] = sum(
        jnp.where(band == item_band[i], d_pre[i : i + 1], 0.0) for i in range(ITEMS)
    )
    d_b_ada[...] = (grad_mod[0:1] + grad_mod[1:2]).reshape(d_b_ada.shape)
    d_attn_in[...] = late[0:1].reshape(d_attn_in.shape)
    d_attn_out[...] = early[0:1].reshape(d_attn_out.shape)
    d_ffn_in[...] = early[1:2].reshape(d_ffn_in.shape)
    d_ffn_out[...] = early[2:3].reshape(d_ffn_out.shape)

    def joined(row, part):
        return jnp.concatenate(
            [heads_in[z, row : row + 1, part * wq : (part + 1) * wq] for z in range(SPLIT)], axis=1
        ).reshape(d_g_key.shape)

    d_g_key[...] = joined(0, 0)
    d_g_query[...] = joined(0, 1)
    d_g_ckey[...] = joined(1, 0)
    heads = wq // HEAD
    lane = lax.broadcasted_iota(jnp.int32, (wq, 128), 0) // HEAD
    col = lax.broadcasted_iota(jnp.int32, (wq, 128), 1)
    total = jnp.zeros((8, 128), F32)
    for z in range(SPLIT):
        gate = jnp.tanh(gate_lanes(cross_gate, z, wq))
        terms = heads_in[z, 2:3, :wq] * (1.0 - gate * gate)
        terms = jnp.concatenate([terms, jnp.zeros((7, wq), F32)], axis=0)
        pick = jnp.where(col == lane + z * heads, 1.0, 0.0)
        total = total + jnp.dot(terms, pick, precision=HIGH, preferred_element_type=F32)
    d_cross[...] = total[0:1, : d_cross.shape[0]].reshape(d_cross.shape)


def conditioning(band_table, item_band):
    band = lax.broadcasted_iota(jnp.int32, (BANDS, 1), 0)
    table = band_table[...]
    pre = jnp.concatenate(
        [
            jnp.sum(jnp.where(band == item_band[i], table, 0.0), axis=0, keepdims=True)
            for i in range(ITEMS)
        ],
        axis=0,
    )
    return pre, jax.nn.sigmoid(pre)


def layer_call(ins):
    tok_rows, width = ins["patches"].shape
    rows = tok_rows // 2
    row_dev, q_cols = ins["w_query"].shape
    wq, wf = q_cols // SPLIT, ins["w_gate"].shape[1] // SPLIT
    two = 2 * wq
    heads = wq // HEAD
    lanes = 4
    group = SPLIT * tok_rows
    text, features = ins["caption"].shape
    words = text // lanes
    feat_dev = ins["w_ckey"].shape[0]
    mod = (ITEMS, 4 * width)
    tile, sem = pltpu.VMEM, lambda count: pltpu.SemaphoreType.DMA((count,))
    cap = (words, two)
    shard = (SPLIT, row_dev)
    both, half = (SPLIT, tok_rows), (rows, width)

    def sum_tile(size, steps):
        return tile((steps,) + size, F32)

    scratch = dict(
        text_sem=pltpu.SemaphoreType.DMA,
        qkvo_in=tile(shard + (2 * two,), BF),
        ffn_in=tile(shard + (3 * wf,), BF),
        qkvo=tile((SPLIT * lanes, row_dev, 2 * two), BF),
        ffn=tile((SPLIT * lanes, row_dev, 3 * wf), BF),
        w_send=sem(16),
        w_recv=sem(16),
        f_send=sem(16),
        f_recv=sem(16),
        x_buf=tile((2 * SPLIT,) + half, BF),
        n_buf=tile((2 * SPLIT,) + half, BF),
        g_buf=tile((2 * SPLIT,) + half, BF),
        x_send=sem(10),
        x_recv=sem(10),
        n_send=sem(10),
        n_recv=sem(10),
        g_send=sem(10),
        g_recv=sem(10),
        a_send=sem(10),
        a_recv=sem(10),
        part=tile((SPLIT, 2) + half, BF),
        from_x=tile((SPLIT,) + half, BF),
        from_z=tile((SPLIT,) + half, BF),
        s1=sem(8),
        r1=sem(8),
        s2=sem(8),
        r2=sem(8),
        s3=sem(8),
        r3=sem(8),
        s4=sem(8),
        r4=sem(8),
        m_acc=sum_tile((ITEMS, 4 * width), 4),
        m_land=sum_tile((ITEMS, 4 * width), 4),
        m_send=sem(6),
        m_recv=sem(6),
        e_acc=sum_tile((16, width), 5),
        e_land=sum_tile((16, width), 5),
        e_send=sem(6),
        e_recv=sem(6),
        l_acc=sum_tile((ITEMS, width), 5),
        l_land=sum_tile((ITEMS, width), 5),
        l_send=sem(6),
        l_recv=sem(6),
        h_acc=sum_tile((8, two), 2),
        h_land=sum_tile((8, two), 2),
        hz_send=sem(3),
        hz_recv=sem(3),
        h_send=sem(6),
        h_recv=sem(6),
        mod=tile((ITEMS, 4 * width), F32),
        pos_buf=tile((SPLIT, 8, tok_rows), F32),
        pos_send=sem(3),
        pos_recv=sem(3),
        cap_part=tile((4 * SPLIT,) + cap, BF),
        cap_fc=tile((2 * SPLIT,) + cap, BF),
        cap_fy=tile((SPLIT,) + cap, BF),
        cap_s=sem(2),
        cap_r=sem(2),
        cap_z=tile((SPLIT,) + cap, BF),
        cz_send=sem(4),
        cz_recv=sem(4),
        cap_kv=tile((lanes,) + cap, BF),
        ckv_send=sem(3),
        ckv_recv=sem(3),
        cap_hat=tile(cap, F32),
        cap_recip=tile(cap, F32),
        cap_k=tile((text, wq), BF),
        cap_v=tile((text, wq + HEAD), BF),
        items=tile((group, 1), jnp.int32),
        key_items=tile((lanes, 1, group), jnp.int32),
        key_cols=tile((lanes, group, 1), jnp.int32),
        cos_t=tile(both + (2 * HEAD,), F32),
        sin_t=tile(both + (2 * HEAD,), F32),
        norm_in=tile(both + (width,), BF),
        hat_in=tile(both + (width,), BF),
        kq_hat=tile(both + (two,), F32),
        kq_recip=tile(both + (two,), F32),
        kv=tile((lanes, group, two), BF),
        kv_send=sem(3),
        kv_recv=sem(3),
        k_all=tile((lanes, group, wq), BF),
        v_all=tile((lanes, group, wq + HEAD), BF),
        queries=tile((group, wq), BF),
        totals=tile((group, 128), F32),
        cross_logs=tile((group, 128), F32),
        attn_self=tile((group, wq), F32),
        attn_cross=tile((group, wq), F32),
        mix_s=tile((group, two), BF),
        gate_s=tile(both + (wf,), F32),
        up_s=tile(both + (wf,), F32),
        hid_s=tile(both + (wf,), BF),
        gg_s=tile(both + (wf,), BF),
        gu_s=tile(both + (wf,), BF),
        o_send=pltpu.SemaphoreType.DMA,
        o_recv=pltpu.SemaphoreType.DMA,
        dp_send=pltpu.SemaphoreType.DMA,
        dp_recv=pltpu.SemaphoreType.DMA,
        f_fc=tile((2 * SPLIT, row_dev, 3 * wf), BF),
        f_fy=tile((SPLIT, row_dev, 3 * wf), BF),
        f_s=sem(12),
        f_r=sem(12),
        a_part=tile((4 * SPLIT, row_dev, two), BF),
        a_fc=tile((2 * SPLIT, row_dev, two), BF),
        a_fy=tile((SPLIT, row_dev, two), BF),
        a_s=sem(12),
        a_r=sem(12),
        b_fc=tile((2 * SPLIT, row_dev, two), BF),
        b_fy=tile((SPLIT, row_dev, two), BF),
        b_s=sem(12),
        b_r=sem(12),
        kv_fc=tile((2, group, two), BF),
        kv_fy=tile((1, group, two), BF),
        kvh_s=sem(2),
        kvh_r=sem(2),
        t_part=tile((4,) + cap, BF),
        t_fc=tile((2,) + cap, BF),
        t_fy=tile((1,) + cap, BF),
        t_s=sem(2),
        t_r=sem(2),
        t_z=tile((SPLIT,) + cap, BF),
        tz_s=sem(3),
        tz_r=sem(3),
        ta_s=sem(3),
        ta_r=sem(3),
        dk_acc=tile((lanes, group, wq), F32),
        dv_acc=tile((lanes, group, wq), F32),
        dck_acc=tile((text, wq), F32),
        dcv_acc=tile((text, wq), F32),
        q_stack=tile((heads * tok_rows, wq), BF),
        c_stack=tile((heads * tok_rows, wq), BF),
        m_stack=tile((heads * tok_rows, wq), BF),
        dq_stack=tile((heads * tok_rows, wq), F32),
        dq_s=tile((group, wq), BF),
        dq_raw=tile((group, two), BF),
        dkv_raw=tile((group, two), BF),
    )
    shape = jax.ShapeDtypeStruct
    outs = dict(
        out_own=shape((rows, width), F32),
        out_half=shape((2, rows, width), BF),
        dp_own=shape((rows, width), F32),
        dp_half=shape((2, rows, width), BF),
        f_land=shape((SPLIT, row_dev, 3 * wf), BF),
        a_land=shape((SPLIT, row_dev, two), BF),
        b_land=shape((SPLIT, row_dev, two), BF),
        t_all=shape((lanes, SPLIT) + cap, BF),
        early=shape((16, width), F32),
        late=shape((8, width), F32),
        h_slots=shape((SPLIT, 8, two), F32),
        text=shape((text, feat_dev), BF),
    )
    vmem = pl.BlockSpec(memory_space=pltpu.VMEM)
    hbm = pl.BlockSpec(memory_space=pl.ANY)
    smem = pl.BlockSpec(memory_space=pltpu.SMEM)
    places = dict(caption=hbm, block_item=smem, item_band=smem, cross_gate=smem)
    names = list(ins) + list(outs) + list(scratch)
    results = pl.pallas_call(
        functools.partial(layer_kernel, names),
        out_shape=tuple(outs.values()),
        in_specs=[places.get(name, vmem) for name in ins],
        out_specs=[hbm if name.endswith("_land") else vmem for name in outs],
        scratch_shapes=list(scratch.values()),
        compiler_params=pltpu.CompilerParams(
            collective_id=1, has_side_effects=True, vmem_limit_bytes=VMEM_LIMIT
        ),
        name="layer",
    )(*ins.values())
    return dict(zip(outs, results))


def local_any(
    patches,
    caption,
    band_table,
    block_item,
    item_band,
    positions,
    out_grad,
    w_query,
    w_key,
    w_value,
    w_out,
    w_gate,
    w_up,
    w_down,
    w_ckey,
    w_cvalue,
    w_ada,
    b_ada,
    g_attn_in,
    g_attn_out,
    g_ffn_in,
    g_ffn_out,
    g_query,
    g_key,
    g_ckey,
    cross_gate,
):
    scale = 1.0 / math.sqrt(HEAD)
    rank = lax.axis_index("sp")
    half = lax.axis_index("tp")
    cycle = lax.axis_size("sp")
    halves = lax.axis_size("tp")
    lanes = cycle // SPLIT
    along_z, along_g = groups_of(cycle)
    my_z, my_g = rank // lanes, rank % lanes
    tok_rows, width = patches.shape
    own_rows = tok_rows // halves
    text_count = caption.shape[0]
    blocks_dev = tok_rows // BLK
    wq, wf = w_query.shape[1] // SPLIT, w_gate.shape[1] // SPLIT
    heads = wq // HEAD
    sizes = (wq, wq, wq, wq, wf, wf, wf)
    starts = [sum(sizes[:i]) for i in range(8)]

    def gather_z(block):
        return lax.all_gather(block, "sp", axis_index_groups=along_z, axis=0, tiled=False)

    def gather_g(block):
        return lax.all_gather(block, "sp", axis_index_groups=along_g, axis=0, tiled=False)

    def scatter_z(block):
        return lax.psum_scatter(
            block, "sp", axis_index_groups=along_z, scatter_dimension=0, tiled=False
        )

    def scatter_g(block):
        return lax.psum_scatter(
            block, "sp", axis_index_groups=along_g, scatter_dimension=0, tiled=False
        )

    def turn_z(block):
        return lax.all_to_all(
            block, "sp", 0, 0, axis_index_groups=along_z, tiled=True
        )

    def sum_g(block):
        return lax.psum(block, "sp", axis_index_groups=along_g)

    def gather_tokens(own):
        both = lax.all_gather(own, "tp", axis=0, tiled=True)
        return gather_z(both).reshape(SPLIT * tok_rows, -1)

    def scatter_tokens(part):
        part = part.astype(BF).reshape(SPLIT, halves, own_rows, width)
        mine = lax.psum_scatter(part, "tp", scatter_dimension=1, tiled=False)
        return scatter_z(mine.astype(BF)).astype(F32)

    def by_z(block):
        rows, cols = block.shape
        return block.reshape(rows, SPLIT, cols // SPLIT).transpose(1, 0, 2)

    shards = jnp.concatenate(
        [by_z(m) for m in (w_query, w_key, w_value, w_out.T, w_gate, w_up, w_down.T)], axis=2
    )
    rows_dev = shards.shape[1]
    merged = gather_g(turn_z(shards)).transpose(1, 0, 2, 3).reshape(cycle * rows_dev, -1)
    f_query, f_key, f_value, f_out, f_gate, f_up, f_down = (
        merged[:, starts[i] : starts[i + 1]] for i in range(7)
    )

    items_all = block_item.reshape(SPLIT, lanes, blocks_dev)
    grp_items = jnp.repeat(
        lax.dynamic_index_in_dim(items_all, my_g, 1, keepdims=False).reshape(-1), BLK
    )
    key_items = jnp.repeat(items_all.transpose(1, 0, 2).reshape(-1), BLK)
    row0 = half * own_rows

    def own_part(block):
        return lax.dynamic_slice_in_dim(block, row0, own_rows, 0)

    own_items = own_part(
        jnp.repeat(lax.dynamic_slice_in_dim(block_item, rank * blocks_dev, blocks_dev), BLK)
    )

    band_hot = (item_band[:, None] == jnp.arange(BANDS, dtype=jnp.int32)[None, :]).astype(F32)
    cond_pre = jnp.dot(band_hot, band_table, precision=HIGH)
    cond_sig = jax.nn.sigmoid(cond_pre)
    cond_low = (cond_pre * cond_sig).astype(BF)
    text_rows = w_ckey.shape[0]
    text_local = lax.dynamic_slice_in_dim(caption, rank * text_rows, text_rows, 1)
    modulation = lax.psum(bdot(cond_low, w_ada), "sp") + b_ada
    cap_part = jnp.stack([by_z(bdot(text_local, w_ckey)), by_z(bdot(text_local, w_cvalue))], 1)
    cap_raw = sum_g(scatter_z(cap_part))
    ckey_hat, ckey_recip = normed_pair(cap_raw[0].reshape(text_count, heads, HEAD))

    def per_head(vector):
        return lax.dynamic_slice_in_dim(vector, my_z * wq, wq, 0).reshape(heads, HEAD)

    gain_query, gain_key, gain_ckey = per_head(g_query), per_head(g_key), per_head(g_ckey)
    gate_tanh = jnp.tanh(lax.dynamic_slice_in_dim(cross_gate, my_z * heads, heads, 0))
    cap_keys = (ckey_hat * gain_ckey).astype(BF)
    cap_values = cap_raw[1].astype(BF).reshape(text_count, heads, HEAD)

    def of_items(rows, items):
        return jnp.where(items[:, None] == 0, rows[0], rows[1])

    mod_own = of_items(modulation, own_items)
    scale_attn, gate_attn, scale_ffn, gate_ffn = (
        mod_own[:, i * width : (i + 1) * width] for i in range(4)
    )
    group_rows = SPLIT * tok_rows

    patch_f = own_part(patches).astype(F32)
    grad_out = own_part(out_grad).astype(F32)
    hat_one, recip_one = normed_pair(patch_f)
    factor_one = g_attn_in * (1.0 + scale_attn)
    norm_in = gather_tokens((hat_one * factor_one).astype(BF))
    pos_all = gather_z(positions).transpose(1, 0, 2).reshape(2, group_rows)
    cos_row, sin_row, cos_col, sin_col = angles(pos_all)
    split_heads = (group_rows, heads, HEAD)
    query_raw = bdot(norm_in, f_query).reshape(split_heads)
    key_raw = bdot(norm_in, f_key).reshape(split_heads)
    values_low = bdot(norm_in, f_value).astype(BF)
    query_hat, query_recip = normed_pair(query_raw)
    queries = rotate(query_hat * gain_query, cos_row, sin_row, cos_col, sin_col).astype(BF)
    key_hat, key_recip = normed_pair(key_raw)
    keys_low = rotate(key_hat * gain_key, cos_row, sin_row, cos_col, sin_col).astype(BF)
    all_keys, all_values = (
        gather_g(block).reshape(lanes * group_rows, heads, HEAD)
        for block in (keys_low.reshape(group_rows, wq), values_low)
    )
    same = (grp_items[:, None] == key_items[None, :])[None]
    scores = jnp.einsum("qhd,khd->hqk", queries, all_keys, preferred_element_type=F32) * scale
    scores = jnp.where(same, scores, NEG)
    exps = jnp.exp(scores - jnp.max(scores, axis=-1, keepdims=True))
    probs = exps / jnp.sum(exps, axis=-1, keepdims=True)
    probs_low = probs.astype(BF)
    attn_self = jnp.einsum("hqk,khd->qhd", probs_low, all_values, preferred_element_type=F32)
    cross_scores = (
        jnp.einsum("qhd,khd->hqk", queries, cap_keys, preferred_element_type=F32) * scale
    )
    cross_exp = jnp.exp(cross_scores - jnp.max(cross_scores, axis=-1, keepdims=True))
    cross_probs = cross_exp / jnp.sum(cross_exp, axis=-1, keepdims=True)
    cross_low = cross_probs.astype(BF)
    attn_cross = jnp.einsum("hqk,khd->qhd", cross_low, cap_values, preferred_element_type=F32)
    mixed = (attn_self + gate_tanh[None, :, None] * attn_cross).astype(BF).reshape(group_rows, wq)
    attn_branch = scatter_tokens(dot_t(mixed, f_out))

    hat_two, recip_two = normed_pair(attn_branch)
    tanh_one = jnp.tanh(gate_attn)
    resid = patch_f + tanh_one * hat_two * g_attn_out
    hat_three, recip_three = normed_pair(resid)
    factor_three = g_ffn_in * (1.0 + scale_ffn)
    norm_ffn = gather_tokens((hat_three * factor_three).astype(BF))
    gate_val = bdot(norm_ffn, f_gate)
    up_val = bdot(norm_ffn, f_up)
    gate_sig = jax.nn.sigmoid(gate_val)
    hidden = (gate_val * gate_sig * up_val).astype(BF)
    ffn_branch = scatter_tokens(dot_t(hidden, f_down))
    hat_four, recip_four = normed_pair(ffn_branch)
    tanh_two = jnp.tanh(gate_ffn)
    output = resid + tanh_two * hat_four * g_ffn_out

    grad_gate_ffn = grad_out * hat_four * g_ffn_out * (1.0 - tanh_two * tanh_two)
    grad_four = grad_out * tanh_two
    grad_g_ffn_out = jnp.sum(grad_four * hat_four, axis=0)
    grad_ffn = gather_tokens(
        normed_back(grad_four * g_ffn_out, hat_four, recip_four).astype(BF)
    )
    grad_hidden = bdot(grad_ffn, f_down)
    grad_gate = (grad_hidden * up_val * gate_sig * (1.0 + gate_val * (1.0 - gate_sig))).astype(BF)
    grad_up = (grad_hidden * gate_val * gate_sig).astype(BF)
    grad_norm_ffn = scatter_tokens(dot_t(grad_gate, f_gate) + dot_t(grad_up, f_up))
    grad_scale_ffn = grad_norm_ffn * hat_three * g_ffn_in
    grad_g_ffn_in = jnp.sum(grad_norm_ffn * hat_three * (1.0 + scale_ffn), axis=0)
    grad_resid = grad_out + normed_back(grad_norm_ffn * factor_three, hat_three, recip_three)

    grad_gate_attn = grad_resid * hat_two * g_attn_out * (1.0 - tanh_one * tanh_one)
    grad_two = grad_resid * tanh_one
    grad_g_attn_out = jnp.sum(grad_two * hat_two, axis=0)
    grad_attn = gather_tokens(normed_back(grad_two * g_attn_out, hat_two, recip_two).astype(BF))
    grad_mixed = bdot(grad_attn, f_out).astype(BF).reshape(split_heads)
    grad_mixed_f = grad_mixed.astype(F32)
    grad_cross_gate = jnp.sum(grad_mixed_f * attn_cross, axis=(0, 2)) * (
        1.0 - gate_tanh * gate_tanh
    )
    grad_cross = (gate_tanh[None, :, None] * grad_mixed_f).astype(BF)
    grad_cprobs = jnp.einsum("qhd,khd->hqk", grad_cross, cap_values, preferred_element_type=F32)
    grad_cscores = (
        cross_probs * (grad_cprobs - jnp.sum(cross_probs * grad_cprobs, axis=-1, keepdims=True))
    ).astype(BF)
    query_grad = jnp.einsum("hqk,khd->qhd", grad_cscores, cap_keys, preferred_element_type=F32)
    grad_ckeys_part = (
        jnp.einsum("hqk,qhd->khd", grad_cscores, queries, preferred_element_type=F32) * scale
    )
    grad_cvals_part = jnp.einsum(
        "hqk,qhd->khd", cross_low, grad_cross, preferred_element_type=F32
    )
    row_delta = jnp.sum(grad_mixed_f * attn_self, axis=-1).T
    grad_probs = jnp.einsum("qhd,khd->hqk", grad_mixed, all_values, preferred_element_type=F32)
    grad_scores = (probs * (grad_probs - row_delta[..., None])).astype(BF)
    query_grad = query_grad + jnp.einsum(
        "hqk,khd->qhd", grad_scores, all_keys, preferred_element_type=F32
    )
    key_part = (
        jnp.einsum("hqk,qhd->khd", grad_scores, queries, preferred_element_type=F32) * scale
    )
    value_part = jnp.einsum("hqk,qhd->khd", probs_low, grad_mixed, preferred_element_type=F32)
    key_grad, value_grad = (
        scatter_g(block.astype(BF).reshape(lanes, group_rows, wq)) for block in (key_part, value_part)
    )
    grad_queries = (query_grad * scale).astype(BF).astype(F32)
    grad_qnorm = rotate(grad_queries, cos_row, -sin_row, cos_col, -sin_col)
    grad_g_query = jnp.sum(grad_qnorm * query_hat, axis=0).reshape(-1)
    grad_query_raw = (
        normed_back(grad_qnorm * gain_query, query_hat, query_recip).astype(BF).reshape(-1, wq)
    )
    grad_keys = key_grad.astype(F32).reshape(split_heads)
    grad_knorm = rotate(grad_keys, cos_row, -sin_row, cos_col, -sin_col)
    grad_g_key = jnp.sum(grad_knorm * key_hat, axis=0).reshape(-1)
    grad_key_raw = (
        normed_back(grad_knorm * gain_key, key_hat, key_recip).astype(BF).reshape(-1, wq)
    )
    grad_values = value_grad.astype(BF)
    grad_norm_in = scatter_tokens(
        dot_t(grad_query_raw, f_query) + dot_t(grad_key_raw, f_key) + dot_t(grad_values, f_value)
    )
    grad_scale_attn = grad_norm_in * hat_one * g_attn_in
    grad_g_attn_in = jnp.sum(grad_norm_in * hat_one * (1.0 + scale_attn), axis=0)
    grad_patches = grad_resid + normed_back(grad_norm_in * factor_one, hat_one, recip_one)

    grad_merged = jnp.concatenate(
        [
            t_dot(norm_in, grad_query_raw),
            t_dot(norm_in, grad_key_raw),
            t_dot(norm_in, grad_values),
            t_dot(grad_attn, mixed),
            t_dot(norm_ffn, grad_gate),
            t_dot(norm_ffn, grad_up),
            t_dot(grad_ffn, hidden),
        ],
        axis=1,
    ).astype(BF)
    grad_merged = grad_merged.reshape(SPLIT, lanes, rows_dev, -1).transpose(1, 0, 2, 3)
    shard_grads = turn_z(scatter_g(grad_merged)).astype(F32)
    (shard_query, shard_key, shard_value, shard_out, shard_gate, shard_up, shard_down) = (
        shard_grads[:, :, starts[i] : starts[i + 1]].transpose(1, 0, 2).reshape(rows_dev, -1)
        for i in range(7)
    )

    token_sums = lax.psum(
        (
            jnp.stack(
                [
                    jnp.concatenate(
                        [
                            jnp.sum(
                                jnp.where((own_items == item)[:, None], block, 0.0), axis=0
                            )
                            for block in (
                                grad_scale_attn,
                                grad_gate_attn,
                                grad_scale_ffn,
                                grad_gate_ffn,
                            )
                        ]
                    )
                    for item in range(ITEMS)
                ]
            ),
            grad_g_attn_in,
            grad_g_attn_out,
            grad_g_ffn_in,
            grad_g_ffn_out,
        ),
        ("sp", "tp"),
    )
    head_sums = jnp.concatenate([grad_g_query, grad_g_key, grad_cross_gate])
    head_sums = gather_z(sum_g(head_sums))
    grad_ckeys = sum_g(grad_ckeys_part).astype(BF).astype(F32)
    grad_cvals = sum_g(grad_cvals_part).astype(BF).reshape(text_count, wq)
    grad_g_ckey = gather_z(jnp.sum(grad_ckeys * ckey_hat, axis=0).reshape(-1)).reshape(-1)
    grad_ckey_raw = (
        normed_back(grad_ckeys * gain_ckey, ckey_hat, ckey_recip).astype(BF).reshape(text_count, wq)
    )
    cap_grads = gather_z(jnp.stack([grad_ckey_raw, grad_cvals])).transpose(1, 2, 0, 3)
    cap_grads = cap_grads.reshape(2, text_count, SPLIT * wq)
    grad_mod = token_sums[0]
    grad_b_ada = jnp.sum(grad_mod, axis=0)
    grad_w_ada = jnp.dot(cond_low.astype(F32).T, grad_mod, precision=HIGH)
    grad_cond_act = jnp.dot(grad_mod, w_ada.astype(F32).T, precision=HIGH)
    grad_cond_pre = grad_cond_act * cond_sig * (1.0 + cond_pre * (1.0 - cond_sig))
    grad_band_table = jnp.dot(band_hot.T, grad_cond_pre, precision=HIGH)
    return (
        lax.all_gather(output, "tp", axis=0, tiled=True),
        lax.all_gather(grad_patches, "tp", axis=0, tiled=True),
        shard_query,
        shard_key,
        shard_value,
        shard_out.T,
        shard_gate,
        shard_up,
        shard_down.T,
        t_dot(text_local, cap_grads[0]),
        t_dot(text_local, cap_grads[1]),
        grad_w_ada,
        grad_b_ada,
        token_sums[1],
        token_sums[2],
        token_sums[3],
        token_sums[4],
        head_sums[:, :wq].reshape(-1),
        head_sums[:, wq : 2 * wq].reshape(-1),
        grad_g_ckey,
        head_sums[:, 2 * wq :].reshape(-1),
        grad_band_table,
    )


def local(
    patches,
    caption,
    band_table,
    block_item,
    item_band,
    positions,
    out_grad,
    w_query,
    w_key,
    w_value,
    w_out,
    w_gate,
    w_up,
    w_down,
    w_ckey,
    w_cvalue,
    w_ada,
    b_ada,
    g_attn_in,
    g_attn_out,
    g_ffn_in,
    g_ffn_out,
    g_query,
    g_key,
    g_ckey,
    cross_gate,
):
    done = layer_call(
        dict(
            patches=patches,
            caption=caption,
            band_table=band_table,
            block_item=block_item,
            item_band=item_band,
            positions=positions,
            out_grad=out_grad,
            w_query=w_query,
            w_key=w_key,
            w_value=w_value,
            w_out=w_out.T,
            w_gate=w_gate,
            w_up=w_up,
            w_down=w_down.T,
            w_ckey=w_ckey,
            w_cvalue=w_cvalue,
            w_ada=w_ada,
            b_ada=b_ada,
            g_attn_in=g_attn_in,
            g_attn_out=g_attn_out,
            g_ffn_in=g_ffn_in,
            g_ffn_out=g_ffn_out,
            g_query=g_query,
            g_key=g_key,
            g_ckey=g_ckey,
            cross_gate=cross_gate,
        )
    )
    shape = jax.ShapeDtypeStruct
    like = lambda array: shape(array.shape, F32)
    vmem = pl.BlockSpec(memory_space=pltpu.VMEM)
    smem = pl.BlockSpec(memory_space=pltpu.SMEM)
    results = pl.pallas_call(
        finish_kernel,
        out_shape=(
            like(patches), like(patches), like(w_query), like(w_key), like(w_value), like(w_out.T),
            like(w_gate), like(w_up), like(w_down.T), like(w_ckey), like(w_cvalue), like(w_ada),
            like(b_ada), like(g_attn_in), like(g_attn_out), like(g_ffn_in), like(g_ffn_out),
            like(g_query), like(g_key), like(g_ckey), like(cross_gate), like(band_table),
        ),
        in_specs=[vmem] * 12 + [smem, vmem, smem, vmem],
        out_specs=[vmem] * 22,
        compiler_params=pltpu.CompilerParams(vmem_limit_bytes=VMEM_LIMIT),
        name="finish",
    )(*done.values(), cross_gate, band_table, item_band, w_ada)
    results = list(results)
    results[5], results[8] = results[5].T, results[8].T
    return tuple(results)


def solution(mesh):
    lanes = mesh.shape["sp"] // SPLIT
    body = local if lanes == 4 and mesh.shape["tp"] == 2 else local_any
    in_specs = (
        P("sp", None),
        P(),
        P(None, "sp"),
        P(),
        P(),
        P(None, "sp"),
        P("sp", None),
        P("sp", "tp"),
        P("sp", "tp"),
        P("sp", "tp"),
        P("tp", "sp"),
        P("sp", "tp"),
        P("sp", "tp"),
        P("tp", "sp"),
        P("sp", "tp"),
        P("sp", "tp"),
        P("sp", None),
        P(),
        P(),
        P(),
        P(),
        P(),
        P("tp"),
        P("tp"),
        P("tp"),
        P("tp"),
    )
    out_specs = (
        P("sp", None),
        P("sp", None),
        P("sp", "tp"),
        P("sp", "tp"),
        P("sp", "tp"),
        P("tp", "sp"),
        P("sp", "tp"),
        P("sp", "tp"),
        P("tp", "sp"),
        P("sp", "tp"),
        P("sp", "tp"),
        P("sp", None),
        P(),
        P(),
        P(),
        P(),
        P(),
        P("tp"),
        P("tp"),
        P("tp"),
        P("tp"),
        P(None, "sp"),
    )
    return jax.shard_map(body, mesh=mesh, in_specs=in_specs, out_specs=out_specs, check_vma=False)
```
